32 devices in a mesh: fact: 8 (over z, y), feat: 4 (over x, core).
Axes of the slice: x: 2, y: 2, z: 4, core: 2. Of those that a mesh axis runs over, the one named last changes fastest.
Arguments:
- fact_x: bfloat16 [8192, 512], P('fact', 'feat'), may hold values from -6 to 6
- dim_owner: int32 [8192, 1], P('fact'), may hold values from 0 to 7; in each aligned block of 1024 rows (0 to 1023, 1024 to 2047, ...) at most 384 rows name the same one
- dim_slot: int32 [8192], P('fact'), may hold values from 0 to 1023
- fact_owner: int32 [8192, 1], P('fact'), may hold values from 0 to 7; in each aligned block of 1024 rows (0 to 1023, 1024 to 2047, ...) at most 384 rows name the same one
- fact_slot: int32 [8192], P('fact'), may hold values from 0 to 127
- dim_table: bfloat16 [8192, 512], P('fact', 'feat'), may hold values from -6 to 6
- entity_h: bfloat16 [1024, 512], P('fact', 'feat'), may hold values from -6 to 6
- w_msg: bfloat16 [512, 512], P(None, 'feat'), may hold values from -0.25 to 0.25
- w_self: bfloat16 [512, 512], P(None, 'feat'), may hold values from -0.25 to 0.25
- w_neigh: bfloat16 [512, 512], P(None, 'feat'), may hold values from -0.25 to 0.25
- cotangent: bfloat16 [1024, 512], P('fact', 'feat'), may hold values from -0.59765625 to 0.59765625
Outputs:
- output_h: bfloat16 [1024, 512], P('fact', 'feat')
- grad_w_msg: float32 [512, 512], P('fact', 'feat')
- grad_w_self: float32 [512, 512], P('fact', 'feat')
- grad_w_neigh: float32 [512, 512], P('fact', 'feat')
- grad_dim: float32 [8192, 512], P('fact', 'feat')
The draws below stay inside these ranges and needn't reach their ends.
Inputs may be any that keep to these rules, and one draw needn't show every extreme that they name: `fact_owner`: among the fact rows of one index of fact, no key range is named by more than 384 rows, and some key range by exactly 384. `dim_owner`: among the fact rows of one index of fact, no block of the dimension table is named by more than 384 rows, and some block by exactly 384.
All inputs are finite; a program needn't handle non-finite values.
Results may differ from the reference program's by a relative error of at most 0.0059.
Values may be sent and summed in bfloat16 or wider, within the bound.
No kernel may reach another device: no remote copies, remote signals or barrier semaphores. Data moves between devices by JAX's collectives and lax.ppermute only.
A program may use at most 64 MiB of HBM per device.

```python
import math
import jax
import jax.numpy as jnp
import numpy as np

D = 512
DIM_ROWS = 8192
F_DEV = 1024
E_DEV = 128
FACTS = 8192
ENTITIES = 1024
OWNERS = 8
CAP = 384
N_FACT = 8


def touch_ends(entries, key, smallest, high):
    longest = entries.shape.index(max(entries.shape))
    spots = []
    for shift in (0, 1):
        where = [jax.random.randint(jax.random.fold_in(key, axis), (), 0, length) for axis, length in enumerate(entries.shape)]
        where[longest] = (where[longest] + shift) % entries.shape[longest]
        spots.append(tuple(where))
    return entries.at[spots[0]].set(smallest).at[spots[1]].set(high)


def with_spikes(array, rng, source, target, blocks, factor):
    def block_of(dim):
        return (jnp.arange(array.shape[dim]) // (array.shape[dim] // blocks)).reshape((-1,) + (1,) * (array.ndim - 1 - dim))

    first = jax.random.permutation(rng, blocks)[block_of(target)]
    other_side = (block_of(target) + blocks // 2) % blocks
    return jnp.where((block_of(source) == first) | (block_of(source) == other_side), factor * array, array)


def block_levels(stream_key, extent, split, least, high):
    loudness = 1.0
    for position, parts in split:
        heights = jax.random.uniform(jax.random.fold_in(jax.random.fold_in(stream_key, 6), position), (parts,), jnp.float32, least / len(split), high / len(split))
        loudness = loudness * jnp.repeat(jnp.exp(heights), extent[position] // parts).reshape((-1,) + (1,) * (len(extent) - 1 - position))
    return loudness


def deal_out(own_key, own, number, rows, amount, top, bound, skew):
    order = jax.random.permutation(own_key, amount)
    heavy_load, common = portions_of(amount, rows * top, bound, skew, True), portions_of(amount, rows * top, bound, skew, False)
    places = jnp.arange(amount)

    def named(sizes, offset_by):
        used = int((sizes > 0).sum())
        fixed = max(1, used // 4)
        passed = fixed + (places - fixed + offset_by * (used - fixed)) % max(1, amount - fixed)
        return jnp.zeros((amount,), jnp.int32).at[order[jnp.where(places < fixed, places, passed)]].set(jnp.asarray(sizes, jnp.int32))

    sizes = jnp.where(number % 4 == 0, named(heavy_load, number // 4), named(common, number - number // 4 - 1))
    mixed = jax.random.permutation(jax.random.fold_in(own, 3), amount)
    donor, taker = mixed[0:amount // 2 * 2:2], mixed[1:amount // 2 * 2:2]
    slack = jnp.minimum(sizes[donor] - 1, bound - sizes[taker]) // 2
    slack = jnp.where((donor == order[0]) | (taker == order[0]) | (sizes[taker] == 0), 0, jnp.maximum(slack, 0))
    passed = jax.random.randint(jax.random.fold_in(own, 4), (amount // 2,), 0, 1 << 20) % (slack + 1)
    sizes = sizes.at[donor].add(-passed).at[taker].add(passed)
    items = jnp.searchsorted(jnp.cumsum(sizes), jnp.arange(rows * top), side="right").astype(jnp.int32)
    table = items.reshape(top, rows).T
    table = table[jax.random.permutation(jax.random.fold_in(own, 1), rows)]
    offset_by = jax.random.randint(jax.random.fold_in(own, 2), (rows, 1), 0, top)
    return jnp.take_along_axis(table, (jnp.arange(top)[None, :] + offset_by) % top, axis=1)


def portions_of(number_of, total, bound, lean, full):
    weights = [(1 << 20) // math.isqrt(standing ** lean) + 1 for standing in range(1, number_of + 1)]
    largest = bound if full else min(bound, max(-(-total // number_of), total * weights[0] // sum(weights)))
    least = 1 if total - largest >= number_of - 1 else 0
    holding, surplus = [largest] + [least] * (number_of - 1), total - largest - least * (number_of - 1)
    while surplus > 0:
        movable = [i for i in range(1, number_of) if holding[i] < largest] or [i for i in range(1, number_of) if holding[i] < bound]
        pool, remaining = sum([weights[i] for i in movable]), surplus
        for i in movable:
            more = min(bound - holding[i], max(1, remaining * weights[i] // pool), surplus)
            holding[i] = holding[i] + more
            surplus = surplus - more
    return np.array(holding)


def scatter_about(own_key, extent, scale, limit, split=(), kind=jnp.bfloat16):
    values = jax.random.normal(own_key, extent, jnp.float32) * scale
    if len(split) > 0:
        values = block_levels(own_key, extent, split, -0.22, 0.18) * values
    return jnp.clip(values, min=-limit, max=limit).astype(kind)


def bell_draw_with(own_key, shape, spread, reach, pieces, heavy, held_as=jnp.bfloat16):
    drawn = spread * jax.random.normal(own_key, shape, jnp.float32)
    if pieces:
        drawn = drawn * block_levels(own_key, shape, pieces, -0.22, 0.18)
    return jnp.clip(with_spikes(drawn, jax.random.fold_in(own_key, 3), *heavy), -reach, reach).astype(held_as)


def setup_inputs(seed: int = 0) -> dict:
    key_of = jax.random.split(jax.random.key(seed), 12)
    fact_x = bell_draw_with(key_of[0], (FACTS, D), 1.0, 6.0, ((0, 8), (1, 4)), (0, 1, 8, 2.0))
    dim_owner_keys = jax.random.split(jax.random.fold_in(key_of[1], 1), FACTS // F_DEV)
    dim_owner_turns = jax.random.permutation(jax.random.fold_in(key_of[1], 3), FACTS // F_DEV)
    dim_owner = jax.vmap(lambda own, number: deal_out(jax.random.fold_in(key_of[1], 2), own, number, F_DEV, OWNERS, 1, CAP, 2))(dim_owner_keys, dim_owner_turns).reshape((FACTS, 1))
    dim_slot = touch_ends(jax.random.randint(key_of[2], (FACTS,), 0, DIM_ROWS // N_FACT), jax.random.fold_in(key_of[2], 1), 0, (DIM_ROWS // N_FACT) - 1).astype(jnp.int32)
    fact_owner_keys = jax.random.split(jax.random.fold_in(key_of[3], 1), FACTS // F_DEV)
    fact_owner_turns = jax.random.permutation(jax.random.fold_in(key_of[3], 3), FACTS // F_DEV)
    fact_owner = jax.vmap(lambda own, number: deal_out(jax.random.fold_in(key_of[3], 2), own, number, F_DEV, OWNERS, 1, CAP, 2))(fact_owner_keys, fact_owner_turns).reshape((FACTS, 1))
    fact_slot = touch_ends(jax.random.randint(key_of[4], (FACTS,), 0, E_DEV), jax.random.fold_in(key_of[4], 1), 0, E_DEV - 1).astype(jnp.int32)
    dim_table = scatter_about(key_of[5], (DIM_ROWS, D), 1.0, 6.0, ((0, 8), (1, 4)))
    entity_h = bell_draw_with(key_of[6], (ENTITIES, D), 1.0, 6.0, ((0, 8), (1, 4)), (0, 1, 8, 2.0))
    w_msg = scatter_about(key_of[7], (D, D), D ** -0.5, 0.25, ((1, 4),))
    w_self = scatter_about(key_of[8], (D, D), D ** -0.5, 0.25, ((1, 4),))
    w_neigh = scatter_about(key_of[9], (D, D), D ** -0.5, 0.25, ((1, 4),))
    cotangent = scatter_about(key_of[10], (ENTITIES, D), 0.1, 0.59765625, ((0, 8), (1, 4)))
    return dict(fact_x=fact_x, dim_owner=dim_owner, dim_slot=dim_slot, fact_owner=fact_owner, fact_slot=fact_slot, dim_table=dim_table, entity_h=entity_h, w_msg=w_msg, w_self=w_self, w_neigh=w_neigh, cotangent=cotangent)


def silu_slope(values):
    sigmoid_v = jax.nn.sigmoid(values)
    return sigmoid_v * (1.0 + values * (1.0 - sigmoid_v))


def reference(fact_x, dim_owner, dim_slot, fact_owner, fact_slot, dim_table, entity_h, w_msg, w_self, w_neigh, cotangent):
    entity = (fact_owner[:, 0] * E_DEV + fact_slot).astype(jnp.int32)
    fact_dim = (dim_owner[:, 0] * (DIM_ROWS // N_FACT) + dim_slot).astype(jnp.int32)
    msg_pre = jnp.dot(fact_x, w_msg, preferred_element_type=jnp.float32) + dim_table[fact_dim].astype(jnp.float32)
    message = jax.nn.silu(msg_pre).astype(jnp.bfloat16)
    entity_sums = jax.ops.segment_sum(message.astype(jnp.float32), entity, num_segments=ENTITIES)
    counts = jax.ops.segment_sum(jnp.ones(entity.shape, jnp.float32), entity, num_segments=ENTITIES)
    divisor = jnp.maximum(counts, 1.0)
    aggregate = (entity_sums / divisor[:, None]).astype(jnp.bfloat16)
    pre_act = jnp.dot(entity_h, w_self, preferred_element_type=jnp.float32) + jnp.dot(aggregate, w_neigh, preferred_element_type=jnp.float32)
    output_h = jax.nn.silu(pre_act).astype(jnp.bfloat16)
    d_pre = (cotangent.astype(jnp.float32) * silu_slope(pre_act)).astype(jnp.bfloat16)
    grad_w_self = jnp.dot(entity_h.T, d_pre, preferred_element_type=jnp.float32)
    grad_w_neigh = jnp.dot(aggregate.T, d_pre, preferred_element_type=jnp.float32)
    d_agg = jnp.dot(d_pre, w_neigh.T, preferred_element_type=jnp.float32)
    d_scaled = (d_agg / divisor[:, None]).astype(jnp.bfloat16)
    d_msgpre = (d_scaled[entity].astype(jnp.float32) * silu_slope(msg_pre)).astype(jnp.bfloat16)
    grad_w_msg = jnp.dot(fact_x.T, d_msgpre, preferred_element_type=jnp.float32)
    grad_dim = jax.ops.segment_sum(d_msgpre.astype(jnp.float32), fact_dim, num_segments=DIM_ROWS)
    return output_h, grad_w_msg, grad_w_self, grad_w_neigh, grad_dim
```

```python
import functools

import jax
import jax.numpy as jnp
from jax import lax
from jax.experimental import pallas as pl
from jax.experimental.pallas import tpu as pltpu
from jax.sharding import PartitionSpec as P

LANES = 128
BF = jnp.bfloat16
F32 = jnp.float32
VMEM_LIMIT = 40 * 1024 * 1024


def call(kernel, out_shape, scratch, flops, name):
    return pl.pallas_call(
        kernel,
        out_shape=out_shape,
        scratch_shapes=scratch,
        compiler_params=pltpu.CompilerParams(vmem_limit_bytes=VMEM_LIMIT),
        cost_estimate=pl.CostEstimate(flops=flops, bytes_accessed=1 << 20, transcendentals=0),
        name=name,
    )


def shape(dims, dtype):
    return jax.ShapeDtypeStruct(dims, dtype)


def nt(a, b):
    return lax.dot_general(a, b, (((1,), (1,)), ((), ())), preferred_element_type=F32)


def tn(a, b):
    return lax.dot_general(a, b, (((0,), (0,)), ((), ())), preferred_element_type=F32)


def dot(a, b):
    return jnp.dot(a, b, preferred_element_type=F32)


def flag(condition):
    return jnp.where(condition, 1.0, 0.0).astype(BF)


def column_codes(row):
    keys = jnp.broadcast_to(row, (LANES, LANES)).astype(F32).T.astype(jnp.int32)
    lane = lax.broadcasted_iota(jnp.int32, (LANES, LANES), 1)
    return flag((keys & (LANES - 1)) == lane), (keys >> 7).astype(F32).astype(BF)


def row_codes(row):
    keys = jnp.broadcast_to(row, (LANES, LANES))
    sub = lax.broadcasted_iota(jnp.int32, (LANES, LANES), 0)
    high = jnp.broadcast_to((row >> 7).astype(F32), (16, LANES)).astype(BF)
    return flag((keys & (LANES - 1)) == sub), high


def pick_block(low, high, block):
    zero = jnp.zeros((), BF)
    return jnp.where(high == block, low, zero)


def pick_rows(low, high, block):
    wide = low.reshape(LANES // 16, 16, low.shape[1])
    picked = pick_block(wide, high[None], block)
    return picked.reshape(low.shape)


def route_kernel(n, cap, ents, do_ref, ds_ref, fo_ref, fs_ref, pos_ref, ent_ref, out_ref):
    chunks = do_ref.shape[0]
    owner = do_ref[...]
    kind = lax.broadcasted_iota(jnp.int32, (n, chunks, LANES), 0)
    held = jnp.where(kind == owner[None], 1.0, 0.0).reshape(n * chunks, LANES)
    held_bf = held.astype(BF)
    i0 = lax.broadcasted_iota(jnp.int32, (LANES, LANES), 0)
    i1 = lax.broadcasted_iota(jnp.int32, (LANES, LANES), 1)
    inside = dot(held_bf, flag(i0 < i1))
    r0 = lax.broadcasted_iota(jnp.int32, (n * chunks, n * chunks), 0)
    r1 = lax.broadcasted_iota(jnp.int32, (n * chunks, n * chunks), 1)
    earlier = flag((r0 // chunks == r1 // chunks) & (r1 < r0))
    before = dot(dot(earlier, held_bf).astype(BF), jnp.ones((LANES, LANES), BF))
    rank = jnp.sum((held * (inside + before)).reshape(n, chunks, LANES), axis=0)
    rank = rank.astype(jnp.int32)
    pos_ref[...] = owner * cap + rank
    entity_owner = fo_ref[...]
    entity_slot = fs_ref[...]
    ent_ref[...] = entity_owner * ents + entity_slot
    value = ds_ref[...]
    high = (value >> 5).astype(F32)
    low = (value & 31).astype(F32)
    names = lax.broadcasted_iota(jnp.int32, (n, LANES), 0)
    places = lax.broadcasted_iota(jnp.int32, (cap, LANES), 0)
    slots = lax.broadcasted_iota(jnp.int32, (ents, LANES), 0)
    asked_high = jnp.zeros((n, cap), F32)
    asked_low = jnp.zeros((n, cap), F32)
    hits = jnp.zeros((n, ents), F32)
    for k in range(chunks):
        mine = jnp.where(names == owner[k : k + 1], 1.0, 0.0)
        at = flag(places == rank[k : k + 1])
        asked_high += nt((mine * high[k : k + 1]).astype(BF), at)
        asked_low += nt((mine * low[k : k + 1]).astype(BF), at)
        hits += nt(flag(names == entity_owner[k : k + 1]), flag(slots == entity_slot[k : k + 1]))
    asked = (asked_high * 32.0 + asked_low).astype(jnp.int32)
    for r in range(cap // LANES):
        out_ref[:, r, :] = asked[:, r * LANES : (r + 1) * LANES]
    out_ref[:, cap // LANES, :] = hits.astype(jnp.int32)


def answer_kernel(n, cap, req_ref, table_ref, out_ref):
    blocks = table_ref.shape[0] // LANES

    def body(source, carry):
        for r in range(cap // LANES):
            low, high = column_codes(req_ref[source, r : r + 1, :])
            hot = jnp.concatenate([pick_block(low, high, k) for k in range(blocks)], axis=1)
            out_ref[source, r * LANES : (r + 1) * LANES, :] = dot(hot, table_ref[...]).astype(BF)
        return carry

    lax.fori_loop(0, n, body, 0)


def message_kernel(xw_ref, reply_ref, pos_ref, ent_ref, slope_ref, part_ref, hot_ref, msg_ref, low_ref, high_ref):
    chunks = pos_ref.shape[0]
    slots = reply_ref.shape[0] // LANES

    def look(pair, carry):
        for i in range(2):
            low, high = column_codes(pos_ref[pl.ds(pair * 2 + i, 1), :])
            for k in range(slots):
                hot_ref[i * LANES : (i + 1) * LANES, k * LANES : (k + 1) * LANES] = pick_block(low, high, k)
        rows = pl.ds(pl.multiple_of(pair * 256, 256), 256)
        pre = xw_ref[rows, :] + dot(hot_ref[...], reply_ref[...])
        gate = jax.nn.sigmoid(pre)
        msg_ref[rows, :] = (pre * gate).astype(BF)
        slope_ref[rows, :] = gate * (1.0 + pre * (1.0 - gate))
        return carry

    lax.fori_loop(0, chunks // 2, look, 0)
    for k in range(chunks):
        low, high = row_codes(ent_ref[k : k + 1, :])
        low_ref[:, k * LANES : (k + 1) * LANES] = low
        high_ref[:, k * LANES : (k + 1) * LANES] = high

    def add(block, carry):
        hot = pick_rows(low_ref[...], high_ref[...], block.astype(F32).astype(BF))
        rows = pl.ds(pl.multiple_of(block * LANES, LANES), LANES)
        part_ref[rows, :] = dot(hot, msg_ref[...]).astype(BF)
        return carry

    lax.fori_loop(0, part_ref.shape[0] // LANES, add, 0)


def entity_kernel(n, m, width, me_ref, sums_ref, idx_ref, all_ref, back_ref, share_ref, div_ref):
    rows_each = sums_ref.shape[1]
    ents = rows_each * m
    me = me_ref[0]
    mine = pl.ds(pl.multiple_of(me * rows_each, rows_each), rows_each)
    hits = jnp.sum(idx_ref[:, idx_ref.shape[1] - 1, :], axis=0, keepdims=True).astype(F32)
    div_ref[...] = jnp.maximum(jnp.broadcast_to(hits, (LANES, ents)).T, 1.0)
    divisor = div_ref[mine, :]
    parts = []
    for b in range(m):
        total = sums_ref[b].astype(F32)
        for f in range(1, n):
            total += sums_ref[f * m + b].astype(F32)
        parts.append((total / divisor).astype(BF))
    aggregate = jnp.concatenate(parts, axis=1)
    hidden = jnp.concatenate([all_ref[b, pl.ds(2 * width + me * rows_each, rows_each), :] for b in range(m)], axis=1)
    d_agg = jnp.zeros((rows_each, width), F32)
    for b in range(m):
        pre = dot(hidden, all_ref[b, 0:width, :]) + dot(aggregate, all_ref[b, width : 2 * width, :])
        gate = jax.nn.sigmoid(pre)
        cot = all_ref[b, pl.ds(2 * width + ents + me * rows_each, rows_each), :].astype(F32)
        d_pre = (cot * (gate * (1.0 + pre * (1.0 - gate)))).astype(BF)
        share_ref[b, 0:rows_each, :] = (pre * gate).astype(BF)
        share_ref[b, rows_each : 2 * rows_each, :] = d_pre
        for a in range(m):
            share_ref[b, (2 + a) * rows_each : (3 + a) * rows_each, :] = parts[a]
        d_agg += nt(d_pre, all_ref[b, width : 2 * width, :])
    for b in range(m):
        scaled = (d_agg[:, b * LANES : (b + 1) * LANES] / divisor).astype(BF)
        for f in range(n):
            back_ref[f * m + b] = scaled


def weight_kernel(m, width, rows_each, got_ref, all_ref, out_ref):
    ents = rows_each * m
    d_pre = jnp.concatenate([got_ref[s, rows_each : 2 * rows_each, :] for s in range(m)], axis=0)
    for b in range(m):
        hidden = all_ref[b, 2 * width : 2 * width + ents, :]
        agg = jnp.concatenate(
            [got_ref[s, (2 + b) * rows_each : (3 + b) * rows_each, :] for s in range(m)], axis=0
        )
        out_ref[0, b * LANES : (b + 1) * LANES, :] = tn(hidden, d_pre).astype(BF)
        out_ref[1, b * LANES : (b + 1) * LANES, :] = tn(agg, d_pre).astype(BF)


def backward_kernel(scaled_ref, slope_ref, pos_ref, ent_ref, dmsg_ref, rows_ref, hot_ref, low_ref, high_ref):
    chunks = pos_ref.shape[0]
    blocks = scaled_ref.shape[0] // LANES

    def look(pair, carry):
        for i in range(2):
            low, high = column_codes(ent_ref[pl.ds(pair * 2 + i, 1), :])
            for k in range(blocks):
                hot_ref[i * LANES : (i + 1) * LANES, k * LANES : (k + 1) * LANES] = pick_block(low, high, k)
        rows = pl.ds(pl.multiple_of(pair * 256, 256), 256)
        dmsg_ref[rows, :] = (dot(hot_ref[...], scaled_ref[...]) * slope_ref[rows, :]).astype(BF)
        return carry

    lax.fori_loop(0, chunks // 2, look, 0)
    for k in range(chunks):
        low, high = row_codes(pos_ref[k : k + 1, :])
        low_ref[:, k * LANES : (k + 1) * LANES] = low
        high_ref[:, k * LANES : (k + 1) * LANES] = high

    def spread(block, carry):
        hot = pick_rows(low_ref[...], high_ref[...], block.astype(F32).astype(BF))
        rows = pl.ds(pl.multiple_of(block * LANES, LANES), LANES)
        rows_ref[rows, :] = dot(hot, dmsg_ref[...]).astype(BF)
        return carry

    lax.fori_loop(0, rows_ref.shape[0] // LANES, spread, 0)


def table_kernel(n, cap, rows_ref, req_ref, out_ref, low_ref, high_ref):
    for s in range(n):
        for r in range(cap // LANES):
            low, high = row_codes(req_ref[s, r : r + 1, :])
            at = s * cap + r * LANES
            low_ref[:, at : at + LANES] = low
            high_ref[:, at : at + LANES] = high

    def add(block, carry):
        hot = pick_rows(low_ref[...], high_ref[...], block.astype(F32).astype(BF))
        rows = pl.ds(pl.multiple_of(block * LANES, LANES), LANES)
        out_ref[rows, :] = dot(hot, rows_ref[...])
        return carry

    lax.fori_loop(0, out_ref.shape[0] // LANES, add, 0)


def shards(fact_x, dim_owner, dim_slot, fact_owner, fact_slot, dim_table, entity_h, w_msg, w_self, w_neigh, cotangent):
    n, m = lax.axis_size("fact"), lax.axis_size("feat")
    facts = fact_x.shape[0]
    chunks = facts // LANES
    ents = entity_h.shape[0]
    rows_each = ents // m
    width = w_msg.shape[0]
    cap = -(-(3 * facts // n) // LANES) * LANES
    slots = n * cap
    groups = cap // LANES + 1

    x_full = lax.all_gather(fact_x, "feat", axis=1, tiled=True)
    everything = lax.all_gather(jnp.concatenate([w_self, w_neigh, entity_h, cotangent], axis=0), "feat")

    by_lane = (chunks, LANES)
    pos, entity, asks = call(
        functools.partial(route_kernel, n, cap, ents),
        (shape(by_lane, jnp.int32), shape(by_lane, jnp.int32), shape((n, groups, LANES), jnp.int32)),
        [],
        1 << 24,
        "route",
    )(dim_owner.reshape(by_lane), dim_slot.reshape(by_lane), fact_owner.reshape(by_lane), fact_slot.reshape(by_lane))
    asked = lax.all_to_all(asks, "fact", 0, 0)
    answers = call(
        functools.partial(answer_kernel, n, cap),
        shape((n, cap, LANES), BF),
        [],
        2 * slots * dim_table.shape[0] * LANES,
        "answer",
    )(asked, dim_table)
    reply = lax.all_to_all(answers, "fact", 0, 0).reshape(slots, LANES)
    xw = jnp.dot(x_full, w_msg, preferred_element_type=F32)
    slope, part = call(
        message_kernel,
        (shape((facts, LANES), F32), shape((n * ents, LANES), BF)),
        [
            pltpu.VMEM((256, slots), BF),
            pltpu.VMEM((facts, LANES), BF),
            pltpu.VMEM((LANES, facts), BF),
            pltpu.VMEM((16, facts), BF),
        ],
        2 * facts * slots * LANES,
        "message",
    )(xw, reply, pos, entity)
    sums = lax.all_to_all(part.reshape(n * m, rows_each, LANES), ("fact", "feat"), 0, 0)
    back, share = call(
        functools.partial(entity_kernel, n, m, width),
        (shape((n * m, rows_each, LANES), BF), shape((m, (2 + m) * rows_each, LANES), BF)),
        [pltpu.VMEM((ents, LANES), F32)],
        6 * rows_each * width * width,
        "entity",
    )(
        lax.axis_index("feat").astype(jnp.int32).reshape(1),
        sums,
        asked,
        everything,
    )
    scaled = lax.all_to_all(back, ("fact", "feat"), 0, 0).reshape(n * ents, LANES)
    got = lax.all_to_all(share, "feat", 0, 0)
    output_h = got[:, 0:rows_each].reshape(ents, LANES)
    d_msgpre, rows = call(
        backward_kernel,
        (shape((facts, LANES), BF), shape((slots, LANES), BF)),
        [
            pltpu.VMEM((256, n * ents), BF),
            pltpu.VMEM((LANES, facts), BF),
            pltpu.VMEM((16, facts), BF),
        ],
        2 * facts * slots * LANES,
        "backward",
    )(scaled, slope, pos, entity)
    owned = lax.all_to_all(rows.reshape(n, cap, LANES), "fact", 0, 0).reshape(slots, LANES)
    pair = call(
        functools.partial(weight_kernel, m, width, rows_each),
        shape((2, width, LANES), BF),
        [],
        4 * ents * width * LANES,
        "weight",
    )(got, everything)
    msg_part = jnp.einsum("fa,fb->ab", x_full, d_msgpre, preferred_element_type=F32).astype(BF)
    own = width // n
    weight_parts = jnp.concatenate(
        [pair[0].reshape(n, own, LANES), pair[1].reshape(n, own, LANES), msg_part.reshape(n, own, LANES)], axis=1
    )
    weight_sum = jnp.sum(lax.all_to_all(weight_parts, "fact", 0, 0).astype(F32), axis=0)
    grad_dim = call(
        functools.partial(table_kernel, n, cap),
        shape(dim_table.shape, F32),
        [pltpu.VMEM((LANES, slots), BF), pltpu.VMEM((16, slots), BF)],
        2 * slots * dim_table.shape[0] * LANES,
        "table",
    )(owned, asked)
    return (
        output_h,
        weight_sum[2 * own : 3 * own],
        weight_sum[0:own],
        weight_sum[own : 2 * own],
        grad_dim,
    )


def solution(mesh):
    placed = (
        P("fact", "feat"),
        P("fact", None),
        P("fact"),
        P("fact", None),
        P("fact"),
        P("fact", "feat"),
        P("fact", "feat"),
        P(None, "feat"),
        P(None, "feat"),
        P(None, "feat"),
        P("fact", "feat"),
    )
    return jax.shard_map(
        shards,
        mesh=mesh,
        in_specs=placed,
        out_specs=(P("fact", "feat"),) * 5,
        check_vma=False,
    )
```

```python
import functools

import jax
import jax.numpy as jnp
from jax import lax
from jax.experimental import pallas as pl
from jax.experimental.pallas import tpu as pltpu
from jax.sharding import PartitionSpec as P

LANES = 128
BF = jnp.bfloat16
F32 = jnp.float32
VMEM_LIMIT = 40 * 1024 * 1024


def call(kernel, out_shape, scratch, flops, name):
    return pl.pallas_call(
        kernel,
        out_shape=out_shape,
        scratch_shapes=scratch,
        compiler_params=pltpu.CompilerParams(vmem_limit_bytes=VMEM_LIMIT),
        cost_estimate=pl.CostEstimate(flops=flops, bytes_accessed=1 << 20, transcendentals=0),
        name=name,
    )


def shape(dims, dtype):
    return jax.ShapeDtypeStruct(dims, dtype)


def nt(a, b):
    return lax.dot_general(a, b, (((1,), (1,)), ((), ())), preferred_element_type=F32)


def tn(a, b):
    return lax.dot_general(a, b, (((0,), (0,)), ((), ())), preferred_element_type=F32)


def dot(a, b):
    return jnp.dot(a, b, preferred_element_type=F32)


def flag(condition):
    return jnp.where(condition, 1.0, 0.0).astype(BF)


def column_codes(row):
    keys = jnp.broadcast_to(row, (LANES, LANES)).astype(F32).T.astype(jnp.int32)
    lane = lax.broadcasted_iota(jnp.int32, (LANES, LANES), 1)
    return flag((keys & (LANES - 1)) == lane), (keys >> 7).astype(F32).astype(BF)


def row_codes(row):
    keys = jnp.broadcast_to(row, (LANES, LANES))
    sub = lax.broadcasted_iota(jnp.int32, (LANES, LANES), 0)
    high = jnp.broadcast_to((row >> 7).astype(F32), (16, LANES)).astype(BF)
    return flag((keys & (LANES - 1)) == sub), high


def pick_block(low, high, block):
    zero = jnp.zeros((), BF)
    return jnp.where(high == block, low, zero)


def pick_rows(low, high, block):
    wide = low.reshape(LANES // 16, 16, low.shape[1])
    picked = pick_block(wide, high[None], block)
    return picked.reshape(low.shape)


def route_kernel(n, cap, ents, dims, do_ref, ds_ref, fo_ref, fs_ref, out_ref, dlow_ref, dhigh_ref, elow_ref, ehigh_ref, plow_ref, phigh_ref, erlow_ref, erhigh_ref):
    chunks = do_ref.shape[0]
    owner = do_ref[...]
    kind = lax.broadcasted_iota(jnp.int32, (n, chunks, LANES), 0)
    held = jnp.where(kind == owner[None], 1.0, 0.0).reshape(n * chunks, LANES)
    held_bf = held.astype(BF)
    i0 = lax.broadcasted_iota(jnp.int32, (LANES, LANES), 0)
    i1 = lax.broadcasted_iota(jnp.int32, (LANES, LANES), 1)
    inside = dot(held_bf, flag(i0 < i1))
    r0 = lax.broadcasted_iota(jnp.int32, (n * chunks, n * chunks), 0)
    r1 = lax.broadcasted_iota(jnp.int32, (n * chunks, n * chunks), 1)
    earlier = flag((r0 // chunks == r1 // chunks) & (r1 < r0))
    before = dot(dot(earlier, held_bf).astype(BF), jnp.ones((LANES, LANES), BF))
    rank = jnp.sum((held * (inside + before)).reshape(n, chunks, LANES), axis=0)
    rank = rank.astype(jnp.int32)
    entity_owner = fo_ref[...]
    entity_slot = fs_ref[...]
    value = ds_ref[...]
    position = owner * cap + rank
    entity = entity_owner * ents + entity_slot
    fact_dim = owner * dims + value
    high = (value >> 5).astype(F32)
    low = (value & 31).astype(F32)
    names = lax.broadcasted_iota(jnp.int32, (n, LANES), 0)
    places = lax.broadcasted_iota(jnp.int32, (cap, LANES), 0)
    slots = lax.broadcasted_iota(jnp.int32, (ents, LANES), 0)
    asked_high = jnp.zeros((n, cap), F32)
    asked_low = jnp.zeros((n, cap), F32)
    hits = jnp.zeros((n, ents), F32)
    for k in range(chunks):
        here = slice(k * LANES, (k + 1) * LANES)
        mine = jnp.where(names == owner[k : k + 1], 1.0, 0.0)
        at = flag(places == rank[k : k + 1])
        asked_high += nt((mine * high[k : k + 1]).astype(BF), at)
        asked_low += nt((mine * low[k : k + 1]).astype(BF), at)
        hits += nt(flag(names == entity_owner[k : k + 1]), flag(slots == entity_slot[k : k + 1]))
        dlow_ref[here, :], dhigh_ref[here, :] = column_codes(fact_dim[k : k + 1])
        elow_ref[here, :], ehigh_ref[here, :] = column_codes(entity[k : k + 1])
        plow_ref[:, here], phigh_ref[:, here] = row_codes(position[k : k + 1])
        erlow_ref[:, here], erhigh_ref[:, here] = row_codes(entity[k : k + 1])
    asked = (asked_high * 32.0 + asked_low).astype(jnp.int32)
    for r in range(cap // LANES):
        out_ref[:, r, :] = asked[:, r * LANES : (r + 1) * LANES]
    out_ref[:, cap // LANES, :] = hits.astype(jnp.int32)


def gather_rows(low_ref, high_ref, rows, table_refs, firsts, hot_ref):
    at = 0
    low, high = low_ref[rows, :], high_ref[rows, :]
    for table, first in zip(table_refs, firsts):
        for k in range(table.shape[0] // LANES):
            hot_ref[:, at : at + LANES] = pick_block(low, high, (first + k).astype(F32).astype(BF))
            at += LANES
    total, at = None, 0
    for table in table_refs:
        part = dot(hot_ref[:, at : at + table.shape[0]], table[...])
        total = part if total is None else total + part
        at += table.shape[0]
    return total


def ring_at(place, n):
    place = lax.rem(place + 2 * n, n)
    return jnp.where(place < n // 2, 2 * place, 2 * (n - 1 - place) + 1)


def ring_place(index, n):
    half = lax.div(index, 2)
    return jnp.where(lax.rem(index, 2) == 0, half, n - 1 - half)


def look_kernel(n, pieces, low_ref, high_ref, *refs):
    count = len(pieces)
    tables, base_ref, out_ref, hot_ref = refs[:count], refs[count], refs[-2], refs[-1]
    facts = low_ref.shape[0]
    step = hot_ref.shape[0]
    place = ring_place(lax.axis_index("fact"), n)
    firsts = [lax.div(ring_at(place + hops, n) * dims + row, LANES) for hops, row, dims in pieces]
    for c in range(facts // step):
        rows = slice(c * step, (c + 1) * step)
        out_ref[rows, :] = base_ref[rows, :] + gather_rows(low_ref, high_ref, rows, tables, firsts, hot_ref)


def message_kernel(n, pieces, low_ref, high_ref, *refs):
    count = len(pieces)
    tables, refs = refs[:count], refs[count:]
    base_ref, erlow_ref, erhigh_ref, slope_ref, part_ref, hot_ref, msg_ref = refs
    facts = low_ref.shape[0]
    step = hot_ref.shape[0]
    place = ring_place(lax.axis_index("fact"), n)
    firsts = [lax.div(ring_at(place + hops, n) * dims + row, LANES) for hops, row, dims in pieces]
    for c in range(facts // step):
        rows = slice(c * step, (c + 1) * step)
        pre = base_ref[rows, :]
        if count:
            pre = pre + gather_rows(low_ref, high_ref, rows, tables, firsts, hot_ref)
        gate = jax.nn.sigmoid(pre)
        msg_ref[rows, :] = (pre * gate).astype(BF)
        slope_ref[rows, :] = gate * (1.0 + pre * (1.0 - gate))

    def add(pair, carry):
        hot = jnp.concatenate(
            [pick_rows(erlow_ref[...], erhigh_ref[...], (pair * 2 + i).astype(F32).astype(BF)) for i in range(2)], axis=0
        )
        rows = pl.ds(pl.multiple_of(pair * 256, 256), 256)
        part_ref[rows, :] = dot(hot, msg_ref[...]).astype(BF)
        return carry

    lax.fori_loop(0, part_ref.shape[0] // 256, add, 0)


def entity_kernel(n, m, width, me_ref, sums_ref, idx_ref, all_ref, back_ref, share_ref, div_ref):
    rows_each = sums_ref.shape[1]
    ents = rows_each * m
    me = me_ref[0]
    mine = pl.ds(pl.multiple_of(me * rows_each, rows_each), rows_each)
    hits = jnp.sum(idx_ref[:, idx_ref.shape[1] - 1, :], axis=0, keepdims=True).astype(F32)
    div_ref[...] = jnp.maximum(jnp.broadcast_to(hits, (LANES, ents)).T, 1.0)
    divisor = div_ref[mine, :]
    parts = []
    for b in range(m):
        total = sums_ref[b].astype(F32)
        for f in range(1, n):
            total += sums_ref[f * m + b].astype(F32)
        parts.append((total / divisor).astype(BF))
    aggregate = jnp.concatenate(parts, axis=1)
    share_ref[2] = aggregate
    hidden = jnp.concatenate([all_ref[b, pl.ds(2 * width + me * rows_each, rows_each), :] for b in range(m)], axis=1)
    d_agg = jnp.zeros((rows_each, width), F32)
    for b in range(m):
        here = slice(b * LANES, (b + 1) * LANES)
        pre = dot(hidden, all_ref[b, 0:width, :]) + dot(aggregate, all_ref[b, width : 2 * width, :])
        gate = jax.nn.sigmoid(pre)
        cot = all_ref[b, pl.ds(2 * width + ents + me * rows_each, rows_each), :].astype(F32)
        d_pre = (cot * (gate * (1.0 + pre * (1.0 - gate)))).astype(BF)
        share_ref[0, :, here] = (pre * gate).astype(BF)
        share_ref[1, :, here] = d_pre
        d_agg += nt(d_pre, all_ref[b, width : 2 * width, :])
    for b in range(m):
        scaled = (d_agg[:, b * LANES : (b + 1) * LANES] / divisor).astype(BF)
        for f in range(n):
            back_ref[f * m + b] = scaled


def store_shares(n, stride, own, at, total, out_ref):
    for d in range(n):
        piece = total[d * own : (d + 1) * own, :]
        if stride > own:
            piece = jnp.concatenate([piece, jnp.zeros((stride - own, LANES), F32)], axis=0)
        out_ref[d, at : at + stride, :] = piece.astype(BF)


def weight_kernel(n, m, width, stride, me_ref, got_ref, all_ref, out_ref, back_ref, total_ref):
    rows_each = got_ref.shape[2]
    ents = rows_each * m
    own = width // n
    mine = pl.ds(pl.multiple_of(me_ref[0] * LANES, LANES), LANES)
    out_ref[...] = jnp.concatenate([got_ref[s, 0, :, mine] for s in range(m)], axis=0)
    d_pre = jnp.concatenate([got_ref[s, 1, :, mine] for s in range(m)], axis=0)
    aggregate = jnp.concatenate([got_ref[s, 2] for s in range(m)], axis=0)
    for b in range(m):
        here = slice(b * LANES, (b + 1) * LANES)
        total_ref[here, :] = tn(all_ref[b, 2 * width : 2 * width + ents, :], d_pre)
    store_shares(n, stride, own, 0, total_ref[...], back_ref)
    for b in range(m):
        here = slice(b * LANES, (b + 1) * LANES)
        total_ref[here, :] = tn(aggregate[:, here], d_pre)
    store_shares(n, stride, own, stride, total_ref[...], back_ref)


def backward_kernel(n, cap, stride, scaled_ref, slope_ref, low_ref, high_ref, plow_ref, phigh_ref, xt_ref, out_ref, hot_ref, dmsg_ref):
    facts = slope_ref.shape[0]
    own = xt_ref.shape[0] // n
    step = hot_ref.shape[0]
    for c in range(facts // step):
        rows = slice(c * step, (c + 1) * step)
        found = gather_rows(low_ref, high_ref, rows, [scaled_ref], [jnp.int32(0)], hot_ref)
        dmsg_ref[rows, :] = (found * slope_ref[rows, :]).astype(BF)

    def spread(d, carry):
        hot = jnp.concatenate(
            [
                pick_rows(plow_ref[...], phigh_ref[...], (d * (cap // LANES) + i).astype(F32).astype(BF))
                for i in range(cap // LANES)
            ],
            axis=0,
        )
        out_ref[d, 0:cap, :] = dot(hot, dmsg_ref[...]).astype(BF)
        return carry

    lax.fori_loop(0, n, spread, 0)
    store_shares(n, stride, own, cap, dot(xt_ref[...], dmsg_ref[...]), out_ref)


def codes_kernel(n, cap, req_ref, low_ref, high_ref):
    for s in range(n):
        for r in range(cap // LANES):
            at = s * cap + r * LANES
            low_ref[:, at : at + LANES], high_ref[:, at : at + LANES] = row_codes(req_ref[s, r : r + 1, :])


def table_kernel(n, cap, stride, got_ref, low_ref, high_ref, out_ref, msg_ref, self_ref, neigh_ref, rows_ref):
    for s in range(n):
        rows_ref[s * cap : (s + 1) * cap, :] = got_ref[s, 0:cap, :]
    own = msg_ref.shape[0]
    for j, ref in enumerate((msg_ref, self_ref, neigh_ref)):
        at = cap + j * stride
        total = got_ref[0, at : at + stride, :].astype(F32)
        for s in range(1, n):
            total += got_ref[s, at : at + stride, :].astype(F32)
        ref[...] = total[0:own, :]
    blocks = out_ref.shape[0] // LANES
    join = 2 if blocks % 2 == 0 else 1

    def add(group, carry):
        hot = jnp.concatenate(
            [pick_rows(low_ref[...], high_ref[...], (group * join + i).astype(F32).astype(BF)) for i in range(join)], axis=0
        )
        rows = pl.ds(pl.multiple_of(group * join * LANES, LANES), join * LANES)
        out_ref[rows, :] = dot(hot, rows_ref[...])
        return carry

    lax.fori_loop(0, blocks // join, add, 0)


def shards(fact_x, dim_owner, dim_slot, fact_owner, fact_slot, dim_table, entity_h, w_msg, w_self, w_neigh, cotangent):
    n, m = lax.axis_size("fact"), lax.axis_size("feat")
    facts = fact_x.shape[0]
    chunks = facts // LANES
    ents = entity_h.shape[0]
    rows_each = ents // m
    width = w_msg.shape[0]
    dims = dim_table.shape[0]
    cap = -(-(3 * facts // n) // LANES) * LANES
    slots = n * cap
    groups = cap // LANES + 1
    own = width // n
    stride = max(16, own)
    me = lax.axis_index("feat").astype(jnp.int32).reshape(1)

    x_full = lax.all_gather(fact_x, "feat", axis=1, tiled=True)
    everything = lax.all_gather(jnp.concatenate([w_self, w_neigh, entity_h, cotangent], axis=0), "feat")

    by_lane = (chunks, LANES)
    columns, down, high_down = shape((facts, LANES), BF), shape((LANES, facts), BF), shape((16, facts), BF)
    asks, dlow, dhigh, elow, ehigh, plow, phigh, erlow, erhigh = call(
        functools.partial(route_kernel, n, cap, ents, dims),
        (
            shape((n, groups, LANES), jnp.int32),
            columns,
            columns,
            columns,
            columns,
            down,
            high_down,
            down,
            high_down,
        ),
        [],
        1 << 28,
        "route",
    )(dim_owner.reshape(by_lane), dim_slot.reshape(by_lane), fact_owner.reshape(by_lane), fact_slot.reshape(by_lane))

    step = 512

    def look(pieces, tables, base):
        rows = sum(t.shape[0] for t in tables)
        return call(
            functools.partial(look_kernel, n, pieces),
            shape((facts, LANES), F32),
            [pltpu.VMEM((step, rows), BF)],
            2 * facts * rows * LANES,
            "look",
        )(dlow, dhigh, *tables, base)

    ring = [2 * p if p < n // 2 else 2 * (n - 1 - p) + 1 for p in range(n)]
    to_right = [(ring[p], ring[(p + 1) % n]) for p in range(n)]
    to_left = [(ring[(p + 1) % n], ring[p]) for p in range(n)]
    if n <= 8:
        rights, lefts = [dim_table], [dim_table]
        for k in range(1, n // 2):
            rights.append(lax.ppermute(rights[-1], "fact", to_right))
            lefts.append(lax.ppermute(lefts[-1], "fact", to_left))
        half = dims // 2
        last = [
            lax.ppermute(rights[-1][:half], "fact", to_right),
            lax.ppermute(lefts[-1][half:], "fact", to_left),
        ]
        last_pieces = [(-(n // 2), 0, dims), (n // 2, half, dims)]
        base = jnp.dot(x_full, w_msg, preferred_element_type=F32)
        found = look([(0, 0, dims)], [dim_table], jnp.zeros((facts, LANES), F32))
        for k in range(1, n // 2):
            found = look([(-k, 0, dims), (k, 0, dims)], [rights[k], lefts[k]], found)
        base = base + found
    else:
        whole = lax.all_gather(dim_table, "fact")
        order = jnp.take(whole, ring_at(ring_place(lax.axis_index("fact"), n) + jnp.arange(n), n), axis=0)
        base = jnp.dot(x_full, w_msg, preferred_element_type=F32)
        for k in range(0, n, 8):
            base = look([(k + i, 0, dims) for i in range(8)], [order[k + i] for i in range(8)], base)
        last, last_pieces = [], []
    last_rows = max(LANES, sum(t.shape[0] for t in last))
    slope, part = call(
        functools.partial(message_kernel, n, last_pieces),
        (shape((facts, LANES), F32), shape((n * ents, LANES), BF)),
        [pltpu.VMEM((step, last_rows), BF), pltpu.VMEM((facts, LANES), BF)],
        2 * facts * (last_rows + n * ents) * LANES,
        "message",
    )(dlow, dhigh, *last, base, erlow, erhigh)
    asked = lax.all_to_all(asks, "fact", 0, 0)
    rlow, rhigh = call(
        functools.partial(codes_kernel, n, cap),
        (shape((LANES, slots), BF), shape((16, slots), BF)),
        [],
        1 << 26,
        "codes",
    )(asked)
    sums = lax.all_to_all(part.reshape(n * m, rows_each, LANES), ("fact", "feat"), 0, 0)
    back, share = call(
        functools.partial(entity_kernel, n, m, width),
        (shape((n * m, rows_each, LANES), BF), shape((3, rows_each, width), BF)),
        [pltpu.VMEM((ents, LANES), F32)],
        6 * rows_each * width * width,
        "entity",
    )(me, sums, asked, everything)
    scaled = lax.all_to_all(back, ("fact", "feat"), 0, 0).reshape(n * ents, LANES)
    got = lax.all_gather(share, "feat")
    output_h, pair = call(
        functools.partial(weight_kernel, n, m, width, stride),
        (shape((ents, LANES), BF), shape((n, 2 * stride, LANES), BF)),
        [pltpu.VMEM((width, LANES), F32)],
        4 * ents * width * LANES,
        "weight",
    )(me, got, everything)
    rows = call(
        functools.partial(backward_kernel, n, cap, stride),
        shape((n, cap + 3 * stride, LANES), BF),
        [pltpu.VMEM((step, n * ents), BF), pltpu.VMEM((facts, LANES), BF)],
        2 * facts * (slots + n * ents + width) * LANES,
        "backward",
    )(scaled, slope, elow, ehigh, plow, phigh, x_full.T)
    rows = rows.at[:, cap + stride :, :].set(pair)
    owned = lax.all_to_all(rows, "fact", 0, 0)
    grad_dim, grad_msg, grad_self, grad_neigh = call(
        functools.partial(table_kernel, n, cap, stride),
        (shape((dims, LANES), F32),) + (shape((own, LANES), F32),) * 3,
        [pltpu.VMEM((slots, LANES), BF)],
        2 * slots * dims * LANES,
        "table",
    )(owned, rlow, rhigh)
    return output_h, grad_msg, grad_self, grad_neigh, grad_dim


def solution(mesh):
    placed = (
        P("fact", "feat"),
        P("fact", None),
        P("fact"),
        P("fact", None),
        P("fact"),
        P("fact", "feat"),
        P("fact", "feat"),
        P(None, "feat"),
        P(None, "feat"),
        P(None, "feat"),
        P("fact", "feat"),
    )
    return jax.shard_map(
        shards,
        mesh=mesh,
        in_specs=placed,
        out_specs=(P("fact", "feat"),) * 5,
        check_vma=False,
    )
```

```python
import functools

import jax
import jax.numpy as jnp
from jax import lax
from jax.experimental import pallas as pl
from jax.experimental.pallas import tpu as pltpu
from jax.sharding import PartitionSpec as P

LANES = 128
BF = jnp.bfloat16
F32 = jnp.float32
VMEM_LIMIT = 40 * 1024 * 1024


def call(kernel, out_shape, scratch, flops, name):
    return pl.pallas_call(
        kernel,
        out_shape=out_shape,
        scratch_shapes=scratch,
        compiler_params=pltpu.CompilerParams(vmem_limit_bytes=VMEM_LIMIT),
        cost_estimate=pl.CostEstimate(flops=flops, bytes_accessed=1 << 20, transcendentals=0),
        name=name,
    )


def shape(dims, dtype):
    return jax.ShapeDtypeStruct(dims, dtype)


def nt(a, b):
    return lax.dot_general(a, b, (((1,), (1,)), ((), ())), preferred_element_type=F32)


def tn(a, b):
    return lax.dot_general(a, b, (((0,), (0,)), ((), ())), preferred_element_type=F32)


def dot(a, b):
    return jnp.dot(a, b, preferred_element_type=F32)


def flag(condition):
    return jnp.where(condition, 1.0, 0.0).astype(BF)


def column_codes(row):
    keys = jnp.broadcast_to(row, (LANES, LANES)).astype(F32).T.astype(jnp.int32)
    lane = lax.broadcasted_iota(jnp.int32, (LANES, LANES), 1)
    return flag((keys & (LANES - 1)) == lane), (keys >> 7).astype(F32).astype(BF)


def row_codes(row):
    keys = jnp.broadcast_to(row, (LANES, LANES))
    sub = lax.broadcasted_iota(jnp.int32, (LANES, LANES), 0)
    high = jnp.broadcast_to((row >> 7).astype(F32), (16, LANES)).astype(BF)
    return flag((keys & (LANES - 1)) == sub), high


def pick_block(low, high, block):
    zero = jnp.zeros((), BF)
    return jnp.where(high == block, low, zero)


def pick_rows(low, high, block):
    wide = low.reshape(LANES // 16, 16, low.shape[1])
    picked = pick_block(wide, high[None], block)
    return picked.reshape(low.shape)


def route_kernel(n, cap, ents, dims, do_ref, ds_ref, fo_ref, fs_ref, out_ref, pos_ref, ent_ref, dlow_ref, dhigh_ref):
    chunks = do_ref.shape[0]
    owner = do_ref[...]
    kind = lax.broadcasted_iota(jnp.int32, (n, chunks, LANES), 0)
    held = jnp.where(kind == owner[None], 1.0, 0.0).reshape(n * chunks, LANES)
    held_bf = held.astype(BF)
    i0 = lax.broadcasted_iota(jnp.int32, (LANES, LANES), 0)
    i1 = lax.broadcasted_iota(jnp.int32, (LANES, LANES), 1)
    inside = dot(held_bf, flag(i0 < i1))
    r0 = lax.broadcasted_iota(jnp.int32, (n * chunks, n * chunks), 0)
    r1 = lax.broadcasted_iota(jnp.int32, (n * chunks, n * chunks), 1)
    earlier = flag((r0 // chunks == r1 // chunks) & (r1 < r0))
    before = dot(dot(earlier, held_bf).astype(BF), jnp.ones((LANES, LANES), BF))
    rank = jnp.sum((held * (inside + before)).reshape(n, chunks, LANES), axis=0)
    rank = rank.astype(jnp.int32)
    entity_owner = fo_ref[...]
    entity_slot = fs_ref[...]
    value = ds_ref[...]
    pos_ref[...] = owner * cap + rank
    ent_ref[...] = entity_owner * ents + entity_slot
    fact_dim = owner * dims + value
    high = (value >> 5).astype(F32)
    low = (value & 31).astype(F32)
    names = lax.broadcasted_iota(jnp.int32, (n, LANES), 0)
    places = lax.broadcasted_iota(jnp.int32, (cap, LANES), 0)
    slots = lax.broadcasted_iota(jnp.int32, (ents, LANES), 0)
    asked_high = jnp.zeros((n, cap), F32)
    asked_low = jnp.zeros((n, cap), F32)
    hits = jnp.zeros((n, ents), F32)
    for k in range(chunks):
        here = slice(k * LANES, (k + 1) * LANES)
        mine = jnp.where(names == owner[k : k + 1], 1.0, 0.0)
        at = flag(places == rank[k : k + 1])
        asked_high += nt((mine * high[k : k + 1]).astype(BF), at)
        asked_low += nt((mine * low[k : k + 1]).astype(BF), at)
        hits += nt(flag(names == entity_owner[k : k + 1]), flag(slots == entity_slot[k : k + 1]))
        dlow_ref[here, :], dhigh_ref[here, :] = column_codes(fact_dim[k : k + 1])
    asked = (asked_high * 32.0 + asked_low).astype(jnp.int32)
    for r in range(cap // LANES):
        out_ref[:, r, :] = asked[:, r * LANES : (r + 1) * LANES]
    out_ref[:, cap // LANES, :] = hits.astype(jnp.int32)


def gather_rows(low_ref, high_ref, rows, table_refs, firsts, hot_ref):
    at = 0
    low, high = low_ref[rows, :], high_ref[rows, :]
    for table, first in zip(table_refs, firsts):
        for k in range(table.shape[0] // LANES):
            hot_ref[:, at : at + LANES] = pick_block(low, high, (first + k).astype(F32).astype(BF))
            at += LANES
    total, at = None, 0
    for table in table_refs:
        part = dot(hot_ref[:, at : at + table.shape[0]], table[...])
        total = part if total is None else total + part
        at += table.shape[0]
    return total


def ring_at(place, n):
    place = lax.rem(place + 2 * n, n)
    return jnp.where(place < n // 2, 2 * place, 2 * (n - 1 - place) + 1)


def ring_place(index, n):
    half = lax.div(index, 2)
    return jnp.where(lax.rem(index, 2) == 0, half, n - 1 - half)


def look_kernel(n, pieces, low_ref, high_ref, *refs):
    count = len(pieces)
    tables, base_ref, out_ref, hot_ref = refs[:count], refs[count], refs[-2], refs[-1]
    facts = low_ref.shape[0]
    step = hot_ref.shape[0]
    place = ring_place(lax.axis_index("fact"), n)
    firsts = [lax.div(ring_at(place + hops, n) * dims + row, LANES) for hops, row, dims in pieces]
    for c in range(facts // step):
        rows = slice(c * step, (c + 1) * step)
        out_ref[rows, :] = base_ref[rows, :] + gather_rows(low_ref, high_ref, rows, tables, firsts, hot_ref)


def message_kernel(n, pieces, low_ref, high_ref, *refs):
    count = len(pieces)
    tables, refs = refs[:count], refs[count:]
    base_ref, xw_ref, ent_ref, slope_ref, part_ref, hot_ref, msg_ref, erlow_ref, erhigh_ref = refs
    facts = low_ref.shape[0]
    step = hot_ref.shape[0]
    place = ring_place(lax.axis_index("fact"), n)
    firsts = [lax.div(ring_at(place + hops, n) * dims + row, LANES) for hops, row, dims in pieces]
    for k in range(ent_ref.shape[0]):
        here = slice(k * LANES, (k + 1) * LANES)
        erlow_ref[:, here], erhigh_ref[:, here] = row_codes(ent_ref[k : k + 1, :])
    for c in range(facts // step):
        rows = slice(c * step, (c + 1) * step)
        pre = xw_ref[rows, :] + base_ref[rows, :]
        if count:
            pre = pre + gather_rows(low_ref, high_ref, rows, tables, firsts, hot_ref)
        gate = jax.nn.sigmoid(pre)
        msg_ref[rows, :] = (pre * gate).astype(BF)
        slope_ref[rows, :] = gate * (1.0 + pre * (1.0 - gate))

    def add(pair, carry):
        hot = jnp.concatenate(
            [pick_rows(erlow_ref[...], erhigh_ref[...], (pair * 2 + i).astype(F32).astype(BF)) for i in range(2)], axis=0
        )
        rows = pl.ds(pl.multiple_of(pair * 256, 256), 256)
        part_ref[rows, :] = dot(hot, msg_ref[...]).astype(BF)
        return carry

    lax.fori_loop(0, part_ref.shape[0] // 256, add, 0)


def project_kernel(x_ref, w_ref, out_ref):
    out_ref[...] = dot(x_ref[...], w_ref[...])


def ready_kernel(m, width, ents, me_ref, all_ref, idx_ref, x_ref, self_ref, cot_ref, neigh_ref, hidden_ref, div_ref, xt_ref, hold_ref):
    rows_each = ents // m
    me = me_ref[0]
    mine = pl.ds(pl.multiple_of(me * rows_each, rows_each), rows_each)
    hits = jnp.sum(idx_ref[:, idx_ref.shape[1] - 1, :], axis=0, keepdims=True).astype(F32)
    hold_ref[...] = jnp.maximum(jnp.broadcast_to(hits, (LANES, ents)).T, 1.0)
    div_ref[...] = hold_ref[mine, :]
    hidden = jnp.concatenate([all_ref[b, pl.ds(2 * width + me * rows_each, rows_each), :] for b in range(m)], axis=1)
    for b in range(m):
        here = slice(b * LANES, (b + 1) * LANES)
        self_ref[:, here] = dot(hidden, all_ref[b, 0:width, :])
        cot_ref[:, here] = all_ref[b, pl.ds(2 * width + ents + me * rows_each, rows_each), :]
        neigh_ref[b] = all_ref[b, width : 2 * width, :]
        hidden_ref[b] = all_ref[b, 2 * width : 2 * width + ents, :]
    xt_ref[...] = x_ref[...].T


def entity_kernel(n, m, sums_ref, div_ref, self_ref, cot_ref, neigh_ref, back_ref, share_ref):
    rows_each = sums_ref.shape[1]
    width = neigh_ref.shape[1]
    divisor = div_ref[...]
    parts = []
    for b in range(m):
        total = sums_ref[b].astype(F32)
        for f in range(1, n):
            total += sums_ref[f * m + b].astype(F32)
        parts.append((total / divisor).astype(BF))
    aggregate = jnp.concatenate(parts, axis=1)
    share_ref[2] = aggregate
    d_agg = jnp.zeros((rows_each, width), F32)
    for b in range(m):
        here = slice(b * LANES, (b + 1) * LANES)
        pre = self_ref[:, here] + dot(aggregate, neigh_ref[b])
        gate = jax.nn.sigmoid(pre)
        d_pre = (cot_ref[:, here].astype(F32) * (gate * (1.0 + pre * (1.0 - gate)))).astype(BF)
        share_ref[0, :, here] = (pre * gate).astype(BF)
        share_ref[1, :, here] = d_pre
        d_agg += nt(d_pre, neigh_ref[b])
    for b in range(m):
        scaled = (d_agg[:, b * LANES : (b + 1) * LANES] / divisor).astype(BF)
        for f in range(n):
            back_ref[f * m + b] = scaled


def store_shares(n, stride, own, at, total, out_ref):
    for d in range(n):
        piece = total[d * own : (d + 1) * own, :]
        if stride > own:
            piece = jnp.concatenate([piece, jnp.zeros((stride - own, LANES), F32)], axis=0)
        out_ref[d, at : at + stride, :] = piece.astype(BF)


def weight_kernel(n, m, width, stride, me_ref, got_ref, hidden_ref, out_ref, back_ref, total_ref):
    own = width // n
    mine = pl.ds(pl.multiple_of(me_ref[0] * LANES, LANES), LANES)
    out_ref[...] = jnp.concatenate([got_ref[s, 0, :, mine] for s in range(m)], axis=0)
    d_pre = jnp.concatenate([got_ref[s, 1, :, mine] for s in range(m)], axis=0)
    aggregate = jnp.concatenate([got_ref[s, 2] for s in range(m)], axis=0)
    for b in range(m):
        total_ref[b * LANES : (b + 1) * LANES, :] = tn(hidden_ref[b], d_pre)
    store_shares(n, stride, own, 0, total_ref[...], back_ref)
    for b in range(m):
        here = slice(b * LANES, (b + 1) * LANES)
        total_ref[here, :] = tn(aggregate[:, here], d_pre)
    store_shares(n, stride, own, stride, total_ref[...], back_ref)


def codes_kernel(pos_ref, ent_ref, plow_ref, phigh_ref, elow_ref, ehigh_ref):
    for k in range(pos_ref.shape[0]):
        here = slice(k * LANES, (k + 1) * LANES)
        plow_ref[:, here], phigh_ref[:, here] = row_codes(pos_ref[k : k + 1, :])
        elow_ref[here, :], ehigh_ref[here, :] = column_codes(ent_ref[k : k + 1, :])


def request_kernel(n, cap, req_ref, low_ref, high_ref):
    for s in range(n):
        for r in range(cap // LANES):
            at = s * cap + r * LANES
            low_ref[:, at : at + LANES], high_ref[:, at : at + LANES] = row_codes(req_ref[s, r : r + 1, :])


def backward_kernel(n, stride, scaled_ref, slope_ref, low_ref, high_ref, xt_ref, dmsg_ref, share_ref, hot_ref):
    facts = slope_ref.shape[0]
    own = xt_ref.shape[0] // n
    step = hot_ref.shape[0]
    for c in range(facts // step):
        rows = slice(c * step, (c + 1) * step)
        found = gather_rows(low_ref, high_ref, rows, [scaled_ref], [jnp.int32(0)], hot_ref)
        dmsg_ref[rows, :] = (found * slope_ref[rows, :]).astype(BF)
    store_shares(n, stride, own, 0, dot(xt_ref[...], dmsg_ref[...]), share_ref)


def spread_kernel(n, cap, stride, offsets, plow_ref, phigh_ref, dmsg_ref, share_ref, pair_ref, *out_refs):
    me = lax.axis_index("fact")
    for offset, out_ref in zip(offsets, out_refs):
        d = lax.rem(me + offset, n)
        hot = jnp.concatenate(
            [
                pick_rows(plow_ref[...], phigh_ref[...], (d * (cap // LANES) + i).astype(F32).astype(BF))
                for i in range(cap // LANES)
            ],
            axis=0,
        )
        out_ref[0:cap, :] = dot(hot, dmsg_ref[...]).astype(BF)
        out_ref[cap : cap + stride, :] = share_ref[d]
        out_ref[cap + stride : cap + 3 * stride, :] = pair_ref[d]


def table_kernel(n, cap, offsets, first, low_ref, high_ref, *refs):
    count = len(offsets)
    got, refs = refs[:count], refs[count:]
    if not first:
        (base_ref, weight_base_ref), refs = refs[:2], refs[2:]
    out_ref, weight_ref, rows_ref, klow_ref, khigh_ref = refs
    me = lax.axis_index("fact")
    total = None
    for j, (offset, ref) in enumerate(zip(offsets, got)):
        source = lax.rem(me + (n - offset), n)
        here = slice(j * cap, (j + 1) * cap)
        there = pl.ds(pl.multiple_of(source * cap, LANES), cap)
        rows_ref[here, :] = ref[0:cap, :]
        klow_ref[:, here] = low_ref[:, there]
        khigh_ref[:, here] = high_ref[:, there]
        share = ref[cap:, :].astype(F32)
        total = share if total is None else total + share
    weight_ref[...] = total if first else total + weight_base_ref[...]
    blocks = out_ref.shape[0] // LANES
    join = 2 if blocks % 2 == 0 else 1

    def add(group, carry):
        hot = jnp.concatenate(
            [pick_rows(klow_ref[...], khigh_ref[...], (group * join + i).astype(F32).astype(BF)) for i in range(join)], axis=0
        )
        rows = pl.ds(pl.multiple_of(group * join * LANES, LANES), join * LANES)
        sums = dot(hot, rows_ref[...])
        out_ref[rows, :] = sums if first else base_ref[rows, :] + sums
        return carry

    lax.fori_loop(0, blocks // join, add, 0)


def shards(fact_x, dim_owner, dim_slot, fact_owner, fact_slot, dim_table, entity_h, w_msg, w_self, w_neigh, cotangent):
    n, m = lax.axis_size("fact"), lax.axis_size("feat")
    facts = fact_x.shape[0]
    chunks = facts // LANES
    ents = entity_h.shape[0]
    rows_each = ents // m
    width = w_msg.shape[0]
    dims = dim_table.shape[0]
    cap = -(-(3 * facts // n) // LANES) * LANES
    slots = n * cap
    groups = cap // LANES + 1
    own = width // n
    stride = max(16, own)
    me = lax.axis_index("feat").astype(jnp.int32).reshape(1)
    tie = lax.optimization_barrier
    ringed = n <= 8

    x_full = lax.all_gather(fact_x, "feat", axis=1, tiled=True)
    ring = [2 * p if p < n // 2 else 2 * (n - 1 - p) + 1 for p in range(n)]
    to_right = [(ring[p], ring[(p + 1) % n]) for p in range(n)]
    to_left = [(ring[(p + 1) % n], ring[p]) for p in range(n)]

    def pass_on(right, left):
        return lax.ppermute(right, "fact", to_right), lax.ppermute(left, "fact", to_left)

    if ringed:
        right, left = pass_on(dim_table, dim_table)

    by_lane = (chunks, LANES)
    columns = shape((facts, LANES), BF)
    asks, pos, entity, dlow, dhigh = call(
        functools.partial(route_kernel, n, cap, ents, dims),
        (
            shape((n, groups, LANES), jnp.int32),
            shape(by_lane, jnp.int32),
            shape(by_lane, jnp.int32),
            columns,
            columns,
        ),
        [],
        1 << 28,
        "route",
    )(dim_owner.reshape(by_lane), dim_slot.reshape(by_lane), fact_owner.reshape(by_lane), fact_slot.reshape(by_lane))
    if ringed:
        right, left, asks, pos, entity, dlow, dhigh = tie((right, left, asks, pos, entity, dlow, dhigh))
    weights, _ = tie(((w_self, w_neigh, entity_h, cotangent), pos))
    everything = lax.all_gather(jnp.concatenate(weights, axis=0), "feat")

    step = 512

    def look(pieces, tables, base):
        rows = sum(t.shape[0] for t in tables)
        return call(
            functools.partial(look_kernel, n, pieces),
            shape((facts, LANES), F32),
            [pltpu.VMEM((step, rows), BF)],
            2 * facts * rows * LANES,
            "look",
        )(dlow, dhigh, *tables, base)

    found = jnp.zeros((facts, LANES), F32)
    asked = lax.all_to_all(asks, "fact", 0, 0)
    if ringed:
        last, last_pieces = [dim_table], [(0, 0, dims)]
        for k in range(1, n // 2):
            if k < n // 2 - 1:
                after = pass_on(right, left)
            else:
                half = dims // 2
                after = pass_on(right[:half], left[half:])
            if k > 1:
                pieces, tables = [(-k, 0, dims), (k, 0, dims)], [right, left]
            else:
                pieces, tables = [(0, 0, dims), (-k, 0, dims), (k, 0, dims)], [dim_table, right, left]
            found = look(pieces, tables, found)
            right, left = after
            if k < n // 2 - 1:
                right, left, found = tie((right, left, found))
        last = [right, left]
        last_pieces = [(-(n // 2), 0, dims), (n // 2, half, dims)]
    else:
        whole = lax.all_gather(dim_table, "fact")
        order = jnp.take(whole, ring_at(ring_place(lax.axis_index("fact"), n) + jnp.arange(n), n), axis=0)
        for k in range(0, n, 8):
            found = look([(k + i, 0, dims) for i in range(8)], [order[k + i] for i in range(8)], found)
        last, last_pieces = [], []
    xw = call(project_kernel, shape((facts, LANES), F32), [], 2 * facts * width * LANES, "project")(x_full, w_msg)
    last_rows = max(LANES, sum(t.shape[0] for t in last))
    slope, part = call(
        functools.partial(message_kernel, n, last_pieces),
        (shape((facts, LANES), F32), shape((n * ents, LANES), BF)),
        [
            pltpu.VMEM((step, last_rows), BF),
            pltpu.VMEM((facts, LANES), BF),
            pltpu.VMEM((LANES, facts), BF),
            pltpu.VMEM((16, facts), BF),
        ],
        2 * facts * (last_rows + n * ents) * LANES,
        "message",
    )(dlow, dhigh, *last, found, xw, entity)
    sums = lax.all_to_all(part.reshape(n * m, rows_each, LANES), ("fact", "feat"), 0, 0)
    everything, x_later, asked, pos, entity, _ = tie((everything, x_full, asked, pos, entity, part))
    self_part, cot, neigh, hidden, divisor, x_turned = call(
        functools.partial(ready_kernel, m, width, ents),
        (
            shape((rows_each, width), F32),
            shape((rows_each, width), BF),
            shape((m, width, LANES), BF),
            shape((m, ents, LANES), BF),
            shape((rows_each, LANES), F32),
            shape((width, facts), BF),
        ),
        [pltpu.VMEM((ents, LANES), F32)],
        1 << 28,
        "ready",
    )(me, everything, asked, x_later)
    back, share = call(
        functools.partial(entity_kernel, n, m),
        (shape((n * m, rows_each, LANES), BF), shape((3, rows_each, width), BF)),
        [],
        4 * rows_each * width * width,
        "entity",
    )(sums, divisor, self_part, cot, neigh)
    scaled = lax.all_to_all(back, ("fact", "feat"), 0, 0).reshape(n * ents, LANES)
    got = lax.all_gather(share, "feat")
    pos, entity, asked, _ = tie((pos, entity, asked, back))
    plow, phigh, elow, ehigh = call(
        codes_kernel,
        (shape((LANES, facts), BF), shape((16, facts), BF), columns, columns),
        [],
        1 << 26,
        "codes",
    )(pos, entity)
    rlow, rhigh = call(
        functools.partial(request_kernel, n, cap),
        (shape((LANES, slots), BF), shape((16, slots), BF)),
        [],
        1 << 26,
        "requests",
    )(asked)
    output_h, pair = call(
        functools.partial(weight_kernel, n, m, width, stride),
        (shape((ents, LANES), BF), shape((n, 2 * stride, LANES), BF)),
        [pltpu.VMEM((width, LANES), F32)],
        4 * ents * width * LANES,
        "weight",
    )(me, got, hidden)
    d_msg, msg_share = call(
        functools.partial(backward_kernel, n, stride),
        (columns, shape((n, stride, LANES), BF)),
        [pltpu.VMEM((step, n * ents), BF)],
        2 * facts * (n * ents + width) * LANES,
        "backward",
    )(scaled, slope, elow, ehigh, x_turned)

    long = cap + 3 * stride

    def spread(offsets):
        return call(
            functools.partial(spread_kernel, n, cap, stride, offsets),
            tuple(shape((long, LANES), BF) for _ in offsets),
            [],
            2 * facts * cap * LANES * len(offsets),
            "spread",
        )(plow, phigh, d_msg, msg_share, pair)

    def add_up(offsets, got, base):
        return call(
            functools.partial(table_kernel, n, cap, offsets, base is None),
            (shape((dims, LANES), F32), shape((3 * stride, LANES), F32)),
            [
                pltpu.VMEM((cap * len(got), LANES), BF),
                pltpu.VMEM((LANES, cap * len(got)), BF),
                pltpu.VMEM((16, cap * len(got)), BF),
            ],
            2 * cap * dims * LANES * len(got),
            "table",
        )(rlow, rhigh, *got, *(base or ()))

    totals = None
    if ringed:
        turns = [[n // 2]] + [[k, n - k] for k in range(n // 2 - 1, 0, -1)]
        arrived = []
        for offsets in turns:
            sent = spread(offsets)
            arrived.append(
                [
                    lax.ppermute(message, "fact", [(i, (i + offset) % n) for i in range(n)])
                    for offset, message in zip(offsets, sent)
                ]
            )
        kept = spread([0])
        turns[0], arrived[0] = [0] + turns[0], [kept[0]] + arrived[0]
        for offsets, got in zip(turns, arrived):
            totals = add_up(offsets, got, totals)
    else:
        fact_me = lax.axis_index("fact")
        sent = [message for k in range(0, n, 8) for message in spread(list(range(k, k + 8)))]
        by_owner = jnp.take(jnp.stack(sent), lax.rem(jnp.arange(n) - fact_me + n, n), axis=0)
        owned = lax.all_to_all(by_owner, "fact", 0, 0)
        by_offset = jnp.take(owned, lax.rem(fact_me - jnp.arange(n) + n, n), axis=0)
        for k in range(0, n, 8):
            totals = add_up(list(range(k, k + 8)), [by_offset[k + i] for i in range(8)], totals)
    grad_dim, weight = totals
    return (
        output_h,
        weight[0:own],
        weight[stride : stride + own],
        weight[2 * stride : 2 * stride + own],
        grad_dim,
    )


def solution(mesh):
    placed = (
        P("fact", "feat"),
        P("fact", None),
        P("fact"),
        P("fact", None),
        P("fact"),
        P("fact", "feat"),
        P("fact", "feat"),
        P(None, "feat"),
        P(None, "feat"),
        P(None, "feat"),
        P("fact", "feat"),
    )
    return jax.shard_map(
        shards,
        mesh=mesh,
        in_specs=placed,
        out_specs=(P("fact", "feat"),) * 5,
        check_vma=False,
    )
```

```python
import functools

import jax
import jax.numpy as jnp
from jax import lax
from jax.experimental import pallas as pl
from jax.experimental.pallas import tpu as pltpu
from jax.sharding import PartitionSpec as P

LANES = 128
BF = jnp.bfloat16
F32 = jnp.float32
VMEM_LIMIT = 16 * 1024 * 1024
VMEM_LIMIT_LARGE = 40 * 1024 * 1024


def call(kernel, out_shape, scratch, flops, name, limit=VMEM_LIMIT):
    return pl.pallas_call(
        kernel,
        out_shape=out_shape,
        scratch_shapes=scratch,
        compiler_params=pltpu.CompilerParams(vmem_limit_bytes=limit),
        cost_estimate=pl.CostEstimate(flops=flops, bytes_accessed=1 << 20, transcendentals=0),
        name=name,
    )


def shape(dims, dtype):
    return jax.ShapeDtypeStruct(dims, dtype)


def nt(a, b):
    return lax.dot_general(a, b, (((1,), (1,)), ((), ())), preferred_element_type=F32)


def tn(a, b):
    return lax.dot_general(a, b, (((0,), (0,)), ((), ())), preferred_element_type=F32)


def dot(a, b):
    return jnp.dot(a, b, preferred_element_type=F32)


def flag(condition):
    return jnp.where(condition, 1.0, 0.0).astype(BF)


def column_codes(row):
    keys = jnp.broadcast_to(row, (LANES, LANES)).astype(F32).T.astype(jnp.int32)
    lane = lax.broadcasted_iota(jnp.int32, (LANES, LANES), 1)
    return flag((keys & (LANES - 1)) == lane), (keys >> 7).astype(F32).astype(BF)


def row_codes(row):
    keys = jnp.broadcast_to(row, (LANES, LANES))
    sub = lax.broadcasted_iota(jnp.int32, (LANES, LANES), 0)
    high = jnp.broadcast_to((row >> 7).astype(F32), (16, LANES)).astype(BF)
    return flag((keys & (LANES - 1)) == sub), high


def pick_block(low, high, block):
    zero = jnp.zeros((), BF)
    return jnp.where(high == block, low, zero)


def pick_rows(low, high, block):
    wide = low.reshape(LANES // 16, 16, low.shape[1])
    picked = pick_block(wide, high[None], block)
    return picked.reshape(low.shape)


def route_kernel(n, cap, ents, dims, do_ref, ds_ref, fo_ref, fs_ref, out_ref, pos_ref, ent_ref, dlow_ref, dhigh_ref):
    chunks = do_ref.shape[0]
    owner = do_ref[...]
    kind = lax.broadcasted_iota(jnp.int32, (n, chunks, LANES), 0)
    held = jnp.where(kind == owner[None], 1.0, 0.0).reshape(n * chunks, LANES)
    held_bf = held.astype(BF)
    i0 = lax.broadcasted_iota(jnp.int32, (LANES, LANES), 0)
    i1 = lax.broadcasted_iota(jnp.int32, (LANES, LANES), 1)
    inside = dot(held_bf, flag(i0 < i1))
    r0 = lax.broadcasted_iota(jnp.int32, (n * chunks, n * chunks), 0)
    r1 = lax.broadcasted_iota(jnp.int32, (n * chunks, n * chunks), 1)
    earlier = flag((r0 // chunks == r1 // chunks) & (r1 < r0))
    before = dot(dot(earlier, held_bf).astype(BF), jnp.ones((LANES, LANES), BF))
    rank = jnp.sum((held * (inside + before)).reshape(n, chunks, LANES), axis=0)
    rank = rank.astype(jnp.int32)
    entity_owner = fo_ref[...]
    entity_slot = fs_ref[...]
    value = ds_ref[...]
    pos_ref[...] = owner * cap + rank
    fact_dim = owner * dims + value
    entity = entity_owner * ents + entity_slot
    ent_ref[...] = entity
    words = [(value >> 5).astype(F32), (value & 31).astype(F32), (entity >> 5).astype(F32), (entity & 31).astype(F32)]
    names = lax.broadcasted_iota(jnp.int32, (n, LANES), 0)
    places = lax.broadcasted_iota(jnp.int32, (cap, LANES), 0)
    slots = lax.broadcasted_iota(jnp.int32, (ents, LANES), 0)
    asked = [jnp.zeros((n, cap), F32) for _ in words]
    hits = jnp.zeros((n, ents), F32)
    for k in range(chunks):
        here = slice(k * LANES, (k + 1) * LANES)
        mine = jnp.where(names == owner[k : k + 1], 1.0, 0.0)
        at = flag(places == rank[k : k + 1])
        for w, word in enumerate(words):
            asked[w] += nt((mine * word[k : k + 1]).astype(BF), at)
        hits += nt(flag(names == entity_owner[k : k + 1]), flag(slots == entity_slot[k : k + 1]))
        dlow_ref[here, :], dhigh_ref[here, :] = column_codes(fact_dim[k : k + 1])
    groups = cap // LANES
    asked_dim = (asked[0] * 32.0 + asked[1]).astype(jnp.int32)
    asked_ent = (asked[2] * 32.0 + asked[3]).astype(jnp.int32)
    for r in range(groups):
        out_ref[:, r, :] = asked_dim[:, r * LANES : (r + 1) * LANES]
        out_ref[:, groups + r, :] = asked_ent[:, r * LANES : (r + 1) * LANES]
    out_ref[:, 2 * groups, :] = hits.astype(jnp.int32)


def gather_rows(low_ref, high_ref, rows, table_refs, firsts, hot_ref):
    at = 0
    low, high = low_ref[rows, :], high_ref[rows, :]
    for table, first in zip(table_refs, firsts):
        for k in range(table.shape[0] // LANES):
            hot_ref[:, at : at + LANES] = pick_block(low, high, (first + k).astype(F32).astype(BF))
            at += LANES
    total, at = None, 0
    for table in table_refs:
        part = dot(hot_ref[:, at : at + table.shape[0]], table[...])
        total = part if total is None else total + part
        at += table.shape[0]
    return total


def ring_at(place, n):
    place = lax.rem(place + 2 * n, n)
    return jnp.where(place < n // 2, 2 * place, 2 * (n - 1 - place) + 1)


def ring_place(index, n):
    half = lax.div(index, 2)
    return jnp.where(lax.rem(index, 2) == 0, half, n - 1 - half)


def look_kernel(n, pieces, low_ref, high_ref, *refs):
    count = len(pieces)
    tables, base_ref, out_ref, hot_ref = refs[:count], refs[count], refs[-2], refs[-1]
    facts = low_ref.shape[0]
    step = hot_ref.shape[0]
    place = ring_place(lax.axis_index("fact"), n)
    firsts = [lax.div(ring_at(place + hops, n) * dims + row, LANES) for hops, row, dims in pieces]
    for c in range(facts // step):
        rows = slice(c * step, (c + 1) * step)
        out_ref[rows, :] = base_ref[rows, :] + gather_rows(low_ref, high_ref, rows, tables, firsts, hot_ref)


def message_kernel(n, pieces, low_ref, high_ref, *refs):
    count = len(pieces)
    tables, refs = refs[:count], refs[count:]
    base_ref, xw_ref, ent_ref, slope_ref, part_ref, hot_ref, msg_ref, erlow_ref, erhigh_ref = refs
    facts = low_ref.shape[0]
    step = hot_ref.shape[0]
    place = ring_place(lax.axis_index("fact"), n)
    firsts = [lax.div(ring_at(place + hops, n) * dims + row, LANES) for hops, row, dims in pieces]
    for k in range(ent_ref.shape[0]):
        here = slice(k * LANES, (k + 1) * LANES)
        erlow_ref[:, here], erhigh_ref[:, here] = row_codes(ent_ref[k : k + 1, :])
    for c in range(facts // step):
        rows = slice(c * step, (c + 1) * step)
        pre = xw_ref[rows, :] + base_ref[rows, :]
        if count:
            pre = pre + gather_rows(low_ref, high_ref, rows, tables, firsts, hot_ref)
        gate = jax.nn.sigmoid(pre)
        msg_ref[rows, :] = (pre * gate).astype(BF)
        slope_ref[rows, :] = gate * (1.0 + pre * (1.0 - gate))

    def add(pair, carry):
        hot = jnp.concatenate(
            [pick_rows(erlow_ref[...], erhigh_ref[...], (pair * 2 + i).astype(F32).astype(BF)) for i in range(2)], axis=0
        )
        rows = pl.ds(pl.multiple_of(pair * 256, 256), 256)
        part_ref[rows, :] = dot(hot, msg_ref[...]).astype(BF)
        return carry

    lax.fori_loop(0, part_ref.shape[0] // 256, add, 0)


def project_kernel(x_ref, w_ref, out_ref):
    out_ref[...] = dot(x_ref[...], w_ref[...])


def ready_kernel(m, width, ents, me_ref, all_ref, idx_ref, x_ref, self_ref, cot_ref, neigh_ref, hidden_ref, div_ref, xt_ref, hold_ref):
    rows_each = ents // m
    me = me_ref[0]
    mine = pl.ds(pl.multiple_of(me * rows_each, rows_each), rows_each)
    hits = jnp.sum(idx_ref[:, idx_ref.shape[1] - 1, :], axis=0, keepdims=True).astype(F32)
    hold_ref[...] = jnp.maximum(jnp.broadcast_to(hits, (LANES, ents)).T, 1.0)
    div_ref[...] = hold_ref[mine, :]
    hidden = jnp.concatenate([all_ref[b, pl.ds(2 * width + me * rows_each, rows_each), :] for b in range(m)], axis=1)
    for b in range(m):
        here = slice(b * LANES, (b + 1) * LANES)
        self_ref[:, here] = dot(hidden, all_ref[b, 0:width, :])
        cot_ref[:, here] = all_ref[b, pl.ds(2 * width + ents + me * rows_each, rows_each), :]
        neigh_ref[b] = all_ref[b, width : 2 * width, :]
        hidden_ref[b] = all_ref[b, 2 * width : 2 * width + ents, :]
    xt_ref[...] = x_ref[...].T


def entity_kernel(n, m, sums_ref, div_ref, self_ref, cot_ref, neigh_ref, back_ref, share_ref):
    rows_each = sums_ref.shape[1]
    width = neigh_ref.shape[1]
    divisor = div_ref[...]
    parts = []
    for b in range(m):
        total = sums_ref[b].astype(F32)
        for f in range(1, n):
            total += sums_ref[f * m + b].astype(F32)
        parts.append((total / divisor).astype(BF))
    aggregate = jnp.concatenate(parts, axis=1)
    share_ref[2] = aggregate
    d_agg = jnp.zeros((rows_each, width), F32)
    for b in range(m):
        here = slice(b * LANES, (b + 1) * LANES)
        pre = self_ref[:, here] + dot(aggregate, neigh_ref[b])
        gate = jax.nn.sigmoid(pre)
        d_pre = (cot_ref[:, here].astype(F32) * (gate * (1.0 + pre * (1.0 - gate)))).astype(BF)
        share_ref[0, :, here] = (pre * gate).astype(BF)
        share_ref[1, :, here] = d_pre
        d_agg += nt(d_pre, neigh_ref[b])
    for b in range(m):
        scaled = (d_agg[:, b * LANES : (b + 1) * LANES] / divisor).astype(BF)
        for f in range(n):
            back_ref[f * m + b] = scaled


def store_shares(n, stride, own, at, total, out_ref):
    for d in range(n):
        piece = total[d * own : (d + 1) * own, :]
        if stride > own:
            piece = jnp.concatenate([piece, jnp.zeros((stride - own, LANES), F32)], axis=0)
        out_ref[d, at : at + stride, :] = piece.astype(BF)


def weight_kernel(n, m, width, stride, me_ref, got_ref, hidden_ref, out_ref, back_ref, total_ref):
    own = width // n
    mine = pl.ds(pl.multiple_of(me_ref[0] * LANES, LANES), LANES)
    out_ref[...] = jnp.concatenate([got_ref[s, 0, :, mine] for s in range(m)], axis=0)
    d_pre = jnp.concatenate([got_ref[s, 1, :, mine] for s in range(m)], axis=0)
    aggregate = jnp.concatenate([got_ref[s, 2] for s in range(m)], axis=0)
    for b in range(m):
        total_ref[b * LANES : (b + 1) * LANES, :] = tn(hidden_ref[b], d_pre)
    store_shares(n, stride, own, 0, total_ref[...], back_ref)
    for b in range(m):
        here = slice(b * LANES, (b + 1) * LANES)
        total_ref[here, :] = tn(aggregate[:, here], d_pre)
    store_shares(n, stride, own, stride, total_ref[...], back_ref)


def codes_kernel(ent_ref, elow_ref, ehigh_ref):
    for k in range(ent_ref.shape[0]):
        here = slice(k * LANES, (k + 1) * LANES)
        elow_ref[here, :], ehigh_ref[here, :] = column_codes(ent_ref[k : k + 1, :])


def request_kernel(n, cap, req_ref, low_ref, high_ref, clow_ref, chigh_ref):
    groups = cap // LANES

    def body(s, carry):
        for r in range(groups):
            here = pl.ds(pl.multiple_of(s * cap + r * LANES, LANES), LANES)
            low_ref[:, here], high_ref[:, here] = row_codes(req_ref[s, r : r + 1, :])
            clow_ref[here, :], chigh_ref[here, :] = column_codes(req_ref[s, groups + r : groups + r + 1, :])
        return carry

    lax.fori_loop(0, n, body, 0)


def spread_kernel(n, cap, slope_ref, pos_ref, out_ref, slope_bf_ref, plow_ref, phigh_ref):
    slope_bf_ref[...] = slope_ref[...].astype(BF)
    for k in range(pos_ref.shape[0]):
        here = slice(k * LANES, (k + 1) * LANES)
        plow_ref[:, here], phigh_ref[:, here] = row_codes(pos_ref[k : k + 1, :])

    def body(d, carry):
        hot = jnp.concatenate(
            [
                pick_rows(plow_ref[...], phigh_ref[...], (d * (cap // LANES) + i).astype(F32).astype(BF))
                for i in range(cap // LANES)
            ],
            axis=0,
        )
        out_ref[d] = dot(hot, slope_bf_ref[...]).astype(BF)
        return carry

    lax.fori_loop(0, n, body, 0)


def backward_kernel(n, stride, scaled_ref, slope_ref, low_ref, high_ref, xt_ref, pair_ref, share_ref, hot_ref, dmsg_ref):
    facts = slope_ref.shape[0]
    own = xt_ref.shape[0] // n
    step = hot_ref.shape[0]
    for c in range(facts // step):
        rows = slice(c * step, (c + 1) * step)
        found = gather_rows(low_ref, high_ref, rows, [scaled_ref], [jnp.int32(0)], hot_ref)
        dmsg_ref[rows, :] = (found * slope_ref[rows, :]).astype(BF)
    share_ref[:, stride:, :] = pair_ref[...]
    store_shares(n, stride, own, 0, dot(xt_ref[...], dmsg_ref[...]), share_ref)


def table_kernel(scaled_ref, slopes_ref, low_ref, high_ref, clow_ref, chigh_ref, out_ref, hot_ref, rows_ref):
    slots = rows_ref.shape[0]
    step = hot_ref.shape[0]

    def form(c, carry):
        rows = pl.ds(pl.multiple_of(c * step, step), step)
        found = gather_rows(clow_ref, chigh_ref, rows, [scaled_ref], [jnp.int32(0)], hot_ref)
        rows_ref[rows, :] = (found * slopes_ref[rows, :].astype(F32)).astype(BF)
        return carry

    lax.fori_loop(0, slots // step, form, 0)
    blocks = out_ref.shape[0] // LANES
    join = 2 if blocks % 2 == 0 else 1

    def add(group, carry):
        hot = jnp.concatenate(
            [pick_rows(low_ref[...], high_ref[...], (group * join + i).astype(F32).astype(BF)) for i in range(join)], axis=0
        )
        rows = pl.ds(pl.multiple_of(group * join * LANES, LANES), join * LANES)
        out_ref[rows, :] = dot(hot, rows_ref[...])
        return carry

    lax.fori_loop(0, blocks // join, add, 0)


def total_kernel(stride, got_ref, *out_refs):
    for j, ref in enumerate(out_refs):
        here = slice(j * stride, (j + 1) * stride)
        total = got_ref[0, here, :].astype(F32)
        for s in range(1, got_ref.shape[0]):
            total += got_ref[s, here, :].astype(F32)
        ref[...] = total[0 : ref.shape[0], :]


def shards(fact_x, dim_owner, dim_slot, fact_owner, fact_slot, dim_table, entity_h, w_msg, w_self, w_neigh, cotangent):
    n, m = lax.axis_size("fact"), lax.axis_size("feat")
    facts = fact_x.shape[0]
    chunks = facts // LANES
    ents = entity_h.shape[0]
    rows_each = ents // m
    width = w_msg.shape[0]
    dims = dim_table.shape[0]
    cap = -(-(3 * facts // n) // LANES) * LANES
    slots = n * cap
    groups = 2 * (cap // LANES) + 1
    own = width // n
    stride = max(16, own)
    me = lax.axis_index("feat").astype(jnp.int32).reshape(1)
    tie = lax.optimization_barrier
    ringed = n <= 8

    x_full = lax.all_gather(fact_x, "feat", axis=1, tiled=True)
    ring = [2 * p if p < n // 2 else 2 * (n - 1 - p) + 1 for p in range(n)]
    to_right = [(ring[p], ring[(p + 1) % n]) for p in range(n)]
    to_left = [(ring[(p + 1) % n], ring[p]) for p in range(n)]

    def pass_on(right, left):
        return lax.ppermute(right, "fact", to_right), lax.ppermute(left, "fact", to_left)

    if ringed:
        right, left = pass_on(dim_table, dim_table)

    by_lane = (chunks, LANES)
    columns = shape((facts, LANES), BF)
    asks, pos, entity, dlow, dhigh = call(
        functools.partial(route_kernel, n, cap, ents, dims),
        (
            shape((n, groups, LANES), jnp.int32),
            shape(by_lane, jnp.int32),
            shape(by_lane, jnp.int32),
            columns,
            columns,
        ),
        [],
        1 << 28,
        "route",
    )(dim_owner.reshape(by_lane), dim_slot.reshape(by_lane), fact_owner.reshape(by_lane), fact_slot.reshape(by_lane))
    if ringed:
        right, left, asks, pos, entity, dlow, dhigh = tie((right, left, asks, pos, entity, dlow, dhigh))

    step = 512
    limit = VMEM_LIMIT if ringed else VMEM_LIMIT_LARGE

    def look(pieces, tables, base):
        rows = sum(t.shape[0] for t in tables)
        return call(
            functools.partial(look_kernel, n, pieces),
            shape((facts, LANES), F32),
            [pltpu.VMEM((step, rows), BF)],
            2 * facts * rows * LANES,
            "look",
            limit,
        )(dlow, dhigh, *tables, base)

    found = jnp.zeros((facts, LANES), F32)
    asked = lax.all_to_all(asks, "fact", 0, 0)
    if ringed:
        last, last_pieces = [dim_table], [(0, 0, dims)]
        for k in range(1, n // 2):
            if k < n // 2 - 1:
                after = pass_on(right, left)
            else:
                half = dims // 2
                after = pass_on(right[:half], left[half:])
            if k > 1:
                pieces, tables = [(-k, 0, dims), (k, 0, dims)], [right, left]
            else:
                pieces, tables = [(0, 0, dims), (-k, 0, dims), (k, 0, dims)], [dim_table, right, left]
            found = look(pieces, tables, found)
            right, left = after
            if k == n // 2 - 2:
                right, left, found, asked, x_full = tie((right, left, found, asked, x_full))
            elif k < n // 2 - 1:
                right, left, found = tie((right, left, found))
            if k == 1:
                weights, _ = tie(((w_self, w_neigh, entity_h, cotangent), found))
        last = [right, left]
        last_pieces = [(-(n // 2), 0, dims), (n // 2, half, dims)]
    else:
        whole = lax.all_gather(dim_table, "fact")
        order = jnp.take(whole, ring_at(ring_place(lax.axis_index("fact"), n) + jnp.arange(n), n), axis=0)
        for k in range(0, n, 8):
            found = look([(k + i, 0, dims) for i in range(8)], [order[k + i] for i in range(8)], found)
        last, last_pieces = [], []
        weights = (w_self, w_neigh, entity_h, cotangent)
    everything = lax.all_gather(jnp.concatenate(weights, axis=0), "feat")
    xw = call(project_kernel, shape((facts, LANES), F32), [], 2 * facts * width * LANES, "project")(x_full, w_msg)
    last_rows = max(LANES, sum(t.shape[0] for t in last))
    slope, part = call(
        functools.partial(message_kernel, n, last_pieces),
        (shape((facts, LANES), F32), shape((n * ents, LANES), BF)),
        [
            pltpu.VMEM((step, last_rows), BF),
            pltpu.VMEM((facts, LANES), BF),
            pltpu.VMEM((LANES, facts), BF),
            pltpu.VMEM((16, facts), BF),
        ],
        2 * facts * (last_rows + n * ents) * LANES,
        "message",
    )(dlow, dhigh, *last, found, xw, entity)
    sums = lax.all_to_all(part.reshape(n * m, rows_each, LANES), ("fact", "feat"), 0, 0)
    slopes = call(
        functools.partial(spread_kernel, n, cap),
        shape((n, cap, LANES), BF),
        [pltpu.VMEM((facts, LANES), BF), pltpu.VMEM((LANES, facts), BF), pltpu.VMEM((16, facts), BF)],
        2 * facts * slots * LANES,
        "spread",
        limit,
    )(slope, pos)
    slopes = lax.all_to_all(slopes, "fact", 0, 0).reshape(slots, LANES)
    everything, x_later, asked, entity, _ = tie((everything, x_full, asked, entity, part))
    self_part, cot, neigh, hidden, divisor, x_turned = call(
        functools.partial(ready_kernel, m, width, ents),
        (
            shape((rows_each, width), F32),
            shape((rows_each, width), BF),
            shape((m, width, LANES), BF),
            shape((m, ents, LANES), BF),
            shape((rows_each, LANES), F32),
            shape((width, facts), BF),
        ),
        [pltpu.VMEM((ents, LANES), F32)],
        1 << 28,
        "ready",
    )(me, everything, asked, x_later)
    back, share = call(
        functools.partial(entity_kernel, n, m),
        (shape((n * m, rows_each, LANES), BF), shape((3, rows_each, width), BF)),
        [],
        4 * rows_each * width * width,
        "entity",
    )(sums, divisor, self_part, cot, neigh)
    scaled = lax.all_to_all(back, ("fact", "feat"), 0, 0).reshape(n * ents, LANES)
    got = lax.all_gather(share, "feat")
    entity, asked, _ = tie((entity, asked, back))
    elow, ehigh = call(codes_kernel, (columns, columns), [], 1 << 26, "codes")(entity)
    slot_columns = shape((slots, LANES), BF)
    rlow, rhigh, clow, chigh = call(
        functools.partial(request_kernel, n, cap),
        (shape((LANES, slots), BF), shape((16, slots), BF), slot_columns, slot_columns),
        [],
        1 << 26,
        "requests",
        limit,
    )(asked)
    output_h, pair = call(
        functools.partial(weight_kernel, n, m, width, stride),
        (shape((ents, LANES), BF), shape((n, 2 * stride, LANES), BF)),
        [pltpu.VMEM((width, LANES), F32)],
        4 * ents * width * LANES,
        "weight",
    )(me, got, hidden)
    shares = call(
        functools.partial(backward_kernel, n, stride),
        shape((n, 3 * stride, LANES), BF),
        [pltpu.VMEM((step, n * ents), BF), pltpu.VMEM((facts, LANES), BF)],
        2 * facts * (n * ents + width) * LANES,
        "backward",
        limit,
    )(scaled, slope, elow, ehigh, x_turned, pair)
    owned = lax.all_to_all(shares, "fact", 0, 0)
    scaled, _ = tie((scaled, shares))
    grad_dim = call(
        table_kernel,
        shape((dims, LANES), F32),
        [pltpu.VMEM((step, n * ents), BF), pltpu.VMEM((slots, LANES), BF)],
        2 * slots * (dims + n * ents) * LANES,
        "table",
        limit,
    )(scaled, slopes, rlow, rhigh, clow, chigh)
    grad_msg, grad_self, grad_neigh = call(
        functools.partial(total_kernel, stride), (shape((own, LANES), F32),) * 3, [], 1 << 20, "total"
    )(owned)
    return output_h, grad_msg, grad_self, grad_neigh, grad_dim


def solution(mesh):
    placed = (
        P("fact", "feat"),
        P("fact", None),
        P("fact"),
        P("fact", None),
        P("fact"),
        P("fact", "feat"),
        P("fact", "feat"),
        P(None, "feat"),
        P(None, "feat"),
        P(None, "feat"),
        P("fact", "feat"),
    )
    return jax.shard_map(
        shards,
        mesh=mesh,
        in_specs=placed,
        out_specs=(P("fact", "feat"),) * 5,
        check_vma=False,
    )
```

```python
import functools

import jax
import jax.numpy as jnp
from jax import lax
from jax.experimental import pallas as pl
from jax.experimental.pallas import tpu as pltpu
from jax.sharding import PartitionSpec as P

LANES = 128
BF = jnp.bfloat16
F32 = jnp.float32
VMEM_LIMIT = 16 * 1024 * 1024
VMEM_LIMIT_LARGE = 40 * 1024 * 1024


def call(kernel, out_shape, scratch, flops, name, limit=VMEM_LIMIT):
    return pl.pallas_call(
        kernel,
        out_shape=out_shape,
        scratch_shapes=scratch,
        compiler_params=pltpu.CompilerParams(vmem_limit_bytes=limit),
        cost_estimate=pl.CostEstimate(flops=flops, bytes_accessed=1 << 20, transcendentals=0),
        name=name,
    )


def shape(dims, dtype):
    return jax.ShapeDtypeStruct(dims, dtype)


def nt(a, b):
    return lax.dot_general(a, b, (((1,), (1,)), ((), ())), preferred_element_type=F32)


def tn(a, b):
    return lax.dot_general(a, b, (((0,), (0,)), ((), ())), preferred_element_type=F32)


def dot(a, b):
    return jnp.dot(a, b, preferred_element_type=F32)


def flag(condition):
    return jnp.where(condition, 1.0, 0.0).astype(BF)


def column_codes(row):
    keys = jnp.broadcast_to(row, (LANES, LANES)).astype(F32).T.astype(jnp.int32)
    lane = lax.broadcasted_iota(jnp.int32, (LANES, LANES), 1)
    return flag((keys & (LANES - 1)) == lane), (keys >> 7).astype(F32).astype(BF)


def row_codes(row):
    keys = jnp.broadcast_to(row, (LANES, LANES))
    sub = lax.broadcasted_iota(jnp.int32, (LANES, LANES), 0)
    high = jnp.broadcast_to((row >> 7).astype(F32), (16, LANES)).astype(BF)
    return flag((keys & (LANES - 1)) == sub), high


def pick_block(low, high, block):
    zero = jnp.zeros((), BF)
    return jnp.where(high == block, low, zero)


def pick_rows(low, high, block):
    wide = low.reshape(LANES // 16, 16, low.shape[1])
    picked = pick_block(wide, high[None], block)
    return picked.reshape(low.shape)


def route_kernel(n, cap, ents, dims, do_ref, ds_ref, fo_ref, fs_ref, out_ref, hits_ref, pos_ref, ent_ref, dlow_ref, dhigh_ref, words_ref):
    chunks = do_ref.shape[0]
    owner = do_ref[...]
    kind = lax.broadcasted_iota(jnp.int32, (n, chunks, LANES), 0)
    held = jnp.where(kind == owner[None], 1.0, 0.0).reshape(n * chunks, LANES)
    held_bf = held.astype(BF)
    i0 = lax.broadcasted_iota(jnp.int32, (LANES, LANES), 0)
    i1 = lax.broadcasted_iota(jnp.int32, (LANES, LANES), 1)
    inside = dot(held_bf, flag(i0 < i1))
    r0 = lax.broadcasted_iota(jnp.int32, (n * chunks, n * chunks), 0)
    r1 = lax.broadcasted_iota(jnp.int32, (n * chunks, n * chunks), 1)
    earlier = flag((r0 // chunks == r1 // chunks) & (r1 < r0))
    before = dot(dot(earlier, held_bf).astype(BF), jnp.ones((LANES, LANES), BF))
    rank = jnp.sum((held * (inside + before)).reshape(n, chunks, LANES), axis=0)
    rank = rank.astype(jnp.int32)
    entity_owner = fo_ref[...]
    entity_slot = fs_ref[...]
    value = ds_ref[...]
    pos_ref[...] = owner * cap + rank
    fact_dim = owner * dims + value
    entity = entity_owner * ents + entity_slot
    ent_ref[...] = entity
    words = [(value >> 5).astype(F32), (value & 31).astype(F32), (entity >> 5).astype(F32), (entity & 31).astype(F32)]
    names = lax.broadcasted_iota(jnp.int32, (n, LANES), 0)
    places = lax.broadcasted_iota(jnp.int32, (cap, LANES), 0)
    slots = lax.broadcasted_iota(jnp.int32, (ents, LANES), 0)
    asked = [jnp.zeros((n, cap), F32) for _ in words]
    hits = jnp.zeros((n, ents), F32)
    for k in range(chunks):
        here = slice(k * LANES, (k + 1) * LANES)
        mine = jnp.where(names == owner[k : k + 1], 1.0, 0.0)
        at = flag(places == rank[k : k + 1])
        for w, word in enumerate(words):
            asked[w] += nt((mine * word[k : k + 1]).astype(BF), at)
        hits += nt(flag(names == entity_owner[k : k + 1]), flag(slots == entity_slot[k : k + 1]))
        dlow_ref[here, :], dhigh_ref[here, :] = column_codes(fact_dim[k : k + 1])
    groups = cap // LANES
    words_ref[...] = jnp.zeros(words_ref.shape, F32)
    for w, word in enumerate(asked):
        for r in range(groups):
            words_ref[:, w * groups + r, :] = word[:, r * LANES : (r + 1) * LANES]
    out_ref[...] = words_ref[...].astype(BF)
    hits_ref[...] = hits


def gather_rows(low_ref, high_ref, rows, table_refs, firsts, hot_ref):
    at = 0
    low, high = low_ref[rows, :], high_ref[rows, :]
    for table, first in zip(table_refs, firsts):
        for k in range(table.shape[0] // LANES):
            hot_ref[:, at : at + LANES] = pick_block(low, high, (first + k).astype(F32).astype(BF))
            at += LANES
    total, at = None, 0
    for table in table_refs:
        part = dot(hot_ref[:, at : at + table.shape[0]], table[...])
        total = part if total is None else total + part
        at += table.shape[0]
    return total


def ring_at(place, n):
    place = lax.rem(place + 2 * n, n)
    return jnp.where(place < n // 2, 2 * place, 2 * (n - 1 - place) + 1)


def ring_place(index, n):
    half = lax.div(index, 2)
    return jnp.where(lax.rem(index, 2) == 0, half, n - 1 - half)


def look_kernel(n, pieces, low_ref, high_ref, *refs):
    count = len(pieces)
    tables, base_ref, out_ref, hot_ref = refs[:count], refs[count], refs[-2], refs[-1]
    facts = low_ref.shape[0]
    step = hot_ref.shape[0]
    place = ring_place(lax.axis_index("fact"), n)
    firsts = [lax.div(ring_at(place + hops, n) * dims + row, LANES) for hops, row, dims in pieces]
    for c in range(facts // step):
        rows = slice(c * step, (c + 1) * step)
        out_ref[rows, :] = base_ref[rows, :] + gather_rows(low_ref, high_ref, rows, tables, firsts, hot_ref)


def message_kernel(n, pieces, low_ref, high_ref, *refs):
    count = len(pieces)
    tables, refs = refs[:count], refs[count:]
    base_ref, xw_ref, ent_ref, slope_ref, part_ref, hot_ref, msg_ref, erlow_ref, erhigh_ref = refs
    facts = low_ref.shape[0]
    step = hot_ref.shape[0]
    place = ring_place(lax.axis_index("fact"), n)
    firsts = [lax.div(ring_at(place + hops, n) * dims + row, LANES) for hops, row, dims in pieces]
    for k in range(ent_ref.shape[0]):
        here = slice(k * LANES, (k + 1) * LANES)
        erlow_ref[:, here], erhigh_ref[:, here] = row_codes(ent_ref[k : k + 1, :])
    for c in range(facts // step):
        rows = slice(c * step, (c + 1) * step)
        pre = xw_ref[rows, :] + base_ref[rows, :]
        if count:
            pre = pre + gather_rows(low_ref, high_ref, rows, tables, firsts, hot_ref)
        gate = jax.nn.sigmoid(pre)
        msg_ref[rows, :] = (pre * gate).astype(BF)
        slope_ref[rows, :] = gate * (1.0 + pre * (1.0 - gate))

    def add(pair, carry):
        hot = jnp.concatenate(
            [pick_rows(erlow_ref[...], erhigh_ref[...], (pair * 2 + i).astype(F32).astype(BF)) for i in range(2)], axis=0
        )
        rows = pl.ds(pl.multiple_of(pair * 256, 256), 256)
        part_ref[rows, :] = dot(hot, msg_ref[...]).astype(BF)
        return carry

    lax.fori_loop(0, part_ref.shape[0] // 256, add, 0)


def project_kernel(x_ref, w_ref, out_ref):
    out_ref[...] = dot(x_ref[...], w_ref[...])


def ready_kernel(m, width, ents, count, me_ref, all_ref, x_ref, *refs):
    hits_refs, (self_ref, cot_ref, neigh_ref, hidden_ref, div_ref, xt_ref, hold_ref) = refs[:count], refs[count:]
    rows_each = ents // m
    key_range = pl.ds(lax.axis_index("fact"), 1)
    hits = hits_refs[0][key_range, :]
    for ref in hits_refs[1:]:
        hits = hits + ref[key_range, :]
    me = me_ref[0]
    mine = pl.ds(pl.multiple_of(me * rows_each, rows_each), rows_each)
    hold_ref[...] = jnp.maximum(jnp.broadcast_to(hits, (LANES, ents)).T, 1.0)
    div_ref[...] = hold_ref[mine, :]
    hidden = jnp.concatenate([all_ref[b, pl.ds(2 * width + me * rows_each, rows_each), :] for b in range(m)], axis=1)
    for b in range(m):
        here = slice(b * LANES, (b + 1) * LANES)
        self_ref[:, here] = dot(hidden, all_ref[b, 0:width, :])
        cot_ref[:, here] = all_ref[b, pl.ds(2 * width + ents + me * rows_each, rows_each), :]
        neigh_ref[b] = all_ref[b, width : 2 * width, :]
        hidden_ref[b] = all_ref[b, 2 * width : 2 * width + ents, :]
    xt_ref[...] = x_ref[...].T


def entity_kernel(n, m, sums_ref, div_ref, self_ref, cot_ref, neigh_ref, back_ref, share_ref):
    rows_each = sums_ref.shape[1]
    width = neigh_ref.shape[1]
    divisor = div_ref[...]
    parts = []
    for b in range(m):
        total = sums_ref[b].astype(F32)
        for f in range(1, n):
            total += sums_ref[f * m + b].astype(F32)
        parts.append((total / divisor).astype(BF))
    aggregate = jnp.concatenate(parts, axis=1)
    share_ref[2] = aggregate
    d_agg = jnp.zeros((rows_each, width), F32)
    for b in range(m):
        here = slice(b * LANES, (b + 1) * LANES)
        pre = self_ref[:, here] + dot(aggregate, neigh_ref[b])
        gate = jax.nn.sigmoid(pre)
        d_pre = (cot_ref[:, here].astype(F32) * (gate * (1.0 + pre * (1.0 - gate)))).astype(BF)
        share_ref[0, :, here] = (pre * gate).astype(BF)
        share_ref[1, :, here] = d_pre
        d_agg += nt(d_pre, neigh_ref[b])
    for b in range(m):
        scaled = (d_agg[:, b * LANES : (b + 1) * LANES] / divisor).astype(BF)
        for f in range(n):
            back_ref[f * m + b] = scaled


def store_shares(n, stride, own, at, total, out_ref):
    for d in range(n):
        piece = total[d * own : (d + 1) * own, :]
        if stride > own:
            piece = jnp.concatenate([piece, jnp.zeros((stride - own, LANES), F32)], axis=0)
        out_ref[d, at : at + stride, :] = piece.astype(BF)


def weight_kernel(n, m, width, stride, me_ref, got_ref, hidden_ref, out_ref, back_ref, total_ref):
    own = width // n
    mine = pl.ds(pl.multiple_of(me_ref[0] * LANES, LANES), LANES)
    out_ref[...] = jnp.concatenate([got_ref[s, 0, :, mine] for s in range(m)], axis=0)
    d_pre = jnp.concatenate([got_ref[s, 1, :, mine] for s in range(m)], axis=0)
    aggregate = jnp.concatenate([got_ref[s, 2] for s in range(m)], axis=0)
    for b in range(m):
        total_ref[b * LANES : (b + 1) * LANES, :] = tn(hidden_ref[b], d_pre)
    store_shares(n, stride, own, 0, total_ref[...], back_ref)
    for b in range(m):
        here = slice(b * LANES, (b + 1) * LANES)
        total_ref[here, :] = tn(aggregate[:, here], d_pre)
    store_shares(n, stride, own, stride, total_ref[...], back_ref)


def codes_kernel(ent_ref, elow_ref, ehigh_ref):
    for k in range(ent_ref.shape[0]):
        here = slice(k * LANES, (k + 1) * LANES)
        elow_ref[here, :], ehigh_ref[here, :] = column_codes(ent_ref[k : k + 1, :])


def messages(refs, n):
    return refs if len(refs) == n else [refs[0].at[s] for s in range(n)]


def request_kernel(n, cap, count, *refs):
    got, (low_ref, high_ref, clow_ref, chigh_ref) = messages(refs[:count], n), refs[count:]
    groups = cap // LANES
    for s, ref in enumerate(got):
        words = ref[cap:, :].astype(F32)
        for r in range(groups):
            parts = [words[w * groups + r : w * groups + r + 1, :] for w in range(4)]
            here = slice(s * cap + r * LANES, s * cap + (r + 1) * LANES)
            low_ref[:, here], high_ref[:, here] = row_codes((parts[0] * 32.0 + parts[1]).astype(jnp.int32))
            clow_ref[here, :], chigh_ref[here, :] = column_codes((parts[2] * 32.0 + parts[3]).astype(jnp.int32))


def spread_kernel(n, cap, offsets, slope_ref, pos_ref, words_ref, *refs):
    count = len(offsets)
    out_refs, (slope_bf_ref, plow_ref, phigh_ref) = refs[:count], refs[count:]
    slope_bf_ref[...] = slope_ref[...].astype(BF)
    for k in range(pos_ref.shape[0]):
        here = slice(k * LANES, (k + 1) * LANES)
        plow_ref[:, here], phigh_ref[:, here] = row_codes(pos_ref[k : k + 1, :])
    me = lax.axis_index("fact")
    for offset, out_ref in zip(offsets, out_refs):
        d = lax.rem(me + offset, n)
        hot = jnp.concatenate(
            [
                pick_rows(plow_ref[...], phigh_ref[...], (d * (cap // LANES) + i).astype(F32).astype(BF))
                for i in range(cap // LANES)
            ],
            axis=0,
        )
        out_ref[0:cap, :] = dot(hot, slope_bf_ref[...]).astype(BF)
        out_ref[cap:, :] = words_ref[d]


def backward_kernel(n, stride, scaled_ref, slope_ref, low_ref, high_ref, xt_ref, pair_ref, share_ref, hot_ref, dmsg_ref):
    facts = slope_ref.shape[0]
    own = xt_ref.shape[0] // n
    step = hot_ref.shape[0]
    for c in range(facts // step):
        rows = slice(c * step, (c + 1) * step)
        found = gather_rows(low_ref, high_ref, rows, [scaled_ref], [jnp.int32(0)], hot_ref)
        dmsg_ref[rows, :] = (found * slope_ref[rows, :]).astype(BF)
    share_ref[:, stride:, :] = pair_ref[...]
    store_shares(n, stride, own, 0, dot(xt_ref[...], dmsg_ref[...]), share_ref)


def table_kernel(n, cap, count, scaled_ref, low_ref, high_ref, clow_ref, chigh_ref, *refs):
    got, (out_ref, hot_ref, rows_ref) = messages(refs[:count], n), refs[count:]
    slots = rows_ref.shape[0]
    for s, ref in enumerate(got):
        rows_ref[s * cap : (s + 1) * cap, :] = ref[0:cap, :]
    step = hot_ref.shape[0]

    def form(c, carry):
        rows = pl.ds(pl.multiple_of(c * step, step), step)
        found = gather_rows(clow_ref, chigh_ref, rows, [scaled_ref], [jnp.int32(0)], hot_ref)
        rows_ref[rows, :] = (found * rows_ref[rows, :].astype(F32)).astype(BF)
        return carry

    lax.fori_loop(0, slots // step, form, 0)
    blocks = out_ref.shape[0] // LANES
    join = 2 if blocks % 2 == 0 else 1

    def add(group, carry):
        hot = jnp.concatenate(
            [pick_rows(low_ref[...], high_ref[...], (group * join + i).astype(F32).astype(BF)) for i in range(join)], axis=0
        )
        rows = pl.ds(pl.multiple_of(group * join * LANES, LANES), join * LANES)
        out_ref[rows, :] = dot(hot, rows_ref[...])
        return carry

    lax.fori_loop(0, blocks // join, add, 0)


def total_kernel(stride, got_ref, *out_refs):
    for j, ref in enumerate(out_refs):
        here = slice(j * stride, (j + 1) * stride)
        total = got_ref[0, here, :].astype(F32)
        for s in range(1, got_ref.shape[0]):
            total += got_ref[s, here, :].astype(F32)
        ref[...] = total[0 : ref.shape[0], :]


def shards(fact_x, dim_owner, dim_slot, fact_owner, fact_slot, dim_table, entity_h, w_msg, w_self, w_neigh, cotangent):
    n, m = lax.axis_size("fact"), lax.axis_size("feat")
    facts = fact_x.shape[0]
    chunks = facts // LANES
    ents = entity_h.shape[0]
    rows_each = ents // m
    width = w_msg.shape[0]
    dims = dim_table.shape[0]
    cap = -(-(3 * facts // n) // LANES) * LANES
    slots = n * cap
    extra = -(-(4 * (cap // LANES)) // 16) * 16
    own = width // n
    stride = max(16, own)
    me = lax.axis_index("feat").astype(jnp.int32).reshape(1)
    tie = lax.optimization_barrier
    ringed = n <= 8

    x_full = lax.all_gather(fact_x, "feat", axis=1, tiled=True)
    ring = [2 * p if p < n // 2 else 2 * (n - 1 - p) + 1 for p in range(n)]
    to_right = [(ring[p], ring[(p + 1) % n]) for p in range(n)]
    to_left = [(ring[(p + 1) % n], ring[p]) for p in range(n)]

    def pass_on(right, left):
        return lax.ppermute(right, "fact", to_right), lax.ppermute(left, "fact", to_left)

    if ringed:
        right, left = pass_on(dim_table, dim_table)

    by_lane = (chunks, LANES)
    columns = shape((facts, LANES), BF)
    words, hits, pos, entity, dlow, dhigh = call(
        functools.partial(route_kernel, n, cap, ents, dims),
        (
            shape((n, extra, LANES), BF),
            shape((n, ents), F32),
            shape(by_lane, jnp.int32),
            shape(by_lane, jnp.int32),
            columns,
            columns,
        ),
        [pltpu.VMEM((n, extra, LANES), F32)],
        1 << 28,
        "route",
    )(dim_owner.reshape(by_lane), dim_slot.reshape(by_lane), fact_owner.reshape(by_lane), fact_slot.reshape(by_lane))
    if ringed:
        right, left, words, hits, pos, entity, dlow, dhigh = tie((right, left, words, hits, pos, entity, dlow, dhigh))

    step = 512
    limit = VMEM_LIMIT if ringed else VMEM_LIMIT_LARGE

    def look(pieces, tables, base):
        rows = sum(t.shape[0] for t in tables)
        return call(
            functools.partial(look_kernel, n, pieces),
            shape((facts, LANES), F32),
            [pltpu.VMEM((step, rows), BF)],
            2 * facts * rows * LANES,
            "look",
            limit,
        )(dlow, dhigh, *tables, base)

    def project(x):
        return call(project_kernel, shape((facts, LANES), F32), [], 2 * facts * width * LANES, "project")(x, w_msg)

    found = jnp.zeros((facts, LANES), F32)
    if ringed:
        hits_right, hits_left, all_hits = hits, hits, [hits]
        for k in range(1, n // 2):
            if k < n // 2 - 1:
                after = pass_on(right, left)
            else:
                half = dims // 2
                after = pass_on(right[:half], left[half:])
            if k > 1:
                pieces, tables = [(-k, 0, dims), (k, 0, dims)], [right, left]
            else:
                pieces, tables = [(0, 0, dims), (-k, 0, dims), (k, 0, dims)], [dim_table, right, left]
            found = look(pieces, tables, found)
            right, left = after
            hits_right, hits_left = pass_on(hits_right, hits_left)
            all_hits += [hits_right, hits_left]
            if k == n // 2 - 2:
                xw = project(x_full)
                right, left, found, xw = tie((right, left, found, xw))
            elif k < n // 2 - 1:
                right, left, found = tie((right, left, found))
            if k == 1:
                weights, _ = tie(((w_self, w_neigh, entity_h, cotangent), found))
        all_hits.append(lax.ppermute(hits_right, "fact", to_right))
        last = [right, left]
        last_pieces = [(-(n // 2), 0, dims), (n // 2, half, dims)]
    else:
        whole = lax.all_gather(dim_table, "fact")
        order = jnp.take(whole, ring_at(ring_place(lax.axis_index("fact"), n) + jnp.arange(n), n), axis=0)
        for k in range(0, n, 8):
            found = look([(k + i, 0, dims) for i in range(8)], [order[k + i] for i in range(8)], found)
        last, last_pieces = [], []
        weights = (w_self, w_neigh, entity_h, cotangent)
        xw = project(x_full)
        all_hits = [lax.psum(hits, "fact")]
    everything = lax.all_gather(jnp.concatenate(weights, axis=0), "feat")
    last_rows = max(LANES, sum(t.shape[0] for t in last))
    slope, part = call(
        functools.partial(message_kernel, n, last_pieces),
        (shape((facts, LANES), F32), shape((n * ents, LANES), BF)),
        [
            pltpu.VMEM((step, last_rows), BF),
            pltpu.VMEM((facts, LANES), BF),
            pltpu.VMEM((LANES, facts), BF),
            pltpu.VMEM((16, facts), BF),
        ],
        2 * facts * (last_rows + n * ents) * LANES,
        "message",
    )(dlow, dhigh, *last, found, xw, entity)
    sums = lax.all_to_all(part.reshape(n * m, rows_each, LANES), ("fact", "feat"), 0, 0)
    long = cap + extra

    def spread(offsets, slope):
        return call(
            functools.partial(spread_kernel, n, cap, offsets),
            tuple(shape((long, LANES), BF) for _ in offsets),
            [pltpu.VMEM((facts, LANES), BF), pltpu.VMEM((LANES, facts), BF), pltpu.VMEM((16, facts), BF)],
            2 * facts * cap * len(offsets) * LANES,
            "spread",
            limit,
        )(slope, pos, words)

    def send(offsets, sent):
        return [
            lax.ppermute(message, "fact", [(i, (i + offset) % n) for i in range(n)])
            for offset, message in zip(offsets, sent)
        ]

    everything, x_later, entity, _ = tie((everything, x_full, entity, part))
    self_part, cot, neigh, hidden, divisor, x_turned = call(
        functools.partial(ready_kernel, m, width, ents, len(all_hits)),
        (
            shape((rows_each, width), F32),
            shape((rows_each, width), BF),
            shape((m, width, LANES), BF),
            shape((m, ents, LANES), BF),
            shape((rows_each, LANES), F32),
            shape((width, facts), BF),
        ),
        [pltpu.VMEM((ents, LANES), F32)],
        1 << 28,
        "ready",
    )(me, everything, x_later, *all_hits)
    if ringed:
        early = [n // 2, n // 2 - 1, n // 2 + 1]
        early_sent = spread(early, slope)
        early_got = send(early, early_sent)
        divisor, *_ = tie((divisor, *early_sent))
    back, share = call(
        functools.partial(entity_kernel, n, m),
        (shape((n * m, rows_each, LANES), BF), shape((3, rows_each, width), BF)),
        [],
        4 * rows_each * width * width,
        "entity",
    )(sums, divisor, self_part, cot, neigh)
    scaled = lax.all_to_all(back, ("fact", "feat"), 0, 0).reshape(n * ents, LANES)
    got = lax.all_gather(share, "feat")
    entity, slope_later, _ = tie((entity, slope, back))
    if ringed:
        late = [k for k in range(n) if k not in early]
        late_sent = spread(late, slope_later)
        got_slopes = early_got + [late_sent[0]] + send(late[1:], late_sent[1:])
    else:
        fact_me = lax.axis_index("fact")
        sent = [message for k in range(0, n, 8) for message in spread(list(range(k, k + 8)), slope_later)]
        by_owner = jnp.take(jnp.stack(sent), lax.rem(jnp.arange(n) - fact_me + n, n), axis=0)
        got_slopes = [lax.all_to_all(by_owner, "fact", 0, 0)]
    elow, ehigh = call(codes_kernel, (columns, columns), [], 1 << 26, "codes")(entity)
    output_h, pair = call(
        functools.partial(weight_kernel, n, m, width, stride),
        (shape((ents, LANES), BF), shape((n, 2 * stride, LANES), BF)),
        [pltpu.VMEM((width, LANES), F32)],
        4 * ents * width * LANES,
        "weight",
    )(me, got, hidden)
    shares = call(
        functools.partial(backward_kernel, n, stride),
        shape((n, 3 * stride, LANES), BF),
        [pltpu.VMEM((step, n * ents), BF), pltpu.VMEM((facts, LANES), BF)],
        2 * facts * (n * ents + width) * LANES,
        "backward",
        limit,
    )(scaled, slope, elow, ehigh, x_turned, pair)
    owned = lax.all_to_all(shares, "fact", 0, 0)
    scaled, _ = tie((scaled, shares))
    slot_columns = shape((slots, LANES), BF)
    rlow, rhigh, clow, chigh = call(
        functools.partial(request_kernel, n, cap, len(got_slopes)),
        (shape((LANES, slots), BF), shape((16, slots), BF), slot_columns, slot_columns),
        [],
        1 << 26,
        "requests",
        limit,
    )(*got_slopes)
    grad_dim = call(
        functools.partial(table_kernel, n, cap, len(got_slopes)),
        shape((dims, LANES), F32),
        [pltpu.VMEM((step, n * ents), BF), pltpu.VMEM((slots, LANES), BF)],
        2 * slots * (dims + n * ents) * LANES,
        "table",
        limit,
    )(scaled, rlow, rhigh, clow, chigh, *got_slopes)
    grad_msg, grad_self, grad_neigh = call(
        functools.partial(total_kernel, stride), (shape((own, LANES), F32),) * 3, [], 1 << 20, "total"
    )(owned)
    return output_h, grad_msg, grad_self, grad_neigh, grad_dim


def solution(mesh):
    placed = (
        P("fact", "feat"),
        P("fact", None),
        P("fact"),
        P("fact", None),
        P("fact"),
        P("fact", "feat"),
        P("fact", "feat"),
        P(None, "feat"),
        P(None, "feat"),
        P(None, "feat"),
        P("fact", "feat"),
    )
    return jax.shard_map(
        shards,
        mesh=mesh,
        in_specs=placed,
        out_specs=(P("fact", "feat"),) * 5,
        check_vma=False,
    )
```

```python
import functools

import jax
import jax.numpy as jnp
from jax import lax
from jax.experimental import pallas as pl
from jax.experimental.pallas import tpu as pltpu
from jax.sharding import PartitionSpec as P

LANES = 128
BF = jnp.bfloat16
F32 = jnp.float32
VMEM_LIMIT = 16 * 1024 * 1024
VMEM_LIMIT_LARGE = 40 * 1024 * 1024


def call(kernel, out_shape, scratch, flops, name, limit=VMEM_LIMIT):
    return pl.pallas_call(
        kernel,
        out_shape=out_shape,
        scratch_shapes=scratch,
        compiler_params=pltpu.CompilerParams(vmem_limit_bytes=limit),
        cost_estimate=pl.CostEstimate(flops=flops, bytes_accessed=1 << 20, transcendentals=0),
        name=name,
    )


def shape(dims, dtype):
    return jax.ShapeDtypeStruct(dims, dtype)


def nt(a, b):
    return lax.dot_general(a, b, (((1,), (1,)), ((), ())), preferred_element_type=F32)


def tn(a, b):
    return lax.dot_general(a, b, (((0,), (0,)), ((), ())), preferred_element_type=F32)


def dot(a, b):
    return jnp.dot(a, b, preferred_element_type=F32)


def flag(condition):
    return jnp.where(condition, 1.0, 0.0).astype(BF)


def column_codes(row):
    keys = jnp.broadcast_to(row, (LANES, LANES)).astype(F32).T.astype(jnp.int32)
    lane = lax.broadcasted_iota(jnp.int32, (LANES, LANES), 1)
    return flag((keys & (LANES - 1)) == lane), (keys >> 7).astype(F32).astype(BF)


def row_codes(row):
    keys = jnp.broadcast_to(row, (LANES, LANES))
    sub = lax.broadcasted_iota(jnp.int32, (LANES, LANES), 0)
    high = jnp.broadcast_to((row >> 7).astype(F32), (16, LANES)).astype(BF)
    return flag((keys & (LANES - 1)) == sub), high


def pick_block(low, high, block):
    zero = jnp.zeros((), BF)
    return jnp.where(high == block, low, zero)


def pick_rows(low, high, block):
    wide = low.reshape(LANES // 16, 16, low.shape[1])
    picked = pick_block(wide, high[None], block)
    return picked.reshape(low.shape)


def route_kernel(n, cap, ents, dims, do_ref, ds_ref, fo_ref, fs_ref, out_ref, hits_ref, pos_ref, ent_ref, dlow_ref, dhigh_ref, words_ref):
    chunks = do_ref.shape[0]
    owner = do_ref[...]
    kind = lax.broadcasted_iota(jnp.int32, (n, chunks, LANES), 0)
    held = jnp.where(kind == owner[None], 1.0, 0.0).reshape(n * chunks, LANES)
    held_bf = held.astype(BF)
    i0 = lax.broadcasted_iota(jnp.int32, (LANES, LANES), 0)
    i1 = lax.broadcasted_iota(jnp.int32, (LANES, LANES), 1)
    inside = dot(held_bf, flag(i0 < i1))
    r0 = lax.broadcasted_iota(jnp.int32, (n * chunks, n * chunks), 0)
    r1 = lax.broadcasted_iota(jnp.int32, (n * chunks, n * chunks), 1)
    earlier = flag((r0 // chunks == r1 // chunks) & (r1 < r0))
    before = dot(dot(earlier, held_bf).astype(BF), jnp.ones((LANES, LANES), BF))
    rank = jnp.sum((held * (inside + before)).reshape(n, chunks, LANES), axis=0)
    rank = rank.astype(jnp.int32)
    entity_owner = fo_ref[...]
    entity_slot = fs_ref[...]
    value = ds_ref[...]
    pos_ref[...] = owner * cap + rank
    fact_dim = owner * dims + value
    entity = entity_owner * ents + entity_slot
    ent_ref[...] = entity
    words = [(value >> 5).astype(F32), (value & 31).astype(F32), (entity >> 5).astype(F32), (entity & 31).astype(F32)]
    names = lax.broadcasted_iota(jnp.int32, (n, LANES), 0)
    places = lax.broadcasted_iota(jnp.int32, (cap, LANES), 0)
    slots = lax.broadcasted_iota(jnp.int32, (ents, LANES), 0)
    asked = [jnp.zeros((n, cap), F32) for _ in words]
    hits = jnp.zeros((n, ents), F32)
    for k in range(chunks):
        here = slice(k * LANES, (k + 1) * LANES)
        mine = jnp.where(names == owner[k : k + 1], 1.0, 0.0)
        at = flag(places == rank[k : k + 1])
        for w, word in enumerate(words):
            asked[w] += nt((mine * word[k : k + 1]).astype(BF), at)
        hits += nt(flag(names == entity_owner[k : k + 1]), flag(slots == entity_slot[k : k + 1]))
        dlow_ref[here, :], dhigh_ref[here, :] = column_codes(fact_dim[k : k + 1])
    groups = cap // LANES
    words_ref[...] = jnp.zeros(words_ref.shape, F32)
    for w, word in enumerate(asked):
        for r in range(groups):
            words_ref[:, w * groups + r, :] = word[:, r * LANES : (r + 1) * LANES]
    out_ref[...] = words_ref[...].astype(BF)
    hits_ref[...] = hits


def gather_rows(low_ref, high_ref, rows, table_refs, firsts, hot_ref):
    at = 0
    low, high = low_ref[rows, :], high_ref[rows, :]
    for table, first in zip(table_refs, firsts):
        for k in range(table.shape[0] // LANES):
            hot_ref[:, at : at + LANES] = pick_block(low, high, (first + k).astype(F32).astype(BF))
            at += LANES
    total, at = None, 0
    for table in table_refs:
        part = dot(hot_ref[:, at : at + table.shape[0]], table[...])
        total = part if total is None else total + part
        at += table.shape[0]
    return total


def ring_at(place, n):
    place = lax.rem(place + 2 * n, n)
    return jnp.where(place < n // 2, 2 * place, 2 * (n - 1 - place) + 1)


def ring_place(index, n):
    half = lax.div(index, 2)
    return jnp.where(lax.rem(index, 2) == 0, half, n - 1 - half)


def add_hits(refs, out_ref):
    total = refs[0][...]
    for ref in refs[1:]:
        total = total + ref[...]
    out_ref[...] = total


def look_kernel(n, pieces, counts, low_ref, high_ref, *refs):
    count = len(pieces)
    tables, hits, refs = refs[:count], refs[count : count + counts], refs[count + counts :]
    base_ref, out_ref, sum_ref, hot_ref = refs
    add_hits(hits, sum_ref)
    facts = low_ref.shape[0]
    step = hot_ref.shape[0]
    place = ring_place(lax.axis_index("fact"), n)
    firsts = [lax.div(ring_at(place + hops, n) * dims + row, LANES) for hops, row, dims in pieces]
    for c in range(facts // step):
        rows = slice(c * step, (c + 1) * step)
        out_ref[rows, :] = base_ref[rows, :] + gather_rows(low_ref, high_ref, rows, tables, firsts, hot_ref)


def message_kernel(n, pieces, counts, low_ref, high_ref, *refs):
    count = len(pieces)
    tables, hits, refs = refs[:count], refs[count : count + counts], refs[count + counts :]
    base_ref, xw_ref, ent_ref, slope_ref, part_ref, sum_ref, hot_ref, msg_ref, erlow_ref, erhigh_ref = refs
    add_hits(hits, sum_ref)
    facts = low_ref.shape[0]
    step = hot_ref.shape[0]
    place = ring_place(lax.axis_index("fact"), n)
    firsts = [lax.div(ring_at(place + hops, n) * dims + row, LANES) for hops, row, dims in pieces]
    for k in range(ent_ref.shape[0]):
        here = slice(k * LANES, (k + 1) * LANES)
        erlow_ref[:, here], erhigh_ref[:, here] = row_codes(ent_ref[k : k + 1, :])
    for c in range(facts // step):
        rows = slice(c * step, (c + 1) * step)
        pre = xw_ref[rows, :] + base_ref[rows, :]
        if count:
            pre = pre + gather_rows(low_ref, high_ref, rows, tables, firsts, hot_ref)
        gate = jax.nn.sigmoid(pre)
        msg_ref[rows, :] = (pre * gate).astype(BF)
        slope_ref[rows, :] = gate * (1.0 + pre * (1.0 - gate))

    def add(pair, carry):
        hot = jnp.concatenate(
            [pick_rows(erlow_ref[...], erhigh_ref[...], (pair * 2 + i).astype(F32).astype(BF)) for i in range(2)], axis=0
        )
        rows = pl.ds(pl.multiple_of(pair * 256, 256), 256)
        part_ref[rows, :] = dot(hot, msg_ref[...]).astype(BF)
        return carry

    lax.fori_loop(0, part_ref.shape[0] // 256, add, 0)


def project_kernel(x_ref, w_ref, out_ref):
    out_ref[...] = dot(x_ref[...], w_ref[...])


def ready_kernel(m, width, ents, me_ref, all_ref, x_ref, hits_ref, self_ref, cot_ref, neigh_ref, hidden_ref, div_ref, xt_ref, hold_ref):
    rows_each = ents // m
    hits = hits_ref[pl.ds(lax.axis_index("fact"), 1), :]
    me = me_ref[0]
    mine = pl.ds(pl.multiple_of(me * rows_each, rows_each), rows_each)
    hold_ref[...] = jnp.maximum(jnp.broadcast_to(hits, (LANES, ents)).T, 1.0)
    div_ref[...] = hold_ref[mine, :]
    hidden = jnp.concatenate([all_ref[b, pl.ds(2 * width + me * rows_each, rows_each), :] for b in range(m)], axis=1)
    for b in range(m):
        here = slice(b * LANES, (b + 1) * LANES)
        self_ref[:, here] = dot(hidden, all_ref[b, 0:width, :])
        cot_ref[:, here] = all_ref[b, pl.ds(2 * width + ents + me * rows_each, rows_each), :]
        neigh_ref[b] = all_ref[b, width : 2 * width, :]
        hidden_ref[b] = all_ref[b, 2 * width : 2 * width + ents, :]
    xt_ref[...] = x_ref[...].T


def entity_kernel(n, m, sums_ref, div_ref, self_ref, cot_ref, neigh_ref, back_ref, out_ref, pre_ref, agg_ref):
    rows_each = sums_ref.shape[1]
    width = neigh_ref.shape[1]
    divisor = div_ref[...]
    parts = []
    for b in range(m):
        total = sums_ref[b].astype(F32)
        for f in range(1, n):
            total += sums_ref[f * m + b].astype(F32)
        parts.append((total / divisor).astype(BF))
    aggregate = jnp.concatenate(parts, axis=1)
    for b in range(m):
        agg_ref[b * rows_each : (b + 1) * rows_each, :] = parts[b]
    d_agg = jnp.zeros((rows_each, width), F32)
    for b in range(m):
        here = slice(b * LANES, (b + 1) * LANES)
        pre = self_ref[:, here] + dot(aggregate, neigh_ref[b])
        gate = jax.nn.sigmoid(pre)
        d_pre = (cot_ref[:, here].astype(F32) * (gate * (1.0 + pre * (1.0 - gate)))).astype(BF)
        out_ref[b] = (pre * gate).astype(BF)
        pre_ref[b] = d_pre
        d_agg += nt(d_pre, neigh_ref[b])
    for b in range(m):
        scaled = (d_agg[:, b * LANES : (b + 1) * LANES] / divisor).astype(BF)
        for f in range(n):
            back_ref[f * m + b] = scaled


def store_shares(n, stride, own, at, total, out_ref):
    for d in range(n):
        piece = total[d * own : (d + 1) * own, :]
        if stride > own:
            piece = jnp.concatenate([piece, jnp.zeros((stride - own, LANES), F32)], axis=0)
        out_ref[d, at : at + stride, :] = piece.astype(BF)


def share_kernel(m, out_ref, pre_ref, agg_ref, *share_refs):
    rows_each = out_ref.shape[1]
    me = lax.axis_index("feat")
    for offset, ref in enumerate(share_refs):
        to = lax.rem(me + offset, m)
        ref[0:rows_each, :] = out_ref[to]
        ref[rows_each : 2 * rows_each, :] = pre_ref[to]
        ref[2 * rows_each :, :] = agg_ref[...]


def weight_kernel(n, m, width, stride, hidden_ref, *refs):
    got, (out_ref, back_ref, total_ref, pre_ref, agg_ref) = refs[:m], refs[m:]
    rows_each = got[0].shape[0] // (2 + m)
    own = width // n
    me = lax.axis_index("feat")
    for offset, ref in enumerate(got):
        source = lax.rem(me + (m - offset), m)
        here = pl.ds(pl.multiple_of(source * rows_each, rows_each), rows_each)
        out_ref[here, :] = ref[0:rows_each, :]
        pre_ref[here, :] = ref[rows_each : 2 * rows_each, :]
        for b in range(m):
            agg_ref[b, here, :] = ref[(2 + b) * rows_each : (3 + b) * rows_each, :]
    d_pre = pre_ref[...]
    for b in range(m):
        total_ref[b * LANES : (b + 1) * LANES, :] = tn(hidden_ref[b], d_pre)
    store_shares(n, stride, own, 0, total_ref[...], back_ref)
    for b in range(m):
        total_ref[b * LANES : (b + 1) * LANES, :] = tn(agg_ref[b], d_pre)
    store_shares(n, stride, own, stride, total_ref[...], back_ref)


def codes_kernel(ent_ref, elow_ref, ehigh_ref):
    for k in range(ent_ref.shape[0]):
        here = slice(k * LANES, (k + 1) * LANES)
        elow_ref[here, :], ehigh_ref[here, :] = column_codes(ent_ref[k : k + 1, :])


def spread_kernel(n, cap, offsets, slope_ref, pos_ref, words_ref, *refs):
    count = len(offsets)
    out_refs, (slope_bf_ref, plow_ref, phigh_ref) = refs[:count], refs[count:]
    slope_bf_ref[...] = slope_ref[...].astype(BF)
    for k in range(pos_ref.shape[0]):
        here = slice(k * LANES, (k + 1) * LANES)
        plow_ref[:, here], phigh_ref[:, here] = row_codes(pos_ref[k : k + 1, :])
    me = lax.axis_index("fact")
    for offset, out_ref in zip(offsets, out_refs):
        d = lax.rem(me + offset, n)
        hot = jnp.concatenate(
            [
                pick_rows(plow_ref[...], phigh_ref[...], (d * (cap // LANES) + i).astype(F32).astype(BF))
                for i in range(cap // LANES)
            ],
            axis=0,
        )
        out_ref[0:cap, :] = dot(hot, slope_bf_ref[...]).astype(BF)
        out_ref[cap:, :] = words_ref[d]


def backward_kernel(n, stride, scaled_ref, slope_ref, low_ref, high_ref, xt_ref, pair_ref, share_ref, hot_ref, dmsg_ref):
    facts = slope_ref.shape[0]
    own = xt_ref.shape[0] // n
    step = hot_ref.shape[0]
    for c in range(facts // step):
        rows = slice(c * step, (c + 1) * step)
        found = gather_rows(low_ref, high_ref, rows, [scaled_ref], [jnp.int32(0)], hot_ref)
        dmsg_ref[rows, :] = (found * slope_ref[rows, :]).astype(BF)
    share_ref[:, stride:, :] = pair_ref[...]
    store_shares(n, stride, own, 0, dot(xt_ref[...], dmsg_ref[...]), share_ref)


def table_kernel(cap, count, first, scaled_ref, *refs):
    got, refs = refs[:count], refs[count:]
    if len(got[0].shape) == 3:
        got = [got[0].at[s] for s in range(got[0].shape[0])]
    if not first:
        base_ref, refs = refs[0], refs[1:]
    out_ref, hot_ref, rows_ref, low_ref, high_ref, clow_ref, chigh_ref = refs
    groups = cap // LANES
    for s, ref in enumerate(got):
        rows_ref[s * cap : (s + 1) * cap, :] = ref[0:cap, :]
        words = ref[cap:, :].astype(F32)
        for r in range(groups):
            parts = [words[w * groups + r : w * groups + r + 1, :] for w in range(4)]
            here = slice(s * cap + r * LANES, s * cap + (r + 1) * LANES)
            low_ref[:, here], high_ref[:, here] = row_codes((parts[0] * 32.0 + parts[1]).astype(jnp.int32))
            clow_ref[here, :], chigh_ref[here, :] = column_codes((parts[2] * 32.0 + parts[3]).astype(jnp.int32))
    slots = rows_ref.shape[0]
    step = hot_ref.shape[0]

    def form(c, carry):
        rows = pl.ds(pl.multiple_of(c * step, step), step)
        found = gather_rows(clow_ref, chigh_ref, rows, [scaled_ref], [jnp.int32(0)], hot_ref)
        rows_ref[rows, :] = (found * rows_ref[rows, :].astype(F32)).astype(BF)
        return carry

    lax.fori_loop(0, slots // step, form, 0)
    blocks = out_ref.shape[0] // LANES
    join = 2 if blocks % 2 == 0 else 1

    def add(group, carry):
        hot = jnp.concatenate(
            [pick_rows(low_ref[...], high_ref[...], (group * join + i).astype(F32).astype(BF)) for i in range(join)], axis=0
        )
        rows = pl.ds(pl.multiple_of(group * join * LANES, LANES), join * LANES)
        sums = dot(hot, rows_ref[...])
        out_ref[rows, :] = sums if first else base_ref[rows, :] + sums
        return carry

    lax.fori_loop(0, blocks // join, add, 0)


def total_kernel(stride, got_ref, *out_refs):
    for j, ref in enumerate(out_refs):
        here = slice(j * stride, (j + 1) * stride)
        total = got_ref[0, here, :].astype(F32)
        for s in range(1, got_ref.shape[0]):
            total += got_ref[s, here, :].astype(F32)
        ref[...] = total[0 : ref.shape[0], :]


def shards(fact_x, dim_owner, dim_slot, fact_owner, fact_slot, dim_table, entity_h, w_msg, w_self, w_neigh, cotangent):
    n, m = lax.axis_size("fact"), lax.axis_size("feat")
    facts = fact_x.shape[0]
    chunks = facts // LANES
    ents = entity_h.shape[0]
    rows_each = ents // m
    width = w_msg.shape[0]
    dims = dim_table.shape[0]
    cap = -(-(3 * facts // n) // LANES) * LANES
    slots = n * cap
    extra = -(-(4 * (cap // LANES)) // 16) * 16
    own = width // n
    stride = max(16, own)
    me = lax.axis_index("feat").astype(jnp.int32).reshape(1)
    tie = lax.optimization_barrier
    ringed = n <= 8

    x_full = lax.all_gather(fact_x, "feat", axis=1, tiled=True)
    ring = [2 * p if p < n // 2 else 2 * (n - 1 - p) + 1 for p in range(n)]
    to_right = [(ring[p], ring[(p + 1) % n]) for p in range(n)]
    to_left = [(ring[(p + 1) % n], ring[p]) for p in range(n)]

    def pass_on(right, left):
        return lax.ppermute(right, "fact", to_right), lax.ppermute(left, "fact", to_left)

    if ringed:
        right, left = pass_on(dim_table, dim_table)

    by_lane = (chunks, LANES)
    columns = shape((facts, LANES), BF)
    words, hits, pos, entity, dlow, dhigh = call(
        functools.partial(route_kernel, n, cap, ents, dims),
        (
            shape((n, extra, LANES), BF),
            shape((n, ents), F32),
            shape(by_lane, jnp.int32),
            shape(by_lane, jnp.int32),
            columns,
            columns,
        ),
        [pltpu.VMEM((n, extra, LANES), F32)],
        1 << 28,
        "route",
    )(dim_owner.reshape(by_lane), dim_slot.reshape(by_lane), fact_owner.reshape(by_lane), fact_slot.reshape(by_lane))
    if ringed:
        right, left, words, hits, pos, entity, dlow, dhigh = tie((right, left, words, hits, pos, entity, dlow, dhigh))

    step = 512
    limit = VMEM_LIMIT if ringed else VMEM_LIMIT_LARGE

    by_range = shape((n, ents), F32)

    def look(pieces, tables, base, hits):
        rows = sum(t.shape[0] for t in tables)
        return call(
            functools.partial(look_kernel, n, pieces, len(hits)),
            (shape((facts, LANES), F32), by_range),
            [pltpu.VMEM((step, rows), BF)],
            2 * facts * rows * LANES,
            "look",
            limit,
        )(dlow, dhigh, *tables, *hits, base)

    def project(x):
        return call(project_kernel, shape((facts, LANES), F32), [], 2 * facts * width * LANES, "project")(x, w_msg)

    found = jnp.zeros((facts, LANES), F32)
    if ringed:
        hits_right, hits_left, due = hits, hits, [hits]
        for k in range(1, n // 2):
            if k < n // 2 - 1:
                after = pass_on(right, left)
            else:
                half = dims // 2
                after = pass_on(right[:half], left[half:])
            hits_right, hits_left = pass_on(hits_right, hits_left)
            arriving = [hits_right, hits_left]
            if k == n // 2 - 1:
                arriving.append(lax.ppermute(hits, "fact", [(ring[p], ring[(p + n // 2) % n]) for p in range(n)]))
            if k > 1:
                pieces, tables = [(-k, 0, dims), (k, 0, dims)], [right, left]
            else:
                pieces, tables = [(0, 0, dims), (-k, 0, dims), (k, 0, dims)], [dim_table, right, left]
            found, total_hits = look(pieces, tables, found, due)
            right, left = after
            if k == 1:
                weights, _ = tie(((w_self, w_neigh, entity_h, cotangent), found))
            if k == n // 2 - 2:
                xw = project(x_full)
                right, left, found, xw, arriving = tie((right, left, found, xw, arriving))
            else:
                right, left, found, arriving = tie((right, left, found, arriving))
            hits_right, hits_left = arriving[:2]
            due = [total_hits] + list(arriving)
        last = [right, left]
        last_pieces = [(-(n // 2), 0, dims), (n // 2, half, dims)]
    else:
        whole = lax.all_gather(dim_table, "fact")
        order = jnp.take(whole, ring_at(ring_place(lax.axis_index("fact"), n) + jnp.arange(n), n), axis=0)
        for k in range(0, n, 8):
            found, _ = look([(k + i, 0, dims) for i in range(8)], [order[k + i] for i in range(8)], found, [hits])
        last, last_pieces = [], []
        weights = (w_self, w_neigh, entity_h, cotangent)
        xw = project(x_full)
        due = [lax.psum(hits, "fact")]
    everything = lax.all_gather(jnp.concatenate(weights, axis=0), "feat")
    last_rows = max(LANES, sum(t.shape[0] for t in last))
    slope, part, total_hits = call(
        functools.partial(message_kernel, n, last_pieces, len(due)),
        (shape((facts, LANES), F32), shape((n * ents, LANES), BF), by_range),
        [
            pltpu.VMEM((step, last_rows), BF),
            pltpu.VMEM((facts, LANES), BF),
            pltpu.VMEM((LANES, facts), BF),
            pltpu.VMEM((16, facts), BF),
        ],
        2 * facts * (last_rows + n * ents) * LANES,
        "message",
        limit,
    )(dlow, dhigh, *last, *due, found, xw, entity)
    sums = lax.all_to_all(part.reshape(n * m, rows_each, LANES), ("fact", "feat"), 0, 0)
    long = cap + extra

    def spread(offsets, slope):
        return call(
            functools.partial(spread_kernel, n, cap, offsets),
            tuple(shape((long, LANES), BF) for _ in offsets),
            [pltpu.VMEM((facts, LANES), BF), pltpu.VMEM((LANES, facts), BF), pltpu.VMEM((16, facts), BF)],
            2 * facts * cap * len(offsets) * LANES,
            "spread",
            limit,
        )(slope, pos, words)

    def send(offsets, sent):
        return [
            lax.ppermute(message, "fact", [(i, (i + offset) % n) for i in range(n)])
            for offset, message in zip(offsets, sent)
        ]

    everything, x_later, entity, _ = tie((everything, x_full, entity, part))
    self_part, cot, neigh, hidden, divisor, x_turned = call(
        functools.partial(ready_kernel, m, width, ents),
        (
            shape((rows_each, width), F32),
            shape((rows_each, width), BF),
            shape((m, width, LANES), BF),
            shape((m, ents, LANES), BF),
            shape((rows_each, LANES), F32),
            shape((width, facts), BF),
        ),
        [pltpu.VMEM((ents, LANES), F32)],
        1 << 28,
        "ready",
    )(me, everything, x_later, total_hits)
    if ringed:
        early = [n // 2, n // 2 - 1]
        early_got = send(early, spread(early, slope))
        divisor, early_got = tie((divisor, early_got))
    by_feat = shape((m, rows_each, LANES), BF)
    back, out_parts, pre_parts, agg_parts = call(
        functools.partial(entity_kernel, n, m),
        (shape((n * m, rows_each, LANES), BF), by_feat, by_feat, shape((m * rows_each, LANES), BF)),
        [],
        4 * rows_each * width * width,
        "entity",
    )(sums, divisor, self_part, cot, neigh)
    scaled = lax.all_to_all(back, ("fact", "feat"), 0, 0).reshape(n * ents, LANES)
    shares = call(
        functools.partial(share_kernel, m),
        tuple(shape(((2 + m) * rows_each, LANES), BF) for _ in range(m)),
        [],
        1 << 20,
        "share",
    )(out_parts, pre_parts, agg_parts)
    got = [shares[0]] + [
        lax.ppermute(shares[k], "feat", [(i, (i + k) % m) for i in range(m)]) for k in range(1, m)
    ]
    output_h, pair = call(
        functools.partial(weight_kernel, n, m, width, stride),
        (shape((ents, LANES), BF), shape((n, 2 * stride, LANES), BF)),
        [pltpu.VMEM((width, LANES), F32), pltpu.VMEM((ents, LANES), BF), pltpu.VMEM((m, ents, LANES), BF)],
        4 * ents * width * LANES,
        "weight",
    )(hidden, *got)
    entity, slope_later, _ = tie((entity, slope, back))
    elow, ehigh = call(codes_kernel, (columns, columns), [], 1 << 26, "codes")(entity)
    if ringed:
        middle = [n // 2 + 1, n // 2 - 2]
        mid_got = send(middle, spread(middle, slope_later))
        elow, mid_got = tie((elow, mid_got))
    shares = call(
        functools.partial(backward_kernel, n, stride),
        shape((n, 3 * stride, LANES), BF),
        [pltpu.VMEM((step, n * ents), BF), pltpu.VMEM((facts, LANES), BF)],
        2 * facts * (n * ents + width) * LANES,
        "backward",
        limit,
    )(scaled, slope, elow, ehigh, x_turned, pair)
    owned = lax.all_to_all(shares, "fact", 0, 0)
    scaled, slope_later, _ = tie((scaled, slope_later, shares))

    def add_up(got, base):
        found = sum(g.size // (long * LANES) for g in got) * cap
        return call(
            functools.partial(table_kernel, cap, len(got), base is None),
            shape((dims, LANES), F32),
            [
                pltpu.VMEM((cap, n * ents), BF),
                pltpu.VMEM((found, LANES), BF),
                pltpu.VMEM((LANES, found), BF),
                pltpu.VMEM((16, found), BF),
                pltpu.VMEM((found, LANES), BF),
                pltpu.VMEM((found, LANES), BF),
            ],
            2 * found * (dims + n * ents) * LANES,
            "table",
            limit,
        )(scaled, *got, *(() if base is None else (base,)))

    if ringed:
        late = [k for k in range(n) if k not in early + middle]
        late_sent = spread(late, slope_later)
        late_got = send(late[1:], late_sent[1:])
        grad_dim = add_up([late_sent[0], *early_got, *mid_got], None)
        grad_dim = add_up(late_got, grad_dim)
    else:
        fact_me = lax.axis_index("fact")
        sent = [message for k in range(0, n, 8) for message in spread(list(range(k, k + 8)), slope_later)]
        by_owner = jnp.take(jnp.stack(sent), lax.rem(jnp.arange(n) - fact_me + n, n), axis=0)
        grad_dim = add_up([lax.all_to_all(by_owner, "fact", 0, 0)], None)
    grad_msg, grad_self, grad_neigh = call(
        functools.partial(total_kernel, stride), (shape((own, LANES), F32),) * 3, [], 1 << 20, "total"
    )(owned)
    return output_h, grad_msg, grad_self, grad_neigh, grad_dim


def solution(mesh):
    placed = (
        P("fact", "feat"),
        P("fact", None),
        P("fact"),
        P("fact", None),
        P("fact"),
        P("fact", "feat"),
        P("fact", "feat"),
        P(None, "feat"),
        P(None, "feat"),
        P(None, "feat"),
        P("fact", "feat"),
    )
    return jax.shard_map(
        shards,
        mesh=mesh,
        in_specs=placed,
        out_specs=(P("fact", "feat"),) * 5,
        check_vma=False,
    )
```

```python
import functools

import jax
import jax.numpy as jnp
from jax import lax
from jax.experimental import pallas as pl
from jax.experimental.pallas import tpu as pltpu
from jax.sharding import PartitionSpec as P

LANES = 128
BF = jnp.bfloat16
F32 = jnp.float32
VMEM_LIMIT = 16 * 1024 * 1024
VMEM_LIMIT_LARGE = 40 * 1024 * 1024


def call(kernel, out_shape, scratch, flops, name, limit=VMEM_LIMIT):
    return pl.pallas_call(
        kernel,
        out_shape=out_shape,
        scratch_shapes=scratch,
        compiler_params=pltpu.CompilerParams(vmem_limit_bytes=limit),
        cost_estimate=pl.CostEstimate(flops=flops, bytes_accessed=1 << 20, transcendentals=0),
        name=name,
    )


def shape(dims, dtype):
    return jax.ShapeDtypeStruct(dims, dtype)


def nt(a, b):
    return lax.dot_general(a, b, (((1,), (1,)), ((), ())), preferred_element_type=F32)


def tn(a, b):
    return lax.dot_general(a, b, (((0,), (0,)), ((), ())), preferred_element_type=F32)


def dot(a, b):
    return jnp.dot(a, b, preferred_element_type=F32)


def flag(condition):
    return jnp.where(condition, 1.0, 0.0).astype(BF)


def column_codes(row):
    keys = jnp.broadcast_to(row, (LANES, LANES)).astype(F32).T.astype(jnp.int32)
    lane = lax.broadcasted_iota(jnp.int32, (LANES, LANES), 1)
    return flag((keys & (LANES - 1)) == lane), (keys >> 7).astype(F32).astype(BF)


def row_codes(row):
    keys = jnp.broadcast_to(row, (LANES, LANES))
    sub = lax.broadcasted_iota(jnp.int32, (LANES, LANES), 0)
    high = jnp.broadcast_to((row >> 7).astype(F32), (16, LANES)).astype(BF)
    return flag((keys & (LANES - 1)) == sub), high


def pick_block(low, high, block):
    zero = jnp.zeros((), BF)
    return jnp.where(high == block, low, zero)


def pick_rows(low, high, block):
    wide = low.reshape(LANES // 16, 16, low.shape[1])
    picked = pick_block(wide, high[None], block)
    return picked.reshape(low.shape)


def route_kernel(n, cap, ents, dims, do_ref, ds_ref, fo_ref, fs_ref, out_ref, pos_ref, ent_ref, dlow_ref, dhigh_ref):
    chunks = do_ref.shape[0]
    owner = do_ref[...]
    kind = lax.broadcasted_iota(jnp.int32, (n, chunks, LANES), 0)
    held = jnp.where(kind == owner[None], 1.0, 0.0).reshape(n * chunks, LANES)
    held_bf = held.astype(BF)
    i0 = lax.broadcasted_iota(jnp.int32, (LANES, LANES), 0)
    i1 = lax.broadcasted_iota(jnp.int32, (LANES, LANES), 1)
    inside = dot(held_bf, flag(i0 < i1))
    r0 = lax.broadcasted_iota(jnp.int32, (n * chunks, n * chunks), 0)
    r1 = lax.broadcasted_iota(jnp.int32, (n * chunks, n * chunks), 1)
    earlier = flag((r0 // chunks == r1 // chunks) & (r1 < r0))
    before = dot(dot(earlier, held_bf).astype(BF), jnp.ones((LANES, LANES), BF))
    rank = jnp.sum((held * (inside + before)).reshape(n, chunks, LANES), axis=0)
    rank = rank.astype(jnp.int32)
    entity_owner = fo_ref[...]
    entity_slot = fs_ref[...]
    value = ds_ref[...]
    pos_ref[...] = owner * cap + rank
    ent_ref[...] = entity_owner * ents + entity_slot
    fact_dim = owner * dims + value
    high = (value >> 5).astype(F32)
    low = (value & 31).astype(F32)
    names = lax.broadcasted_iota(jnp.int32, (n, LANES), 0)
    places = lax.broadcasted_iota(jnp.int32, (cap, LANES), 0)
    slots = lax.broadcasted_iota(jnp.int32, (ents, LANES), 0)
    asked_high = jnp.zeros((n, cap), F32)
    asked_low = jnp.zeros((n, cap), F32)
    hits = jnp.zeros((n, ents), F32)
    for k in range(chunks):
        here = slice(k * LANES, (k + 1) * LANES)
        mine = jnp.where(names == owner[k : k + 1], 1.0, 0.0)
        at = flag(places == rank[k : k + 1])
        asked_high += nt((mine * high[k : k + 1]).astype(BF), at)
        asked_low += nt((mine * low[k : k + 1]).astype(BF), at)
        hits += nt(flag(names == entity_owner[k : k + 1]), flag(slots == entity_slot[k : k + 1]))
        dlow_ref[here, :], dhigh_ref[here, :] = column_codes(fact_dim[k : k + 1])
    asked = (asked_high * 32.0 + asked_low).astype(jnp.int32)
    for r in range(cap // LANES):
        out_ref[:, r, :] = asked[:, r * LANES : (r + 1) * LANES]
    out_ref[:, cap // LANES, :] = hits.astype(jnp.int32)


def gather_rows(low_ref, high_ref, rows, table_refs, firsts, hot_ref):
    at = 0
    low, high = low_ref[rows, :], high_ref[rows, :]
    for table, first in zip(table_refs, firsts):
        for k in range(table.shape[0] // LANES):
            hot_ref[:, at : at + LANES] = pick_block(low, high, (first + k).astype(F32).astype(BF))
            at += LANES
    total, at = None, 0
    for table in table_refs:
        part = dot(hot_ref[:, at : at + table.shape[0]], table[...])
        total = part if total is None else total + part
        at += table.shape[0]
    return total


def ring_at(place, n):
    place = lax.rem(place + 2 * n, n)
    return jnp.where(place < n // 2, 2 * place, 2 * (n - 1 - place) + 1)


def ring_place(index, n):
    half = lax.div(index, 2)
    return jnp.where(lax.rem(index, 2) == 0, half, n - 1 - half)


def look_kernel(n, pieces, low_ref, high_ref, *refs):
    count = len(pieces)
    tables, base_ref, out_ref, hot_ref = refs[:count], refs[count], refs[-2], refs[-1]
    facts = low_ref.shape[0]
    step = hot_ref.shape[0]
    place = ring_place(lax.axis_index("fact"), n)
    firsts = [lax.div(ring_at(place + hops, n) * dims + row, LANES) for hops, row, dims in pieces]
    for c in range(facts // step):
        rows = slice(c * step, (c + 1) * step)
        out_ref[rows, :] = base_ref[rows, :] + gather_rows(low_ref, high_ref, rows, tables, firsts, hot_ref)


def message_kernel(n, pieces, low_ref, high_ref, *refs):
    count = len(pieces)
    tables, refs = refs[:count], refs[count:]
    base_ref, xw_ref, ent_ref, slope_ref, part_ref, hot_ref, msg_ref, erlow_ref, erhigh_ref = refs
    facts = low_ref.shape[0]
    step = hot_ref.shape[0]
    place = ring_place(lax.axis_index("fact"), n)
    firsts = [lax.div(ring_at(place + hops, n) * dims + row, LANES) for hops, row, dims in pieces]
    for k in range(ent_ref.shape[0]):
        here = slice(k * LANES, (k + 1) * LANES)
        erlow_ref[:, here], erhigh_ref[:, here] = row_codes(ent_ref[k : k + 1, :])
    for c in range(facts // step):
        rows = slice(c * step, (c + 1) * step)
        pre = xw_ref[rows, :] + base_ref[rows, :]
        if count:
            pre = pre + gather_rows(low_ref, high_ref, rows, tables, firsts, hot_ref)
        gate = jax.nn.sigmoid(pre)
        msg_ref[rows, :] = (pre * gate).astype(BF)
        slope_ref[rows, :] = gate * (1.0 + pre * (1.0 - gate))

    def add(pair, carry):
        hot = jnp.concatenate(
            [pick_rows(erlow_ref[...], erhigh_ref[...], (pair * 2 + i).astype(F32).astype(BF)) for i in range(2)], axis=0
        )
        rows = pl.ds(pl.multiple_of(pair * 256, 256), 256)
        part_ref[rows, :] = dot(hot, msg_ref[...]).astype(BF)
        return carry

    lax.fori_loop(0, part_ref.shape[0] // 256, add, 0)


def project_kernel(m, w_ref, *refs):
    blocks, out_ref = refs[:m], refs[m]
    me = lax.axis_index("feat")
    total = None
    for j, ref in enumerate(blocks):
        rows = pl.ds(pl.multiple_of((me ^ j) * LANES, LANES), LANES)
        part = dot(ref[...], w_ref[rows, :])
        total = part if total is None else total + part
    out_ref[...] = total


def ready_kernel(m, width, ents, idx_ref, *refs):
    x_refs, all_refs, (hidden_ref, div_ref, xt_ref, hold_ref) = refs[:m], refs[m : 2 * m], refs[2 * m :]
    rows_each = ents // m
    me = lax.axis_index("feat")
    hits = jnp.sum(idx_ref[:, idx_ref.shape[1] - 1, :], axis=0, keepdims=True).astype(F32)
    hold_ref[...] = jnp.maximum(jnp.broadcast_to(hits, (LANES, ents)).T, 1.0)
    div_ref[...] = hold_ref[pl.ds(pl.multiple_of(me * rows_each, rows_each), rows_each), :]
    for j in range(m):
        hidden_ref[me ^ j] = all_refs[j][2 * width : 2 * width + ents, :]
        xt_ref[pl.ds(pl.multiple_of((me ^ j) * LANES, LANES), LANES), :] = x_refs[j][...].T


def entity_kernel(n, m, width, ents, sums_ref, div_ref, *refs):
    all_refs, (back_ref, out_ref, pre_ref, agg_ref, own_ref) = refs[:m], refs[m:]
    rows_each = ents // m
    me = lax.axis_index("feat")
    divisor = div_ref[...]
    for b in range(m):
        total = sums_ref[b].astype(F32)
        for f in range(1, n):
            total += sums_ref[f * m + b].astype(F32)
        agg_ref[b * rows_each : (b + 1) * rows_each, :] = (total / divisor).astype(BF)
    at = pl.multiple_of(2 * width + me * rows_each, rows_each)
    for j in range(m):
        own_ref[me ^ j] = all_refs[j][pl.ds(at, rows_each), :]
    aggregate = jnp.concatenate([agg_ref[b * rows_each : (b + 1) * rows_each, :] for b in range(m)], axis=1)
    hidden = jnp.concatenate([own_ref[b] for b in range(m)], axis=1)
    d_agg = None
    for j in range(m):
        pre = dot(hidden, all_refs[j][0:width, :]) + dot(aggregate, all_refs[j][width : 2 * width, :])
        gate = jax.nn.sigmoid(pre)
        cot = all_refs[j][pl.ds(at + ents, rows_each), :].astype(F32)
        d_pre = (cot * (gate * (1.0 + pre * (1.0 - gate)))).astype(BF)
        out_ref[me ^ j] = (pre * gate).astype(BF)
        pre_ref[me ^ j] = d_pre
        term = nt(d_pre, all_refs[j][width : 2 * width, :])
        d_agg = term if d_agg is None else d_agg + term
    for b in range(m):
        scaled = (d_agg[:, b * LANES : (b + 1) * LANES] / divisor).astype(BF)
        for f in range(n):
            back_ref[f * m + b] = scaled


def share_kernel(m, out_ref, pre_ref, agg_ref, *share_refs):
    rows_each = out_ref.shape[1]
    me = lax.axis_index("feat")
    for j, ref in enumerate(share_refs):
        ref[0:rows_each, :] = out_ref[me ^ j]
        ref[rows_each : 2 * rows_each, :] = pre_ref[me ^ j]
        ref[2 * rows_each :, :] = agg_ref[...]


def weight_kernel(n, m, width, stride, hidden_ref, *refs):
    got, (out_ref, back_ref, total_ref, pre_ref, agg_ref) = refs[:m], refs[m:]
    rows_each = got[0].shape[0] // (2 + m)
    own = width // n
    me = lax.axis_index("feat")
    for j, ref in enumerate(got):
        here = pl.ds(pl.multiple_of((me ^ j) * rows_each, rows_each), rows_each)
        out_ref[here, :] = ref[0:rows_each, :]
        pre_ref[here, :] = ref[rows_each : 2 * rows_each, :]
        for b in range(m):
            agg_ref[b, here, :] = ref[(2 + b) * rows_each : (3 + b) * rows_each, :]
    d_pre = pre_ref[...]
    for which, blocks in enumerate((hidden_ref, agg_ref)):
        for b in range(m):
            total_ref[b * LANES : (b + 1) * LANES, :] = tn(blocks[b], d_pre)
        for d in range(n):
            back_ref[d % 2, d // 2, which * stride : (which + 1) * stride, :] = padded(
                total_ref[d * own : (d + 1) * own, :], stride
            )


def halves_kernel(back_ref, keep_ref, give_ref):
    odd = lax.rem(lax.axis_index("fact"), 2)
    keep_ref[...] = back_ref[odd]
    give_ref[...] = back_ref[1 - odd].astype(BF)


def padded(piece, rows):
    if piece.shape[0] == rows:
        return piece
    return jnp.concatenate([piece, jnp.zeros((rows - piece.shape[0], LANES), F32)], axis=0)


def codes_kernel(pos_ref, ent_ref, plow_ref, phigh_ref, elow_ref, ehigh_ref):
    for k in range(pos_ref.shape[0]):
        here = slice(k * LANES, (k + 1) * LANES)
        plow_ref[:, here], phigh_ref[:, here] = row_codes(pos_ref[k : k + 1, :])
        elow_ref[here, :], ehigh_ref[here, :] = column_codes(ent_ref[k : k + 1, :])


def request_kernel(n, cap, req_ref, low_ref, high_ref):
    for s in range(n):
        for r in range(cap // LANES):
            at = s * cap + r * LANES
            low_ref[:, at : at + LANES], high_ref[:, at : at + LANES] = row_codes(req_ref[s, r : r + 1, :])


def backward_kernel(n, stride, scaled_ref, slope_ref, low_ref, high_ref, xt_ref, dmsg_ref, share_ref, hot_ref):
    facts = slope_ref.shape[0]
    own = xt_ref.shape[0] // n
    step = hot_ref.shape[0]
    for c in range(facts // step):
        rows = slice(c * step, (c + 1) * step)
        found = gather_rows(low_ref, high_ref, rows, [scaled_ref], [jnp.int32(0)], hot_ref)
        dmsg_ref[rows, :] = (found * slope_ref[rows, :]).astype(BF)
    total = dot(xt_ref[...], dmsg_ref[...])
    for d in range(n):
        share_ref[d] = padded(total[d * own : (d + 1) * own, :], stride).astype(BF)


def spread_kernel(n, cap, stride, offsets, plow_ref, phigh_ref, dmsg_ref, share_ref, *refs):
    pair_refs, out_refs = refs[:-len(offsets)], refs[-len(offsets) :]
    me = lax.axis_index("fact")
    for offset, out_ref in zip(offsets, out_refs):
        d = lax.rem(me + offset, n)
        hot = jnp.concatenate(
            [
                pick_rows(plow_ref[...], phigh_ref[...], (d * (cap // LANES) + i).astype(F32).astype(BF))
                for i in range(cap // LANES)
            ],
            axis=0,
        )
        out_ref[0:cap, :] = dot(hot, dmsg_ref[...]).astype(BF)
        out_ref[cap : cap + stride, :] = share_ref[d]
        if out_ref.shape[0] > cap + stride:
            pair = pair_refs[0][lax.div(d, 2)]
            for ref in pair_refs[1:]:
                pair = pair + ref[lax.div(d, 2)].astype(F32)
            out_ref[cap + stride :, :] = pair.astype(BF)


def table_kernel(n, cap, stride, offsets, first, low_ref, high_ref, *refs):
    count = len(offsets)
    got, refs = refs[:count], refs[count:]
    if not first:
        (base_ref, weight_base_ref), refs = refs[:2], refs[2:]
    out_ref, weight_ref, rows_ref, klow_ref, khigh_ref = refs
    me = lax.axis_index("fact")
    if first:
        weight_ref[...] = jnp.zeros(weight_ref.shape, F32)
    else:
        weight_ref[...] = weight_base_ref[...]
    for j, (offset, ref) in enumerate(zip(offsets, got)):
        source = lax.rem(me + (n - offset), n)
        here = slice(j * cap, (j + 1) * cap)
        there = pl.ds(pl.multiple_of(source * cap, LANES), cap)
        rows_ref[here, :] = ref[0:cap, :]
        klow_ref[:, here] = low_ref[:, there]
        khigh_ref[:, here] = high_ref[:, there]
        rows = ref.shape[0] - cap
        weight_ref[0:rows, :] += ref[cap:, :].astype(F32)
    blocks = out_ref.shape[0] // LANES
    join = 2 if blocks % 2 == 0 else 1

    def add(group, carry):
        hot = jnp.concatenate(
            [pick_rows(klow_ref[...], khigh_ref[...], (group * join + i).astype(F32).astype(BF)) for i in range(join)], axis=0
        )
        rows = pl.ds(pl.multiple_of(group * join * LANES, LANES), join * LANES)
        sums = dot(hot, rows_ref[...])
        out_ref[rows, :] = sums if first else base_ref[rows, :] + sums
        return carry

    lax.fori_loop(0, blocks // join, add, 0)


def shards(fact_x, dim_owner, dim_slot, fact_owner, fact_slot, dim_table, entity_h, w_msg, w_self, w_neigh, cotangent):
    n, m = lax.axis_size("fact"), lax.axis_size("feat")
    assert m == 4 and n % 2 == 0
    facts = fact_x.shape[0]
    chunks = facts // LANES
    ents = entity_h.shape[0]
    rows_each = ents // m
    width = w_msg.shape[0]
    dims = dim_table.shape[0]
    cap = -(-(3 * facts // n) // LANES) * LANES
    slots = n * cap
    groups = cap // LANES + 1
    own = width // n
    stride = max(16, own)
    step = 512
    tie = lax.optimization_barrier
    ringed = n <= 8
    limit = VMEM_LIMIT if ringed else VMEM_LIMIT_LARGE

    ring = [2 * p if p < n // 2 else 2 * (n - 1 - p) + 1 for p in range(n)]
    to_right = [(ring[p], ring[(p + 1) % n]) for p in range(n)]
    to_left = [(ring[(p + 1) % n], ring[p]) for p in range(n)]

    def pass_on(right, left):
        return lax.ppermute(right, "fact", to_right), lax.ppermute(left, "fact", to_left)

    def swap(block, bit):
        return lax.ppermute(block, "feat", [(i, i ^ bit) for i in range(m)])

    if ringed:
        right, left = pass_on(dim_table, dim_table)
    x_far, x_near = swap(fact_x, 2), swap(fact_x, 1)

    by_lane = (chunks, LANES)
    columns = shape((facts, LANES), BF)
    asks, pos, entity, dlow, dhigh = call(
        functools.partial(route_kernel, n, cap, ents, dims),
        (
            shape((n, groups, LANES), jnp.int32),
            shape(by_lane, jnp.int32),
            shape(by_lane, jnp.int32),
            columns,
            columns,
        ),
        [],
        1 << 28,
        "route",
    )(dim_owner.reshape(by_lane), dim_slot.reshape(by_lane), fact_owner.reshape(by_lane), fact_slot.reshape(by_lane))
    if ringed:
        right, left, x_far, x_near, asks, pos, entity, dlow, dhigh = tie(
            (right, left, x_far, x_near, asks, pos, entity, dlow, dhigh)
        )

    def look(pieces, tables, base):
        rows = sum(t.shape[0] for t in tables)
        return call(
            functools.partial(look_kernel, n, pieces),
            shape((facts, LANES), F32),
            [pltpu.VMEM((step, rows), BF)],
            2 * facts * rows * LANES,
            "look",
            limit,
        )(dlow, dhigh, *tables, base)

    def project(blocks):
        return call(
            functools.partial(project_kernel, m), shape((facts, LANES), F32), [], 2 * facts * width * LANES, "project"
        )(w_msg, *blocks)

    found = jnp.zeros((facts, LANES), F32)
    weights = jnp.concatenate([w_self, w_neigh, entity_h, cotangent], axis=0)
    if ringed:
        half = dims // 2
        near = (right, left)
        after = pass_on(*near)
        x_last = swap(x_far, 1)
        found = look([(0, 0, dims), (-1, 0, dims), (1, 0, dims)], [dim_table, *near], found)
        right, left, x_last, found, weights = tie((*after, x_last, found, weights))
        for k in range(2, n // 2):
            last_round = k == n // 2 - 1
            after = pass_on(right[:half], left[half:]) if last_round else pass_on(right, left)
            if last_round:
                all_last = swap(all_far, 1)
            else:
                all_far, all_near = swap(weights, 2), swap(weights, 1)
                xw = project([fact_x, x_near, x_far, x_last])
            found = look([(-k, 0, dims), (k, 0, dims)], [right, left], found)
            if last_round:
                found, all_last = tie((found, all_last))
            else:
                *after, found, xw, all_far, all_near = tie((*after, found, xw, all_far, all_near))
            right, left = after
        last = [right, left]
        last_pieces = [(-(n // 2), 0, dims), (n // 2, half, dims)]
    else:
        x_last = swap(x_far, 1)
        xw = project([fact_x, x_near, x_far, x_last])
        all_far, all_near = swap(weights, 2), swap(weights, 1)
        all_last = swap(all_far, 1)
        whole = lax.all_gather(dim_table, "fact")
        order = jnp.take(whole, ring_at(ring_place(lax.axis_index("fact"), n) + jnp.arange(n), n), axis=0)
        for k in range(0, n, 8):
            found = look([(k + i, 0, dims) for i in range(8)], [order[k + i] for i in range(8)], found)
        last, last_pieces = [], []
    x_blocks, all_blocks = [fact_x, x_near, x_far, x_last], [weights, all_near, all_far, all_last]
    asked = lax.all_to_all(asks, "fact", 0, 0)
    last_rows = max(LANES, sum(t.shape[0] for t in last))
    slope, part = call(
        functools.partial(message_kernel, n, last_pieces),
        (shape((facts, LANES), F32), shape((n * ents, LANES), BF)),
        [
            pltpu.VMEM((step, last_rows), BF),
            pltpu.VMEM((facts, LANES), BF),
            pltpu.VMEM((LANES, facts), BF),
            pltpu.VMEM((16, facts), BF),
        ],
        2 * facts * (last_rows + n * ents) * LANES,
        "message",
        limit,
    )(dlow, dhigh, *last, found, xw, entity)
    sums = lax.all_to_all(part.reshape(n * m, rows_each, LANES), ("fact", "feat"), 0, 0)
    asked, pos, entity, _ = tie((asked, pos, entity, part))
    hidden, divisor, x_turned = call(
        functools.partial(ready_kernel, m, width, ents),
        (
            shape((m, ents, LANES), BF),
            shape((rows_each, LANES), F32),
            shape((width, facts), BF),
        ),
        [pltpu.VMEM((ents, LANES), F32)],
        1 << 28,
        "ready",
    )(asked, *x_blocks, *all_blocks)
    by_feat = shape((m, rows_each, LANES), BF)
    back, out_parts, pre_parts, agg_parts = call(
        functools.partial(entity_kernel, n, m, width, ents),
        (shape((n * m, rows_each, LANES), BF), by_feat, by_feat, shape((m * rows_each, LANES), BF)),
        [pltpu.VMEM((m, rows_each, LANES), BF)],
        6 * rows_each * width * width,
        "entity",
    )(sums, divisor, *all_blocks)
    scaled = lax.all_to_all(back, ("fact", "feat"), 0, 0).reshape(n * ents, LANES)
    shares = call(
        functools.partial(share_kernel, m),
        tuple(shape(((2 + m) * rows_each, LANES), BF) for _ in range(m)),
        [],
        1 << 20,
        "share",
    )(out_parts, pre_parts, agg_parts)
    got = [shares[0]] + [swap(shares[j], j) for j in range(1, m)]
    pos, entity, asked, _ = tie((pos, entity, asked, back))
    plow, phigh, elow, ehigh = call(
        codes_kernel,
        (shape((LANES, facts), BF), shape((16, facts), BF), columns, columns),
        [],
        1 << 26,
        "codes",
    )(pos, entity)
    rlow, rhigh = call(
        functools.partial(request_kernel, n, cap),
        (shape((LANES, slots), BF), shape((16, slots), BF)),
        [],
        1 << 26,
        "requests",
        limit,
    )(asked)
    pair_shape = (n // 2, 2 * stride, LANES)
    output_h, pair = call(
        functools.partial(weight_kernel, n, m, width, stride),
        (shape((ents, LANES), BF), shape((2, *pair_shape), F32)),
        [pltpu.VMEM((width, LANES), F32), pltpu.VMEM((ents, LANES), BF), pltpu.VMEM((m, ents, LANES), BF)],
        4 * ents * width * LANES,
        "weight",
    )(hidden, *got)
    if ringed:
        keep, give = call(halves_kernel, (shape(pair_shape, F32), shape(pair_shape, BF)), [], 1 << 20, "halves")(pair)
        pairs = [keep, lax.ppermute(give, "fact", [(i, i ^ 1) for i in range(n)])]
        elow, pairs = tie((elow, pairs))
    else:
        pairs = [jnp.stack([pair[0], pair[1]], axis=1).reshape(n, 2 * stride, LANES)]
    d_msg, msg_share = call(
        functools.partial(backward_kernel, n, stride),
        (columns, shape((n, stride, LANES), BF)),
        [pltpu.VMEM((step, n * ents), BF)],
        2 * facts * (n * ents + width) * LANES,
        "backward",
        limit,
    )(scaled, slope, elow, ehigh, x_turned)

    def spread(offsets):
        lengths = [cap + (3 if ringed and k % 2 == 0 else 1) * stride for k in offsets]
        return call(
            functools.partial(spread_kernel, n, cap, stride, offsets),
            tuple(shape((rows, LANES), BF) for rows in lengths),
            [],
            2 * facts * cap * LANES * len(offsets),
            "spread",
            limit,
        )(plow, phigh, d_msg, msg_share, *(pairs if ringed else ()))

    def add_up(offsets, got, base):
        return call(
            functools.partial(table_kernel, n, cap, stride, offsets, base is None),
            (shape((dims, LANES), F32), shape((3 * stride, LANES), F32)),
            [
                pltpu.VMEM((cap * len(got), LANES), BF),
                pltpu.VMEM((LANES, cap * len(got)), BF),
                pltpu.VMEM((16, cap * len(got)), BF),
            ],
            2 * cap * dims * LANES * len(got),
            "table",
            limit,
        )(rlow, rhigh, *got, *(base or ()))

    totals = None
    if ringed:
        messages = {}
        for offsets in [[n // 2], [1, n - 1]] + [[k, n - k] for k in range(n // 2 - 1, 1, -1)]:
            for offset, message in zip(offsets, spread(offsets)):
                messages[offset] = lax.ppermute(message, "fact", [(i, (i + offset) % n) for i in range(n)])
        messages[0] = spread([0])[0]
        for offsets in [[0, 1, n - 1], [n // 2]] + [[k, n - k] for k in range(n // 2 - 1, 1, -1)]:
            totals = add_up(offsets, [messages[k] for k in offsets], totals)
        grad_dim, weight = totals
    else:
        fact_me = lax.axis_index("fact")
        sent = [message for k in range(0, n, 8) for message in spread(list(range(k, k + 8)))]
        by_owner = jnp.take(jnp.stack(sent), lax.rem(jnp.arange(n) - fact_me + n, n), axis=0)
        owned = lax.all_to_all(by_owner, "fact", 0, 0)
        by_offset = jnp.take(owned, lax.rem(fact_me - jnp.arange(n) + n, n), axis=0)
        for k in range(0, n, 8):
            totals = add_up(list(range(k, k + 8)), [by_offset[k + i] for i in range(8)], totals)
        grad_dim, weight = totals
        pair_sum = lax.psum_scatter(pairs[0], "fact", scatter_dimension=0, tiled=True)[0]
        weight = weight + jnp.concatenate([jnp.zeros((stride, LANES), F32), pair_sum], axis=0)
    return (
        output_h,
        weight[0:own],
        weight[stride : stride + own],
        weight[2 * stride : 2 * stride + own],
        grad_dim,
    )


def solution(mesh):
    placed = (
        P("fact", "feat"),
        P("fact", None),
        P("fact"),
        P("fact", None),
        P("fact"),
        P("fact", "feat"),
        P("fact", "feat"),
        P(None, "feat"),
        P(None, "feat"),
        P(None, "feat"),
        P("fact", "feat"),
    )
    return jax.shard_map(
        shards,
        mesh=mesh,
        in_specs=placed,
        out_specs=(P("fact", "feat"),) * 5,
        check_vma=False,
    )
```

```python
import functools

import jax
import jax.numpy as jnp
from jax import lax
from jax.experimental import pallas as pl
from jax.experimental.pallas import tpu as pltpu
from jax.sharding import PartitionSpec as P

LANES = 128
BF = jnp.bfloat16
F32 = jnp.float32
VMEM_LIMIT = 16 * 1024 * 1024
VMEM_LIMIT_LARGE = 40 * 1024 * 1024


def call(kernel, out_shape, scratch, flops, name, limit=VMEM_LIMIT, **specs):
    return pl.pallas_call(
        kernel,
        out_shape=out_shape,
        scratch_shapes=scratch,
        compiler_params=pltpu.CompilerParams(vmem_limit_bytes=limit),
        cost_estimate=pl.CostEstimate(flops=flops, bytes_accessed=1 << 20, transcendentals=0),
        name=name,
        **specs,
    )


def shape(dims, dtype):
    return jax.ShapeDtypeStruct(dims, dtype)


def nt(a, b):
    return lax.dot_general(a, b, (((1,), (1,)), ((), ())), preferred_element_type=F32)


def tn(a, b):
    return lax.dot_general(a, b, (((0,), (0,)), ((), ())), preferred_element_type=F32)


def dot(a, b):
    return jnp.dot(a, b, preferred_element_type=F32)


def flag(condition):
    return jnp.where(condition, 1.0, 0.0).astype(BF)


def column_codes(row):
    keys = jnp.broadcast_to(row, (LANES, LANES)).astype(F32).T.astype(jnp.int32)
    lane = lax.broadcasted_iota(jnp.int32, (LANES, LANES), 1)
    return flag((keys & (LANES - 1)) == lane), (keys >> 7).astype(F32).astype(BF)


def row_codes(row):
    keys = jnp.broadcast_to(row, (LANES, LANES))
    sub = lax.broadcasted_iota(jnp.int32, (LANES, LANES), 0)
    high = jnp.broadcast_to((row >> 7).astype(F32), (16, LANES)).astype(BF)
    return flag((keys & (LANES - 1)) == sub), high


def pick_block(low, high, block):
    zero = jnp.zeros((), BF)
    return jnp.where(high == block, low, zero)


def pick_rows(low, high, block):
    wide = low.reshape(LANES // 16, 16, low.shape[1])
    picked = pick_block(wide, high[None], block)
    return picked.reshape(low.shape)


def route_kernel(n, cap, ents, dims, do_ref, ds_ref, fo_ref, fs_ref, out_ref, pos_ref, ent_ref, dlow_ref, dhigh_ref):
    chunks = do_ref.shape[0]
    owner = do_ref[...]
    kind = lax.broadcasted_iota(jnp.int32, (n, chunks, LANES), 0)
    held = jnp.where(kind == owner[None], 1.0, 0.0).reshape(n * chunks, LANES)
    held_bf = held.astype(BF)
    i0 = lax.broadcasted_iota(jnp.int32, (LANES, LANES), 0)
    i1 = lax.broadcasted_iota(jnp.int32, (LANES, LANES), 1)
    inside = dot(held_bf, flag(i0 < i1))
    r0 = lax.broadcasted_iota(jnp.int32, (n * chunks, n * chunks), 0)
    r1 = lax.broadcasted_iota(jnp.int32, (n * chunks, n * chunks), 1)
    earlier = flag((r0 // chunks == r1 // chunks) & (r1 < r0))
    before = dot(dot(earlier, held_bf).astype(BF), jnp.ones((LANES, LANES), BF))
    rank = jnp.sum((held * (inside + before)).reshape(n, chunks, LANES), axis=0)
    rank = rank.astype(jnp.int32)
    entity_owner = fo_ref[...]
    entity_slot = fs_ref[...]
    value = ds_ref[...]
    pos_ref[...] = owner * cap + rank
    ent_ref[...] = entity_owner * ents + entity_slot
    fact_dim = owner * dims + value
    high = (value >> 5).astype(F32)
    low = (value & 31).astype(F32)
    names = lax.broadcasted_iota(jnp.int32, (n, LANES), 0)
    places = lax.broadcasted_iota(jnp.int32, (cap, LANES), 0)
    slots = lax.broadcasted_iota(jnp.int32, (ents, LANES), 0)
    asked_high = jnp.zeros((n, cap), F32)
    asked_low = jnp.zeros((n, cap), F32)
    hits = jnp.zeros((n, ents), F32)
    for k in range(chunks):
        here = slice(k * LANES, (k + 1) * LANES)
        mine = jnp.where(names == owner[k : k + 1], 1.0, 0.0)
        at = flag(places == rank[k : k + 1])
        asked_high += nt((mine * high[k : k + 1]).astype(BF), at)
        asked_low += nt((mine * low[k : k + 1]).astype(BF), at)
        hits += nt(flag(names == entity_owner[k : k + 1]), flag(slots == entity_slot[k : k + 1]))
        dlow_ref[here, :], dhigh_ref[here, :] = column_codes(fact_dim[k : k + 1])
    asked = (asked_high * 32.0 + asked_low).astype(jnp.int32)
    for r in range(cap // LANES):
        out_ref[:, r, :] = asked[:, r * LANES : (r + 1) * LANES]
    out_ref[:, cap // LANES, :] = hits.astype(jnp.int32)


def gather_rows(low_ref, high_ref, rows, table_refs, firsts, hot_ref):
    at = 0
    low, high = low_ref[rows, :], high_ref[rows, :]
    for table, first in zip(table_refs, firsts):
        for k in range(table.shape[0] // LANES):
            hot_ref[:, at : at + LANES] = pick_block(low, high, (first + k).astype(F32).astype(BF))
            at += LANES
    total, at = None, 0
    for table in table_refs:
        part = dot(hot_ref[:, at : at + table.shape[0]], table[...])
        total = part if total is None else total + part
        at += table.shape[0]
    return total


def ring_at(place, n):
    place = lax.rem(place + 2 * n, n)
    return jnp.where(place < n // 2, 2 * place, 2 * (n - 1 - place) + 1)


def ring_place(index, n):
    half = lax.div(index, 2)
    return jnp.where(lax.rem(index, 2) == 0, half, n - 1 - half)


def look_kernel(n, pieces, low_ref, high_ref, *refs):
    count = len(pieces)
    tables, base_ref, out_ref, hot_ref = refs[:count], refs[count], refs[-2], refs[-1]
    facts = low_ref.shape[0]
    step = hot_ref.shape[0]
    place = ring_place(lax.axis_index("fact"), n)
    firsts = [lax.div(ring_at(place + hops, n) * dims + row, LANES) for hops, row, dims in pieces]
    for c in range(facts // step):
        rows = slice(c * step, (c + 1) * step)
        out_ref[rows, :] = base_ref[rows, :] + gather_rows(low_ref, high_ref, rows, tables, firsts, hot_ref)


def message_kernel(n, pieces, low_ref, high_ref, *refs):
    count = len(pieces)
    tables, refs = refs[:count], refs[count:]
    base_ref, xw_ref, ent_ref, slope_out, part_ref, slope_ref, hot_ref, msg_ref, erlow_ref, erhigh_ref, sem = refs
    facts = low_ref.shape[0]
    step = hot_ref.shape[0]
    place = ring_place(lax.axis_index("fact"), n)
    firsts = [lax.div(ring_at(place + hops, n) * dims + row, LANES) for hops, row, dims in pieces]
    for k in range(ent_ref.shape[0]):
        here = slice(k * LANES, (k + 1) * LANES)
        erlow_ref[:, here], erhigh_ref[:, here] = row_codes(ent_ref[k : k + 1, :])
    for c in range(facts // step):
        rows = slice(c * step, (c + 1) * step)
        pre = xw_ref[rows, :] + base_ref[rows, :]
        if count:
            pre = pre + gather_rows(low_ref, high_ref, rows, tables, firsts, hot_ref)
        gate = jax.nn.sigmoid(pre)
        msg_ref[rows, :] = (pre * gate).astype(BF)
        slope_ref[rows, :] = gate * (1.0 + pre * (1.0 - gate))
    keep = pltpu.make_async_copy(slope_ref, slope_out, sem)
    keep.start()

    def add(pair, carry):
        hot = jnp.concatenate(
            [pick_rows(erlow_ref[...], erhigh_ref[...], (pair * 2 + i).astype(F32).astype(BF)) for i in range(2)], axis=0
        )
        rows = pl.ds(pl.multiple_of(pair * 256, 256), 256)
        part_ref[rows, :] = dot(hot, msg_ref[...]).astype(BF)
        return carry

    lax.fori_loop(0, part_ref.shape[0] // 256, add, 0)
    keep.wait()


def project_kernel(m, w_ref, *refs):
    blocks, out_ref = refs[:m], refs[m]
    me = lax.axis_index("feat")
    total = None
    for j, ref in enumerate(blocks):
        rows = pl.ds(pl.multiple_of((me ^ j) * LANES, LANES), LANES)
        part = dot(ref[...], w_ref[rows, :])
        total = part if total is None else total + part
    out_ref[...] = total


def ready_kernel(m, width, ents, *refs):
    x_refs, all_refs, (hidden_ref, xt_ref) = refs[:m], refs[m : 2 * m], refs[2 * m :]
    me = lax.axis_index("feat")
    for j in range(m):
        hidden_ref[me ^ j] = all_refs[j][2 * width : 2 * width + ents, :]
        xt_ref[pl.ds(pl.multiple_of((me ^ j) * LANES, LANES), LANES), :] = x_refs[j][...].T


def entity_kernel(n, m, width, ents, sums_ref, idx_ref, *refs):
    all_refs, (back_ref, out_ref, pre_ref, agg_ref, own_ref, hold_ref) = refs[:m], refs[m:]
    rows_each = ents // m
    me = lax.axis_index("feat")
    hits = jnp.sum(idx_ref[:, idx_ref.shape[1] - 1, :], axis=0, keepdims=True).astype(F32)
    hold_ref[...] = jnp.maximum(jnp.broadcast_to(hits, (LANES, ents)).T, 1.0)
    divisor = hold_ref[pl.ds(pl.multiple_of(me * rows_each, rows_each), rows_each), :]
    for b in range(m):
        total = sums_ref[b].astype(F32)
        for f in range(1, n):
            total += sums_ref[f * m + b].astype(F32)
        agg_ref[b * rows_each : (b + 1) * rows_each, :] = (total / divisor).astype(BF)
    at = pl.multiple_of(2 * width + me * rows_each, rows_each)
    for j in range(m):
        own_ref[me ^ j] = all_refs[j][pl.ds(at, rows_each), :]
    aggregate = jnp.concatenate([agg_ref[b * rows_each : (b + 1) * rows_each, :] for b in range(m)], axis=1)
    hidden = jnp.concatenate([own_ref[b] for b in range(m)], axis=1)
    d_agg = None
    for j in range(m):
        pre = dot(hidden, all_refs[j][0:width, :]) + dot(aggregate, all_refs[j][width : 2 * width, :])
        gate = jax.nn.sigmoid(pre)
        cot = all_refs[j][pl.ds(at + ents, rows_each), :].astype(F32)
        d_pre = (cot * (gate * (1.0 + pre * (1.0 - gate)))).astype(BF)
        out_ref[me ^ j] = (pre * gate).astype(BF)
        pre_ref[me ^ j] = d_pre
        term = nt(d_pre, all_refs[j][width : 2 * width, :])
        d_agg = term if d_agg is None else d_agg + term
    for b in range(m):
        scaled = (d_agg[:, b * LANES : (b + 1) * LANES] / divisor).astype(BF)
        for f in range(n):
            back_ref[f * m + b] = scaled


def share_kernel(m, out_ref, pre_ref, agg_ref, *share_refs):
    rows_each = out_ref.shape[1]
    me = lax.axis_index("feat")
    for j, ref in enumerate(share_refs):
        ref[0:rows_each, :] = out_ref[me ^ j]
        ref[rows_each : 2 * rows_each, :] = pre_ref[me ^ j]
        ref[2 * rows_each :, :] = agg_ref[...]


def weight_kernel(n, m, width, stride, hidden_ref, *refs):
    got, (out_ref, back_ref, total_ref, pre_ref, agg_ref) = refs[:m], refs[m:]
    rows_each = got[0].shape[0] // (2 + m)
    own = width // n
    me = lax.axis_index("feat")
    for j, ref in enumerate(got):
        here = pl.ds(pl.multiple_of((me ^ j) * rows_each, rows_each), rows_each)
        out_ref[here, :] = ref[0:rows_each, :]
        pre_ref[here, :] = ref[rows_each : 2 * rows_each, :]
        for b in range(m):
            agg_ref[b, here, :] = ref[(2 + b) * rows_each : (3 + b) * rows_each, :]
    d_pre = pre_ref[...]
    for which, blocks in enumerate((hidden_ref, agg_ref)):
        for b in range(m):
            total_ref[b * LANES : (b + 1) * LANES, :] = tn(blocks[b], d_pre)
        for d in range(n):
            back_ref[d % 2, d // 2, which * stride : (which + 1) * stride, :] = padded(
                total_ref[d * own : (d + 1) * own, :], stride
            )


def halves_kernel(back_ref, keep_ref, give_ref):
    odd = lax.rem(lax.axis_index("fact"), 2)
    keep_ref[...] = back_ref[odd]
    give_ref[...] = back_ref[1 - odd].astype(BF)


def padded(piece, rows):
    if piece.shape[0] == rows:
        return piece
    return jnp.concatenate([piece, jnp.zeros((rows - piece.shape[0], LANES), F32)], axis=0)


def codes_kernel(pos_ref, ent_ref, plow_ref, phigh_ref, elow_ref, ehigh_ref):
    for k in range(pos_ref.shape[0]):
        here = slice(k * LANES, (k + 1) * LANES)
        plow_ref[:, here], phigh_ref[:, here] = row_codes(pos_ref[k : k + 1, :])
        elow_ref[here, :], ehigh_ref[here, :] = column_codes(ent_ref[k : k + 1, :])


def request_kernel(n, cap, req_ref, low_ref, high_ref):
    for s in range(n):
        for r in range(cap // LANES):
            at = s * cap + r * LANES
            low_ref[:, at : at + LANES], high_ref[:, at : at + LANES] = row_codes(req_ref[s, r : r + 1, :])


def backward_kernel(n, stride, slope_in, scaled_ref, low_ref, high_ref, xt_ref, dmsg_ref, share_ref, hot_ref, slope_ref, sem):
    fetch = pltpu.make_async_copy(slope_in, slope_ref, sem)
    fetch.start()
    facts = slope_ref.shape[0]
    own = xt_ref.shape[0] // n
    step = hot_ref.shape[0]
    for c in range(facts // step):
        rows = slice(c * step, (c + 1) * step)
        found = gather_rows(low_ref, high_ref, rows, [scaled_ref], [jnp.int32(0)], hot_ref)
        if c == 0:
            fetch.wait()
        dmsg_ref[rows, :] = (found * slope_ref[rows, :]).astype(BF)
    total = dot(xt_ref[...], dmsg_ref[...])
    for d in range(n):
        share_ref[d] = padded(total[d * own : (d + 1) * own, :], stride).astype(BF)


def spread_kernel(n, cap, stride, offsets, plow_ref, phigh_ref, dmsg_ref, share_ref, *refs):
    pair_refs, out_refs = refs[:-len(offsets)], refs[-len(offsets) :]
    me = lax.axis_index("fact")
    for offset, out_ref in zip(offsets, out_refs):
        d = lax.rem(me + offset, n)
        hot = jnp.concatenate(
            [
                pick_rows(plow_ref[...], phigh_ref[...], (d * (cap // LANES) + i).astype(F32).astype(BF))
                for i in range(cap // LANES)
            ],
            axis=0,
        )
        out_ref[0:cap, :] = dot(hot, dmsg_ref[...]).astype(BF)
        out_ref[cap : cap + stride, :] = share_ref[d]
        if out_ref.shape[0] > cap + stride:
            pair = pair_refs[0][lax.div(d, 2)]
            for ref in pair_refs[1:]:
                pair = pair + ref[lax.div(d, 2)].astype(F32)
            out_ref[cap + stride :, :] = pair.astype(BF)


def table_kernel(n, cap, stride, offsets, first, final, low_ref, high_ref, *refs):
    count = len(offsets)
    got, refs = refs[:count], refs[count:]
    if not first:
        (base_ref, weight_base_ref), refs = refs[:2], refs[2:]
    out_ref, refs = refs[0], refs[1:]
    final_refs, refs = (refs[:3], refs[3:]) if final else ((), refs[1:] + refs[:1])
    rows_ref, klow_ref, khigh_ref, weight_ref = refs
    me = lax.axis_index("fact")
    if first:
        weight_ref[...] = jnp.zeros(weight_ref.shape, F32)
    else:
        weight_ref[...] = weight_base_ref[...]
    for j, (offset, ref) in enumerate(zip(offsets, got)):
        source = lax.rem(me + (n - offset), n)
        here = slice(j * cap, (j + 1) * cap)
        there = pl.ds(pl.multiple_of(source * cap, LANES), cap)
        rows_ref[here, :] = ref[0:cap, :]
        klow_ref[:, here] = low_ref[:, there]
        khigh_ref[:, here] = high_ref[:, there]
        rows = ref.shape[0] - cap
        weight_ref[0:rows, :] += ref[cap:, :].astype(F32)
    for which, ref in enumerate(final_refs):
        ref[...] = weight_ref[which * stride : which * stride + ref.shape[0], :]
    blocks = out_ref.shape[0] // LANES
    join = 2 if blocks % 2 == 0 else 1

    def add(group, carry):
        hot = jnp.concatenate(
            [pick_rows(klow_ref[...], khigh_ref[...], (group * join + i).astype(F32).astype(BF)) for i in range(join)], axis=0
        )
        rows = pl.ds(pl.multiple_of(group * join * LANES, LANES), join * LANES)
        sums = dot(hot, rows_ref[...])
        out_ref[rows, :] = sums if first else base_ref[rows, :] + sums
        return carry

    lax.fori_loop(0, blocks // join, add, 0)


def shards(fact_x, dim_owner, dim_slot, fact_owner, fact_slot, dim_table, entity_h, w_msg, w_self, w_neigh, cotangent):
    n, m = lax.axis_size("fact"), lax.axis_size("feat")
    assert m == 4 and n % 2 == 0
    facts = fact_x.shape[0]
    chunks = facts // LANES
    ents = entity_h.shape[0]
    rows_each = ents // m
    width = w_msg.shape[0]
    dims = dim_table.shape[0]
    cap = -(-(3 * facts // n) // LANES) * LANES
    slots = n * cap
    groups = cap // LANES + 1
    own = width // n
    stride = max(16, own)
    step = 512
    tie = lax.optimization_barrier
    ringed = n <= 8
    limit = VMEM_LIMIT if ringed else VMEM_LIMIT_LARGE

    ring = [2 * p if p < n // 2 else 2 * (n - 1 - p) + 1 for p in range(n)]
    to_right = [(ring[p], ring[(p + 1) % n]) for p in range(n)]
    to_left = [(ring[(p + 1) % n], ring[p]) for p in range(n)]

    def pass_on(right, left):
        return lax.ppermute(right, "fact", to_right), lax.ppermute(left, "fact", to_left)

    def swap(block, bit):
        return lax.ppermute(block, "feat", [(i, i ^ bit) for i in range(m)])

    if ringed:
        right, left = pass_on(dim_table, dim_table)
    x_near = swap(fact_x, 1)

    by_lane = (chunks, LANES)
    columns = shape((facts, LANES), BF)
    asks, pos, entity, dlow, dhigh = call(
        functools.partial(route_kernel, n, cap, ents, dims),
        (
            shape((n, groups, LANES), jnp.int32),
            shape(by_lane, jnp.int32),
            shape(by_lane, jnp.int32),
            columns,
            columns,
        ),
        [],
        1 << 28,
        "route",
    )(dim_owner.reshape(by_lane), dim_slot.reshape(by_lane), fact_owner.reshape(by_lane), fact_slot.reshape(by_lane))
    if ringed:
        right, left, x_near, asks, pos, entity, dlow, dhigh = tie(
            (right, left, x_near, asks, pos, entity, dlow, dhigh)
        )

    def look(pieces, tables, base):
        rows = sum(t.shape[0] for t in tables)
        return call(
            functools.partial(look_kernel, n, pieces),
            shape((facts, LANES), F32),
            [pltpu.VMEM((step, rows), BF)],
            2 * facts * rows * LANES,
            "look",
            limit,
        )(dlow, dhigh, *tables, base)

    def project(blocks):
        return call(
            functools.partial(project_kernel, m), shape((facts, LANES), F32), [], 2 * facts * width * LANES, "project"
        )(w_msg, *blocks)

    found = jnp.zeros((facts, LANES), F32)
    weights = jnp.concatenate([w_self, w_neigh, entity_h, cotangent], axis=0)
    if ringed:
        near = (right, left)
        after = pass_on(*near)
        x_far = swap(fact_x, 2)
        found = look([(0, 0, dims), (-1, 0, dims), (1, 0, dims)], [dim_table, *near], found)
        right, left, x_far, found, weights = tie((*after, x_far, found, weights))
        for k in range(2, n // 2 - 1):
            after = pass_on(right, left)
            x_last = swap(x_far, 1)
            found = look([(-k, 0, dims), (k, 0, dims)], [right, left], found)
            right, left, found, x_last = tie((*after, found, x_last))
        all_far = swap(weights, 2)
        k = n // 2 - 1
        after = lax.ppermute(right, "fact", to_right)
        xw = project([fact_x, x_near, x_far, x_last])
        found = look([(-k, 0, dims), (k, 0, dims)], [right, left], found)
        all_near = swap(weights, 1)
        found, all_far, all_near = tie((found, all_far, all_near))
        last, last_pieces = [after], [(n // 2, 0, dims)]
    else:
        x_far = swap(fact_x, 2)
        x_last = swap(x_far, 1)
        xw = project([fact_x, x_near, x_far, x_last])
        all_far, all_near = swap(weights, 2), swap(weights, 1)
        whole = lax.all_gather(dim_table, "fact")
        order = jnp.take(whole, ring_at(ring_place(lax.axis_index("fact"), n) + jnp.arange(n), n), axis=0)
        for k in range(0, n, 8):
            found = look([(k + i, 0, dims) for i in range(8)], [order[k + i] for i in range(8)], found)
        last, last_pieces = [], []
    all_last = swap(all_far, 1)
    x_blocks, all_blocks = [fact_x, x_near, x_far, x_last], [weights, all_near, all_far, all_last]
    asked = lax.all_to_all(asks, "fact", 0, 0)
    last_rows = max(LANES, sum(t.shape[0] for t in last))
    slope, part = call(
        functools.partial(message_kernel, n, last_pieces),
        (shape((facts, LANES), F32), shape((n * ents, LANES), BF)),
        [
            pltpu.VMEM((facts, LANES), F32),
            pltpu.VMEM((step, last_rows), BF),
            pltpu.VMEM((facts, LANES), BF),
            pltpu.VMEM((LANES, facts), BF),
            pltpu.VMEM((16, facts), BF),
            pltpu.SemaphoreType.DMA,
        ],
        2 * facts * (last_rows + n * ents) * LANES,
        "message",
        limit,
        out_specs=(pl.BlockSpec(memory_space=pl.ANY), pl.BlockSpec(memory_space=pltpu.VMEM)),
    )(dlow, dhigh, *last, found, xw, entity)
    sums = lax.all_to_all(part.reshape(n * m, rows_each, LANES), ("fact", "feat"), 0, 0)
    pos, entity, x_blocks, _ = tie((pos, entity, x_blocks, part))
    hidden, x_turned = call(
        functools.partial(ready_kernel, m, width, ents),
        (shape((m, ents, LANES), BF), shape((width, facts), BF)),
        [],
        1 << 28,
        "ready",
    )(*x_blocks, *all_blocks)
    by_feat = shape((m, rows_each, LANES), BF)
    back, out_parts, pre_parts, agg_parts = call(
        functools.partial(entity_kernel, n, m, width, ents),
        (shape((n * m, rows_each, LANES), BF), by_feat, by_feat, shape((m * rows_each, LANES), BF)),
        [pltpu.VMEM((m, rows_each, LANES), BF), pltpu.VMEM((ents, LANES), F32)],
        6 * rows_each * width * width,
        "entity",
    )(sums, asked, *all_blocks)
    scaled = lax.all_to_all(back, ("fact", "feat"), 0, 0).reshape(n * ents, LANES)
    shares = call(
        functools.partial(share_kernel, m),
        tuple(shape(((2 + m) * rows_each, LANES), BF) for _ in range(m)),
        [],
        1 << 20,
        "share",
    )(out_parts, pre_parts, agg_parts)
    got = [shares[0]] + [swap(shares[j], j) for j in range(1, m)]
    pos, entity, asked, _ = tie((pos, entity, asked, back))
    plow, phigh, elow, ehigh = call(
        codes_kernel,
        (shape((LANES, facts), BF), shape((16, facts), BF), columns, columns),
        [],
        1 << 26,
        "codes",
    )(pos, entity)
    rlow, rhigh = call(
        functools.partial(request_kernel, n, cap),
        (shape((LANES, slots), BF), shape((16, slots), BF)),
        [],
        1 << 26,
        "requests",
        limit,
    )(asked)
    pair_shape = (n // 2, 2 * stride, LANES)
    output_h, pair = call(
        functools.partial(weight_kernel, n, m, width, stride),
        (shape((ents, LANES), BF), shape((2, *pair_shape), F32)),
        [pltpu.VMEM((width, LANES), F32), pltpu.VMEM((ents, LANES), BF), pltpu.VMEM((m, ents, LANES), BF)],
        4 * ents * width * LANES,
        "weight",
    )(hidden, *got)
    if ringed:
        keep, give = call(halves_kernel, (shape(pair_shape, F32), shape(pair_shape, BF)), [], 1 << 20, "halves")(pair)
        pairs = [keep, lax.ppermute(give, "fact", [(i, i ^ 1) for i in range(n)])]
    else:
        pairs = [jnp.stack([pair[0], pair[1]], axis=1).reshape(n, 2 * stride, LANES)]
    d_msg, msg_share = call(
        functools.partial(backward_kernel, n, stride),
        (columns, shape((n, stride, LANES), BF)),
        [pltpu.VMEM((step, n * ents), BF), pltpu.VMEM((facts, LANES), F32), pltpu.SemaphoreType.DMA],
        2 * facts * (n * ents + width) * LANES,
        "backward",
        limit,
        in_specs=[pl.BlockSpec(memory_space=pl.ANY)] + [pl.BlockSpec(memory_space=pltpu.VMEM)] * 4,
    )(slope, scaled, elow, ehigh, x_turned)

    def spread(offsets):
        lengths = [cap + (3 if ringed and k % 2 == 0 else 1) * stride for k in offsets]
        return call(
            functools.partial(spread_kernel, n, cap, stride, offsets),
            tuple(shape((rows, LANES), BF) for rows in lengths),
            [],
            2 * facts * cap * LANES * len(offsets),
            "spread",
            limit,
        )(plow, phigh, d_msg, msg_share, *(pairs if ringed else ()))

    def add_up(offsets, got, base, final):
        weight = shape((3 * stride, LANES), F32)
        scratch = [
            pltpu.VMEM((cap * len(got), LANES), BF),
            pltpu.VMEM((LANES, cap * len(got)), BF),
            pltpu.VMEM((16, cap * len(got)), BF),
        ]
        return call(
            functools.partial(table_kernel, n, cap, stride, offsets, base is None, final),
            (shape((dims, LANES), F32),) + ((shape((own, LANES), F32),) * 3 if final else (weight,)),
            scratch + ([pltpu.VMEM(weight.shape, F32)] if final else []),
            2 * cap * dims * LANES * len(got),
            "table",
            limit,
        )(rlow, rhigh, *got, *(base or ()))

    totals = None
    if ringed:
        messages = {}
        rest = [[k, n - k] for k in range(n // 2 - 1, 1, -1)]
        for offsets in [rest[0], [n // 2], [1, n - 1], *rest[1:]]:
            for offset, message in zip(offsets, spread(offsets)):
                messages[offset] = lax.ppermute(message, "fact", [(i, (i + offset) % n) for i in range(n)])
        messages[0] = spread([0])[0]
        for offsets in [[0, 1, n - 1], [n // 2], *rest[::-1]]:
            totals = add_up(offsets, [messages[k] for k in offsets], totals, offsets == rest[0])
        grad_dim, grad_msg, grad_self, grad_neigh = totals
    else:
        fact_me = lax.axis_index("fact")
        sent = [message for k in range(0, n, 8) for message in spread(list(range(k, k + 8)))]
        by_owner = jnp.take(jnp.stack(sent), lax.rem(jnp.arange(n) - fact_me + n, n), axis=0)
        owned = lax.all_to_all(by_owner, "fact", 0, 0)
        by_offset = jnp.take(owned, lax.rem(fact_me - jnp.arange(n) + n, n), axis=0)
        for k in range(0, n, 8):
            totals = add_up(list(range(k, k + 8)), [by_offset[k + i] for i in range(8)], totals, k + 8 >= n)
        grad_dim, grad_msg, _, _ = totals
        pair_sum = lax.psum_scatter(pairs[0], "fact", scatter_dimension=0, tiled=True)[0]
        grad_self, grad_neigh = pair_sum[0:own], pair_sum[stride : stride + own]
    return output_h, grad_msg, grad_self, grad_neigh, grad_dim


def solution(mesh):
    placed = (
        P("fact", "feat"),
        P("fact", None),
        P("fact"),
        P("fact", None),
        P("fact"),
        P("fact", "feat"),
        P("fact", "feat"),
        P(None, "feat"),
        P(None, "feat"),
        P(None, "feat"),
        P("fact", "feat"),
    )
    return jax.shard_map(
        shards,
        mesh=mesh,
        in_specs=placed,
        out_specs=(P("fact", "feat"),) * 5,
        check_vma=False,
    )
```

```python
import functools

import jax
import jax.numpy as jnp
from jax import lax
from jax.experimental import pallas as pl
from jax.experimental.pallas import tpu as pltpu
from jax.sharding import PartitionSpec as P

LANES = 128
BF = jnp.bfloat16
IN_HBM = pl.BlockSpec(memory_space=pltpu.HBM)
IN_VMEM = pl.BlockSpec(memory_space=pltpu.VMEM)
F32 = jnp.float32
VMEM_LIMIT = 16 * 1024 * 1024
VMEM_LIMIT_LARGE = 40 * 1024 * 1024


def call(kernel, out_shape, scratch, flops, name, limit=VMEM_LIMIT, **specs):
    return pl.pallas_call(
        kernel,
        out_shape=out_shape,
        scratch_shapes=scratch,
        compiler_params=pltpu.CompilerParams(vmem_limit_bytes=limit),
        cost_estimate=pl.CostEstimate(flops=flops, bytes_accessed=1 << 20, transcendentals=0),
        name=name,
        **specs,
    )


def shape(dims, dtype):
    return jax.ShapeDtypeStruct(dims, dtype)


def nt(a, b):
    return lax.dot_general(a, b, (((1,), (1,)), ((), ())), preferred_element_type=F32)


def tn(a, b):
    return lax.dot_general(a, b, (((0,), (0,)), ((), ())), preferred_element_type=F32)


def dot(a, b):
    return jnp.dot(a, b, preferred_element_type=F32)


def flag(condition):
    return jnp.where(condition, 1.0, 0.0).astype(BF)


def column_codes(row):
    keys = jnp.broadcast_to(row, (LANES, LANES)).astype(F32).T.astype(jnp.int32)
    lane = lax.broadcasted_iota(jnp.int32, (LANES, LANES), 1)
    return flag((keys & (LANES - 1)) == lane), (keys >> 7).astype(F32).astype(BF)


def row_codes(row):
    keys = jnp.broadcast_to(row, (LANES, LANES))
    sub = lax.broadcasted_iota(jnp.int32, (LANES, LANES), 0)
    high = jnp.broadcast_to((row >> 7).astype(F32), (16, LANES)).astype(BF)
    return flag((keys & (LANES - 1)) == sub), high


def pick_block(low, high, block):
    zero = jnp.zeros((), BF)
    return jnp.where(high == block, low, zero)


def pick_rows(low, high, block):
    wide = low.reshape(LANES // 16, 16, low.shape[1])
    picked = pick_block(wide, high[None], block)
    return picked.reshape(low.shape)


def route_kernel(n, cap, ents, dims, *refs):
    given, (out_ref, pos_ref, ent_ref, dlow_ref, dhigh_ref), held_refs, sems = refs[:4], refs[4:9], refs[9:13], refs[13]
    copies = [pltpu.make_async_copy(src, dst, sems.at[i]) for i, (src, dst) in enumerate(zip(given, held_refs))]
    for copy in copies:
        copy.start()
    for copy in copies:
        copy.wait()
    do_ref, ds_ref, fo_ref, fs_ref = held_refs
    chunks = do_ref.shape[0]
    owner = do_ref[...]
    kind = lax.broadcasted_iota(jnp.int32, (n, chunks, LANES), 0)
    held = jnp.where(kind == owner[None], 1.0, 0.0).reshape(n * chunks, LANES)
    held_bf = held.astype(BF)
    i0 = lax.broadcasted_iota(jnp.int32, (LANES, LANES), 0)
    i1 = lax.broadcasted_iota(jnp.int32, (LANES, LANES), 1)
    inside = dot(held_bf, flag(i0 < i1))
    r0 = lax.broadcasted_iota(jnp.int32, (n * chunks, n * chunks), 0)
    r1 = lax.broadcasted_iota(jnp.int32, (n * chunks, n * chunks), 1)
    earlier = flag((r0 // chunks == r1 // chunks) & (r1 < r0))
    before = dot(dot(earlier, held_bf).astype(BF), jnp.ones((LANES, LANES), BF))
    rank = jnp.sum((held * (inside + before)).reshape(n, chunks, LANES), axis=0)
    rank = rank.astype(jnp.int32)
    entity_owner = fo_ref[...]
    entity_slot = fs_ref[...]
    value = ds_ref[...]
    pos_ref[...] = owner * cap + rank
    ent_ref[...] = entity_owner * ents + entity_slot
    fact_dim = owner * dims + value
    high = (value >> 5).astype(F32)
    low = (value & 31).astype(F32)
    names = lax.broadcasted_iota(jnp.int32, (n, LANES), 0)
    places = lax.broadcasted_iota(jnp.int32, (cap, LANES), 0)
    slots = lax.broadcasted_iota(jnp.int32, (ents, LANES), 0)
    asked_high = jnp.zeros((n, cap), F32)
    asked_low = jnp.zeros((n, cap), F32)
    hits = jnp.zeros((n, ents), F32)
    for k in range(chunks):
        here = slice(k * LANES, (k + 1) * LANES)
        mine = jnp.where(names == owner[k : k + 1], 1.0, 0.0)
        at = flag(places == rank[k : k + 1])
        asked_high += nt((mine * high[k : k + 1]).astype(BF), at)
        asked_low += nt((mine * low[k : k + 1]).astype(BF), at)
        hits += nt(flag(names == entity_owner[k : k + 1]), flag(slots == entity_slot[k : k + 1]))
        dlow_ref[here, :], dhigh_ref[here, :] = column_codes(fact_dim[k : k + 1])
    asked = (asked_high * 32.0 + asked_low).astype(jnp.int32)
    for r in range(cap // LANES):
        out_ref[:, r, :] = asked[:, r * LANES : (r + 1) * LANES]
    out_ref[:, cap // LANES, :] = hits.astype(jnp.int32)


def gather_rows(low_ref, high_ref, rows, table_refs, firsts, hot_ref):
    at = 0
    low, high = low_ref[rows, :], high_ref[rows, :]
    for table, first in zip(table_refs, firsts):
        for k in range(table.shape[0] // LANES):
            hot_ref[:, at : at + LANES] = pick_block(low, high, (first + k).astype(F32).astype(BF))
            at += LANES
    total, at = None, 0
    for table in table_refs:
        part = dot(hot_ref[:, at : at + table.shape[0]], table[...])
        total = part if total is None else total + part
        at += table.shape[0]
    return total


def ring_at(place, n):
    place = lax.rem(place + 2 * n, n)
    return jnp.where(place < n // 2, 2 * place, 2 * (n - 1 - place) + 1)


def ring_place(index, n):
    half = lax.div(index, 2)
    return jnp.where(lax.rem(index, 2) == 0, half, n - 1 - half)


def look_kernel(n, pieces, low_ref, high_ref, *refs):
    count = len(pieces)
    tables, base_ref, out_ref, hot_ref = refs[:count], refs[count], refs[-2], refs[-1]
    facts = low_ref.shape[0]
    step = hot_ref.shape[0]
    place = ring_place(lax.axis_index("fact"), n)
    firsts = [lax.div(ring_at(place + hops, n) * dims + row, LANES) for hops, row, dims in pieces]
    for c in range(facts // step):
        rows = slice(c * step, (c + 1) * step)
        out_ref[rows, :] = base_ref[rows, :] + gather_rows(low_ref, high_ref, rows, tables, firsts, hot_ref)


def message_kernel(n, pieces, low_ref, high_ref, *refs):
    count = len(pieces)
    sources, refs = refs[:count], refs[count:]
    base_ref, xw_ref, ent_ref, slope_out, part_ref, slope_ref, hot_ref, msg_ref, erlow_ref, erhigh_ref = refs[:10]
    tables, (sem, table_sem) = refs[10 : 10 + count], refs[10 + count :]
    arrivals = [pltpu.make_async_copy(src, dst, table_sem) for src, dst in zip(sources, tables)]
    for copy in arrivals:
        copy.start()
    facts = low_ref.shape[0]
    step = hot_ref.shape[0]
    place = ring_place(lax.axis_index("fact"), n)
    firsts = [lax.div(ring_at(place + hops, n) * dims + row, LANES) for hops, row, dims in pieces]
    for k in range(ent_ref.shape[0]):
        here = slice(k * LANES, (k + 1) * LANES)
        erlow_ref[:, here], erhigh_ref[:, here] = row_codes(ent_ref[k : k + 1, :])
    for copy in arrivals:
        copy.wait()
    for c in range(facts // step):
        rows = slice(c * step, (c + 1) * step)
        pre = xw_ref[rows, :] + base_ref[rows, :]
        if count:
            pre = pre + gather_rows(low_ref, high_ref, rows, tables, firsts, hot_ref)
        gate = jax.nn.sigmoid(pre)
        msg_ref[rows, :] = (pre * gate).astype(BF)
        slope_ref[rows, :] = gate * (1.0 + pre * (1.0 - gate))
    keep = pltpu.make_async_copy(slope_ref, slope_out, sem)
    keep.start()

    def add(pair, carry):
        hot = jnp.concatenate(
            [pick_rows(erlow_ref[...], erhigh_ref[...], (pair * 2 + i).astype(F32).astype(BF)) for i in range(2)], axis=0
        )
        rows = pl.ds(pl.multiple_of(pair * 256, 256), 256)
        part_ref[rows, :] = dot(hot, msg_ref[...]).astype(BF)
        return carry

    lax.fori_loop(0, part_ref.shape[0] // 256, add, 0)
    keep.wait()


def project_kernel(m, w_ref, *refs):
    blocks, out_ref = refs[:m], refs[m]
    me = lax.axis_index("feat")
    total = None
    for j, ref in enumerate(blocks):
        rows = pl.ds(pl.multiple_of((me ^ j) * LANES, LANES), LANES)
        part = dot(ref[...], w_ref[rows, :])
        total = part if total is None else total + part
    out_ref[...] = total


def ready_kernel(m, width, ents, *refs):
    x_refs, all_refs, (hidden_ref, xt_ref) = refs[:m], refs[m : 2 * m], refs[2 * m :]
    me = lax.axis_index("feat")
    for j in range(m):
        hidden_ref[me ^ j] = all_refs[j][2 * width : 2 * width + ents, :]
        xt_ref[pl.ds(pl.multiple_of((me ^ j) * LANES, LANES), LANES), :] = x_refs[j][...].T


def entity_kernel(n, m, width, ents, sums_ref, idx_ref, *refs):
    all_refs, (back_ref, out_ref, pre_ref, agg_ref, own_ref, hold_ref, words_ref, sem) = refs[:m], refs[m:]
    fetch = pltpu.make_async_copy(idx_ref, words_ref, sem)
    fetch.start()
    rows_each = ents // m
    me = lax.axis_index("feat")
    totals = []
    for b in range(m):
        total = sums_ref[b].astype(F32)
        for f in range(1, n):
            total += sums_ref[f * m + b].astype(F32)
        totals.append(total)
    fetch.wait()
    hits = jnp.sum(words_ref[:, words_ref.shape[1] - 1, :], axis=0, keepdims=True).astype(F32)
    hold_ref[...] = jnp.maximum(jnp.broadcast_to(hits, (LANES, ents)).T, 1.0)
    divisor = hold_ref[pl.ds(pl.multiple_of(me * rows_each, rows_each), rows_each), :]
    for b in range(m):
        agg_ref[b * rows_each : (b + 1) * rows_each, :] = (totals[b] / divisor).astype(BF)
    at = pl.multiple_of(2 * width + me * rows_each, rows_each)
    for j in range(m):
        own_ref[me ^ j] = all_refs[j][pl.ds(at, rows_each), :]
    aggregate = jnp.concatenate([agg_ref[b * rows_each : (b + 1) * rows_each, :] for b in range(m)], axis=1)
    hidden = jnp.concatenate([own_ref[b] for b in range(m)], axis=1)
    d_agg = None
    for j in range(m):
        pre = dot(hidden, all_refs[j][0:width, :]) + dot(aggregate, all_refs[j][width : 2 * width, :])
        gate = jax.nn.sigmoid(pre)
        cot = all_refs[j][pl.ds(at + ents, rows_each), :].astype(F32)
        d_pre = (cot * (gate * (1.0 + pre * (1.0 - gate)))).astype(BF)
        out_ref[me ^ j] = (pre * gate).astype(BF)
        pre_ref[me ^ j] = d_pre
        term = nt(d_pre, all_refs[j][width : 2 * width, :])
        d_agg = term if d_agg is None else d_agg + term
    for b in range(m):
        scaled = (d_agg[:, b * LANES : (b + 1) * LANES] / divisor).astype(BF)
        for f in range(n):
            back_ref[f * m + b] = scaled


def share_kernel(m, out_ref, pre_ref, agg_ref, *share_refs):
    rows_each = out_ref.shape[1]
    me = lax.axis_index("feat")
    for j, ref in enumerate(share_refs):
        ref[0:rows_each, :] = out_ref[me ^ j]
        ref[rows_each : 2 * rows_each, :] = pre_ref[me ^ j]
        ref[2 * rows_each :, :] = agg_ref[...]


def weight_kernel(n, m, width, stride, hidden_ref, *refs):
    got, (out_ref, back_ref, total_ref, pre_ref, agg_ref) = refs[:m], refs[m:]
    rows_each = got[0].shape[0] // (2 + m)
    own = width // n
    me = lax.axis_index("feat")
    for j, ref in enumerate(got):
        here = pl.ds(pl.multiple_of((me ^ j) * rows_each, rows_each), rows_each)
        out_ref[here, :] = ref[0:rows_each, :]
        pre_ref[here, :] = ref[rows_each : 2 * rows_each, :]
        for b in range(m):
            agg_ref[b, here, :] = ref[(2 + b) * rows_each : (3 + b) * rows_each, :]
    d_pre = pre_ref[...]
    for which, blocks in enumerate((hidden_ref, agg_ref)):
        for b in range(m):
            total_ref[b * LANES : (b + 1) * LANES, :] = tn(blocks[b], d_pre)
        for d in range(n):
            back_ref[d % 2, d // 2, which * stride : (which + 1) * stride, :] = padded(
                total_ref[d * own : (d + 1) * own, :], stride
            )


def halves_kernel(back_ref, keep_ref, give_ref):
    odd = lax.rem(lax.axis_index("fact"), 2)
    keep_ref[...] = back_ref[odd]
    give_ref[...] = back_ref[1 - odd].astype(BF)


def padded(piece, rows):
    if piece.shape[0] == rows:
        return piece
    return jnp.concatenate([piece, jnp.zeros((rows - piece.shape[0], LANES), F32)], axis=0)


def codes_kernel(pos_ref, ent_ref, plow_ref, phigh_ref, elow_ref, ehigh_ref):
    for k in range(pos_ref.shape[0]):
        here = slice(k * LANES, (k + 1) * LANES)
        plow_ref[:, here], phigh_ref[:, here] = row_codes(pos_ref[k : k + 1, :])
        elow_ref[here, :], ehigh_ref[here, :] = column_codes(ent_ref[k : k + 1, :])


def request_kernel(n, cap, req_ref, low_ref, high_ref):
    for s in range(n):
        for r in range(cap // LANES):
            at = s * cap + r * LANES
            low_ref[:, at : at + LANES], high_ref[:, at : at + LANES] = row_codes(req_ref[s, r : r + 1, :])


def backward_kernel(n, stride, slope_in, scaled_ref, low_ref, high_ref, xt_ref, dmsg_ref, share_ref, hot_ref, slope_ref, sem):
    fetch = pltpu.make_async_copy(slope_in, slope_ref, sem)
    fetch.start()
    facts = slope_ref.shape[0]
    own = xt_ref.shape[0] // n
    step = hot_ref.shape[0]
    for c in range(facts // step):
        rows = slice(c * step, (c + 1) * step)
        found = gather_rows(low_ref, high_ref, rows, [scaled_ref], [jnp.int32(0)], hot_ref)
        if c == 0:
            fetch.wait()
        dmsg_ref[rows, :] = (found * slope_ref[rows, :]).astype(BF)
    total = dot(xt_ref[...], dmsg_ref[...])
    for d in range(n):
        share_ref[d] = padded(total[d * own : (d + 1) * own, :], stride).astype(BF)


def spread_kernel(n, cap, stride, offsets, plow_ref, phigh_ref, dmsg_ref, share_ref, *refs):
    pair_refs, out_refs = refs[:-len(offsets)], refs[-len(offsets) :]
    me = lax.axis_index("fact")
    for offset, out_ref in zip(offsets, out_refs):
        d = lax.rem(me + offset, n)
        hot = jnp.concatenate(
            [
                pick_rows(plow_ref[...], phigh_ref[...], (d * (cap // LANES) + i).astype(F32).astype(BF))
                for i in range(cap // LANES)
            ],
            axis=0,
        )
        out_ref[0:cap, :] = dot(hot, dmsg_ref[...]).astype(BF)
        out_ref[cap : cap + stride, :] = share_ref[d]
        if out_ref.shape[0] > cap + stride:
            pair = pair_refs[0][lax.div(d, 2)]
            for ref in pair_refs[1:]:
                pair = pair + ref[lax.div(d, 2)].astype(F32)
            out_ref[cap + stride :, :] = pair.astype(BF)


def table_kernel(n, cap, stride, offsets, first, final, low_ref, high_ref, *refs):
    count = len(offsets)
    got, refs = refs[:count], refs[count:]
    if not first:
        (base_ref, weight_base_ref), refs = refs[:2], refs[2:]
    out_ref, refs = refs[0], refs[1:]
    final_refs, refs = (refs[:3], refs[3:]) if final else ((), refs[1:] + refs[:1])
    rows_ref, klow_ref, khigh_ref, weight_ref = refs[:4]
    me = lax.axis_index("fact")
    if first:
        weight_ref[...] = jnp.zeros(weight_ref.shape, F32)
    else:
        weight_ref[...] = weight_base_ref[...]
    for j, (offset, ref) in enumerate(zip(offsets, got)):
        source = lax.rem(me + (n - offset), n)
        here = slice(j * cap, (j + 1) * cap)
        there = pl.ds(pl.multiple_of(source * cap, LANES), cap)
        rows_ref[here, :] = ref[0:cap, :]
        klow_ref[:, here] = low_ref[:, there]
        khigh_ref[:, here] = high_ref[:, there]
        rows = ref.shape[0] - cap
        weight_ref[0:rows, :] += ref[cap:, :].astype(F32)
    for which, ref in enumerate(final_refs):
        ref[...] = weight_ref[which * stride : which * stride + ref.shape[0], :]
    blocks = out_ref.shape[0] // LANES
    join = 2 if blocks % 2 == 0 else 1

    target_ref = refs[4] if final else out_ref
    copies = []
    for group in range(blocks // join):
        hot = jnp.concatenate(
            [pick_rows(klow_ref[...], khigh_ref[...], jnp.array(group * join + i, BF)) for i in range(join)], axis=0
        )
        rows = slice(group * join * LANES, (group + 1) * join * LANES)
        sums = dot(hot, rows_ref[...])
        target_ref[rows, :] = sums if first else base_ref[rows, :] + sums
        if final:
            copies.append(pltpu.make_async_copy(target_ref.at[rows, :], out_ref.at[rows, :], refs[5].at[group]))
            copies[-1].start()
    for copy in copies:
        copy.wait()


def shards(fact_x, dim_owner, dim_slot, fact_owner, fact_slot, dim_table, entity_h, w_msg, w_self, w_neigh, cotangent):
    n, m = lax.axis_size("fact"), lax.axis_size("feat")
    assert m == 4 and n % 2 == 0
    facts = fact_x.shape[0]
    chunks = facts // LANES
    ents = entity_h.shape[0]
    rows_each = ents // m
    width = w_msg.shape[0]
    dims = dim_table.shape[0]
    cap = -(-(3 * facts // n) // LANES) * LANES
    slots = n * cap
    groups = cap // LANES + 1
    own = width // n
    stride = max(16, own)
    step = 512
    tie = lax.optimization_barrier
    ringed = n <= 8
    limit = VMEM_LIMIT if ringed else VMEM_LIMIT_LARGE

    ring = [2 * p if p < n // 2 else 2 * (n - 1 - p) + 1 for p in range(n)]
    to_right = [(ring[p], ring[(p + 1) % n]) for p in range(n)]
    to_left = [(ring[(p + 1) % n], ring[p]) for p in range(n)]

    def pass_on(right, left):
        return lax.ppermute(right, "fact", to_right), lax.ppermute(left, "fact", to_left)

    def swap(block, bit):
        return lax.ppermute(block, "feat", [(i, i ^ bit) for i in range(m)])

    if ringed:
        right, left = pass_on(dim_table, dim_table)
    by_lane = (chunks, LANES)
    columns = shape((facts, LANES), BF)
    asks, pos, entity, dlow, dhigh = call(
        functools.partial(route_kernel, n, cap, ents, dims),
        (
            shape((n, groups, LANES), jnp.int32),
            shape(by_lane, jnp.int32),
            shape(by_lane, jnp.int32),
            columns,
            columns,
        ),
        [pltpu.VMEM(by_lane, jnp.int32)] * 4 + [pltpu.SemaphoreType.DMA((4,))],
        1 << 28,
        "route",
        in_specs=[IN_HBM] * 4,
    )(dim_owner.reshape(by_lane), dim_slot.reshape(by_lane), fact_owner.reshape(by_lane), fact_slot.reshape(by_lane))
    if ringed:
        asked = lax.all_to_all(asks, "fact", 0, 0)
        right, left, asked, pos, entity, dlow, dhigh = tie((right, left, asked, pos, entity, dlow, dhigh))

    def look(pieces, tables, base):
        rows = sum(t.shape[0] for t in tables)
        return call(
            functools.partial(look_kernel, n, pieces),
            shape((facts, LANES), F32),
            [pltpu.VMEM((step, rows), BF)],
            2 * facts * rows * LANES,
            "look",
            limit,
        )(dlow, dhigh, *tables, base)

    def project(blocks):
        return call(
            functools.partial(project_kernel, m), shape((facts, LANES), F32), [], 2 * facts * width * LANES, "project"
        )(w_msg, *blocks)

    found = jnp.zeros((facts, LANES), F32)
    weights = jnp.concatenate([w_self, w_neigh, entity_h, cotangent], axis=0)
    if ringed:
        near = (right, left)
        after = pass_on(*near)
        x_far, x_near = swap(fact_x, 2), swap(fact_x, 1)
        found = look([(0, 0, dims), (-1, 0, dims), (1, 0, dims)], [dim_table, *near], found)
        right, left, x_far, x_near, found, weights = tie((*after, x_far, x_near, found, weights))
        for k in range(2, n // 2 - 1):
            after = pass_on(right, left)
            x_last = swap(x_far, 1)
            found = look([(-k, 0, dims), (k, 0, dims)], [right, left], found)
            right, left, found, x_last = tie((*after, found, x_last))
        all_far = swap(weights, 2)
        k = n // 2 - 1
        after = lax.ppermute(right, "fact", to_right)
        xw = project([fact_x, x_near, x_far, x_last])
        found = look([(-k, 0, dims), (k, 0, dims)], [right, left], found)
        all_near = swap(weights, 1)
        found, all_far, all_near = tie((found, all_far, all_near))
        last, last_pieces = [after], [(n // 2, 0, dims)]
    else:
        asked = lax.all_to_all(asks, "fact", 0, 0)
        x_far, x_near = swap(fact_x, 2), swap(fact_x, 1)
        x_last = swap(x_far, 1)
        xw = project([fact_x, x_near, x_far, x_last])
        all_far, all_near = swap(weights, 2), swap(weights, 1)
        whole = lax.all_gather(dim_table, "fact")
        order = jnp.take(whole, ring_at(ring_place(lax.axis_index("fact"), n) + jnp.arange(n), n), axis=0)
        for k in range(0, n, 8):
            found = look([(k + i, 0, dims) for i in range(8)], [order[k + i] for i in range(8)], found)
        last, last_pieces = [], []
    all_last = swap(all_far, 1)
    x_blocks, all_blocks = [fact_x, x_near, x_far, x_last], [weights, all_near, all_far, all_last]
    last_rows = max(LANES, sum(t.shape[0] for t in last))
    slope, part = call(
        functools.partial(message_kernel, n, last_pieces),
        (shape((facts, LANES), F32), shape((n * ents, LANES), BF)),
        [
            pltpu.VMEM((facts, LANES), F32),
            pltpu.VMEM((step, last_rows), BF),
            pltpu.VMEM((facts, LANES), BF),
            pltpu.VMEM((LANES, facts), BF),
            pltpu.VMEM((16, facts), BF),
            *[pltpu.VMEM(t.shape, BF) for t in last],
            pltpu.SemaphoreType.DMA,
            pltpu.SemaphoreType.DMA,
        ],
        2 * facts * (last_rows + n * ents) * LANES,
        "message",
        limit,
        in_specs=[IN_VMEM] * 2 + [pl.BlockSpec(memory_space=pl.ANY)] * len(last) + [IN_VMEM] * 3,
        out_specs=(IN_HBM, IN_VMEM),
    )(dlow, dhigh, *last, found, xw, entity)
    sums = lax.all_to_all(part.reshape(n * m, rows_each, LANES), ("fact", "feat"), 0, 0)
    pos, entity, x_blocks, _ = tie((pos, entity, x_blocks, part))
    hidden, x_turned = call(
        functools.partial(ready_kernel, m, width, ents),
        (shape((m, ents, LANES), BF), shape((width, facts), BF)),
        [],
        1 << 28,
        "ready",
    )(*x_blocks, *all_blocks)
    by_feat = shape((m, rows_each, LANES), BF)
    back, out_parts, pre_parts, agg_parts = call(
        functools.partial(entity_kernel, n, m, width, ents),
        (shape((n * m, rows_each, LANES), BF), by_feat, by_feat, shape((m * rows_each, LANES), BF)),
        [
            pltpu.VMEM((m, rows_each, LANES), BF),
            pltpu.VMEM((ents, LANES), F32),
            pltpu.VMEM(asked.shape, jnp.int32),
            pltpu.SemaphoreType.DMA,
        ],
        6 * rows_each * width * width,
        "entity",
        in_specs=[IN_VMEM, pl.BlockSpec(memory_space=pl.ANY)] + [IN_VMEM] * m,
    )(sums, asked, *all_blocks)
    scaled = lax.all_to_all(back, ("fact", "feat"), 0, 0).reshape(n * ents, LANES)
    shares = call(
        functools.partial(share_kernel, m),
        tuple(shape(((2 + m) * rows_each, LANES), BF) for _ in range(m)),
        [],
        1 << 20,
        "share",
    )(out_parts, pre_parts, agg_parts)
    got = [shares[0]] + [swap(shares[j], j) for j in range(1, m)]
    pos, entity, asked, _ = tie((pos, entity, asked, back))
    plow, phigh, elow, ehigh = call(
        codes_kernel,
        (shape((LANES, facts), BF), shape((16, facts), BF), columns, columns),
        [],
        1 << 26,
        "codes",
    )(pos, entity)
    rlow, rhigh = call(
        functools.partial(request_kernel, n, cap),
        (shape((LANES, slots), BF), shape((16, slots), BF)),
        [],
        1 << 26,
        "requests",
        limit,
    )(asked)
    pair_shape = (n // 2, 2 * stride, LANES)
    output_h, pair = call(
        functools.partial(weight_kernel, n, m, width, stride),
        (shape((ents, LANES), BF), shape((2, *pair_shape), F32)),
        [pltpu.VMEM((width, LANES), F32), pltpu.VMEM((ents, LANES), BF), pltpu.VMEM((m, ents, LANES), BF)],
        4 * ents * width * LANES,
        "weight",
    )(hidden, *got)
    if ringed:
        keep, give = call(halves_kernel, (shape(pair_shape, F32), shape(pair_shape, BF)), [], 1 << 20, "halves")(pair)
        pairs = [keep, lax.ppermute(give, "fact", [(i, i ^ 1) for i in range(n)])]
    else:
        pairs = [jnp.stack([pair[0], pair[1]], axis=1).reshape(n, 2 * stride, LANES)]
    d_msg, msg_share = call(
        functools.partial(backward_kernel, n, stride),
        (columns, shape((n, stride, LANES), BF)),
        [pltpu.VMEM((step, n * ents), BF), pltpu.VMEM((facts, LANES), F32), pltpu.SemaphoreType.DMA],
        2 * facts * (n * ents + width) * LANES,
        "backward",
        limit,
        in_specs=[IN_HBM] + [IN_VMEM] * 4,
    )(slope, scaled, elow, ehigh, x_turned)

    def spread(offsets):
        lengths = [cap + (3 if ringed and k % 2 == 0 else 1) * stride for k in offsets]
        return call(
            functools.partial(spread_kernel, n, cap, stride, offsets),
            tuple(shape((rows, LANES), BF) for rows in lengths),
            [],
            2 * facts * cap * LANES * len(offsets),
            "spread",
            limit,
        )(plow, phigh, d_msg, msg_share, *(pairs if max(lengths) > cap + stride else ()))

    def add_up(offsets, got, base, final):
        weight = shape((3 * stride, LANES), F32)
        scratch = [
            pltpu.VMEM((cap * len(got), LANES), BF),
            pltpu.VMEM((LANES, cap * len(got)), BF),
            pltpu.VMEM((16, cap * len(got)), BF),
        ]
        return call(
            functools.partial(table_kernel, n, cap, stride, offsets, base is None, final),
            (shape((dims, LANES), F32),) + ((shape((own, LANES), F32),) * 3 if final else (weight,)),
            scratch
            + (
                [
                    pltpu.VMEM(weight.shape, F32),
                    pltpu.VMEM((dims, LANES), F32),
                    pltpu.SemaphoreType.DMA((dims // LANES,)),
                ]
                if final
                else []
            ),
            2 * cap * dims * LANES * len(got),
            "table",
            limit,
            **(dict(out_specs=(IN_HBM, IN_VMEM, IN_VMEM, IN_VMEM)) if final else {}),
        )(rlow, rhigh, *got, *(base or ()))

    totals = None
    if ringed:
        messages = {}
        rest = [[k, n - k] for k in range(n // 2 - 1, 1, -1)]
        for offsets in [rest[0], [n // 2], [1, n - 1], *rest[1:]]:
            for offset, message in zip(offsets, spread(offsets)):
                messages[offset] = lax.ppermute(message, "fact", [(i, (i + offset) % n) for i in range(n)])
        messages[0] = spread([0])[0]
        for offsets in [[0, 1, n - 1], [n // 2], *rest[::-1]]:
            totals = add_up(offsets, [messages[k] for k in offsets], totals, offsets == rest[0])
        grad_dim, grad_msg, grad_self, grad_neigh = totals
    else:
        fact_me = lax.axis_index("fact")
        sent = [message for k in range(0, n, 8) for message in spread(list(range(k, k + 8)))]
        by_owner = jnp.take(jnp.stack(sent), lax.rem(jnp.arange(n) - fact_me + n, n), axis=0)
        owned = lax.all_to_all(by_owner, "fact", 0, 0)
        by_offset = jnp.take(owned, lax.rem(fact_me - jnp.arange(n) + n, n), axis=0)
        for k in range(0, n, 8):
            totals = add_up(list(range(k, k + 8)), [by_offset[k + i] for i in range(8)], totals, k + 8 >= n)
        grad_dim, grad_msg, _, _ = totals
        pair_sum = lax.psum_scatter(pairs[0], "fact", scatter_dimension=0, tiled=True)[0]
        grad_self, grad_neigh = pair_sum[0:own], pair_sum[stride : stride + own]
    return output_h, grad_msg, grad_self, grad_neigh, grad_dim


def solution(mesh):
    placed = (
        P("fact", "feat"),
        P("fact", None),
        P("fact"),
        P("fact", None),
        P("fact"),
        P("fact", "feat"),
        P("fact", "feat"),
        P(None, "feat"),
        P(None, "feat"),
        P(None, "feat"),
        P("fact", "feat"),
    )
    return jax.shard_map(
        shards,
        mesh=mesh,
        in_specs=placed,
        out_specs=(P("fact", "feat"),) * 5,
        check_vma=False,
    )
```

```python
import functools

import jax
import jax.numpy as jnp
from jax import lax
from jax.experimental import pallas as pl
from jax.experimental.pallas import tpu as pltpu
from jax.sharding import PartitionSpec as P

LANES = 128
BF = jnp.bfloat16
IN_HBM = pl.BlockSpec(memory_space=pltpu.HBM)
IN_VMEM = pl.BlockSpec(memory_space=pltpu.VMEM)
F32 = jnp.float32
VMEM_LIMIT = 16 * 1024 * 1024
VMEM_LIMIT_LARGE = 40 * 1024 * 1024


def call(kernel, out_shape, scratch, flops, name, limit=VMEM_LIMIT, **specs):
    return pl.pallas_call(
        kernel,
        out_shape=out_shape,
        scratch_shapes=scratch,
        compiler_params=pltpu.CompilerParams(vmem_limit_bytes=limit),
        cost_estimate=pl.CostEstimate(flops=flops, bytes_accessed=1 << 20, transcendentals=0),
        name=name,
        **specs,
    )


def shape(dims, dtype):
    return jax.ShapeDtypeStruct(dims, dtype)


def nt(a, b):
    return lax.dot_general(a, b, (((1,), (1,)), ((), ())), preferred_element_type=F32)


def tn(a, b):
    return lax.dot_general(a, b, (((0,), (0,)), ((), ())), preferred_element_type=F32)


def dot(a, b):
    return jnp.dot(a, b, preferred_element_type=F32)


def flag(condition):
    return jnp.where(condition, 1.0, 0.0).astype(BF)


def column_codes(row):
    keys = jnp.broadcast_to(row, (LANES, LANES)).astype(F32).T.astype(jnp.int32)
    lane = lax.broadcasted_iota(jnp.int32, (LANES, LANES), 1)
    return flag((keys & (LANES - 1)) == lane), (keys >> 7).astype(F32).astype(BF)


def row_codes(row):
    keys = jnp.broadcast_to(row, (LANES, LANES))
    sub = lax.broadcasted_iota(jnp.int32, (LANES, LANES), 0)
    high = jnp.broadcast_to((row >> 7).astype(F32), (16, LANES)).astype(BF)
    return flag((keys & (LANES - 1)) == sub), high


def pick_block(low, high, block):
    zero = jnp.zeros((), BF)
    return jnp.where(high == block, low, zero)


def pick_rows(low, high, block):
    wide = low.reshape(LANES // 16, 16, low.shape[1])
    picked = pick_block(wide, high[None], block)
    return picked.reshape(low.shape)


def route_kernel(n, cap, ents, dims, *refs):
    given, (out_ref, pos_ref, ent_ref, dlow_ref, dhigh_ref), held_refs, sems = refs[:4], refs[4:9], refs[9:13], refs[13]
    copies = [pltpu.make_async_copy(src, dst, sems.at[i]) for i, (src, dst) in enumerate(zip(given, held_refs))]
    for copy in copies:
        copy.start()
    for copy in copies:
        copy.wait()
    do_ref, ds_ref, fo_ref, fs_ref = held_refs
    chunks = do_ref.shape[0]
    owner = do_ref[...]
    kind = lax.broadcasted_iota(jnp.int32, (n, chunks, LANES), 0)
    held = jnp.where(kind == owner[None], 1.0, 0.0).reshape(n * chunks, LANES)
    held_bf = held.astype(BF)
    i0 = lax.broadcasted_iota(jnp.int32, (LANES, LANES), 0)
    i1 = lax.broadcasted_iota(jnp.int32, (LANES, LANES), 1)
    inside = dot(held_bf, flag(i0 < i1))
    r0 = lax.broadcasted_iota(jnp.int32, (n * chunks, n * chunks), 0)
    r1 = lax.broadcasted_iota(jnp.int32, (n * chunks, n * chunks), 1)
    earlier = flag((r0 // chunks == r1 // chunks) & (r1 < r0))
    before = dot(dot(earlier, held_bf).astype(BF), jnp.ones((LANES, LANES), BF))
    rank = jnp.sum((held * (inside + before)).reshape(n, chunks, LANES), axis=0)
    rank = rank.astype(jnp.int32)
    entity_owner = fo_ref[...]
    entity_slot = fs_ref[...]
    value = ds_ref[...]
    pos_ref[...] = owner * cap + rank
    ent_ref[...] = entity_owner * ents + entity_slot
    fact_dim = owner * dims + value
    high = (value >> 5).astype(F32)
    low = (value & 31).astype(F32)
    names = lax.broadcasted_iota(jnp.int32, (n, LANES), 0)
    places = lax.broadcasted_iota(jnp.int32, (cap, LANES), 0)
    slots = lax.broadcasted_iota(jnp.int32, (ents, LANES), 0)
    asked_high = jnp.zeros((n, cap), F32)
    asked_low = jnp.zeros((n, cap), F32)
    hits = jnp.zeros((n, ents), F32)
    for k in range(chunks):
        here = slice(k * LANES, (k + 1) * LANES)
        mine = jnp.where(names == owner[k : k + 1], 1.0, 0.0)
        at = flag(places == rank[k : k + 1])
        asked_high += nt((mine * high[k : k + 1]).astype(BF), at)
        asked_low += nt((mine * low[k : k + 1]).astype(BF), at)
        hits += nt(flag(names == entity_owner[k : k + 1]), flag(slots == entity_slot[k : k + 1]))
        dlow_ref[here, :], dhigh_ref[here, :] = column_codes(fact_dim[k : k + 1])
    asked = (asked_high * 32.0 + asked_low).astype(jnp.int32)
    for r in range(cap // LANES):
        out_ref[:, r, :] = asked[:, r * LANES : (r + 1) * LANES]
    out_ref[:, cap // LANES, :] = hits.astype(jnp.int32)


def gather_rows(low_ref, high_ref, rows, table_refs, firsts, hot_ref):
    at = 0
    low, high = low_ref[rows, :], high_ref[rows, :]
    for table, first in zip(table_refs, firsts):
        for k in range(table.shape[0] // LANES):
            hot_ref[:, at : at + LANES] = pick_block(low, high, (first + k).astype(F32).astype(BF))
            at += LANES
    total, at = None, 0
    for table in table_refs:
        part = dot(hot_ref[:, at : at + table.shape[0]], table[...])
        total = part if total is None else total + part
        at += table.shape[0]
    return total


def ring_at(place, n):
    place = lax.rem(place + 2 * n, n)
    return jnp.where(place < n // 2, 2 * place, 2 * (n - 1 - place) + 1)


def ring_place(index, n):
    half = lax.div(index, 2)
    return jnp.where(lax.rem(index, 2) == 0, half, n - 1 - half)


def look_kernel(n, pieces, low_ref, high_ref, *refs):
    count = len(pieces)
    tables, base_ref, out_ref, hot_ref = refs[:count], refs[count], refs[-2], refs[-1]
    facts = low_ref.shape[0]
    step = hot_ref.shape[0]
    place = ring_place(lax.axis_index("fact"), n)
    firsts = [lax.div(ring_at(place + hops, n) * dims + row, LANES) for hops, row, dims in pieces]
    for c in range(facts // step):
        rows = slice(c * step, (c + 1) * step)
        out_ref[rows, :] = base_ref[rows, :] + gather_rows(low_ref, high_ref, rows, tables, firsts, hot_ref)


def message_kernel(n, pieces, low_ref, high_ref, *refs):
    count = len(pieces)
    sources, refs = refs[:count], refs[count:]
    base_ref, xw_ref, ent_ref, slope_ref, part_ref, hot_ref, msg_ref, erlow_ref, erhigh_ref = refs[:9]
    tables, table_sem = refs[9 : 9 + count], refs[9 + count]
    arrivals = [
        pltpu.make_async_copy(src, dst, table_sem.at[i]) for i, (src, dst) in enumerate(zip(sources, tables))
    ]
    for copy in arrivals:
        copy.start()
    facts = low_ref.shape[0]
    step = hot_ref.shape[0]
    place = ring_place(lax.axis_index("fact"), n)
    firsts = [lax.div(ring_at(place + hops, n) * dims + row, LANES) for hops, row, dims in pieces]
    for k in range(ent_ref.shape[0]):
        here = slice(k * LANES, (k + 1) * LANES)
        erlow_ref[:, here], erhigh_ref[:, here] = row_codes(ent_ref[k : k + 1, :])
    for copy in arrivals:
        copy.wait()
    for c in range(facts // step):
        rows = slice(c * step, (c + 1) * step)
        pre = xw_ref[rows, :] + base_ref[rows, :]
        if count:
            pre = pre + gather_rows(low_ref, high_ref, rows, tables, firsts, hot_ref)
        gate = jax.nn.sigmoid(pre)
        msg_ref[rows, :] = (pre * gate).astype(BF)
        slope_ref[rows, :] = gate * (1.0 + pre * (1.0 - gate))

    def add(pair, carry):
        hot = jnp.concatenate(
            [pick_rows(erlow_ref[...], erhigh_ref[...], (pair * 2 + i).astype(F32).astype(BF)) for i in range(2)], axis=0
        )
        rows = pl.ds(pl.multiple_of(pair * 256, 256), 256)
        part_ref[rows, :] = dot(hot, msg_ref[...]).astype(BF)
        return carry

    lax.fori_loop(0, part_ref.shape[0] // 256, add, 0)


def project_kernel(m, w_ref, *refs):
    blocks, out_ref = refs[:m], refs[m]
    me = lax.axis_index("feat")
    total = None
    for j, ref in enumerate(blocks):
        rows = pl.ds(pl.multiple_of((me ^ j) * LANES, LANES), LANES)
        part = dot(ref[...], w_ref[rows, :])
        total = part if total is None else total + part
    out_ref[...] = total


def ready_kernel(m, width, ents, *refs):
    x_refs, all_refs, (slope_ref, hidden_ref, xt_ref, out_ref) = refs[:m], refs[m : 2 * m], refs[2 * m :]
    out_ref[...] = slope_ref[...]
    me = lax.axis_index("feat")
    for j in range(m):
        hidden_ref[me ^ j] = all_refs[j][2 * width : 2 * width + ents, :]
        xt_ref[pl.ds(pl.multiple_of((me ^ j) * LANES, LANES), LANES), :] = x_refs[j][...].T


def entity_kernel(n, m, width, ents, sums_ref, idx_ref, *refs):
    all_refs, (back_ref, out_ref, pre_ref, agg_ref, own_ref, hold_ref, words_ref, sem) = refs[:m], refs[m:]
    fetch = pltpu.make_async_copy(idx_ref, words_ref, sem)
    fetch.start()
    rows_each = ents // m
    me = lax.axis_index("feat")
    totals = []
    for b in range(m):
        total = sums_ref[b].astype(F32)
        for f in range(1, n):
            total += sums_ref[f * m + b].astype(F32)
        totals.append(total)
    fetch.wait()
    hits = jnp.sum(words_ref[:, words_ref.shape[1] - 1, :], axis=0, keepdims=True).astype(F32)
    hold_ref[...] = jnp.maximum(jnp.broadcast_to(hits, (LANES, ents)).T, 1.0)
    divisor = hold_ref[pl.ds(pl.multiple_of(me * rows_each, rows_each), rows_each), :]
    for b in range(m):
        agg_ref[b * rows_each : (b + 1) * rows_each, :] = (totals[b] / divisor).astype(BF)
    at = pl.multiple_of(2 * width + me * rows_each, rows_each)
    for j in range(m):
        own_ref[me ^ j] = all_refs[j][pl.ds(at, rows_each), :]
    aggregate = jnp.concatenate([agg_ref[b * rows_each : (b + 1) * rows_each, :] for b in range(m)], axis=1)
    hidden = jnp.concatenate([own_ref[b] for b in range(m)], axis=1)
    d_agg = None
    for j in range(m):
        pre = dot(hidden, all_refs[j][0:width, :]) + dot(aggregate, all_refs[j][width : 2 * width, :])
        gate = jax.nn.sigmoid(pre)
        cot = all_refs[j][pl.ds(at + ents, rows_each), :].astype(F32)
        d_pre = (cot * (gate * (1.0 + pre * (1.0 - gate)))).astype(BF)
        out_ref[me ^ j] = (pre * gate).astype(BF)
        pre_ref[me ^ j] = d_pre
        term = nt(d_pre, all_refs[j][width : 2 * width, :])
        d_agg = term if d_agg is None else d_agg + term
    for b in range(m):
        scaled = (d_agg[:, b * LANES : (b + 1) * LANES] / divisor).astype(BF)
        for f in range(n):
            back_ref[f * m + b] = scaled


def share_kernel(m, out_ref, pre_ref, agg_ref, *share_refs):
    rows_each = out_ref.shape[1]
    me = lax.axis_index("feat")
    for j, ref in enumerate(share_refs):
        ref[0:rows_each, :] = out_ref[me ^ j]
        ref[rows_each : 2 * rows_each, :] = pre_ref[me ^ j]
        ref[2 * rows_each :, :] = agg_ref[...]


def weight_kernel(n, m, width, stride, hidden_ref, *refs):
    got, (out_ref, back_ref, total_ref, pre_ref, agg_ref) = refs[:m], refs[m:]
    rows_each = got[0].shape[0] // (2 + m)
    own = width // n
    me = lax.axis_index("feat")
    for j, ref in enumerate(got):
        here = pl.ds(pl.multiple_of((me ^ j) * rows_each, rows_each), rows_each)
        out_ref[here, :] = ref[0:rows_each, :]
        pre_ref[here, :] = ref[rows_each : 2 * rows_each, :]
        for b in range(m):
            agg_ref[b, here, :] = ref[(2 + b) * rows_each : (3 + b) * rows_each, :]
    d_pre = pre_ref[...]
    for which, blocks in enumerate((hidden_ref, agg_ref)):
        for b in range(m):
            total_ref[b * LANES : (b + 1) * LANES, :] = tn(blocks[b], d_pre)
        for d in range(n):
            back_ref[d % 2, d // 2, which * stride : (which + 1) * stride, :] = padded(
                total_ref[d * own : (d + 1) * own, :], stride
            )


def halves_kernel(back_ref, keep_ref, give_ref):
    odd = lax.rem(lax.axis_index("fact"), 2)
    keep_ref[...] = back_ref[odd]
    give_ref[...] = back_ref[1 - odd].astype(BF)


def padded(piece, rows):
    if piece.shape[0] == rows:
        return piece
    return jnp.concatenate([piece, jnp.zeros((rows - piece.shape[0], LANES), F32)], axis=0)


def codes_kernel(pos_ref, ent_ref, plow_ref, phigh_ref, elow_ref, ehigh_ref):
    for k in range(pos_ref.shape[0]):
        here = slice(k * LANES, (k + 1) * LANES)
        plow_ref[:, here], phigh_ref[:, here] = row_codes(pos_ref[k : k + 1, :])
        elow_ref[here, :], ehigh_ref[here, :] = column_codes(ent_ref[k : k + 1, :])


def request_kernel(n, cap, req_ref, low_ref, high_ref):
    for s in range(n):
        for r in range(cap // LANES):
            at = s * cap + r * LANES
            low_ref[:, at : at + LANES], high_ref[:, at : at + LANES] = row_codes(req_ref[s, r : r + 1, :])


def backward_kernel(n, stride, slope_in, scaled_ref, low_ref, high_ref, xt_ref, dmsg_ref, share_ref, hot_ref, slope_ref, sem):
    fetch = pltpu.make_async_copy(slope_in, slope_ref, sem)
    fetch.start()
    facts = slope_ref.shape[0]
    own = xt_ref.shape[0] // n
    step = hot_ref.shape[0]
    for c in range(facts // step):
        rows = slice(c * step, (c + 1) * step)
        found = gather_rows(low_ref, high_ref, rows, [scaled_ref], [jnp.int32(0)], hot_ref)
        if c == 0:
            fetch.wait()
        dmsg_ref[rows, :] = (found * slope_ref[rows, :]).astype(BF)
    total = dot(xt_ref[...], dmsg_ref[...])
    for d in range(n):
        share_ref[d] = padded(total[d * own : (d + 1) * own, :], stride).astype(BF)


def spread_kernel(n, cap, stride, offsets, plow_ref, phigh_ref, dmsg_ref, share_ref, *refs):
    pair_refs, out_refs = refs[:-len(offsets)], refs[-len(offsets) :]
    me = lax.axis_index("fact")
    for offset, out_ref in zip(offsets, out_refs):
        d = lax.rem(me + offset, n)
        hot = jnp.concatenate(
            [
                pick_rows(plow_ref[...], phigh_ref[...], (d * (cap // LANES) + i).astype(F32).astype(BF))
                for i in range(cap // LANES)
            ],
            axis=0,
        )
        out_ref[0:cap, :] = dot(hot, dmsg_ref[...]).astype(BF)
        out_ref[cap : cap + stride, :] = share_ref[d]
        if out_ref.shape[0] > cap + stride:
            pair = pair_refs[0][lax.div(d, 2)]
            for ref in pair_refs[1:]:
                pair = pair + ref[lax.div(d, 2)].astype(F32)
            out_ref[cap + stride :, :] = pair.astype(BF)


def table_kernel(n, cap, stride, offsets, first, final, low_ref, high_ref, *refs):
    count = len(offsets)
    got, refs = refs[:count], refs[count:]
    if not first:
        (base_ref, weight_base_ref), refs = refs[:2], refs[2:]
    out_ref, refs = refs[0], refs[1:]
    final_refs, refs = (refs[:3], refs[3:]) if final else ((), refs[1:] + refs[:1])
    rows_ref, klow_ref, khigh_ref, weight_ref = refs[:4]
    me = lax.axis_index("fact")
    if first:
        weight_ref[...] = jnp.zeros(weight_ref.shape, F32)
    else:
        weight_ref[...] = weight_base_ref[...]
    for j, (offset, ref) in enumerate(zip(offsets, got)):
        source = lax.rem(me + (n - offset), n)
        here = slice(j * cap, (j + 1) * cap)
        there = pl.ds(pl.multiple_of(source * cap, LANES), cap)
        rows_ref[here, :] = ref[0:cap, :]
        klow_ref[:, here] = low_ref[:, there]
        khigh_ref[:, here] = high_ref[:, there]
        rows = ref.shape[0] - cap
        weight_ref[0:rows, :] += ref[cap:, :].astype(F32)
    copies = []
    for which, ref in enumerate(final_refs):
        copies.append(
            pltpu.make_async_copy(
                weight_ref.at[which * stride : which * stride + ref.shape[0], :], ref, refs[6].at[which]
            )
        )
        copies[-1].start()
    blocks = out_ref.shape[0] // LANES
    join = 2 if blocks % 2 == 0 else 1

    target_ref = refs[4] if final else out_ref
    for group in range(blocks // join):
        hot = jnp.concatenate(
            [pick_rows(klow_ref[...], khigh_ref[...], jnp.array(group * join + i, BF)) for i in range(join)], axis=0
        )
        rows = slice(group * join * LANES, (group + 1) * join * LANES)
        sums = dot(hot, rows_ref[...])
        target_ref[rows, :] = sums if first else base_ref[rows, :] + sums
        if final:
            copies.append(pltpu.make_async_copy(target_ref.at[rows, :], out_ref.at[rows, :], refs[5].at[group]))
            copies[-1].start()
    for copy in copies:
        copy.wait()


def shards(fact_x, dim_owner, dim_slot, fact_owner, fact_slot, dim_table, entity_h, w_msg, w_self, w_neigh, cotangent):
    n, m = lax.axis_size("fact"), lax.axis_size("feat")
    assert m == 4 and n % 2 == 0
    facts = fact_x.shape[0]
    chunks = facts // LANES
    ents = entity_h.shape[0]
    rows_each = ents // m
    width = w_msg.shape[0]
    dims = dim_table.shape[0]
    cap = -(-(3 * facts // n) // LANES) * LANES
    slots = n * cap
    groups = cap // LANES + 1
    own = width // n
    stride = max(16, own)
    step = 512
    tie = lax.optimization_barrier
    ringed = n <= 8
    limit = VMEM_LIMIT if ringed else VMEM_LIMIT_LARGE

    ring = [2 * p if p < n // 2 else 2 * (n - 1 - p) + 1 for p in range(n)]
    to_right = [(ring[p], ring[(p + 1) % n]) for p in range(n)]
    to_left = [(ring[(p + 1) % n], ring[p]) for p in range(n)]

    def pass_on(right, left):
        return lax.ppermute(right, "fact", to_right), lax.ppermute(left, "fact", to_left)

    def swap(block, bit):
        return lax.ppermute(block, "feat", [(i, i ^ bit) for i in range(m)])

    half = dims // 2
    if ringed:
        tops = pass_on(dim_table[:half], dim_table[:half])
        bottoms = pass_on(dim_table[half:], dim_table[half:])
        x_far = swap(fact_x, 2)
    by_lane = (chunks, LANES)
    columns = shape((facts, LANES), BF)
    asks, pos, entity, dlow, dhigh = call(
        functools.partial(route_kernel, n, cap, ents, dims),
        (
            shape((n, groups, LANES), jnp.int32),
            shape(by_lane, jnp.int32),
            shape(by_lane, jnp.int32),
            columns,
            columns,
        ),
        [pltpu.VMEM(by_lane, jnp.int32)] * 4 + [pltpu.SemaphoreType.DMA((4,))],
        1 << 28,
        "route",
        in_specs=[IN_HBM] * 4,
    )(dim_owner.reshape(by_lane), dim_slot.reshape(by_lane), fact_owner.reshape(by_lane), fact_slot.reshape(by_lane))
    if ringed:
        bottoms, x_far, asks, pos, entity, dlow, dhigh = tie((bottoms, x_far, asks, pos, entity, dlow, dhigh))

    def look(pieces, tables, base):
        rows = sum(t.shape[0] for t in tables)
        return call(
            functools.partial(look_kernel, n, pieces),
            shape((facts, LANES), F32),
            [pltpu.VMEM((step, rows), BF)],
            2 * facts * rows * LANES,
            "look",
            limit,
        )(dlow, dhigh, *tables, base)

    def project(blocks):
        return call(
            functools.partial(project_kernel, m), shape((facts, LANES), F32), [], 2 * facts * width * LANES, "project"
        )(w_msg, *blocks)

    found = jnp.zeros((facts, LANES), F32)
    weights = jnp.concatenate([w_self, w_neigh, entity_h, cotangent], axis=0)
    if ringed:
        def pieces(k):
            return [(-k, 0, dims), (k, 0, dims), (-k, half, dims), (k, half, dims)]

        for k in range(1, n // 2):
            far = k == n // 2 - 1
            if far:
                next_tops = (lax.ppermute(tops[0], "fact", to_right),)
                next_bottoms = (lax.ppermute(bottoms[1], "fact", to_left),)
                xw = project([fact_x, x_near, x_far, x_last])
            else:
                next_tops, next_bottoms = pass_on(*tops), pass_on(*bottoms)
            if k == 1:
                x_near, x_last = swap(fact_x, 1), swap(x_far, 1)
                found = look([(0, 0, dims)] + pieces(k), [dim_table, *tops, *bottoms], found)
                next_bottoms, x_near, x_last, found, weights = tie((next_bottoms, x_near, x_last, found, weights))
            else:
                found = look(pieces(k), [*tops, *bottoms], found)
                if far:
                    found, asks = tie((found, asks))
                else:
                    all_far = swap(weights, 2)
                    next_bottoms, all_far, found = tie((next_bottoms, all_far, found))
            tops, bottoms = next_tops, next_bottoms
        asked = lax.all_to_all(asks, "fact", 0, 0)
        all_near = swap(weights, 1)
        last = [*tops, *bottoms]
        last_pieces = [(-(n // 2), 0, dims), (n // 2, half, dims)]
    else:
        asked = lax.all_to_all(asks, "fact", 0, 0)
        x_far, x_near = swap(fact_x, 2), swap(fact_x, 1)
        x_last = swap(x_far, 1)
        xw = project([fact_x, x_near, x_far, x_last])
        all_far, all_near = swap(weights, 2), swap(weights, 1)
        whole = lax.all_gather(dim_table, "fact")
        order = jnp.take(whole, ring_at(ring_place(lax.axis_index("fact"), n) + jnp.arange(n), n), axis=0)
        for k in range(0, n, 8):
            found = look([(k + i, 0, dims) for i in range(8)], [order[k + i] for i in range(8)], found)
        last, last_pieces = [], []
    all_last = swap(all_far, 1)
    x_blocks, all_blocks = [fact_x, x_near, x_far, x_last], [weights, all_near, all_far, all_last]
    last_rows = max(LANES, sum(t.shape[0] for t in last))
    slope, part = call(
        functools.partial(message_kernel, n, last_pieces),
        (shape((facts, LANES), F32), shape((n * ents, LANES), BF)),
        [
            pltpu.VMEM((step, last_rows), BF),
            pltpu.VMEM((facts, LANES), BF),
            pltpu.VMEM((LANES, facts), BF),
            pltpu.VMEM((16, facts), BF),
            *[pltpu.VMEM(t.shape, BF) for t in last],
            pltpu.SemaphoreType.DMA((2,)),
        ],
        2 * facts * (last_rows + n * ents) * LANES,
        "message",
        limit,
        in_specs=[IN_VMEM] * 2 + [pl.BlockSpec(memory_space=pl.ANY)] * len(last) + [IN_VMEM] * 3,
    )(dlow, dhigh, *last, found, xw, entity)
    sums = lax.all_to_all(part.reshape(n * m, rows_each, LANES), ("fact", "feat"), 0, 0)
    pos, entity, x_blocks, _ = tie((pos, entity, x_blocks, part))
    hidden, x_turned, slope = call(
        functools.partial(ready_kernel, m, width, ents),
        (shape((m, ents, LANES), BF), shape((width, facts), BF), shape((facts, LANES), F32)),
        [],
        1 << 28,
        "ready",
    )(*x_blocks, *all_blocks, slope)
    asked, slope = tie((asked, slope))
    by_feat = shape((m, rows_each, LANES), BF)
    back, out_parts, pre_parts, agg_parts = call(
        functools.partial(entity_kernel, n, m, width, ents),
        (shape((n * m, rows_each, LANES), BF), by_feat, by_feat, shape((m * rows_each, LANES), BF)),
        [
            pltpu.VMEM((m, rows_each, LANES), BF),
            pltpu.VMEM((ents, LANES), F32),
            pltpu.VMEM(asked.shape, jnp.int32),
            pltpu.SemaphoreType.DMA,
        ],
        6 * rows_each * width * width,
        "entity",
        in_specs=[IN_VMEM, pl.BlockSpec(memory_space=pl.ANY)] + [IN_VMEM] * m,
    )(sums, asked, *all_blocks)
    scaled = lax.all_to_all(back, ("fact", "feat"), 0, 0).reshape(n * ents, LANES)
    shares = call(
        functools.partial(share_kernel, m),
        tuple(shape(((2 + m) * rows_each, LANES), BF) for _ in range(m)),
        [],
        1 << 20,
        "share",
    )(out_parts, pre_parts, agg_parts)
    got = [shares[0]] + [swap(shares[j], j) for j in range(1, m)]
    pos, entity, asked, _ = tie((pos, entity, asked, back))
    plow, phigh, elow, ehigh = call(
        codes_kernel,
        (shape((LANES, facts), BF), shape((16, facts), BF), columns, columns),
        [],
        1 << 26,
        "codes",
    )(pos, entity)
    rlow, rhigh = call(
        functools.partial(request_kernel, n, cap),
        (shape((LANES, slots), BF), shape((16, slots), BF)),
        [],
        1 << 26,
        "requests",
        limit,
    )(asked)
    pair_shape = (n // 2, 2 * stride, LANES)
    output_h, pair = call(
        functools.partial(weight_kernel, n, m, width, stride),
        (shape((ents, LANES), BF), shape((2, *pair_shape), F32)),
        [pltpu.VMEM((width, LANES), F32), pltpu.VMEM((ents, LANES), BF), pltpu.VMEM((m, ents, LANES), BF)],
        4 * ents * width * LANES,
        "weight",
    )(hidden, *got)
    if ringed:
        keep, give = call(halves_kernel, (shape(pair_shape, F32), shape(pair_shape, BF)), [], 1 << 20, "halves")(pair)
        pairs = [keep, lax.ppermute(give, "fact", [(i, i ^ 1) for i in range(n)])]
    else:
        pairs = [jnp.stack([pair[0], pair[1]], axis=1).reshape(n, 2 * stride, LANES)]
    d_msg, msg_share = call(
        functools.partial(backward_kernel, n, stride),
        (columns, shape((n, stride, LANES), BF)),
        [pltpu.VMEM((step, n * ents), BF), pltpu.VMEM((facts, LANES), F32), pltpu.SemaphoreType.DMA],
        2 * facts * (n * ents + width) * LANES,
        "backward",
        limit,
        in_specs=[IN_HBM] + [IN_VMEM] * 4,
    )(slope, scaled, elow, ehigh, x_turned)

    def spread(offsets):
        lengths = [cap + (3 if ringed and k % 2 == 0 else 1) * stride for k in offsets]
        return call(
            functools.partial(spread_kernel, n, cap, stride, offsets),
            tuple(shape((rows, LANES), BF) for rows in lengths),
            [],
            2 * facts * cap * LANES * len(offsets),
            "spread",
            limit,
        )(plow, phigh, d_msg, msg_share, *(pairs if max(lengths) > cap + stride else ()))

    def add_up(offsets, got, base, final):
        weight = shape((3 * stride, LANES), F32)
        scratch = [
            pltpu.VMEM((cap * len(got), LANES), BF),
            pltpu.VMEM((LANES, cap * len(got)), BF),
            pltpu.VMEM((16, cap * len(got)), BF),
        ]
        return call(
            functools.partial(table_kernel, n, cap, stride, offsets, base is None, final),
            (shape((dims, LANES), F32),) + ((shape((own, LANES), F32),) * 3 if final else (weight,)),
            scratch
            + (
                [
                    pltpu.VMEM(weight.shape, F32),
                    pltpu.VMEM((dims, LANES), F32),
                    pltpu.SemaphoreType.DMA((dims // LANES,)),
                    pltpu.SemaphoreType.DMA((3,)),
                ]
                if final
                else []
            ),
            2 * cap * dims * LANES * len(got),
            "table",
            limit,
            **(dict(out_specs=(IN_HBM,) * 4) if final else {}),
        )(rlow, rhigh, *got, *(base or ()))

    totals = None
    if ringed:
        messages = {}
        rest = [[k, n - k] for k in range(n // 2 - 1, 1, -1)]
        for offsets in [rest[0], [n // 2], [1, n - 1], *rest[1:]]:
            for offset, message in zip(offsets, spread(offsets)):
                messages[offset] = lax.ppermute(message, "fact", [(i, (i + offset) % n) for i in range(n)])
        messages[0] = spread([0])[0]
        for offsets in [[0, 1, n - 1], [n // 2], *rest[::-1]]:
            totals = add_up(offsets, [messages[k] for k in offsets], totals, offsets == rest[0])
        grad_dim, grad_msg, grad_self, grad_neigh = totals
    else:
        fact_me = lax.axis_index("fact")
        sent = [message for k in range(0, n, 8) for message in spread(list(range(k, k + 8)))]
        by_owner = jnp.take(jnp.stack(sent), lax.rem(jnp.arange(n) - fact_me + n, n), axis=0)
        owned = lax.all_to_all(by_owner, "fact", 0, 0)
        by_offset = jnp.take(owned, lax.rem(fact_me - jnp.arange(n) + n, n), axis=0)
        for k in range(0, n, 8):
            totals = add_up(list(range(k, k + 8)), [by_offset[k + i] for i in range(8)], totals, k + 8 >= n)
        grad_dim, grad_msg, _, _ = totals
        pair_sum = lax.psum_scatter(pairs[0], "fact", scatter_dimension=0, tiled=True)[0]
        grad_self, grad_neigh = pair_sum[0:own], pair_sum[stride : stride + own]
    return output_h, grad_msg, grad_self, grad_neigh, grad_dim


def solution(mesh):
    placed = (
        P("fact", "feat"),
        P("fact", None),
        P("fact"),
        P("fact", None),
        P("fact"),
        P("fact", "feat"),
        P("fact", "feat"),
        P(None, "feat"),
        P(None, "feat"),
        P(None, "feat"),
        P("fact", "feat"),
    )
    return jax.shard_map(
        shards,
        mesh=mesh,
        in_specs=placed,
        out_specs=(P("fact", "feat"),) * 5,
        check_vma=False,
    )
```

```python
import functools

import jax
import jax.numpy as jnp
from jax import lax
from jax.experimental import pallas as pl
from jax.experimental.pallas import tpu as pltpu
from jax.sharding import PartitionSpec as P

LANES = 128
BF = jnp.bfloat16
IN_HBM = pl.BlockSpec(memory_space=pltpu.HBM)
IN_VMEM = pl.BlockSpec(memory_space=pltpu.VMEM)
F32 = jnp.float32
VMEM_LIMIT = 16 * 1024 * 1024
VMEM_LIMIT_LARGE = 40 * 1024 * 1024


def call(kernel, out_shape, scratch, flops, name, limit=VMEM_LIMIT, **specs):
    return pl.pallas_call(
        kernel,
        out_shape=out_shape,
        scratch_shapes=scratch,
        compiler_params=pltpu.CompilerParams(vmem_limit_bytes=limit),
        cost_estimate=pl.CostEstimate(flops=flops, bytes_accessed=1 << 20, transcendentals=0),
        name=name,
        **specs,
    )


def shape(dims, dtype):
    return jax.ShapeDtypeStruct(dims, dtype)


def nt(a, b):
    return lax.dot_general(a, b, (((1,), (1,)), ((), ())), preferred_element_type=F32)


def tn(a, b):
    return lax.dot_general(a, b, (((0,), (0,)), ((), ())), preferred_element_type=F32)


def dot(a, b):
    return jnp.dot(a, b, preferred_element_type=F32)


def flag(condition):
    return jnp.where(condition, 1.0, 0.0).astype(BF)


def column_codes(row):
    keys = jnp.broadcast_to(row, (LANES, LANES)).astype(F32).T.astype(jnp.int32)
    lane = lax.broadcasted_iota(jnp.int32, (LANES, LANES), 1)
    return flag((keys & (LANES - 1)) == lane), (keys >> 7).astype(F32).astype(BF)


def row_codes(row):
    keys = jnp.broadcast_to(row, (LANES, LANES))
    sub = lax.broadcasted_iota(jnp.int32, (LANES, LANES), 0)
    high = jnp.broadcast_to((row >> 7).astype(F32), (16, LANES)).astype(BF)
    return flag((keys & (LANES - 1)) == sub), high


def pick_block(low, high, block):
    zero = jnp.zeros((), BF)
    return jnp.where(high == block, low, zero)


def pick_rows(low, high, block):
    wide = low.reshape(LANES // 16, 16, low.shape[1])
    picked = pick_block(wide, high[None], block)
    return picked.reshape(low.shape)


def route_kernel(n, cap, ents, dims, *refs):
    given, (out_ref, pos_ref, ent_ref, dlow_ref, dhigh_ref), held_refs, sems = refs[:4], refs[4:9], refs[9:13], refs[13]
    copies = [pltpu.make_async_copy(src, dst, sems.at[i]) for i, (src, dst) in enumerate(zip(given, held_refs))]
    for copy in copies:
        copy.start()
    for copy in copies:
        copy.wait()
    do_ref, ds_ref, fo_ref, fs_ref = held_refs
    chunks = do_ref.shape[0]
    owner = do_ref[...]
    kind = lax.broadcasted_iota(jnp.int32, (n, chunks, LANES), 0)
    held = jnp.where(kind == owner[None], 1.0, 0.0).reshape(n * chunks, LANES)
    held_bf = held.astype(BF)
    i0 = lax.broadcasted_iota(jnp.int32, (LANES, LANES), 0)
    i1 = lax.broadcasted_iota(jnp.int32, (LANES, LANES), 1)
    inside = dot(held_bf, flag(i0 < i1))
    r0 = lax.broadcasted_iota(jnp.int32, (n * chunks, n * chunks), 0)
    r1 = lax.broadcasted_iota(jnp.int32, (n * chunks, n * chunks), 1)
    earlier = flag((r0 // chunks == r1 // chunks) & (r1 < r0))
    before = dot(dot(earlier, held_bf).astype(BF), jnp.ones((LANES, LANES), BF))
    rank = jnp.sum((held * (inside + before)).reshape(n, chunks, LANES), axis=0)
    rank = rank.astype(jnp.int32)
    entity_owner = fo_ref[...]
    entity_slot = fs_ref[...]
    value = ds_ref[...]
    pos_ref[...] = owner * cap + rank
    ent_ref[...] = entity_owner * ents + entity_slot
    fact_dim = owner * dims + value
    high = (value >> 5).astype(F32)
    low = (value & 31).astype(F32)
    names = lax.broadcasted_iota(jnp.int32, (n, LANES), 0)
    places = lax.broadcasted_iota(jnp.int32, (cap, LANES), 0)
    slots = lax.broadcasted_iota(jnp.int32, (ents, LANES), 0)
    asked_high = jnp.zeros((n, cap), F32)
    asked_low = jnp.zeros((n, cap), F32)
    hits = jnp.zeros((n, ents), F32)
    for k in range(chunks):
        here = slice(k * LANES, (k + 1) * LANES)
        mine = jnp.where(names == owner[k : k + 1], 1.0, 0.0)
        at = flag(places == rank[k : k + 1])
        asked_high += nt((mine * high[k : k + 1]).astype(BF), at)
        asked_low += nt((mine * low[k : k + 1]).astype(BF), at)
        hits += nt(flag(names == entity_owner[k : k + 1]), flag(slots == entity_slot[k : k + 1]))
        dlow_ref[here, :], dhigh_ref[here, :] = column_codes(fact_dim[k : k + 1])
    asked = (asked_high * 32.0 + asked_low).astype(jnp.int32)
    for r in range(cap // LANES):
        out_ref[:, r, :] = asked[:, r * LANES : (r + 1) * LANES]
    out_ref[:, cap // LANES, :] = hits.astype(jnp.int32)


def gather_rows(low_ref, high_ref, rows, table_refs, firsts, hot_ref):
    at = 0
    low, high = low_ref[rows, :], high_ref[rows, :]
    for table, first in zip(table_refs, firsts):
        for k in range(table.shape[0] // LANES):
            hot_ref[:, at : at + LANES] = pick_block(low, high, (first + k).astype(F32).astype(BF))
            at += LANES
    total, at = None, 0
    for table in table_refs:
        part = dot(hot_ref[:, at : at + table.shape[0]], table[...])
        total = part if total is None else total + part
        at += table.shape[0]
    return total


def ring_at(place, n):
    place = lax.rem(place + 2 * n, n)
    return jnp.where(place < n // 2, 2 * place, 2 * (n - 1 - place) + 1)


def ring_place(index, n):
    half = lax.div(index, 2)
    return jnp.where(lax.rem(index, 2) == 0, half, n - 1 - half)


def look_kernel(n, pieces, low_ref, high_ref, *refs):
    count = len(pieces)
    tables, base_ref, out_ref, hot_ref = refs[:count], refs[count], refs[-2], refs[-1]
    facts = low_ref.shape[0]
    step = hot_ref.shape[0]
    place = ring_place(lax.axis_index("fact"), n)
    firsts = [lax.div(ring_at(place + hops, n) * dims + row, LANES) for hops, row, dims in pieces]
    for c in range(facts // step):
        rows = slice(c * step, (c + 1) * step)
        out_ref[rows, :] = base_ref[rows, :] + gather_rows(low_ref, high_ref, rows, tables, firsts, hot_ref)


def message_kernel(n, pieces, low_ref, high_ref, *refs):
    count = len(pieces)
    sources, refs = refs[:count], refs[count:]
    base_ref, xw_ref, ent_ref, slope_out, part_ref, slope_ref, hot_ref, msg_ref, erlow_ref, erhigh_ref = refs[:10]
    tables, (sem, table_sem) = refs[10 : 10 + count], refs[10 + count :]
    arrivals = [pltpu.make_async_copy(src, dst, table_sem) for src, dst in zip(sources, tables)]
    for copy in arrivals:
        copy.start()
    facts = low_ref.shape[0]
    step = hot_ref.shape[0]
    place = ring_place(lax.axis_index("fact"), n)
    firsts = [lax.div(ring_at(place + hops, n) * dims + row, LANES) for hops, row, dims in pieces]
    for k in range(ent_ref.shape[0]):
        here = slice(k * LANES, (k + 1) * LANES)
        erlow_ref[:, here], erhigh_ref[:, here] = row_codes(ent_ref[k : k + 1, :])
    for copy in arrivals:
        copy.wait()
    for c in range(facts // step):
        rows = slice(c * step, (c + 1) * step)
        pre = xw_ref[rows, :] + base_ref[rows, :]
        if count:
            pre = pre + gather_rows(low_ref, high_ref, rows, tables, firsts, hot_ref)
        gate = jax.nn.sigmoid(pre)
        msg_ref[rows, :] = (pre * gate).astype(BF)
        slope_ref[rows, :] = gate * (1.0 + pre * (1.0 - gate))
    keep = pltpu.make_async_copy(slope_ref, slope_out, sem)
    keep.start()

    def add(pair, carry):
        hot = jnp.concatenate(
            [pick_rows(erlow_ref[...], erhigh_ref[...], (pair * 2 + i).astype(F32).astype(BF)) for i in range(2)], axis=0
        )
        rows = pl.ds(pl.multiple_of(pair * 256, 256), 256)
        part_ref[rows, :] = dot(hot, msg_ref[...]).astype(BF)
        return carry

    lax.fori_loop(0, part_ref.shape[0] // 256, add, 0)
    keep.wait()


def project_kernel(m, w_ref, *refs):
    blocks, out_ref = refs[:m], refs[m]
    me = lax.axis_index("feat")
    total = None
    for j, ref in enumerate(blocks):
        rows = pl.ds(pl.multiple_of((me ^ j) * LANES, LANES), LANES)
        part = dot(ref[...], w_ref[rows, :])
        total = part if total is None else total + part
    out_ref[...] = total


def ready_kernel(m, width, ents, *refs):
    x_refs, all_refs, (hidden_ref, xt_ref) = refs[:m], refs[m : 2 * m], refs[2 * m :]
    me = lax.axis_index("feat")
    for j in range(m):
        hidden_ref[me ^ j] = all_refs[j][2 * width : 2 * width + ents, :]
        xt_ref[pl.ds(pl.multiple_of((me ^ j) * LANES, LANES), LANES), :] = x_refs[j][...].T


def entity_kernel(n, m, width, ents, sums_ref, idx_ref, *refs):
    all_refs, (back_ref, out_ref, pre_ref, agg_ref, own_ref, hold_ref, words_ref, sem) = refs[:m], refs[m:]
    fetch = pltpu.make_async_copy(idx_ref, words_ref, sem)
    fetch.start()
    rows_each = ents // m
    me = lax.axis_index("feat")
    totals = []
    for b in range(m):
        total = sums_ref[b].astype(F32)
        for f in range(1, n):
            total += sums_ref[f * m + b].astype(F32)
        totals.append(total)
    fetch.wait()
    hits = jnp.sum(words_ref[:, words_ref.shape[1] - 1, :], axis=0, keepdims=True).astype(F32)
    hold_ref[...] = jnp.maximum(jnp.broadcast_to(hits, (LANES, ents)).T, 1.0)
    divisor = hold_ref[pl.ds(pl.multiple_of(me * rows_each, rows_each), rows_each), :]
    for b in range(m):
        agg_ref[b * rows_each : (b + 1) * rows_each, :] = (totals[b] / divisor).astype(BF)
    at = pl.multiple_of(2 * width + me * rows_each, rows_each)
    for j in range(m):
        own_ref[me ^ j] = all_refs[j][pl.ds(at, rows_each), :]
    aggregate = jnp.concatenate([agg_ref[b * rows_each : (b + 1) * rows_each, :] for b in range(m)], axis=1)
    hidden = jnp.concatenate([own_ref[b] for b in range(m)], axis=1)
    d_agg = None
    for j in range(m):
        pre = dot(hidden, all_refs[j][0:width, :]) + dot(aggregate, all_refs[j][width : 2 * width, :])
        gate = jax.nn.sigmoid(pre)
        cot = all_refs[j][pl.ds(at + ents, rows_each), :].astype(F32)
        d_pre = (cot * (gate * (1.0 + pre * (1.0 - gate)))).astype(BF)
        out_ref[me ^ j] = (pre * gate).astype(BF)
        pre_ref[me ^ j] = d_pre
        term = nt(d_pre, all_refs[j][width : 2 * width, :])
        d_agg = term if d_agg is None else d_agg + term
    for b in range(m):
        scaled = (d_agg[:, b * LANES : (b + 1) * LANES] / divisor).astype(BF)
        for f in range(n):
            back_ref[f * m + b] = scaled


def share_kernel(m, out_ref, pre_ref, agg_ref, *share_refs):
    rows_each = out_ref.shape[1]
    me = lax.axis_index("feat")
    for j, ref in enumerate(share_refs):
        ref[0:rows_each, :] = out_ref[me ^ j]
        ref[rows_each : 2 * rows_each, :] = pre_ref[me ^ j]
        ref[2 * rows_each :, :] = agg_ref[...]


def weight_kernel(n, m, width, stride, hidden_ref, *refs):
    got, (out_ref, back_ref, total_ref, pre_ref, agg_ref) = refs[:m], refs[m:]
    rows_each = got[0].shape[0] // (2 + m)
    own = width // n
    me = lax.axis_index("feat")
    for j, ref in enumerate(got):
        here = pl.ds(pl.multiple_of((me ^ j) * rows_each, rows_each), rows_each)
        out_ref[here, :] = ref[0:rows_each, :]
        pre_ref[here, :] = ref[rows_each : 2 * rows_each, :]
        for b in range(m):
            agg_ref[b, here, :] = ref[(2 + b) * rows_each : (3 + b) * rows_each, :]
    d_pre = pre_ref[...]
    for which, blocks in enumerate((hidden_ref, agg_ref)):
        for b in range(m):
            total_ref[b * LANES : (b + 1) * LANES, :] = tn(blocks[b], d_pre)
        for d in range(n):
            back_ref[d % 2, d // 2, which * stride : (which + 1) * stride, :] = padded(
                total_ref[d * own : (d + 1) * own, :], stride
            )


def halves_kernel(back_ref, keep_ref, give_ref):
    odd = lax.rem(lax.axis_index("fact"), 2)
    keep_ref[...] = back_ref[odd]
    give_ref[...] = back_ref[1 - odd].astype(BF)


def padded(piece, rows):
    if piece.shape[0] == rows:
        return piece
    return jnp.concatenate([piece, jnp.zeros((rows - piece.shape[0], LANES), F32)], axis=0)


def codes_kernel(pos_ref, ent_ref, plow_ref, phigh_ref, elow_ref, ehigh_ref):
    for k in range(pos_ref.shape[0]):
        here = slice(k * LANES, (k + 1) * LANES)
        plow_ref[:, here], phigh_ref[:, here] = row_codes(pos_ref[k : k + 1, :])
        elow_ref[here, :], ehigh_ref[here, :] = column_codes(ent_ref[k : k + 1, :])


def request_kernel(n, cap, req_ref, low_ref, high_ref):
    for s in range(n):
        for r in range(cap // LANES):
            at = s * cap + r * LANES
            low_ref[:, at : at + LANES], high_ref[:, at : at + LANES] = row_codes(req_ref[s, r : r + 1, :])


def backward_kernel(n, stride, slope_in, scaled_ref, low_ref, high_ref, xt_ref, dmsg_ref, share_ref, hot_ref, slope_ref, sem):
    fetch = pltpu.make_async_copy(slope_in, slope_ref, sem)
    fetch.start()
    facts = slope_ref.shape[0]
    own = xt_ref.shape[0] // n
    step = hot_ref.shape[0]
    for c in range(facts // step):
        rows = slice(c * step, (c + 1) * step)
        found = gather_rows(low_ref, high_ref, rows, [scaled_ref], [jnp.int32(0)], hot_ref)
        if c == 0:
            fetch.wait()
        dmsg_ref[rows, :] = (found * slope_ref[rows, :]).astype(BF)
    total = dot(xt_ref[...], dmsg_ref[...])
    for d in range(n):
        share_ref[d] = padded(total[d * own : (d + 1) * own, :], stride).astype(BF)


def spread_kernel(n, cap, stride, offsets, plow_ref, phigh_ref, dmsg_ref, share_ref, *refs):
    pair_refs, out_refs = refs[:-len(offsets)], refs[-len(offsets) :]
    me = lax.axis_index("fact")
    for offset, out_ref in zip(offsets, out_refs):
        d = lax.rem(me + offset, n)
        hot = jnp.concatenate(
            [
                pick_rows(plow_ref[...], phigh_ref[...], (d * (cap // LANES) + i).astype(F32).astype(BF))
                for i in range(cap // LANES)
            ],
            axis=0,
        )
        out_ref[0:cap, :] = dot(hot, dmsg_ref[...]).astype(BF)
        out_ref[cap : cap + stride, :] = share_ref[d]
        if out_ref.shape[0] > cap + stride:
            pair = pair_refs[0][lax.div(d, 2)]
            for ref in pair_refs[1:]:
                pair = pair + ref[lax.div(d, 2)].astype(F32)
            out_ref[cap + stride :, :] = pair.astype(BF)


def table_kernel(n, cap, stride, offsets, first, final, low_ref, high_ref, *refs):
    count = len(offsets)
    got, refs = refs[:count], refs[count:]
    if not first:
        (base_ref, weight_base_ref), refs = refs[:2], refs[2:]
    out_ref, refs = refs[0], refs[1:]
    final_refs, refs = (refs[:3], refs[3:]) if final else ((), refs[1:] + refs[:1])
    rows_ref, klow_ref, khigh_ref, weight_ref = refs[:4]
    me = lax.axis_index("fact")
    if first:
        weight_ref[...] = jnp.zeros(weight_ref.shape, F32)
    else:
        weight_ref[...] = weight_base_ref[...]
    for j, (offset, ref) in enumerate(zip(offsets, got)):
        source = lax.rem(me + (n - offset), n)
        here = slice(j * cap, (j + 1) * cap)
        there = pl.ds(pl.multiple_of(source * cap, LANES), cap)
        rows_ref[here, :] = ref[0:cap, :]
        klow_ref[:, here] = low_ref[:, there]
        khigh_ref[:, here] = high_ref[:, there]
        rows = ref.shape[0] - cap
        weight_ref[0:rows, :] += ref[cap:, :].astype(F32)
    copies = []
    for which, ref in enumerate(final_refs):
        copies.append(
            pltpu.make_async_copy(
                weight_ref.at[which * stride : which * stride + ref.shape[0], :], ref, refs[6].at[which]
            )
        )
        copies[-1].start()
    blocks = out_ref.shape[0] // LANES
    join = 2 if blocks % 2 == 0 else 1

    target_ref = refs[4] if final else out_ref
    for group in range(blocks // join):
        hot = jnp.concatenate(
            [pick_rows(klow_ref[...], khigh_ref[...], jnp.array(group * join + i, BF)) for i in range(join)], axis=0
        )
        rows = slice(group * join * LANES, (group + 1) * join * LANES)
        sums = dot(hot, rows_ref[...])
        target_ref[rows, :] = sums if first else base_ref[rows, :] + sums
        if final:
            copies.append(pltpu.make_async_copy(target_ref.at[rows, :], out_ref.at[rows, :], refs[5].at[group]))
            copies[-1].start()
    for copy in copies:
        copy.wait()


def shards(fact_x, dim_owner, dim_slot, fact_owner, fact_slot, dim_table, entity_h, w_msg, w_self, w_neigh, cotangent):
    n, m = lax.axis_size("fact"), lax.axis_size("feat")
    assert m == 4 and n % 2 == 0
    facts = fact_x.shape[0]
    chunks = facts // LANES
    ents = entity_h.shape[0]
    rows_each = ents // m
    width = w_msg.shape[0]
    dims = dim_table.shape[0]
    cap = -(-(3 * facts // n) // LANES) * LANES
    slots = n * cap
    groups = cap // LANES + 1
    own = width // n
    stride = max(16, own)
    step = 512
    tie = lax.optimization_barrier
    ringed = n <= 8
    limit = VMEM_LIMIT if ringed else VMEM_LIMIT_LARGE

    ring = [2 * p if p < n // 2 else 2 * (n - 1 - p) + 1 for p in range(n)]
    to_right = [(ring[p], ring[(p + 1) % n]) for p in range(n)]
    to_left = [(ring[(p + 1) % n], ring[p]) for p in range(n)]

    def pass_on(right, left):
        return lax.ppermute(right, "fact", to_right), lax.ppermute(left, "fact", to_left)

    def swap(block, bit):
        return lax.ppermute(block, "feat", [(i, i ^ bit) for i in range(m)])

    if ringed:
        right, left = pass_on(dim_table, dim_table)
    x_near = swap(fact_x, 1)
    by_lane = (chunks, LANES)
    columns = shape((facts, LANES), BF)
    asks, pos, entity, dlow, dhigh = call(
        functools.partial(route_kernel, n, cap, ents, dims),
        (
            shape((n, groups, LANES), jnp.int32),
            shape(by_lane, jnp.int32),
            shape(by_lane, jnp.int32),
            columns,
            columns,
        ),
        [pltpu.VMEM(by_lane, jnp.int32)] * 4 + [pltpu.SemaphoreType.DMA((4,))],
        1 << 28,
        "route",
        in_specs=[IN_HBM] * 4,
    )(dim_owner.reshape(by_lane), dim_slot.reshape(by_lane), fact_owner.reshape(by_lane), fact_slot.reshape(by_lane))
    if ringed:
        right, left, x_near, asks, pos, entity, dlow, dhigh = tie(
            (right, left, x_near, asks, pos, entity, dlow, dhigh)
        )

    def look(pieces, tables, base):
        rows = sum(t.shape[0] for t in tables)
        return call(
            functools.partial(look_kernel, n, pieces),
            shape((facts, LANES), F32),
            [pltpu.VMEM((step, rows), BF)],
            2 * facts * rows * LANES,
            "look",
            limit,
        )(dlow, dhigh, *tables, base)

    def project(blocks):
        return call(
            functools.partial(project_kernel, m), shape((facts, LANES), F32), [], 2 * facts * width * LANES, "project"
        )(w_msg, *blocks)

    found = jnp.zeros((facts, LANES), F32)
    weights = jnp.concatenate([w_self, w_neigh, entity_h, cotangent], axis=0)
    if ringed:
        near = (right, left)
        after = pass_on(*near)
        x_far = swap(fact_x, 2)
        found = look([(0, 0, dims), (-1, 0, dims), (1, 0, dims)], [dim_table, *near], found)
        right, left, x_far, found, weights = tie((*after, x_far, found, weights))
        for k in range(2, n // 2 - 1):
            after = pass_on(right, left)
            x_last = swap(x_far, 1)
            found = look([(-k, 0, dims), (k, 0, dims)], [right, left], found)
            right, left, found, x_last = tie((*after, found, x_last))
        all_far = swap(weights, 2)
        k = n // 2 - 1
        after = lax.ppermute(right, "fact", to_right)
        xw = project([fact_x, x_near, x_far, x_last])
        found = look([(k, 0, dims)], [left], found)
        found, asks = tie((found, asks))
        asked = lax.all_to_all(asks, "fact", 0, 0)
        found = look([(-k, 0, dims)], [right], found)
        all_near = swap(weights, 1)
        found, all_far, all_near = tie((found, all_far, all_near))
        last, last_pieces = [after], [(n // 2, 0, dims)]
    else:
        asked = lax.all_to_all(asks, "fact", 0, 0)
        x_far = swap(fact_x, 2)
        x_last = swap(x_far, 1)
        xw = project([fact_x, x_near, x_far, x_last])
        all_far, all_near = swap(weights, 2), swap(weights, 1)
        whole = lax.all_gather(dim_table, "fact")
        order = jnp.take(whole, ring_at(ring_place(lax.axis_index("fact"), n) + jnp.arange(n), n), axis=0)
        for k in range(0, n, 8):
            found = look([(k + i, 0, dims) for i in range(8)], [order[k + i] for i in range(8)], found)
        last, last_pieces = [], []
    all_last = swap(all_far, 1)
    x_blocks, all_blocks = [fact_x, x_near, x_far, x_last], [weights, all_near, all_far, all_last]
    last_rows = max(LANES, sum(t.shape[0] for t in last))
    slope, part = call(
        functools.partial(message_kernel, n, last_pieces),
        (pltpu.HBM((facts, LANES), F32), shape((n * ents, LANES), BF)),
        [
            pltpu.VMEM((facts, LANES), F32),
            pltpu.VMEM((step, last_rows), BF),
            pltpu.VMEM((facts, LANES), BF),
            pltpu.VMEM((LANES, facts), BF),
            pltpu.VMEM((16, facts), BF),
            *[pltpu.VMEM(t.shape, BF) for t in last],
            pltpu.SemaphoreType.DMA,
            pltpu.SemaphoreType.DMA,
        ],
        2 * facts * (last_rows + n * ents) * LANES,
        "message",
        limit,
        in_specs=[IN_VMEM] * 2 + [pl.BlockSpec(memory_space=pl.ANY)] * len(last) + [IN_VMEM] * 3,
        out_specs=(IN_HBM, IN_VMEM),
    )(dlow, dhigh, *last, found, xw, entity)
    sums = lax.all_to_all(part.reshape(n * m, rows_each, LANES), ("fact", "feat"), 0, 0)
    pos, entity, x_blocks, _ = tie((pos, entity, x_blocks, part))
    hidden, x_turned = call(
        functools.partial(ready_kernel, m, width, ents),
        (shape((m, ents, LANES), BF), shape((width, facts), BF)),
        [],
        1 << 28,
        "ready",
    )(*x_blocks, *all_blocks)
    by_feat = shape((m, rows_each, LANES), BF)
    back, out_parts, pre_parts, agg_parts = call(
        functools.partial(entity_kernel, n, m, width, ents),
        (shape((n * m, rows_each, LANES), BF), by_feat, by_feat, shape((m * rows_each, LANES), BF)),
        [
            pltpu.VMEM((m, rows_each, LANES), BF),
            pltpu.VMEM((ents, LANES), F32),
            pltpu.VMEM(asked.shape, jnp.int32),
            pltpu.SemaphoreType.DMA,
        ],
        6 * rows_each * width * width,
        "entity",
        in_specs=[IN_VMEM, pl.BlockSpec(memory_space=pl.ANY)] + [IN_VMEM] * m,
    )(sums, asked, *all_blocks)
    scaled = lax.all_to_all(back, ("fact", "feat"), 0, 0).reshape(n * ents, LANES)
    shares = call(
        functools.partial(share_kernel, m),
        tuple(shape(((2 + m) * rows_each, LANES), BF) for _ in range(m)),
        [],
        1 << 20,
        "share",
    )(out_parts, pre_parts, agg_parts)
    got = [shares[0]] + [swap(shares[j], j) for j in range(1, m)]
    pos, entity, asked, _ = tie((pos, entity, asked, back))
    plow, phigh, elow, ehigh = call(
        codes_kernel,
        (shape((LANES, facts), BF), shape((16, facts), BF), columns, columns),
        [],
        1 << 26,
        "codes",
    )(pos, entity)
    rlow, rhigh = call(
        functools.partial(request_kernel, n, cap),
        (shape((LANES, slots), BF), shape((16, slots), BF)),
        [],
        1 << 26,
        "requests",
        limit,
    )(asked)
    pair_shape = (n // 2, 2 * stride, LANES)
    output_h, pair = call(
        functools.partial(weight_kernel, n, m, width, stride),
        (shape((ents, LANES), BF), shape((2, *pair_shape), F32)),
        [pltpu.VMEM((width, LANES), F32), pltpu.VMEM((ents, LANES), BF), pltpu.VMEM((m, ents, LANES), BF)],
        4 * ents * width * LANES,
        "weight",
    )(hidden, *got)
    if ringed:
        keep, give = call(halves_kernel, (shape(pair_shape, F32), shape(pair_shape, BF)), [], 1 << 20, "halves")(pair)
        pairs = [keep, lax.ppermute(give, "fact", [(i, i ^ 1) for i in range(n)])]
    else:
        pairs = [jnp.stack([pair[0], pair[1]], axis=1).reshape(n, 2 * stride, LANES)]
    d_msg, msg_share = call(
        functools.partial(backward_kernel, n, stride),
        (columns, shape((n, stride, LANES), BF)),
        [pltpu.VMEM((step, n * ents), BF), pltpu.VMEM((facts, LANES), F32), pltpu.SemaphoreType.DMA],
        2 * facts * (n * ents + width) * LANES,
        "backward",
        limit,
        in_specs=[IN_HBM] + [IN_VMEM] * 4,
    )(slope, scaled, elow, ehigh, x_turned)

    def spread(offsets):
        lengths = [cap + (3 if ringed and k % 2 == 0 else 1) * stride for k in offsets]
        return call(
            functools.partial(spread_kernel, n, cap, stride, offsets),
            tuple(shape((rows, LANES), BF) for rows in lengths),
            [],
            2 * facts * cap * LANES * len(offsets),
            "spread",
            limit,
        )(plow, phigh, d_msg, msg_share, *(pairs if max(lengths) > cap + stride else ()))

    def add_up(offsets, got, base, final):
        weight = shape((3 * stride, LANES), F32)
        scratch = [
            pltpu.VMEM((cap * len(got), LANES), BF),
            pltpu.VMEM((LANES, cap * len(got)), BF),
            pltpu.VMEM((16, cap * len(got)), BF),
        ]
        return call(
            functools.partial(table_kernel, n, cap, stride, offsets, base is None, final),
            (shape((dims, LANES), F32),) + ((shape((own, LANES), F32),) * 3 if final else (weight,)),
            scratch
            + (
                [
                    pltpu.VMEM(weight.shape, F32),
                    pltpu.VMEM((dims, LANES), F32),
                    pltpu.SemaphoreType.DMA((dims // LANES,)),
                    pltpu.SemaphoreType.DMA((3,)),
                ]
                if final
                else []
            ),
            2 * cap * dims * LANES * len(got),
            "table",
            limit,
            **(dict(out_specs=(IN_HBM,) * 4) if final else {}),
        )(rlow, rhigh, *got, *(base or ()))

    totals = None
    if ringed:
        messages = {}
        rest = [[k, n - k] for k in range(n // 2 - 1, 1, -1)]
        for offsets in [rest[0], [n // 2], [1, n - 1], *rest[1:]]:
            for offset, message in zip(offsets, spread(offsets)):
                messages[offset] = lax.ppermute(message, "fact", [(i, (i + offset) % n) for i in range(n)])
        messages[0] = spread([0])[0]
        for offsets in [[0, 1, n - 1], [n // 2], *rest[::-1]]:
            totals = add_up(offsets, [messages[k] for k in offsets], totals, offsets == rest[0])
        grad_dim, grad_msg, grad_self, grad_neigh = totals
    else:
        fact_me = lax.axis_index("fact")
        sent = [message for k in range(0, n, 8) for message in spread(list(range(k, k + 8)))]
        by_owner = jnp.take(jnp.stack(sent), lax.rem(jnp.arange(n) - fact_me + n, n), axis=0)
        owned = lax.all_to_all(by_owner, "fact", 0, 0)
        by_offset = jnp.take(owned, lax.rem(fact_me - jnp.arange(n) + n, n), axis=0)
        for k in range(0, n, 8):
            totals = add_up(list(range(k, k + 8)), [by_offset[k + i] for i in range(8)], totals, k + 8 >= n)
        grad_dim, grad_msg, _, _ = totals
        pair_sum = lax.psum_scatter(pairs[0], "fact", scatter_dimension=0, tiled=True)[0]
        grad_self, grad_neigh = pair_sum[0:own], pair_sum[stride : stride + own]
    return output_h, grad_msg, grad_self, grad_neigh, grad_dim


def solution(mesh):
    placed = (
        P("fact", "feat"),
        P("fact", None),
        P("fact"),
        P("fact", None),
        P("fact"),
        P("fact", "feat"),
        P("fact", "feat"),
        P(None, "feat"),
        P(None, "feat"),
        P(None, "feat"),
        P("fact", "feat"),
    )
    return jax.shard_map(
        shards,
        mesh=mesh,
        in_specs=placed,
        out_specs=(P("fact", "feat"),) * 5,
        check_vma=False,
    )
```

```python
import functools

import jax
import jax.numpy as jnp
from jax import lax
from jax.experimental import pallas as pl
from jax.experimental.pallas import tpu as pltpu
from jax.sharding import PartitionSpec as P

LANES = 128
BF = jnp.bfloat16
IN_HBM = pl.BlockSpec(memory_space=pltpu.HBM)
IN_VMEM = pl.BlockSpec(memory_space=pltpu.VMEM)
F32 = jnp.float32
VMEM_LIMIT = 16 * 1024 * 1024
VMEM_LIMIT_LARGE = 40 * 1024 * 1024


def call(kernel, out_shape, scratch, flops, name, limit=VMEM_LIMIT, **specs):
    return pl.pallas_call(
        kernel,
        out_shape=out_shape,
        scratch_shapes=scratch,
        compiler_params=pltpu.CompilerParams(vmem_limit_bytes=limit),
        cost_estimate=pl.CostEstimate(flops=flops, bytes_accessed=1 << 20, transcendentals=0),
        name=name,
        **specs,
    )


def shape(dims, dtype):
    return jax.ShapeDtypeStruct(dims, dtype)


def nt(a, b):
    return lax.dot_general(a, b, (((1,), (1,)), ((), ())), preferred_element_type=F32)


def tn(a, b):
    return lax.dot_general(a, b, (((0,), (0,)), ((), ())), preferred_element_type=F32)


def dot(a, b):
    return jnp.dot(a, b, preferred_element_type=F32)


def flag(condition):
    return jnp.where(condition, 1.0, 0.0).astype(BF)


def column_codes(row):
    keys = jnp.broadcast_to(row, (LANES, LANES)).astype(F32).T.astype(jnp.int32)
    lane = lax.broadcasted_iota(jnp.int32, (LANES, LANES), 1)
    return flag((keys & (LANES - 1)) == lane), (keys >> 7).astype(F32).astype(BF)


def row_codes(row):
    keys = jnp.broadcast_to(row, (LANES, LANES))
    sub = lax.broadcasted_iota(jnp.int32, (LANES, LANES), 0)
    high = jnp.broadcast_to((row >> 7).astype(F32), (16, LANES)).astype(BF)
    return flag((keys & (LANES - 1)) == sub), high


def pick_block(low, high, block):
    zero = jnp.zeros((), BF)
    return jnp.where(high == block, low, zero)


def pick_rows(low, high, block):
    wide = low.reshape(LANES // 16, 16, low.shape[1])
    picked = pick_block(wide, high[None], block)
    return picked.reshape(low.shape)


def route_kernel(n, cap, ents, dims, *refs):
    given, (out_ref, pos_ref, ent_ref, dlow_ref, dhigh_ref), held_refs, sems = refs[:4], refs[4:9], refs[9:13], refs[13]
    copies = [pltpu.make_async_copy(src, dst, sems.at[i]) for i, (src, dst) in enumerate(zip(given, held_refs))]
    for copy in copies:
        copy.start()
    for copy in copies:
        copy.wait()
    do_ref, ds_ref, fo_ref, fs_ref = held_refs
    chunks = do_ref.shape[0]
    owner = do_ref[...]
    kind = lax.broadcasted_iota(jnp.int32, (n, chunks, LANES), 0)
    held = jnp.where(kind == owner[None], 1.0, 0.0).reshape(n * chunks, LANES)
    held_bf = held.astype(BF)
    i0 = lax.broadcasted_iota(jnp.int32, (LANES, LANES), 0)
    i1 = lax.broadcasted_iota(jnp.int32, (LANES, LANES), 1)
    inside = dot(held_bf, flag(i0 < i1))
    r0 = lax.broadcasted_iota(jnp.int32, (n * chunks, n * chunks), 0)
    r1 = lax.broadcasted_iota(jnp.int32, (n * chunks, n * chunks), 1)
    earlier = flag((r0 // chunks == r1 // chunks) & (r1 < r0))
    before = dot(dot(earlier, held_bf).astype(BF), jnp.ones((LANES, LANES), BF))
    rank = jnp.sum((held * (inside + before)).reshape(n, chunks, LANES), axis=0)
    rank = rank.astype(jnp.int32)
    entity_owner = fo_ref[...]
    entity_slot = fs_ref[...]
    value = ds_ref[...]
    pos_ref[...] = owner * cap + rank
    ent_ref[...] = entity_owner * ents + entity_slot
    fact_dim = owner * dims + value
    high = (value >> 5).astype(F32)
    low = (value & 31).astype(F32)
    names = lax.broadcasted_iota(jnp.int32, (n, LANES), 0)
    places = lax.broadcasted_iota(jnp.int32, (cap, LANES), 0)
    slots = lax.broadcasted_iota(jnp.int32, (ents, LANES), 0)
    asked_high = jnp.zeros((n, cap), F32)
    asked_low = jnp.zeros((n, cap), F32)
    hits = jnp.zeros((n, ents), F32)
    for k in range(chunks):
        here = slice(k * LANES, (k + 1) * LANES)
        mine = jnp.where(names == owner[k : k + 1], 1.0, 0.0)
        at = flag(places == rank[k : k + 1])
        asked_high += nt((mine * high[k : k + 1]).astype(BF), at)
        asked_low += nt((mine * low[k : k + 1]).astype(BF), at)
        hits += nt(flag(names == entity_owner[k : k + 1]), flag(slots == entity_slot[k : k + 1]))
        dlow_ref[here, :], dhigh_ref[here, :] = column_codes(fact_dim[k : k + 1])
    asked = (asked_high * 32.0 + asked_low).astype(jnp.int32)
    for r in range(cap // LANES):
        out_ref[:, r, :] = asked[:, r * LANES : (r + 1) * LANES]
    out_ref[:, cap // LANES, :] = hits.astype(jnp.int32)


def gather_rows(low_ref, high_ref, rows, table_refs, firsts, hot_ref):
    at = 0
    low, high = low_ref[rows, :], high_ref[rows, :]
    for table, first in zip(table_refs, firsts):
        for k in range(table.shape[0] // LANES):
            hot_ref[:, at : at + LANES] = pick_block(low, high, (first + k).astype(F32).astype(BF))
            at += LANES
    total, at = None, 0
    for table in table_refs:
        part = dot(hot_ref[:, at : at + table.shape[0]], table[...])
        total = part if total is None else total + part
        at += table.shape[0]
    return total


def ring_at(place, n):
    place = lax.rem(place + 2 * n, n)
    return jnp.where(place < n // 2, 2 * place, 2 * (n - 1 - place) + 1)


def ring_place(index, n):
    half = lax.div(index, 2)
    return jnp.where(lax.rem(index, 2) == 0, half, n - 1 - half)


def look_kernel(n, pieces, low_ref, high_ref, *refs):
    count = len(pieces)
    tables, base_ref, out_ref, hot_ref = refs[:count], refs[count], refs[-2], refs[-1]
    facts = low_ref.shape[0]
    step = hot_ref.shape[0]
    place = ring_place(lax.axis_index("fact"), n)
    firsts = [lax.div(ring_at(place + hops, n) * dims + row, LANES) for hops, row, dims in pieces]
    for c in range(facts // step):
        rows = slice(c * step, (c + 1) * step)
        out_ref[rows, :] = base_ref[rows, :] + gather_rows(low_ref, high_ref, rows, tables, firsts, hot_ref)


def message_kernel(n, pieces, low_ref, high_ref, *refs):
    count = len(pieces)
    sources, refs = refs[:count], refs[count:]
    base_ref, xw_ref, ent_ref, slope_out, part_ref, slope_ref, hot_ref, msg_ref, erlow_ref, erhigh_ref = refs[:10]
    tables, (sem, table_sem) = refs[10 : 10 + count], refs[10 + count :]
    arrivals = [pltpu.make_async_copy(src, dst, table_sem) for src, dst in zip(sources, tables)]
    for copy in arrivals:
        copy.start()
    facts = low_ref.shape[0]
    step = hot_ref.shape[0]
    place = ring_place(lax.axis_index("fact"), n)
    firsts = [lax.div(ring_at(place + hops, n) * dims + row, LANES) for hops, row, dims in pieces]
    for k in range(ent_ref.shape[0]):
        here = slice(k * LANES, (k + 1) * LANES)
        erlow_ref[:, here], erhigh_ref[:, here] = row_codes(ent_ref[k : k + 1, :])
    for copy in arrivals:
        copy.wait()
    for c in range(facts // step):
        rows = slice(c * step, (c + 1) * step)
        pre = xw_ref[rows, :] + base_ref[rows, :]
        if count:
            pre = pre + gather_rows(low_ref, high_ref, rows, tables, firsts, hot_ref)
        gate = jax.nn.sigmoid(pre)
        msg_ref[rows, :] = (pre * gate).astype(BF)
        slope_ref[rows, :] = gate * (1.0 + pre * (1.0 - gate))
    keep = pltpu.make_async_copy(slope_ref, slope_out, sem)
    keep.start()

    def add(pair, carry):
        hot = jnp.concatenate(
            [pick_rows(erlow_ref[...], erhigh_ref[...], (pair * 2 + i).astype(F32).astype(BF)) for i in range(2)], axis=0
        )
        rows = pl.ds(pl.multiple_of(pair * 256, 256), 256)
        part_ref[rows, :] = dot(hot, msg_ref[...]).astype(BF)
        return carry

    lax.fori_loop(0, part_ref.shape[0] // 256, add, 0)
    keep.wait()


def project_kernel(m, w_ref, *refs):
    blocks, out_ref = refs[:m], refs[m]
    me = lax.axis_index("feat")
    total = None
    for j, ref in enumerate(blocks):
        rows = pl.ds(pl.multiple_of((me ^ j) * LANES, LANES), LANES)
        part = dot(ref[...], w_ref[rows, :])
        total = part if total is None else total + part
    out_ref[...] = total


def ready_kernel(m, width, ents, *refs):
    x_refs, all_refs, (hidden_ref, xt_ref) = refs[:m], refs[m : 2 * m], refs[2 * m :]
    me = lax.axis_index("feat")
    for j in range(m):
        hidden_ref[me ^ j] = all_refs[j][2 * width : 2 * width + ents, :]
        xt_ref[pl.ds(pl.multiple_of((me ^ j) * LANES, LANES), LANES), :] = x_refs[j][...].T


def entity_kernel(n, m, width, ents, sums_ref, idx_ref, *refs):
    all_refs, (back_ref, out_ref, pre_ref, agg_ref, own_ref, hold_ref, words_ref, sem) = refs[:m], refs[m:]
    fetch = pltpu.make_async_copy(idx_ref, words_ref, sem)
    fetch.start()
    rows_each = ents // m
    me = lax.axis_index("feat")
    totals = []
    for b in range(m):
        total = sums_ref[b].astype(F32)
        for f in range(1, n):
            total += sums_ref[f * m + b].astype(F32)
        totals.append(total)
    fetch.wait()
    hits = jnp.sum(words_ref[:, words_ref.shape[1] - 1, :], axis=0, keepdims=True).astype(F32)
    hold_ref[...] = jnp.maximum(jnp.broadcast_to(hits, (LANES, ents)).T, 1.0)
    divisor = hold_ref[pl.ds(pl.multiple_of(me * rows_each, rows_each), rows_each), :]
    for b in range(m):
        agg_ref[b * rows_each : (b + 1) * rows_each, :] = (totals[b] / divisor).astype(BF)
    at = pl.multiple_of(2 * width + me * rows_each, rows_each)
    for j in range(m):
        own_ref[me ^ j] = all_refs[j][pl.ds(at, rows_each), :]
    aggregate = jnp.concatenate([agg_ref[b * rows_each : (b + 1) * rows_each, :] for b in range(m)], axis=1)
    hidden = jnp.concatenate([own_ref[b] for b in range(m)], axis=1)
    d_agg = None
    for j in range(m):
        pre = dot(hidden, all_refs[j][0:width, :]) + dot(aggregate, all_refs[j][width : 2 * width, :])
        gate = jax.nn.sigmoid(pre)
        cot = all_refs[j][pl.ds(at + ents, rows_each), :].astype(F32)
        d_pre = (cot * (gate * (1.0 + pre * (1.0 - gate)))).astype(BF)
        out_ref[me ^ j] = (pre * gate).astype(BF)
        pre_ref[me ^ j] = d_pre
        term = nt(d_pre, all_refs[j][width : 2 * width, :])
        d_agg = term if d_agg is None else d_agg + term
    for b in range(m):
        scaled = (d_agg[:, b * LANES : (b + 1) * LANES] / divisor).astype(BF)
        for f in range(n):
            back_ref[f * m + b] = scaled


def share_kernel(m, out_ref, pre_ref, agg_ref, *share_refs):
    rows_each = out_ref.shape[1]
    me = lax.axis_index("feat")
    for j, ref in enumerate(share_refs):
        ref[0:rows_each, :] = out_ref[me ^ j]
        ref[rows_each : 2 * rows_each, :] = pre_ref[me ^ j]
        ref[2 * rows_each :, :] = agg_ref[...]


def weight_kernel(n, m, width, stride, hidden_ref, *refs):
    got, (out_ref, back_ref, total_ref, pre_ref, agg_ref) = refs[:m], refs[m:]
    rows_each = got[0].shape[0] // (2 + m)
    own = width // n
    me = lax.axis_index("feat")
    for j, ref in enumerate(got):
        here = pl.ds(pl.multiple_of((me ^ j) * rows_each, rows_each), rows_each)
        out_ref[here, :] = ref[0:rows_each, :]
        pre_ref[here, :] = ref[rows_each : 2 * rows_each, :]
        for b in range(m):
            agg_ref[b, here, :] = ref[(2 + b) * rows_each : (3 + b) * rows_each, :]
    d_pre = pre_ref[...]
    for which, blocks in enumerate((hidden_ref, agg_ref)):
        for b in range(m):
            total_ref[b * LANES : (b + 1) * LANES, :] = tn(blocks[b], d_pre)
        for d in range(n):
            back_ref[d % 2, d // 2, which * stride : (which + 1) * stride, :] = padded(
                total_ref[d * own : (d + 1) * own, :], stride
            )


def halves_kernel(back_ref, keep_ref, give_ref):
    odd = lax.rem(lax.axis_index("fact"), 2)
    keep_ref[...] = back_ref[odd]
    give_ref[...] = back_ref[1 - odd].astype(BF)


def padded(piece, rows):
    if piece.shape[0] == rows:
        return piece
    return jnp.concatenate([piece, jnp.zeros((rows - piece.shape[0], LANES), F32)], axis=0)


def codes_kernel(pos_ref, ent_ref, plow_ref, phigh_ref, elow_ref, ehigh_ref):
    for k in range(pos_ref.shape[0]):
        here = slice(k * LANES, (k + 1) * LANES)
        plow_ref[:, here], phigh_ref[:, here] = row_codes(pos_ref[k : k + 1, :])
        elow_ref[here, :], ehigh_ref[here, :] = column_codes(ent_ref[k : k + 1, :])


def request_kernel(n, cap, req_ref, low_ref, high_ref):
    for s in range(n):
        for r in range(cap // LANES):
            at = s * cap + r * LANES
            low_ref[:, at : at + LANES], high_ref[:, at : at + LANES] = row_codes(req_ref[s, r : r + 1, :])


def backward_kernel(n, stride, slope_in, scaled_ref, low_ref, high_ref, xt_ref, dmsg_ref, share_ref, hot_ref, slope_ref, sem):
    fetch = pltpu.make_async_copy(slope_in, slope_ref, sem)
    fetch.start()
    facts = slope_ref.shape[0]
    own = xt_ref.shape[0] // n
    step = hot_ref.shape[0]
    for c in range(facts // step):
        rows = slice(c * step, (c + 1) * step)
        found = gather_rows(low_ref, high_ref, rows, [scaled_ref], [jnp.int32(0)], hot_ref)
        if c == 0:
            fetch.wait()
        dmsg_ref[rows, :] = (found * slope_ref[rows, :]).astype(BF)
    total = dot(xt_ref[...], dmsg_ref[...])
    for d in range(n):
        share_ref[d] = padded(total[d * own : (d + 1) * own, :], stride).astype(BF)


def spread_kernel(n, cap, stride, offsets, plow_ref, phigh_ref, dmsg_ref, share_ref, *refs):
    pair_refs, out_refs = refs[:-len(offsets)], refs[-len(offsets) :]
    me = lax.axis_index("fact")
    for offset, out_ref in zip(offsets, out_refs):
        d = lax.rem(me + offset, n)
        hot = jnp.concatenate(
            [
                pick_rows(plow_ref[...], phigh_ref[...], (d * (cap // LANES) + i).astype(F32).astype(BF))
                for i in range(cap // LANES)
            ],
            axis=0,
        )
        out_ref[0:cap, :] = dot(hot, dmsg_ref[...]).astype(BF)
        out_ref[cap : cap + stride, :] = share_ref[d]
        if out_ref.shape[0] > cap + stride:
            pair = pair_refs[0][lax.div(d, 2)]
            for ref in pair_refs[1:]:
                pair = pair + ref[lax.div(d, 2)].astype(F32)
            out_ref[cap + stride :, :] = pair.astype(BF)


def table_kernel(n, cap, stride, offsets, first, final, low_ref, high_ref, *refs):
    count = len(offsets)
    got, refs = refs[:count], refs[count:]
    if not first:
        (base_ref, weight_base_ref), refs = refs[:2], refs[2:]
    out_ref, refs = refs[0], refs[1:]
    final_refs, refs = (refs[:3], refs[3:]) if final else ((), refs[1:] + refs[:1])
    rows_ref, klow_ref, khigh_ref, weight_ref = refs[:4]
    me = lax.axis_index("fact")
    if first:
        weight_ref[...] = jnp.zeros(weight_ref.shape, F32)
    else:
        weight_ref[...] = weight_base_ref[...]
    for j, (offset, ref) in enumerate(zip(offsets, got)):
        source = lax.rem(me + (n - offset), n)
        here = slice(j * cap, (j + 1) * cap)
        there = pl.ds(pl.multiple_of(source * cap, LANES), cap)
        rows_ref[here, :] = ref[0:cap, :]
        klow_ref[:, here] = low_ref[:, there]
        khigh_ref[:, here] = high_ref[:, there]
        rows = ref.shape[0] - cap
        weight_ref[0:rows, :] += ref[cap:, :].astype(F32)
    copies = []
    for which, ref in enumerate(final_refs):
        copies.append(
            pltpu.make_async_copy(
                weight_ref.at[which * stride : which * stride + ref.shape[0], :], ref, refs[6].at[which]
            )
        )
        copies[-1].start()
    blocks = out_ref.shape[0] // LANES
    join = 2 if blocks % 2 == 0 else 1

    target_ref = refs[4] if final else out_ref
    for group in range(blocks // join):
        hot = jnp.concatenate(
            [pick_rows(klow_ref[...], khigh_ref[...], jnp.array(group * join + i, BF)) for i in range(join)], axis=0
        )
        rows = slice(group * join * LANES, (group + 1) * join * LANES)
        sums = dot(hot, rows_ref[...])
        target_ref[rows, :] = sums if first else base_ref[rows, :] + sums
        if final:
            copies.append(pltpu.make_async_copy(target_ref.at[rows, :], out_ref.at[rows, :], refs[5].at[group]))
            copies[-1].start()
    for copy in copies:
        copy.wait()


def shards(fact_x, dim_owner, dim_slot, fact_owner, fact_slot, dim_table, entity_h, w_msg, w_self, w_neigh, cotangent):
    n, m = lax.axis_size("fact"), lax.axis_size("feat")
    assert m == 4 and n % 2 == 0
    facts = fact_x.shape[0]
    chunks = facts // LANES
    ents = entity_h.shape[0]
    rows_each = ents // m
    width = w_msg.shape[0]
    dims = dim_table.shape[0]
    cap = -(-(3 * facts // n) // LANES) * LANES
    slots = n * cap
    groups = cap // LANES + 1
    own = width // n
    stride = max(16, own)
    step = 512
    tie = lax.optimization_barrier
    ringed = n <= 8
    limit = VMEM_LIMIT if ringed else VMEM_LIMIT_LARGE

    ring = [2 * p if p < n // 2 else 2 * (n - 1 - p) + 1 for p in range(n)]
    to_right = [(ring[p], ring[(p + 1) % n]) for p in range(n)]
    to_left = [(ring[(p + 1) % n], ring[p]) for p in range(n)]

    def pass_on(right, left):
        return lax.ppermute(right, "fact", to_right), lax.ppermute(left, "fact", to_left)

    def swap(block, bit):
        return lax.ppermute(block, "feat", [(i, i ^ bit) for i in range(m)])

    if ringed:
        right, left = pass_on(dim_table, dim_table)
    x_near = swap(fact_x, 1)
    by_lane = (chunks, LANES)
    columns = shape((facts, LANES), BF)
    asks, pos, entity, dlow, dhigh = call(
        functools.partial(route_kernel, n, cap, ents, dims),
        (
            shape((n, groups, LANES), jnp.int32),
            shape(by_lane, jnp.int32),
            shape(by_lane, jnp.int32),
            columns,
            columns,
        ),
        [pltpu.VMEM(by_lane, jnp.int32)] * 4 + [pltpu.SemaphoreType.DMA((4,))],
        1 << 28,
        "route",
        in_specs=[IN_HBM] * 4,
    )(dim_owner.reshape(by_lane), dim_slot.reshape(by_lane), fact_owner.reshape(by_lane), fact_slot.reshape(by_lane))
    if ringed:
        left, x_near, asks, pos, entity, dlow, dhigh = tie((left, x_near, asks, pos, entity, dlow, dhigh))

    def look(pieces, tables, base):
        rows = sum(t.shape[0] for t in tables)
        return call(
            functools.partial(look_kernel, n, pieces),
            shape((facts, LANES), F32),
            [pltpu.VMEM((step, rows), BF)],
            2 * facts * rows * LANES,
            "look",
            limit,
        )(dlow, dhigh, *tables, base)

    def project(blocks):
        return call(
            functools.partial(project_kernel, m), shape((facts, LANES), F32), [], 2 * facts * width * LANES, "project"
        )(w_msg, *blocks)

    found = jnp.zeros((facts, LANES), F32)
    weights = jnp.concatenate([w_self, w_neigh, entity_h, cotangent], axis=0)
    if ringed:
        found = look([(0, 0, dims)], [dim_table], found)
        for k in range(1, n // 2):
            more = k < n // 2 - 1
            right, found = tie((right, found))
            next_right = lax.ppermute(right, "fact", to_right)
            if k == 1:
                x_far = swap(fact_x, 2)
            if not more:
                xw = project([fact_x, x_near, x_far, x_last])
            found = look([(-k, 0, dims)], [right], found)
            left, found = tie((left, found))
            if more:
                next_left = lax.ppermute(left, "fact", to_left)
            else:
                found, asks = tie((found, asks))
                asked = lax.all_to_all(asks, "fact", 0, 0)
            if k == 2:
                x_last, all_far = swap(x_far, 1), swap(weights, 2)
            found = look([(k, 0, dims)], [left], found)
            if k == 1:
                x_far, found, weights = tie((x_far, found, weights))
            if k == 2:
                x_last, found = tie((x_last, found))
            right, left = next_right, next_left
        all_near = swap(weights, 1)
        found, all_far, all_near = tie((found, all_far, all_near))
        last, last_pieces = [right], [(n // 2, 0, dims)]
    else:
        asked = lax.all_to_all(asks, "fact", 0, 0)
        x_far = swap(fact_x, 2)
        x_last = swap(x_far, 1)
        xw = project([fact_x, x_near, x_far, x_last])
        all_far, all_near = swap(weights, 2), swap(weights, 1)
        whole = lax.all_gather(dim_table, "fact")
        order = jnp.take(whole, ring_at(ring_place(lax.axis_index("fact"), n) + jnp.arange(n), n), axis=0)
        for k in range(0, n, 8):
            found = look([(k + i, 0, dims) for i in range(8)], [order[k + i] for i in range(8)], found)
        last, last_pieces = [], []
    all_last = swap(all_far, 1)
    x_blocks, all_blocks = [fact_x, x_near, x_far, x_last], [weights, all_near, all_far, all_last]
    last_rows = max(LANES, sum(t.shape[0] for t in last))
    slope, part = call(
        functools.partial(message_kernel, n, last_pieces),
        (pltpu.HBM((facts, LANES), F32), pltpu.VMEM((n * ents, LANES), BF)),
        [
            pltpu.VMEM((facts, LANES), F32),
            pltpu.VMEM((step, last_rows), BF),
            pltpu.VMEM((facts, LANES), BF),
            pltpu.VMEM((LANES, facts), BF),
            pltpu.VMEM((16, facts), BF),
            *[pltpu.VMEM(t.shape, BF) for t in last],
            pltpu.SemaphoreType.DMA,
            pltpu.SemaphoreType.DMA,
        ],
        2 * facts * (last_rows + n * ents) * LANES,
        "message",
        limit,
        in_specs=[IN_VMEM] * 2 + [pl.BlockSpec(memory_space=pl.ANY)] * len(last) + [IN_VMEM] * 3,
        out_specs=(IN_HBM, IN_VMEM),
    )(dlow, dhigh, *last, found, xw, entity)
    sums = lax.all_to_all(part.reshape(n * m, rows_each, LANES), ("fact", "feat"), 0, 0)
    pos, entity, x_blocks, _ = tie((pos, entity, x_blocks, part))
    hidden, x_turned = call(
        functools.partial(ready_kernel, m, width, ents),
        (shape((m, ents, LANES), BF), shape((width, facts), BF)),
        [],
        1 << 28,
        "ready",
    )(*x_blocks, *all_blocks)
    by_feat = shape((m, rows_each, LANES), BF)
    back, out_parts, pre_parts, agg_parts = call(
        functools.partial(entity_kernel, n, m, width, ents),
        (pltpu.VMEM((n * m, rows_each, LANES), BF), by_feat, by_feat, shape((m * rows_each, LANES), BF)),
        [
            pltpu.VMEM((m, rows_each, LANES), BF),
            pltpu.VMEM((ents, LANES), F32),
            pltpu.VMEM(asked.shape, jnp.int32),
            pltpu.SemaphoreType.DMA,
        ],
        6 * rows_each * width * width,
        "entity",
        in_specs=[IN_VMEM, pl.BlockSpec(memory_space=pl.ANY)] + [IN_VMEM] * m,
    )(sums, asked, *all_blocks)
    scaled = lax.all_to_all(back, ("fact", "feat"), 0, 0).reshape(n * ents, LANES)
    shares = call(
        functools.partial(share_kernel, m),
        tuple(shape(((2 + m) * rows_each, LANES), BF) for _ in range(m)),
        [],
        1 << 20,
        "share",
    )(out_parts, pre_parts, agg_parts)
    got = [shares[0]] + [swap(shares[j], j) for j in range(1, m)]
    pos, entity, asked, _ = tie((pos, entity, asked, back))
    plow, phigh, elow, ehigh = call(
        codes_kernel,
        (shape((LANES, facts), BF), shape((16, facts), BF), columns, columns),
        [],
        1 << 26,
        "codes",
    )(pos, entity)
    rlow, rhigh = call(
        functools.partial(request_kernel, n, cap),
        (shape((LANES, slots), BF), shape((16, slots), BF)),
        [],
        1 << 26,
        "requests",
        limit,
    )(asked)
    pair_shape = (n // 2, 2 * stride, LANES)
    output_h, pair = call(
        functools.partial(weight_kernel, n, m, width, stride),
        (shape((ents, LANES), BF), shape((2, *pair_shape), F32)),
        [pltpu.VMEM((width, LANES), F32), pltpu.VMEM((ents, LANES), BF), pltpu.VMEM((m, ents, LANES), BF)],
        4 * ents * width * LANES,
        "weight",
    )(hidden, *got)
    if ringed:
        keep, give = call(halves_kernel, (shape(pair_shape, F32), shape(pair_shape, BF)), [], 1 << 20, "halves")(pair)
        pairs = [keep, lax.ppermute(give, "fact", [(i, i ^ 1) for i in range(n)])]
    else:
        pairs = [jnp.stack([pair[0], pair[1]], axis=1).reshape(n, 2 * stride, LANES)]
    d_msg, msg_share = call(
        functools.partial(backward_kernel, n, stride),
        (columns, shape((n, stride, LANES), BF)),
        [pltpu.VMEM((step, n * ents), BF), pltpu.VMEM((facts, LANES), F32), pltpu.SemaphoreType.DMA],
        2 * facts * (n * ents + width) * LANES,
        "backward",
        limit,
        in_specs=[IN_HBM] + [IN_VMEM] * 4,
    )(slope, scaled, elow, ehigh, x_turned)

    def spread(offsets):
        lengths = [cap + (3 if ringed and k % 2 == 0 else 1) * stride for k in offsets]
        return call(
            functools.partial(spread_kernel, n, cap, stride, offsets),
            tuple(shape((rows, LANES), BF) for rows in lengths),
            [],
            2 * facts * cap * LANES * len(offsets),
            "spread",
            limit,
        )(plow, phigh, d_msg, msg_share, *(pairs if max(lengths) > cap + stride else ()))

    def add_up(offsets, got, base, final):
        weight = shape((3 * stride, LANES), F32)
        scratch = [
            pltpu.VMEM((cap * len(got), LANES), BF),
            pltpu.VMEM((LANES, cap * len(got)), BF),
            pltpu.VMEM((16, cap * len(got)), BF),
        ]
        return call(
            functools.partial(table_kernel, n, cap, stride, offsets, base is None, final),
            (shape((dims, LANES), F32),) + ((shape((own, LANES), F32),) * 3 if final else (weight,)),
            scratch
            + (
                [
                    pltpu.VMEM(weight.shape, F32),
                    pltpu.VMEM((dims, LANES), F32),
                    pltpu.SemaphoreType.DMA((dims // LANES,)),
                    pltpu.SemaphoreType.DMA((3,)),
                ]
                if final
                else []
            ),
            2 * cap * dims * LANES * len(got),
            "table",
            limit,
            **(dict(out_specs=(IN_HBM,) * 4) if final else {}),
        )(rlow, rhigh, *got, *(base or ()))

    totals = None
    if ringed:
        messages = {}
        rest = [[k, n - k] for k in range(n // 2 - 1, 1, -1)]
        for offsets in [rest[0], [n // 2], [1, n - 1], *rest[1:]]:
            for offset, message in zip(offsets, spread(offsets)):
                messages[offset] = lax.ppermute(message, "fact", [(i, (i + offset) % n) for i in range(n)])
        messages[0] = spread([0])[0]
        for offsets in [[0, 1, n - 1], [n // 2], *rest[::-1]]:
            totals = add_up(offsets, [messages[k] for k in offsets], totals, offsets == rest[0])
        grad_dim, grad_msg, grad_self, grad_neigh = totals
    else:
        fact_me = lax.axis_index("fact")
        sent = [message for k in range(0, n, 8) for message in spread(list(range(k, k + 8)))]
        by_owner = jnp.take(jnp.stack(sent), lax.rem(jnp.arange(n) - fact_me + n, n), axis=0)
        owned = lax.all_to_all(by_owner, "fact", 0, 0)
        by_offset = jnp.take(owned, lax.rem(fact_me - jnp.arange(n) + n, n), axis=0)
        for k in range(0, n, 8):
            totals = add_up(list(range(k, k + 8)), [by_offset[k + i] for i in range(8)], totals, k + 8 >= n)
        grad_dim, grad_msg, _, _ = totals
        pair_sum = lax.psum_scatter(pairs[0], "fact", scatter_dimension=0, tiled=True)[0]
        grad_self, grad_neigh = pair_sum[0:own], pair_sum[stride : stride + own]
    return output_h, grad_msg, grad_self, grad_neigh, grad_dim


def solution(mesh):
    placed = (
        P("fact", "feat"),
        P("fact", None),
        P("fact"),
        P("fact", None),
        P("fact"),
        P("fact", "feat"),
        P("fact", "feat"),
        P(None, "feat"),
        P(None, "feat"),
        P(None, "feat"),
        P("fact", "feat"),
    )
    return jax.shard_map(
        shards,
        mesh=mesh,
        in_specs=placed,
        out_specs=(P("fact", "feat"),) * 5,
        check_vma=False,
    )
```

```python
import functools

import jax
import jax.numpy as jnp
from jax import lax
from jax.experimental import pallas as pl
from jax.experimental.pallas import tpu as pltpu
from jax.sharding import PartitionSpec as P

LANES = 128
BF = jnp.bfloat16
IN_HBM = pl.BlockSpec(memory_space=pltpu.HBM)
IN_VMEM = pl.BlockSpec(memory_space=pltpu.VMEM)
F32 = jnp.float32
VMEM_LIMIT = 16 * 1024 * 1024
VMEM_LIMIT_LARGE = 40 * 1024 * 1024


def call(kernel, out_shape, scratch, flops, name, limit=VMEM_LIMIT, **specs):
    return pl.pallas_call(
        kernel,
        out_shape=out_shape,
        scratch_shapes=scratch,
        compiler_params=pltpu.CompilerParams(vmem_limit_bytes=limit),
        cost_estimate=pl.CostEstimate(flops=flops, bytes_accessed=1 << 20, transcendentals=0),
        name=name,
        **specs,
    )


def shape(dims, dtype):
    return jax.ShapeDtypeStruct(dims, dtype)


def nt(a, b):
    return lax.dot_general(a, b, (((1,), (1,)), ((), ())), preferred_element_type=F32)


def tn(a, b):
    return lax.dot_general(a, b, (((0,), (0,)), ((), ())), preferred_element_type=F32)


def dot(a, b):
    return jnp.dot(a, b, preferred_element_type=F32)


def flag(condition):
    return jnp.where(condition, 1.0, 0.0).astype(BF)


def column_codes(row):
    keys = jnp.broadcast_to(row, (LANES, LANES)).astype(F32).T.astype(jnp.int32)
    lane = lax.broadcasted_iota(jnp.int32, (LANES, LANES), 1)
    return flag((keys & (LANES - 1)) == lane), (keys >> 7).astype(F32).astype(BF)


def row_codes(row):
    keys = jnp.broadcast_to(row, (LANES, LANES))
    sub = lax.broadcasted_iota(jnp.int32, (LANES, LANES), 0)
    high = jnp.broadcast_to((row >> 7).astype(F32), (16, LANES)).astype(BF)
    return flag((keys & (LANES - 1)) == sub), high


def pick_block(low, high, block):
    zero = jnp.zeros((), BF)
    return jnp.where(high == block, low, zero)


def pick_rows(low, high, block):
    wide = low.reshape(LANES // 16, 16, low.shape[1])
    picked = pick_block(wide, high[None], block)
    return picked.reshape(low.shape)


def route_kernel(n, cap, ents, dims, *refs):
    given, (out_ref, pos_ref, ent_ref, dlow_ref, dhigh_ref), held_refs, sems = refs[:4], refs[4:9], refs[9:13], refs[13]
    copies = [pltpu.make_async_copy(src, dst, sems.at[i]) for i, (src, dst) in enumerate(zip(given, held_refs))]
    for copy in copies:
        copy.start()
    for copy in copies:
        copy.wait()
    do_ref, ds_ref, fo_ref, fs_ref = held_refs
    chunks = do_ref.shape[0]
    owner = do_ref[...]
    kind = lax.broadcasted_iota(jnp.int32, (n, chunks, LANES), 0)
    held = jnp.where(kind == owner[None], 1.0, 0.0).reshape(n * chunks, LANES)
    held_bf = held.astype(BF)
    i0 = lax.broadcasted_iota(jnp.int32, (LANES, LANES), 0)
    i1 = lax.broadcasted_iota(jnp.int32, (LANES, LANES), 1)
    inside = dot(held_bf, flag(i0 < i1))
    r0 = lax.broadcasted_iota(jnp.int32, (n * chunks, n * chunks), 0)
    r1 = lax.broadcasted_iota(jnp.int32, (n * chunks, n * chunks), 1)
    earlier = flag((r0 // chunks == r1 // chunks) & (r1 < r0))
    before = dot(dot(earlier, held_bf).astype(BF), jnp.ones((LANES, LANES), BF))
    rank = jnp.sum((held * (inside + before)).reshape(n, chunks, LANES), axis=0)
    rank = rank.astype(jnp.int32)
    entity_owner = fo_ref[...]
    entity_slot = fs_ref[...]
    value = ds_ref[...]
    pos_ref[...] = owner * cap + rank
    ent_ref[...] = entity_owner * ents + entity_slot
    fact_dim = owner * dims + value
    high = (value >> 5).astype(F32)
    low = (value & 31).astype(F32)
    names = lax.broadcasted_iota(jnp.int32, (n, LANES), 0)
    places = lax.broadcasted_iota(jnp.int32, (cap, LANES), 0)
    slots = lax.broadcasted_iota(jnp.int32, (ents, LANES), 0)
    asked_high = jnp.zeros((n, cap), F32)
    asked_low = jnp.zeros((n, cap), F32)
    hits = jnp.zeros((n, ents), F32)
    for k in range(chunks):
        here = slice(k * LANES, (k + 1) * LANES)
        mine = jnp.where(names == owner[k : k + 1], 1.0, 0.0)
        at = flag(places == rank[k : k + 1])
        asked_high += nt((mine * high[k : k + 1]).astype(BF), at)
        asked_low += nt((mine * low[k : k + 1]).astype(BF), at)
        hits += nt(flag(names == entity_owner[k : k + 1]), flag(slots == entity_slot[k : k + 1]))
        dlow_ref[here, :], dhigh_ref[here, :] = column_codes(fact_dim[k : k + 1])
    asked = (asked_high * 32.0 + asked_low).astype(jnp.int32)
    for r in range(cap // LANES):
        out_ref[:, r, :] = asked[:, r * LANES : (r + 1) * LANES]
    out_ref[:, cap // LANES, :] = hits.astype(jnp.int32)


def gather_rows(low_ref, high_ref, rows, table_refs, firsts, hot_ref):
    at = 0
    low, high = low_ref[rows, :], high_ref[rows, :]
    for table, first in zip(table_refs, firsts):
        for k in range(table.shape[0] // LANES):
            hot_ref[:, at : at + LANES] = pick_block(low, high, (first + k).astype(F32).astype(BF))
            at += LANES
    total, at = None, 0
    for table in table_refs:
        part = dot(hot_ref[:, at : at + table.shape[0]], table[...])
        total = part if total is None else total + part
        at += table.shape[0]
    return total


def ring_at(place, n):
    place = lax.rem(place + 2 * n, n)
    return jnp.where(place < n // 2, 2 * place, 2 * (n - 1 - place) + 1)


def ring_place(index, n):
    half = lax.div(index, 2)
    return jnp.where(lax.rem(index, 2) == 0, half, n - 1 - half)


def look_kernel(n, pieces, low_ref, high_ref, *refs):
    count = len(pieces)
    tables, base_ref, out_ref, hot_ref = refs[:count], refs[count], refs[-2], refs[-1]
    facts = low_ref.shape[0]
    step = hot_ref.shape[0]
    place = ring_place(lax.axis_index("fact"), n)
    firsts = [lax.div(ring_at(place + hops, n) * dims + row, LANES) for hops, row, dims in pieces]
    for c in range(facts // step):
        rows = slice(c * step, (c + 1) * step)
        out_ref[rows, :] = base_ref[rows, :] + gather_rows(low_ref, high_ref, rows, tables, firsts, hot_ref)


def message_kernel(n, pieces, low_ref, high_ref, *refs):
    count = len(pieces)
    tables, refs = refs[:count], refs[count:]
    base_ref, xw_ref, ent_ref, slope_out, part_ref, slope_ref, hot_ref, msg_ref, erlow_ref, erhigh_ref = refs[:10]
    sem = refs[10]
    facts = low_ref.shape[0]
    step = hot_ref.shape[0]
    place = ring_place(lax.axis_index("fact"), n)
    firsts = [lax.div(ring_at(place + hops, n) * dims + row, LANES) for hops, row, dims in pieces]
    for k in range(ent_ref.shape[0]):
        here = slice(k * LANES, (k + 1) * LANES)
        erlow_ref[:, here], erhigh_ref[:, here] = row_codes(ent_ref[k : k + 1, :])
    for c in range(facts // step):
        rows = slice(c * step, (c + 1) * step)
        pre = xw_ref[rows, :] + base_ref[rows, :]
        if count:
            pre = pre + gather_rows(low_ref, high_ref, rows, tables, firsts, hot_ref)
        gate = jax.nn.sigmoid(pre)
        msg_ref[rows, :] = (pre * gate).astype(BF)
        slope_ref[rows, :] = gate * (1.0 + pre * (1.0 - gate))
    keep = pltpu.make_async_copy(slope_ref, slope_out, sem)
    keep.start()

    def add(pair, carry):
        hot = jnp.concatenate(
            [pick_rows(erlow_ref[...], erhigh_ref[...], (pair * 2 + i).astype(F32).astype(BF)) for i in range(2)], axis=0
        )
        rows = pl.ds(pl.multiple_of(pair * 256, 256), 256)
        part_ref[rows, :] = dot(hot, msg_ref[...]).astype(BF)
        return carry

    lax.fori_loop(0, part_ref.shape[0] // 256, add, 0)
    keep.wait()


def project_kernel(m, w_ref, *refs):
    blocks, out_ref = refs[:m], refs[m]
    me = lax.axis_index("feat")
    total = None
    for j, ref in enumerate(blocks):
        rows = pl.ds(pl.multiple_of((me ^ j) * LANES, LANES), LANES)
        part = dot(ref[...], w_ref[rows, :])
        total = part if total is None else total + part
    out_ref[...] = total


def ready_kernel(m, width, ents, *refs):
    x_refs, all_refs, (hidden_ref, xt_ref) = refs[:m], refs[m : 2 * m], refs[2 * m :]
    me = lax.axis_index("feat")
    for j in range(m):
        hidden_ref[me ^ j] = all_refs[j][2 * width : 2 * width + ents, :]
        xt_ref[pl.ds(pl.multiple_of((me ^ j) * LANES, LANES), LANES), :] = x_refs[j][...].T


def entity_kernel(n, m, width, ents, sums_ref, idx_ref, *refs):
    all_refs, (back_ref, out_ref, pre_ref, agg_ref, own_ref, hold_ref, words_ref, sem) = refs[:m], refs[m:]
    fetch = pltpu.make_async_copy(idx_ref, words_ref, sem)
    fetch.start()
    rows_each = ents // m
    me = lax.axis_index("feat")
    totals = []
    for b in range(m):
        total = sums_ref[b].astype(F32)
        for f in range(1, n):
            total += sums_ref[f * m + b].astype(F32)
        totals.append(total)
    fetch.wait()
    hits = jnp.sum(words_ref[:, words_ref.shape[1] - 1, :], axis=0, keepdims=True).astype(F32)
    hold_ref[...] = jnp.maximum(jnp.broadcast_to(hits, (LANES, ents)).T, 1.0)
    divisor = hold_ref[pl.ds(pl.multiple_of(me * rows_each, rows_each), rows_each), :]
    for b in range(m):
        agg_ref[b * rows_each : (b + 1) * rows_each, :] = (totals[b] / divisor).astype(BF)
    at = pl.multiple_of(2 * width + me * rows_each, rows_each)
    for j in range(m):
        own_ref[me ^ j] = all_refs[j][pl.ds(at, rows_each), :]
    aggregate = jnp.concatenate([agg_ref[b * rows_each : (b + 1) * rows_each, :] for b in range(m)], axis=1)
    hidden = jnp.concatenate([own_ref[b] for b in range(m)], axis=1)
    d_agg = None
    for j in range(m):
        pre = dot(hidden, all_refs[j][0:width, :]) + dot(aggregate, all_refs[j][width : 2 * width, :])
        gate = jax.nn.sigmoid(pre)
        cot = all_refs[j][pl.ds(at + ents, rows_each), :].astype(F32)
        d_pre = (cot * (gate * (1.0 + pre * (1.0 - gate)))).astype(BF)
        out_ref[me ^ j] = (pre * gate).astype(BF)
        pre_ref[me ^ j] = d_pre
        term = nt(d_pre, all_refs[j][width : 2 * width, :])
        d_agg = term if d_agg is None else d_agg + term
    for b in range(m):
        scaled = (d_agg[:, b * LANES : (b + 1) * LANES] / divisor).astype(BF)
        for f in range(n):
            back_ref[f * m + b] = scaled


def share_kernel(m, out_ref, pre_ref, agg_ref, *share_refs):
    rows_each = out_ref.shape[1]
    me = lax.axis_index("feat")
    for j, ref in enumerate(share_refs):
        ref[0:rows_each, :] = out_ref[me ^ j]
        ref[rows_each : 2 * rows_each, :] = pre_ref[me ^ j]
        ref[2 * rows_each :, :] = agg_ref[...]


def weight_kernel(n, m, width, stride, hidden_ref, *refs):
    got, (out_ref, back_ref, total_ref, pre_ref, agg_ref) = refs[:m], refs[m:]
    rows_each = got[0].shape[0] // (2 + m)
    own = width // n
    me = lax.axis_index("feat")
    for j, ref in enumerate(got):
        here = pl.ds(pl.multiple_of((me ^ j) * rows_each, rows_each), rows_each)
        out_ref[here, :] = ref[0:rows_each, :]
        pre_ref[here, :] = ref[rows_each : 2 * rows_each, :]
        for b in range(m):
            agg_ref[b, here, :] = ref[(2 + b) * rows_each : (3 + b) * rows_each, :]
    d_pre = pre_ref[...]
    for which, blocks in enumerate((hidden_ref, agg_ref)):
        for b in range(m):
            total_ref[b * LANES : (b + 1) * LANES, :] = tn(blocks[b], d_pre)
        for d in range(n):
            back_ref[d % 2, d // 2, which * stride : (which + 1) * stride, :] = padded(
                total_ref[d * own : (d + 1) * own, :], stride
            )


def halves_kernel(back_ref, keep_ref, give_ref):
    odd = lax.rem(lax.axis_index("fact"), 2)
    keep_ref[...] = back_ref[odd]
    give_ref[...] = back_ref[1 - odd].astype(BF)


def padded(piece, rows):
    if piece.shape[0] == rows:
        return piece
    return jnp.concatenate([piece, jnp.zeros((rows - piece.shape[0], LANES), F32)], axis=0)


def codes_kernel(pos_ref, ent_ref, plow_ref, phigh_ref, elow_ref, ehigh_ref):
    for k in range(pos_ref.shape[0]):
        here = slice(k * LANES, (k + 1) * LANES)
        plow_ref[:, here], phigh_ref[:, here] = row_codes(pos_ref[k : k + 1, :])
        elow_ref[here, :], ehigh_ref[here, :] = column_codes(ent_ref[k : k + 1, :])


def request_kernel(n, cap, req_ref, low_ref, high_ref):
    for s in range(n):
        for r in range(cap // LANES):
            at = s * cap + r * LANES
            low_ref[:, at : at + LANES], high_ref[:, at : at + LANES] = row_codes(req_ref[s, r : r + 1, :])


def backward_kernel(n, stride, slope_in, scaled_ref, low_ref, high_ref, xt_ref, dmsg_ref, share_ref, hot_ref, slope_ref, sem):
    fetch = pltpu.make_async_copy(slope_in, slope_ref, sem)
    fetch.start()
    facts = slope_ref.shape[0]
    own = xt_ref.shape[0] // n
    step = hot_ref.shape[0]
    for c in range(facts // step):
        rows = slice(c * step, (c + 1) * step)
        found = gather_rows(low_ref, high_ref, rows, [scaled_ref], [jnp.int32(0)], hot_ref)
        if c == 0:
            fetch.wait()
        dmsg_ref[rows, :] = (found * slope_ref[rows, :]).astype(BF)
    total = dot(xt_ref[...], dmsg_ref[...])
    for d in range(n):
        share_ref[d] = padded(total[d * own : (d + 1) * own, :], stride).astype(BF)


def spread_kernel(n, cap, stride, offsets, plow_ref, phigh_ref, dmsg_ref, share_ref, *refs):
    pair_refs, out_refs = refs[:-len(offsets)], refs[-len(offsets) :]
    me = lax.axis_index("fact")
    for offset, out_ref in zip(offsets, out_refs):
        d = lax.rem(me + offset, n)
        hot = jnp.concatenate(
            [
                pick_rows(plow_ref[...], phigh_ref[...], (d * (cap // LANES) + i).astype(F32).astype(BF))
                for i in range(cap // LANES)
            ],
            axis=0,
        )
        out_ref[0:cap, :] = dot(hot, dmsg_ref[...]).astype(BF)
        out_ref[cap : cap + stride, :] = share_ref[d]
        if out_ref.shape[0] > cap + stride:
            pair = pair_refs[0][lax.div(d, 2)]
            for ref in pair_refs[1:]:
                pair = pair + ref[lax.div(d, 2)].astype(F32)
            out_ref[cap + stride :, :] = pair.astype(BF)


def table_kernel(n, cap, stride, offsets, first, final, low_ref, high_ref, *refs):
    count = len(offsets)
    got, refs = refs[:count], refs[count:]
    if not first:
        (base_ref, weight_base_ref), refs = refs[:2], refs[2:]
    out_ref, refs = refs[0], refs[1:]
    final_refs, refs = (refs[:3], refs[3:]) if final else ((), refs[1:] + refs[:1])
    rows_ref, klow_ref, khigh_ref, weight_ref = refs[:4]
    me = lax.axis_index("fact")
    if first:
        weight_ref[...] = jnp.zeros(weight_ref.shape, F32)
    else:
        weight_ref[...] = weight_base_ref[...]
    for j, (offset, ref) in enumerate(zip(offsets, got)):
        source = lax.rem(me + (n - offset), n)
        here = slice(j * cap, (j + 1) * cap)
        there = pl.ds(pl.multiple_of(source * cap, LANES), cap)
        rows_ref[here, :] = ref[0:cap, :]
        klow_ref[:, here] = low_ref[:, there]
        khigh_ref[:, here] = high_ref[:, there]
        rows = ref.shape[0] - cap
        weight_ref[0:rows, :] += ref[cap:, :].astype(F32)
    copies = []
    for which, ref in enumerate(final_refs):
        copies.append(
            pltpu.make_async_copy(
                weight_ref.at[which * stride : which * stride + ref.shape[0], :], ref, refs[6].at[which]
            )
        )
        copies[-1].start()
    blocks = out_ref.shape[0] // LANES
    join = 2 if blocks % 2 == 0 else 1

    target_ref = refs[4] if final else out_ref
    for group in range(blocks // join):
        hot = jnp.concatenate(
            [pick_rows(klow_ref[...], khigh_ref[...], jnp.array(group * join + i, BF)) for i in range(join)], axis=0
        )
        rows = slice(group * join * LANES, (group + 1) * join * LANES)
        sums = dot(hot, rows_ref[...])
        target_ref[rows, :] = sums if first else base_ref[rows, :] + sums
        if final:
            copies.append(pltpu.make_async_copy(target_ref.at[rows, :], out_ref.at[rows, :], refs[5].at[group]))
            copies[-1].start()
    for copy in copies:
        copy.wait()


def shards(fact_x, dim_owner, dim_slot, fact_owner, fact_slot, dim_table, entity_h, w_msg, w_self, w_neigh, cotangent):
    n, m = lax.axis_size("fact"), lax.axis_size("feat")
    assert m == 4 and n % 2 == 0
    facts = fact_x.shape[0]
    chunks = facts // LANES
    ents = entity_h.shape[0]
    rows_each = ents // m
    width = w_msg.shape[0]
    dims = dim_table.shape[0]
    cap = -(-(3 * facts // n) // LANES) * LANES
    slots = n * cap
    groups = cap // LANES + 1
    own = width // n
    stride = max(16, own)
    step = 512
    tie = lax.optimization_barrier
    ringed = n <= 8
    limit = VMEM_LIMIT if ringed else VMEM_LIMIT_LARGE

    ring = [2 * p if p < n // 2 else 2 * (n - 1 - p) + 1 for p in range(n)]
    to_right = [(ring[p], ring[(p + 1) % n]) for p in range(n)]
    to_left = [(ring[(p + 1) % n], ring[p]) for p in range(n)]

    def pass_on(right, left):
        return lax.ppermute(right, "fact", to_right), lax.ppermute(left, "fact", to_left)

    def swap(block, bit):
        return lax.ppermute(block, "feat", [(i, i ^ bit) for i in range(m)])

    if ringed:
        right, left = pass_on(dim_table, dim_table)
    x_near = swap(fact_x, 1)
    by_lane = (chunks, LANES)
    columns = shape((facts, LANES), BF)
    asks, pos, entity, dlow, dhigh = call(
        functools.partial(route_kernel, n, cap, ents, dims),
        (
            shape((n, groups, LANES), jnp.int32),
            shape(by_lane, jnp.int32),
            shape(by_lane, jnp.int32),
            columns,
            columns,
        ),
        [pltpu.VMEM(by_lane, jnp.int32)] * 4 + [pltpu.SemaphoreType.DMA((4,))],
        1 << 28,
        "route",
        in_specs=[IN_HBM] * 4,
    )(dim_owner.reshape(by_lane), dim_slot.reshape(by_lane), fact_owner.reshape(by_lane), fact_slot.reshape(by_lane))
    if ringed:
        right, left, x_near, asks, pos, entity, dlow, dhigh = tie(
            (right, left, x_near, asks, pos, entity, dlow, dhigh)
        )

    def look(pieces, tables, base):
        rows = sum(t.shape[0] for t in tables)
        return call(
            functools.partial(look_kernel, n, pieces),
            shape((facts, LANES), F32),
            [pltpu.VMEM((step, rows), BF)],
            2 * facts * rows * LANES,
            "look",
            limit,
        )(dlow, dhigh, *tables, base)

    def project(blocks):
        return call(
            functools.partial(project_kernel, m), shape((facts, LANES), F32), [], 2 * facts * width * LANES, "project"
        )(w_msg, *blocks)

    found = jnp.zeros((facts, LANES), F32)
    weights = jnp.concatenate([w_self, w_neigh, entity_h, cotangent], axis=0)
    if ringed:
        near = (right, left)
        after = pass_on(*near)
        x_far = swap(fact_x, 2)
        found = look([(0, 0, dims), (-1, 0, dims), (1, 0, dims)], [dim_table, *near], found)
        right, left, x_far, found, weights = tie((*after, x_far, found, weights))
        for k in range(2, n // 2 - 1):
            after = pass_on(right, left)
            x_last = swap(x_far, 1)
            found = look([(-k, 0, dims), (k, 0, dims)], [right, left], found)
            found, asks = tie((found, asks))
            right, left, found, x_last = tie((*after, found, x_last))
        all_far = swap(weights, 2)
        asked = lax.all_to_all(asks, "fact", 0, 0)
        k = n // 2 - 1
        after = lax.ppermute(right, "fact", to_right)
        xw = project([fact_x, x_near, x_far, x_last])
        found = look([(k, 0, dims)], [left], found)
        found, asked = tie((found, asked))
        found = look([(-k, 0, dims)], [right], found)
        all_near = swap(weights, 1)
        found, all_far, all_near = tie((found, all_far, all_near))
        last, last_pieces = [pltpu.with_memory_space_constraint(after, pltpu.VMEM)], [(n // 2, 0, dims)]
    else:
        asked = lax.all_to_all(asks, "fact", 0, 0)
        x_far = swap(fact_x, 2)
        x_last = swap(x_far, 1)
        xw = project([fact_x, x_near, x_far, x_last])
        all_far, all_near = swap(weights, 2), swap(weights, 1)
        whole = lax.all_gather(dim_table, "fact")
        order = jnp.take(whole, ring_at(ring_place(lax.axis_index("fact"), n) + jnp.arange(n), n), axis=0)
        for k in range(0, n, 8):
            found = look([(k + i, 0, dims) for i in range(8)], [order[k + i] for i in range(8)], found)
        last, last_pieces = [], []
    all_last = swap(all_far, 1)
    x_blocks, all_blocks = [fact_x, x_near, x_far, x_last], [weights, all_near, all_far, all_last]
    last_rows = max(LANES, sum(t.shape[0] for t in last))
    slope, part = call(
        functools.partial(message_kernel, n, last_pieces),
        (pltpu.HBM((facts, LANES), F32), shape((n * ents, LANES), BF)),
        [
            pltpu.VMEM((facts, LANES), F32),
            pltpu.VMEM((step, last_rows), BF),
            pltpu.VMEM((facts, LANES), BF),
            pltpu.VMEM((LANES, facts), BF),
            pltpu.VMEM((16, facts), BF),
            pltpu.SemaphoreType.DMA,
        ],
        2 * facts * (last_rows + n * ents) * LANES,
        "message",
        limit,
        in_specs=[IN_VMEM] * (5 + len(last)),
        out_specs=(IN_HBM, IN_VMEM),
    )(dlow, dhigh, *last, found, xw, entity)
    sums = lax.all_to_all(part.reshape(n * m, rows_each, LANES), ("fact", "feat"), 0, 0)
    pos, entity, x_blocks, _ = tie((pos, entity, x_blocks, part))
    hidden, x_turned = call(
        functools.partial(ready_kernel, m, width, ents),
        (shape((m, ents, LANES), BF), shape((width, facts), BF)),
        [],
        1 << 28,
        "ready",
    )(*x_blocks, *all_blocks)
    by_feat = shape((m, rows_each, LANES), BF)
    back, out_parts, pre_parts, agg_parts = call(
        functools.partial(entity_kernel, n, m, width, ents),
        (shape((n * m, rows_each, LANES), BF), by_feat, by_feat, shape((m * rows_each, LANES), BF)),
        [
            pltpu.VMEM((m, rows_each, LANES), BF),
            pltpu.VMEM((ents, LANES), F32),
            pltpu.VMEM(asked.shape, jnp.int32),
            pltpu.SemaphoreType.DMA,
        ],
        6 * rows_each * width * width,
        "entity",
        in_specs=[IN_VMEM, pl.BlockSpec(memory_space=pl.ANY)] + [IN_VMEM] * m,
    )(sums, asked, *all_blocks)
    scaled = lax.all_to_all(back, ("fact", "feat"), 0, 0).reshape(n * ents, LANES)
    shares = call(
        functools.partial(share_kernel, m),
        tuple(shape(((2 + m) * rows_each, LANES), BF) for _ in range(m)),
        [],
        1 << 20,
        "share",
    )(out_parts, pre_parts, agg_parts)
    got = [shares[0]] + [swap(shares[j], j) for j in range(1, m)]
    pos, entity, asked, _ = tie((pos, entity, asked, back))
    plow, phigh, elow, ehigh = call(
        codes_kernel,
        (shape((LANES, facts), BF), shape((16, facts), BF), columns, columns),
        [],
        1 << 26,
        "codes",
    )(pos, entity)
    rlow, rhigh = call(
        functools.partial(request_kernel, n, cap),
        (shape((LANES, slots), BF), shape((16, slots), BF)),
        [],
        1 << 26,
        "requests",
        limit,
    )(asked)
    pair_shape = (n // 2, 2 * stride, LANES)
    output_h, pair = call(
        functools.partial(weight_kernel, n, m, width, stride),
        (shape((ents, LANES), BF), shape((2, *pair_shape), F32)),
        [pltpu.VMEM((width, LANES), F32), pltpu.VMEM((ents, LANES), BF), pltpu.VMEM((m, ents, LANES), BF)],
        4 * ents * width * LANES,
        "weight",
    )(hidden, *got)
    if ringed:
        keep, give = call(halves_kernel, (shape(pair_shape, F32), shape(pair_shape, BF)), [], 1 << 20, "halves")(pair)
        pairs = [keep, lax.ppermute(give, "fact", [(i, i ^ 1) for i in range(n)])]
    else:
        pairs = [jnp.stack([pair[0], pair[1]], axis=1).reshape(n, 2 * stride, LANES)]
    d_msg, msg_share = call(
        functools.partial(backward_kernel, n, stride),
        (columns, shape((n, stride, LANES), BF)),
        [pltpu.VMEM((step, n * ents), BF), pltpu.VMEM((facts, LANES), F32), pltpu.SemaphoreType.DMA],
        2 * facts * (n * ents + width) * LANES,
        "backward",
        limit,
        in_specs=[IN_HBM] + [IN_VMEM] * 4,
    )(slope, scaled, elow, ehigh, x_turned)

    def spread(offsets):
        lengths = [cap + (3 if ringed and k % 2 == 0 else 1) * stride for k in offsets]
        return call(
            functools.partial(spread_kernel, n, cap, stride, offsets),
            tuple(shape((rows, LANES), BF) for rows in lengths),
            [],
            2 * facts * cap * LANES * len(offsets),
            "spread",
            limit,
        )(plow, phigh, d_msg, msg_share, *(pairs if max(lengths) > cap + stride else ()))

    def add_up(offsets, got, base, final):
        weight = shape((3 * stride, LANES), F32)
        scratch = [
            pltpu.VMEM((cap * len(got), LANES), BF),
            pltpu.VMEM((LANES, cap * len(got)), BF),
            pltpu.VMEM((16, cap * len(got)), BF),
        ]
        return call(
            functools.partial(table_kernel, n, cap, stride, offsets, base is None, final),
            (shape((dims, LANES), F32),) + ((shape((own, LANES), F32),) * 3 if final else (weight,)),
            scratch
            + (
                [
                    pltpu.VMEM(weight.shape, F32),
                    pltpu.VMEM((dims, LANES), F32),
                    pltpu.SemaphoreType.DMA((dims // LANES,)),
                    pltpu.SemaphoreType.DMA((3,)),
                ]
                if final
                else []
            ),
            2 * cap * dims * LANES * len(got),
            "table",
            limit,
            **(dict(out_specs=(IN_HBM,) * 4) if final else {}),
        )(rlow, rhigh, *got, *(base or ()))

    totals = None
    if ringed:
        messages = {}
        rest = [[k, n - k] for k in range(n // 2 - 1, 1, -1)]
        for offsets in [rest[0], [n // 2], [1, n - 1], *rest[1:]]:
            for offset, message in zip(offsets, spread(offsets)):
                messages[offset] = lax.ppermute(message, "fact", [(i, (i + offset) % n) for i in range(n)])
        messages[0] = spread([0])[0]
        for offsets in [[0, 1, n - 1], [n // 2], *rest[::-1]]:
            totals = add_up(offsets, [messages[k] for k in offsets], totals, offsets == rest[0])
        grad_dim, grad_msg, grad_self, grad_neigh = totals
    else:
        fact_me = lax.axis_index("fact")
        sent = [message for k in range(0, n, 8) for message in spread(list(range(k, k + 8)))]
        by_owner = jnp.take(jnp.stack(sent), lax.rem(jnp.arange(n) - fact_me + n, n), axis=0)
        owned = lax.all_to_all(by_owner, "fact", 0, 0)
        by_offset = jnp.take(owned, lax.rem(fact_me - jnp.arange(n) + n, n), axis=0)
        for k in range(0, n, 8):
            totals = add_up(list(range(k, k + 8)), [by_offset[k + i] for i in range(8)], totals, k + 8 >= n)
        grad_dim, grad_msg, _, _ = totals
        pair_sum = lax.psum_scatter(pairs[0], "fact", scatter_dimension=0, tiled=True)[0]
        grad_self, grad_neigh = pair_sum[0:own], pair_sum[stride : stride + own]
    return output_h, grad_msg, grad_self, grad_neigh, grad_dim


def solution(mesh):
    placed = (
        P("fact", "feat"),
        P("fact", None),
        P("fact"),
        P("fact", None),
        P("fact"),
        P("fact", "feat"),
        P("fact", "feat"),
        P(None, "feat"),
        P(None, "feat"),
        P(None, "feat"),
        P("fact", "feat"),
    )
    return jax.shard_map(
        shards,
        mesh=mesh,
        in_specs=placed,
        out_specs=(P("fact", "feat"),) * 5,
        check_vma=False,
    )
```

```python
import functools

import jax
import jax.numpy as jnp
from jax import lax
from jax.experimental import pallas as pl
from jax.experimental.pallas import tpu as pltpu
from jax.sharding import PartitionSpec as P

LANES = 128
BF = jnp.bfloat16
IN_HBM = pl.BlockSpec(memory_space=pltpu.HBM)
IN_VMEM = pl.BlockSpec(memory_space=pltpu.VMEM)
F32 = jnp.float32
VMEM_LIMIT = 16 * 1024 * 1024
VMEM_LIMIT_LARGE = 40 * 1024 * 1024


def call(kernel, out_shape, scratch, flops, name, limit=VMEM_LIMIT, **specs):
    return pl.pallas_call(
        kernel,
        out_shape=out_shape,
        scratch_shapes=scratch,
        compiler_params=pltpu.CompilerParams(vmem_limit_bytes=limit),
        cost_estimate=pl.CostEstimate(flops=flops, bytes_accessed=1 << 20, transcendentals=0),
        name=name,
        **specs,
    )


def shape(dims, dtype):
    return jax.ShapeDtypeStruct(dims, dtype)


def nt(a, b):
    return lax.dot_general(a, b, (((1,), (1,)), ((), ())), preferred_element_type=F32)


def tn(a, b):
    return lax.dot_general(a, b, (((0,), (0,)), ((), ())), preferred_element_type=F32)


def dot(a, b):
    return jnp.dot(a, b, preferred_element_type=F32)


def flag(condition):
    return jnp.where(condition, 1.0, 0.0).astype(BF)


def column_codes(row):
    keys = jnp.broadcast_to(row, (LANES, LANES)).astype(F32).T.astype(jnp.int32)
    lane = lax.broadcasted_iota(jnp.int32, (LANES, LANES), 1)
    return flag((keys & (LANES - 1)) == lane), (keys >> 7).astype(F32).astype(BF)


def row_codes(row):
    keys = jnp.broadcast_to(row, (LANES, LANES))
    sub = lax.broadcasted_iota(jnp.int32, (LANES, LANES), 0)
    high = jnp.broadcast_to((row >> 7).astype(F32), (16, LANES)).astype(BF)
    return flag((keys & (LANES - 1)) == sub), high


def pick_block(low, high, block):
    zero = jnp.zeros((), BF)
    return jnp.where(high == block, low, zero)


def pick_rows(low, high, block):
    wide = low.reshape(LANES // 16, 16, low.shape[1])
    picked = pick_block(wide, high[None], block)
    return picked.reshape(low.shape)


def route_kernel(n, cap, ents, dims, *refs):
    given, (out_ref, pos_ref, ent_ref, dlow_ref, dhigh_ref), held_refs, sems = refs[:4], refs[4:9], refs[9:13], refs[13]
    copies = [pltpu.make_async_copy(src, dst, sems.at[i]) for i, (src, dst) in enumerate(zip(given, held_refs))]
    for copy in copies:
        copy.start()
    for copy in copies:
        copy.wait()
    do_ref, ds_ref, fo_ref, fs_ref = held_refs
    chunks = do_ref.shape[0]
    owner = do_ref[...]
    kind = lax.broadcasted_iota(jnp.int32, (n, chunks, LANES), 0)
    held = jnp.where(kind == owner[None], 1.0, 0.0).reshape(n * chunks, LANES)
    held_bf = held.astype(BF)
    i0 = lax.broadcasted_iota(jnp.int32, (LANES, LANES), 0)
    i1 = lax.broadcasted_iota(jnp.int32, (LANES, LANES), 1)
    inside = dot(held_bf, flag(i0 < i1))
    r0 = lax.broadcasted_iota(jnp.int32, (n * chunks, n * chunks), 0)
    r1 = lax.broadcasted_iota(jnp.int32, (n * chunks, n * chunks), 1)
    earlier = flag((r0 // chunks == r1 // chunks) & (r1 < r0))
    before = dot(dot(earlier, held_bf).astype(BF), jnp.ones((LANES, LANES), BF))
    rank = jnp.sum((held * (inside + before)).reshape(n, chunks, LANES), axis=0)
    rank = rank.astype(jnp.int32)
    entity_owner = fo_ref[...]
    entity_slot = fs_ref[...]
    value = ds_ref[...]
    pos_ref[...] = owner * cap + rank
    ent_ref[...] = entity_owner * ents + entity_slot
    fact_dim = owner * dims + value
    high = (value >> 5).astype(F32)
    low = (value & 31).astype(F32)
    names = lax.broadcasted_iota(jnp.int32, (n, LANES), 0)
    places = lax.broadcasted_iota(jnp.int32, (cap, LANES), 0)
    slots = lax.broadcasted_iota(jnp.int32, (ents, LANES), 0)
    asked_high = jnp.zeros((n, cap), F32)
    asked_low = jnp.zeros((n, cap), F32)
    hits = jnp.zeros((n, ents), F32)
    for k in range(chunks):
        here = slice(k * LANES, (k + 1) * LANES)
        mine = jnp.where(names == owner[k : k + 1], 1.0, 0.0)
        at = flag(places == rank[k : k + 1])
        asked_high += nt((mine * high[k : k + 1]).astype(BF), at)
        asked_low += nt((mine * low[k : k + 1]).astype(BF), at)
        hits += nt(flag(names == entity_owner[k : k + 1]), flag(slots == entity_slot[k : k + 1]))
        dlow_ref[here, :], dhigh_ref[here, :] = column_codes(fact_dim[k : k + 1])
    asked = (asked_high * 32.0 + asked_low).astype(jnp.int32)
    for r in range(cap // LANES):
        out_ref[:, r, :] = asked[:, r * LANES : (r + 1) * LANES]
    out_ref[:, cap // LANES, :] = hits.astype(jnp.int32)


def gather_rows(low_ref, high_ref, rows, table_refs, firsts, hot_ref):
    at = 0
    low, high = low_ref[rows, :], high_ref[rows, :]
    for table, first in zip(table_refs, firsts):
        for k in range(table.shape[0] // LANES):
            hot_ref[:, at : at + LANES] = pick_block(low, high, (first + k).astype(F32).astype(BF))
            at += LANES
    total, at = None, 0
    for table in table_refs:
        part = dot(hot_ref[:, at : at + table.shape[0]], table[...])
        total = part if total is None else total + part
        at += table.shape[0]
    return total


def ring_at(place, n):
    place = lax.rem(place + 2 * n, n)
    return jnp.where(place < n // 2, 2 * place, 2 * (n - 1 - place) + 1)


def ring_place(index, n):
    half = lax.div(index, 2)
    return jnp.where(lax.rem(index, 2) == 0, half, n - 1 - half)


def look_kernel(n, pieces, low_ref, high_ref, *refs):
    count = len(pieces)
    tables, base_ref, out_ref, hot_ref = refs[:count], refs[count], refs[-2], refs[-1]
    facts = low_ref.shape[0]
    step = hot_ref.shape[0]
    place = ring_place(lax.axis_index("fact"), n)
    firsts = [lax.div(ring_at(place + hops, n) * dims + row, LANES) for hops, row, dims in pieces]
    for c in range(facts // step):
        rows = slice(c * step, (c + 1) * step)
        out_ref[rows, :] = base_ref[rows, :] + gather_rows(low_ref, high_ref, rows, tables, firsts, hot_ref)


def message_kernel(n, pieces, low_ref, high_ref, *refs):
    count = len(pieces)
    sources, refs = refs[:count], refs[count:]
    base_ref, xw_ref, ent_ref, slope_out, part_ref, slope_ref, hot_ref, msg_ref, erlow_ref, erhigh_ref = refs[:10]
    tables, (sem, table_sem) = refs[10 : 10 + count], refs[10 + count :]
    arrivals = [pltpu.make_async_copy(src, dst, table_sem) for src, dst in zip(sources, tables)]
    for copy in arrivals:
        copy.start()
    facts = low_ref.shape[0]
    step = hot_ref.shape[0]
    place = ring_place(lax.axis_index("fact"), n)
    firsts = [lax.div(ring_at(place + hops, n) * dims + row, LANES) for hops, row, dims in pieces]
    for k in range(ent_ref.shape[0]):
        here = slice(k * LANES, (k + 1) * LANES)
        erlow_ref[:, here], erhigh_ref[:, here] = row_codes(ent_ref[k : k + 1, :])
    for copy in arrivals:
        copy.wait()
    kept = []
    for c in range(facts // step):
        rows = slice(c * step, (c + 1) * step)
        pre = xw_ref[rows, :] + base_ref[rows, :]
        if count:
            pre = pre + gather_rows(low_ref, high_ref, rows, tables, firsts, hot_ref)
        gate = jax.nn.sigmoid(pre)
        msg_ref[rows, :] = (pre * gate).astype(BF)
        slope_ref[rows, :] = gate * (1.0 + pre * (1.0 - gate))
        kept.append(pltpu.make_async_copy(slope_ref.at[rows, :], slope_out.at[rows, :], sem.at[c]))
        kept[-1].start()

    def add(pair, carry):
        hot = jnp.concatenate(
            [pick_rows(erlow_ref[...], erhigh_ref[...], (pair * 2 + i).astype(F32).astype(BF)) for i in range(2)], axis=0
        )
        rows = pl.ds(pl.multiple_of(pair * 256, 256), 256)
        part_ref[rows, :] = dot(hot, msg_ref[...]).astype(BF)
        return carry

    lax.fori_loop(0, part_ref.shape[0] // 256, add, 0)
    for copy in kept:
        copy.wait()


def project_kernel(m, w_ref, *refs):
    blocks, out_ref = refs[:m], refs[m]
    me = lax.axis_index("feat")
    total = None
    for j, ref in enumerate(blocks):
        rows = pl.ds(pl.multiple_of((me ^ j) * LANES, LANES), LANES)
        part = dot(ref[...], w_ref[rows, :])
        total = part if total is None else total + part
    out_ref[...] = total


def ready_kernel(m, width, ents, *refs):
    x_refs, all_refs, (hidden_ref, xt_ref) = refs[:m], refs[m : 2 * m], refs[2 * m :]
    me = lax.axis_index("feat")
    for j in range(m):
        hidden_ref[me ^ j] = all_refs[j][2 * width : 2 * width + ents, :]
        xt_ref[pl.ds(pl.multiple_of((me ^ j) * LANES, LANES), LANES), :] = x_refs[j][...].T


def own_kernel(m, width, ents, *refs):
    all_refs, (self_ref, own_ref) = refs[:m], refs[m:]
    rows_each = ents // m
    me = lax.axis_index("feat")
    at = pl.multiple_of(2 * width + me * rows_each, rows_each)
    for j in range(m):
        own_ref[me ^ j] = all_refs[j][pl.ds(at, rows_each), :]
    hidden = jnp.concatenate([own_ref[b] for b in range(m)], axis=1)
    for j in range(m):
        self_ref[j] = dot(hidden, all_refs[j][0:width, :])


def entity_kernel(n, m, width, ents, sums_ref, idx_ref, self_in, *refs):
    all_refs, refs = refs[:m], refs[m:]
    back_ref, out_ref, pre_ref, agg_ref, self_ref, hold_ref, words_ref, sems = refs
    fetches = [
        pltpu.make_async_copy(idx_ref, words_ref, sems.at[0]),
        pltpu.make_async_copy(self_in, self_ref, sems.at[1]),
    ]
    for fetch in fetches:
        fetch.start()
    rows_each = ents // m
    me = lax.axis_index("feat")
    totals = []
    for b in range(m):
        total = sums_ref[b].astype(F32)
        for f in range(1, n):
            total += sums_ref[f * m + b].astype(F32)
        totals.append(total)
    for fetch in fetches:
        fetch.wait()
    hits = jnp.sum(words_ref[:, words_ref.shape[1] - 1, :], axis=0, keepdims=True).astype(F32)
    hold_ref[...] = jnp.maximum(jnp.broadcast_to(hits, (LANES, ents)).T, 1.0)
    divisor = hold_ref[pl.ds(pl.multiple_of(me * rows_each, rows_each), rows_each), :]
    for b in range(m):
        agg_ref[b * rows_each : (b + 1) * rows_each, :] = (totals[b] / divisor).astype(BF)
    at = pl.multiple_of(2 * width + me * rows_each, rows_each)
    aggregate = jnp.concatenate([agg_ref[b * rows_each : (b + 1) * rows_each, :] for b in range(m)], axis=1)
    d_agg = None
    for j in range(m):
        pre = self_ref[j] + dot(aggregate, all_refs[j][width : 2 * width, :])
        gate = jax.nn.sigmoid(pre)
        cot = all_refs[j][pl.ds(at + ents, rows_each), :].astype(F32)
        d_pre = (cot * (gate * (1.0 + pre * (1.0 - gate)))).astype(BF)
        out_ref[me ^ j] = (pre * gate).astype(BF)
        pre_ref[me ^ j] = d_pre
        term = nt(d_pre, all_refs[j][width : 2 * width, :])
        d_agg = term if d_agg is None else d_agg + term
    for b in range(m):
        scaled = (d_agg[:, b * LANES : (b + 1) * LANES] / divisor).astype(BF)
        for f in range(n):
            back_ref[f * m + b] = scaled


def share_kernel(m, out_ref, pre_ref, agg_ref, *share_refs):
    rows_each = out_ref.shape[1]
    me = lax.axis_index("feat")
    for j, ref in enumerate(share_refs):
        ref[0:rows_each, :] = out_ref[me ^ j]
        ref[rows_each : 2 * rows_each, :] = pre_ref[me ^ j]
        ref[2 * rows_each :, :] = agg_ref[...]


def weight_kernel(n, m, width, stride, hidden_ref, *refs):
    got, (out_ref, back_ref, total_ref, pre_ref, agg_ref) = refs[:m], refs[m:]
    rows_each = got[0].shape[0] // (2 + m)
    own = width // n
    me = lax.axis_index("feat")
    for j, ref in enumerate(got):
        here = pl.ds(pl.multiple_of((me ^ j) * rows_each, rows_each), rows_each)
        out_ref[here, :] = ref[0:rows_each, :]
        pre_ref[here, :] = ref[rows_each : 2 * rows_each, :]
        for b in range(m):
            agg_ref[b, here, :] = ref[(2 + b) * rows_each : (3 + b) * rows_each, :]
    d_pre = pre_ref[...]
    for which, blocks in enumerate((hidden_ref, agg_ref)):
        for b in range(m):
            total_ref[b * LANES : (b + 1) * LANES, :] = tn(blocks[b], d_pre)
        for d in range(n):
            back_ref[d % 2, d // 2, which * stride : (which + 1) * stride, :] = padded(
                total_ref[d * own : (d + 1) * own, :], stride
            )


def halves_kernel(back_ref, keep_ref, give_ref):
    odd = lax.rem(lax.axis_index("fact"), 2)
    keep_ref[...] = back_ref[odd]
    give_ref[...] = back_ref[1 - odd].astype(BF)


def padded(piece, rows):
    if piece.shape[0] == rows:
        return piece
    return jnp.concatenate([piece, jnp.zeros((rows - piece.shape[0], LANES), F32)], axis=0)


def codes_kernel(pos_ref, ent_ref, plow_ref, phigh_ref, elow_ref, ehigh_ref):
    for k in range(pos_ref.shape[0]):
        here = slice(k * LANES, (k + 1) * LANES)
        plow_ref[:, here], phigh_ref[:, here] = row_codes(pos_ref[k : k + 1, :])
        elow_ref[here, :], ehigh_ref[here, :] = column_codes(ent_ref[k : k + 1, :])


def request_kernel(n, cap, req_ref, low_ref, high_ref):
    for s in range(n):
        for r in range(cap // LANES):
            at = s * cap + r * LANES
            low_ref[:, at : at + LANES], high_ref[:, at : at + LANES] = row_codes(req_ref[s, r : r + 1, :])


def backward_kernel(n, stride, slope_in, scaled_ref, low_ref, high_ref, xt_ref, dmsg_ref, share_ref, hot_ref, slope_ref, sem):
    fetch = pltpu.make_async_copy(slope_in, slope_ref, sem)
    fetch.start()
    facts = slope_ref.shape[0]
    own = xt_ref.shape[0] // n
    step = hot_ref.shape[0]
    for c in range(facts // step):
        rows = slice(c * step, (c + 1) * step)
        found = gather_rows(low_ref, high_ref, rows, [scaled_ref], [jnp.int32(0)], hot_ref)
        if c == 0:
            fetch.wait()
        dmsg_ref[rows, :] = (found * slope_ref[rows, :]).astype(BF)
    total = dot(xt_ref[...], dmsg_ref[...])
    for d in range(n):
        share_ref[d] = padded(total[d * own : (d + 1) * own, :], stride).astype(BF)


def spread_kernel(n, cap, stride, offsets, plow_ref, phigh_ref, dmsg_ref, share_ref, *refs):
    pair_refs, out_refs = refs[:-len(offsets)], refs[-len(offsets) :]
    me = lax.axis_index("fact")
    for offset, out_ref in zip(offsets, out_refs):
        d = lax.rem(me + offset, n)
        hot = jnp.concatenate(
            [
                pick_rows(plow_ref[...], phigh_ref[...], (d * (cap // LANES) + i).astype(F32).astype(BF))
                for i in range(cap // LANES)
            ],
            axis=0,
        )
        out_ref[0:cap, :] = dot(hot, dmsg_ref[...]).astype(BF)
        out_ref[cap : cap + stride, :] = share_ref[d]
        if out_ref.shape[0] > cap + stride:
            pair = pair_refs[0][lax.div(d, 2)]
            for ref in pair_refs[1:]:
                pair = pair + ref[lax.div(d, 2)].astype(F32)
            out_ref[cap + stride :, :] = pair.astype(BF)


def table_kernel(n, cap, stride, offsets, first, final, low_ref, high_ref, *refs):
    count = len(offsets)
    got, refs = refs[:count], refs[count:]
    if not first:
        (base_ref, weight_base_ref), refs = refs[:2], refs[2:]
    out_ref, refs = refs[0], refs[1:]
    final_refs, refs = (refs[:3], refs[3:]) if final else ((), refs[1:] + refs[:1])
    rows_ref, klow_ref, khigh_ref, weight_ref = refs[:4]
    me = lax.axis_index("fact")
    if first:
        weight_ref[...] = jnp.zeros(weight_ref.shape, F32)
    else:
        weight_ref[...] = weight_base_ref[...]
    for j, (offset, ref) in enumerate(zip(offsets, got)):
        source = lax.rem(me + (n - offset), n)
        here = slice(j * cap, (j + 1) * cap)
        there = pl.ds(pl.multiple_of(source * cap, LANES), cap)
        rows_ref[here, :] = ref[0:cap, :]
        klow_ref[:, here] = low_ref[:, there]
        khigh_ref[:, here] = high_ref[:, there]
        rows = ref.shape[0] - cap
        weight_ref[0:rows, :] += ref[cap:, :].astype(F32)
    copies = []
    for which, ref in enumerate(final_refs):
        copies.append(
            pltpu.make_async_copy(
                weight_ref.at[which * stride : which * stride + ref.shape[0], :], ref, refs[6].at[which]
            )
        )
        copies[-1].start()
    blocks = out_ref.shape[0] // LANES
    join = 2 if blocks % 2 == 0 else 1

    target_ref = refs[4] if final else out_ref
    for group in range(blocks // join):
        hot = jnp.concatenate(
            [pick_rows(klow_ref[...], khigh_ref[...], jnp.array(group * join + i, BF)) for i in range(join)], axis=0
        )
        rows = slice(group * join * LANES, (group + 1) * join * LANES)
        sums = dot(hot, rows_ref[...])
        target_ref[rows, :] = sums if first else base_ref[rows, :] + sums
        if final:
            copies.append(pltpu.make_async_copy(target_ref.at[rows, :], out_ref.at[rows, :], refs[5].at[group]))
            copies[-1].start()
    for copy in copies:
        copy.wait()


def shards(fact_x, dim_owner, dim_slot, fact_owner, fact_slot, dim_table, entity_h, w_msg, w_self, w_neigh, cotangent):
    n, m = lax.axis_size("fact"), lax.axis_size("feat")
    assert m == 4 and n % 2 == 0
    facts = fact_x.shape[0]
    chunks = facts // LANES
    ents = entity_h.shape[0]
    rows_each = ents // m
    width = w_msg.shape[0]
    dims = dim_table.shape[0]
    cap = -(-(3 * facts // n) // LANES) * LANES
    slots = n * cap
    groups = cap // LANES + 1
    own = width // n
    stride = max(16, own)
    step = 512
    tie = lax.optimization_barrier
    ringed = n <= 8
    limit = VMEM_LIMIT if ringed else VMEM_LIMIT_LARGE

    ring = [2 * p if p < n // 2 else 2 * (n - 1 - p) + 1 for p in range(n)]
    to_right = [(ring[p], ring[(p + 1) % n]) for p in range(n)]
    to_left = [(ring[(p + 1) % n], ring[p]) for p in range(n)]

    def pass_on(right, left):
        return lax.ppermute(right, "fact", to_right), lax.ppermute(left, "fact", to_left)

    def swap(block, bit):
        return lax.ppermute(block, "feat", [(i, i ^ bit) for i in range(m)])

    if ringed:
        right, left = pass_on(dim_table, dim_table)
    x_near = swap(fact_x, 1)
    by_lane = (chunks, LANES)
    columns = shape((facts, LANES), BF)
    asks, pos, entity, dlow, dhigh = call(
        functools.partial(route_kernel, n, cap, ents, dims),
        (
            shape((n, groups, LANES), jnp.int32),
            shape(by_lane, jnp.int32),
            shape(by_lane, jnp.int32),
            columns,
            columns,
        ),
        [pltpu.VMEM(by_lane, jnp.int32)] * 4 + [pltpu.SemaphoreType.DMA((4,))],
        1 << 28,
        "route",
        in_specs=[IN_HBM] * 4,
    )(dim_owner.reshape(by_lane), dim_slot.reshape(by_lane), fact_owner.reshape(by_lane), fact_slot.reshape(by_lane))
    if ringed:
        right, left, x_near, asks, pos, entity, dlow, dhigh = tie(
            (right, left, x_near, asks, pos, entity, dlow, dhigh)
        )

    def look(pieces, tables, base):
        rows = sum(t.shape[0] for t in tables)
        return call(
            functools.partial(look_kernel, n, pieces),
            shape((facts, LANES), F32),
            [pltpu.VMEM((step, rows), BF)],
            2 * facts * rows * LANES,
            "look",
            limit,
        )(dlow, dhigh, *tables, base)

    def project(blocks):
        return call(
            functools.partial(project_kernel, m), shape((facts, LANES), F32), [], 2 * facts * width * LANES, "project"
        )(w_msg, *blocks)

    found = jnp.zeros((facts, LANES), F32)
    weights = jnp.concatenate([w_self, w_neigh, entity_h, cotangent], axis=0)
    if ringed:
        near = (right, left)
        after = pass_on(*near)
        x_far = swap(fact_x, 2)
        found = look([(0, 0, dims), (-1, 0, dims), (1, 0, dims)], [dim_table, *near], found)
        right, left, x_far, found, weights = tie((*after, x_far, found, weights))
        for k in range(2, n // 2 - 1):
            after = pass_on(right, left)
            x_last = swap(x_far, 1)
            found = look([(-k, 0, dims), (k, 0, dims)], [right, left], found)
            right, left, found, x_last = tie((*after, found, x_last))
        all_far = swap(weights, 2)
        k = n // 2 - 1
        after = lax.ppermute(right, "fact", to_right)
        xw = project([fact_x, x_near, x_far, x_last])
        found = look([(k, 0, dims)], [left], found)
        found, asks = tie((found, asks))
        asked = lax.all_to_all(asks, "fact", 0, 0)
        found = look([(-k, 0, dims)], [right], found)
        all_near = swap(weights, 1)
        found, all_far, all_near = tie((found, all_far, all_near))
        last, last_pieces = [after], [(n // 2, 0, dims)]
    else:
        asked = lax.all_to_all(asks, "fact", 0, 0)
        x_far = swap(fact_x, 2)
        x_last = swap(x_far, 1)
        xw = project([fact_x, x_near, x_far, x_last])
        all_far, all_near = swap(weights, 2), swap(weights, 1)
        whole = lax.all_gather(dim_table, "fact")
        order = jnp.take(whole, ring_at(ring_place(lax.axis_index("fact"), n) + jnp.arange(n), n), axis=0)
        for k in range(0, n, 8):
            found = look([(k + i, 0, dims) for i in range(8)], [order[k + i] for i in range(8)], found)
        last, last_pieces = [], []
    all_last = swap(all_far, 1)
    x_blocks, all_blocks = [fact_x, x_near, x_far, x_last], [weights, all_near, all_far, all_last]
    last_rows = max(LANES, sum(t.shape[0] for t in last))
    slope, part = call(
        functools.partial(message_kernel, n, last_pieces),
        (pltpu.HBM((facts, LANES), F32), pltpu.VMEM((n * ents, LANES), BF)),
        [
            pltpu.VMEM((facts, LANES), F32),
            pltpu.VMEM((step, last_rows), BF),
            pltpu.VMEM((facts, LANES), BF),
            pltpu.VMEM((LANES, facts), BF),
            pltpu.VMEM((16, facts), BF),
            *[pltpu.VMEM(t.shape, BF) for t in last],
            pltpu.SemaphoreType.DMA((facts // step,)),
            pltpu.SemaphoreType.DMA,
        ],
        2 * facts * (last_rows + n * ents) * LANES,
        "message",
        limit,
        in_specs=[IN_VMEM] * 2 + [pl.BlockSpec(memory_space=pl.ANY)] * len(last) + [IN_VMEM] * 3,
        out_specs=(IN_HBM, IN_VMEM),
    )(dlow, dhigh, *last, found, xw, entity)
    sums = lax.all_to_all(part.reshape(n * m, rows_each, LANES), ("fact", "feat"), 0, 0)
    pos, entity, x_blocks, _ = tie((pos, entity, x_blocks, part))
    hidden, x_turned = call(
        functools.partial(ready_kernel, m, width, ents),
        (shape((m, ents, LANES), BF), shape((width, facts), BF)),
        [],
        1 << 28,
        "ready",
    )(*x_blocks, *all_blocks)
    self_part = call(
        functools.partial(own_kernel, m, width, ents),
        shape((m, rows_each, LANES), F32),
        [pltpu.VMEM((m, rows_each, LANES), BF)],
        2 * rows_each * width * width,
        "own",
    )(*all_blocks)
    by_feat = shape((m, rows_each, LANES), BF)
    back, out_parts, pre_parts, agg_parts = call(
        functools.partial(entity_kernel, n, m, width, ents),
        (pltpu.VMEM((n * m, rows_each, LANES), BF), by_feat, by_feat, shape((m * rows_each, LANES), BF)),
        [
            pltpu.VMEM((m, rows_each, LANES), F32),
            pltpu.VMEM((ents, LANES), F32),
            pltpu.VMEM(asked.shape, jnp.int32),
            pltpu.SemaphoreType.DMA((2,)),
        ],
        4 * rows_each * width * width,
        "entity",
        in_specs=[IN_VMEM] + [pl.BlockSpec(memory_space=pl.ANY)] * 2 + [IN_VMEM] * m,
    )(sums, asked, self_part, *all_blocks)
    scaled = lax.all_to_all(back, ("fact", "feat"), 0, 0).reshape(n * ents, LANES)
    shares = call(
        functools.partial(share_kernel, m),
        tuple(shape(((2 + m) * rows_each, LANES), BF) for _ in range(m)),
        [],
        1 << 20,
        "share",
    )(out_parts, pre_parts, agg_parts)
    got = [shares[0]] + [swap(shares[j], j) for j in range(1, m)]
    pos, entity, asked, _ = tie((pos, entity, asked, back))
    plow, phigh, elow, ehigh = call(
        codes_kernel,
        (shape((LANES, facts), BF), shape((16, facts), BF), columns, columns),
        [],
        1 << 26,
        "codes",
    )(pos, entity)
    rlow, rhigh = call(
        functools.partial(request_kernel, n, cap),
        (shape((LANES, slots), BF), shape((16, slots), BF)),
        [],
        1 << 26,
        "requests",
        limit,
    )(asked)
    pair_shape = (n // 2, 2 * stride, LANES)
    output_h, pair = call(
        functools.partial(weight_kernel, n, m, width, stride),
        (shape((ents, LANES), BF), shape((2, *pair_shape), F32)),
        [pltpu.VMEM((width, LANES), F32), pltpu.VMEM((ents, LANES), BF), pltpu.VMEM((m, ents, LANES), BF)],
        4 * ents * width * LANES,
        "weight",
    )(hidden, *got)
    if ringed:
        keep, give = call(halves_kernel, (shape(pair_shape, F32), shape(pair_shape, BF)), [], 1 << 20, "halves")(pair)
        pairs = [keep, lax.ppermute(give, "fact", [(i, i ^ 1) for i in range(n)])]
    else:
        pairs = [jnp.stack([pair[0], pair[1]], axis=1).reshape(n, 2 * stride, LANES)]
    d_msg, msg_share = call(
        functools.partial(backward_kernel, n, stride),
        (columns, shape((n, stride, LANES), BF)),
        [pltpu.VMEM((step, n * ents), BF), pltpu.VMEM((facts, LANES), F32), pltpu.SemaphoreType.DMA],
        2 * facts * (n * ents + width) * LANES,
        "backward",
        limit,
        in_specs=[IN_HBM] + [IN_VMEM] * 4,
    )(slope, scaled, elow, ehigh, x_turned)

    def spread(offsets):
        lengths = [cap + (3 if ringed and k % 2 == 0 else 1) * stride for k in offsets]
        return call(
            functools.partial(spread_kernel, n, cap, stride, offsets),
            tuple(shape((rows, LANES), BF) for rows in lengths),
            [],
            2 * facts * cap * LANES * len(offsets),
            "spread",
            limit,
        )(plow, phigh, d_msg, msg_share, *(pairs if max(lengths) > cap + stride else ()))

    def add_up(offsets, got, base, final):
        weight = shape((3 * stride, LANES), F32)
        scratch = [
            pltpu.VMEM((cap * len(got), LANES), BF),
            pltpu.VMEM((LANES, cap * len(got)), BF),
            pltpu.VMEM((16, cap * len(got)), BF),
        ]
        return call(
            functools.partial(table_kernel, n, cap, stride, offsets, base is None, final),
            (shape((dims, LANES), F32),) + ((shape((own, LANES), F32),) * 3 if final else (weight,)),
            scratch
            + (
                [
                    pltpu.VMEM(weight.shape, F32),
                    pltpu.VMEM((dims, LANES), F32),
                    pltpu.SemaphoreType.DMA((dims // LANES,)),
                    pltpu.SemaphoreType.DMA((3,)),
                ]
                if final
                else []
            ),
            2 * cap * dims * LANES * len(got),
            "table",
            limit,
            **(dict(out_specs=(IN_HBM,) * 4) if final else {}),
        )(rlow, rhigh, *got, *(base or ()))

    totals = None
    if ringed:
        messages = {}
        rest = [[k, n - k] for k in range(n // 2 - 1, 1, -1)]
        for offsets in [rest[0], [n // 2], [1, n - 1], *rest[1:]]:
            for offset, message in zip(offsets, spread(offsets)):
                messages[offset] = lax.ppermute(message, "fact", [(i, (i + offset) % n) for i in range(n)])
        messages[0] = spread([0])[0]
        for offsets in [[0, 1, n - 1], [n // 2], *rest[::-1]]:
            totals = add_up(offsets, [messages[k] for k in offsets], totals, offsets == rest[0])
        grad_dim, grad_msg, grad_self, grad_neigh = totals
    else:
        fact_me = lax.axis_index("fact")
        sent = [message for k in range(0, n, 8) for message in spread(list(range(k, k + 8)))]
        by_owner = jnp.take(jnp.stack(sent), lax.rem(jnp.arange(n) - fact_me + n, n), axis=0)
        owned = lax.all_to_all(by_owner, "fact", 0, 0)
        by_offset = jnp.take(owned, lax.rem(fact_me - jnp.arange(n) + n, n), axis=0)
        for k in range(0, n, 8):
            totals = add_up(list(range(k, k + 8)), [by_offset[k + i] for i in range(8)], totals, k + 8 >= n)
        grad_dim, grad_msg, _, _ = totals
        pair_sum = lax.psum_scatter(pairs[0], "fact", scatter_dimension=0, tiled=True)[0]
        grad_self, grad_neigh = pair_sum[0:own], pair_sum[stride : stride + own]
    return output_h, grad_msg, grad_self, grad_neigh, grad_dim


def solution(mesh):
    placed = (
        P("fact", "feat"),
        P("fact", None),
        P("fact"),
        P("fact", None),
        P("fact"),
        P("fact", "feat"),
        P("fact", "feat"),
        P(None, "feat"),
        P(None, "feat"),
        P(None, "feat"),
        P("fact", "feat"),
    )
    return jax.shard_map(
        shards,
        mesh=mesh,
        in_specs=placed,
        out_specs=(P("fact", "feat"),) * 5,
        check_vma=False,
    )
```

```python
import functools

import jax
import jax.numpy as jnp
from jax import lax
from jax.experimental import pallas as pl
from jax.experimental.pallas import tpu as pltpu
from jax.sharding import PartitionSpec as P

LANES = 128
BF = jnp.bfloat16
IN_HBM = pl.BlockSpec(memory_space=pltpu.HBM)
IN_VMEM = pl.BlockSpec(memory_space=pltpu.VMEM)
F32 = jnp.float32
VMEM_LIMIT = 16 * 1024 * 1024
VMEM_LIMIT_LARGE = 40 * 1024 * 1024


def call(kernel, out_shape, scratch, flops, name, limit=VMEM_LIMIT, **specs):
    return pl.pallas_call(
        kernel,
        out_shape=out_shape,
        scratch_shapes=scratch,
        compiler_params=pltpu.CompilerParams(vmem_limit_bytes=limit),
        cost_estimate=pl.CostEstimate(flops=flops, bytes_accessed=1 << 20, transcendentals=0),
        name=name,
        **specs,
    )


def shape(dims, dtype):
    return jax.ShapeDtypeStruct(dims, dtype)


def nt(a, b):
    return lax.dot_general(a, b, (((1,), (1,)), ((), ())), preferred_element_type=F32)


def tn(a, b):
    return lax.dot_general(a, b, (((0,), (0,)), ((), ())), preferred_element_type=F32)


def dot(a, b):
    return jnp.dot(a, b, preferred_element_type=F32)


def flag(condition):
    return jnp.where(condition, 1.0, 0.0).astype(BF)


def column_codes(row):
    keys = jnp.broadcast_to(row, (LANES, LANES)).astype(F32).T.astype(jnp.int32)
    lane = lax.broadcasted_iota(jnp.int32, (LANES, LANES), 1)
    return flag((keys & (LANES - 1)) == lane), (keys >> 7).astype(F32).astype(BF)


def row_codes(row):
    keys = jnp.broadcast_to(row, (LANES, LANES))
    sub = lax.broadcasted_iota(jnp.int32, (LANES, LANES), 0)
    high = jnp.broadcast_to((row >> 7).astype(F32), (16, LANES)).astype(BF)
    return flag((keys & (LANES - 1)) == sub), high


def pick_block(low, high, block):
    zero = jnp.zeros((), BF)
    return jnp.where(high == block, low, zero)


def pick_rows(low, high, block):
    wide = low.reshape(LANES // 16, 16, low.shape[1])
    picked = pick_block(wide, high[None], block)
    return picked.reshape(low.shape)


def route_kernel(n, cap, ents, dims, *refs):
    given, (out_ref, pos_ref, ent_ref, dlow_ref, dhigh_ref), held_refs, sems = refs[:4], refs[4:9], refs[9:13], refs[13]
    copies = [pltpu.make_async_copy(src, dst, sems.at[i]) for i, (src, dst) in enumerate(zip(given, held_refs))]
    for copy in copies:
        copy.start()
    for copy in copies:
        copy.wait()
    do_ref, ds_ref, fo_ref, fs_ref = held_refs
    chunks = do_ref.shape[0]
    owner = do_ref[...]
    kind = lax.broadcasted_iota(jnp.int32, (n, chunks, LANES), 0)
    held = jnp.where(kind == owner[None], 1.0, 0.0).reshape(n * chunks, LANES)
    held_bf = held.astype(BF)
    i0 = lax.broadcasted_iota(jnp.int32, (LANES, LANES), 0)
    i1 = lax.broadcasted_iota(jnp.int32, (LANES, LANES), 1)
    inside = dot(held_bf, flag(i0 < i1))
    r0 = lax.broadcasted_iota(jnp.int32, (n * chunks, n * chunks), 0)
    r1 = lax.broadcasted_iota(jnp.int32, (n * chunks, n * chunks), 1)
    earlier = flag((r0 // chunks == r1 // chunks) & (r1 < r0))
    before = dot(dot(earlier, held_bf).astype(BF), jnp.ones((LANES, LANES), BF))
    rank = jnp.sum((held * (inside + before)).reshape(n, chunks, LANES), axis=0)
    rank = rank.astype(jnp.int32)
    entity_owner = fo_ref[...]
    entity_slot = fs_ref[...]
    value = ds_ref[...]
    entity = entity_owner * ents + entity_slot
    pos_ref[...] = owner * cap + rank
    ent_ref[...] = entity
    fact_dim = owner * dims + value
    words = [(value >> 5).astype(F32), (value & 31).astype(F32), (entity >> 5).astype(F32), (entity & 31).astype(F32)]
    names = lax.broadcasted_iota(jnp.int32, (n, LANES), 0)
    places = lax.broadcasted_iota(jnp.int32, (cap, LANES), 0)
    slots = lax.broadcasted_iota(jnp.int32, (ents, LANES), 0)
    asked = [jnp.zeros((n, cap), F32) for _ in words]
    hits = jnp.zeros((n, ents), F32)
    for k in range(chunks):
        here = slice(k * LANES, (k + 1) * LANES)
        mine = jnp.where(names == owner[k : k + 1], 1.0, 0.0)
        at = flag(places == rank[k : k + 1])
        for w, word in enumerate(words):
            asked[w] += nt((mine * word[k : k + 1]).astype(BF), at)
        hits += nt(flag(names == entity_owner[k : k + 1]), flag(slots == entity_slot[k : k + 1]))
        dlow_ref[here, :], dhigh_ref[here, :] = column_codes(fact_dim[k : k + 1])
    groups = cap // LANES
    asked_dim = (asked[0] * 32.0 + asked[1]).astype(jnp.int32)
    asked_ent = (asked[2] * 32.0 + asked[3]).astype(jnp.int32)
    for r in range(groups):
        out_ref[:, r, :] = asked_dim[:, r * LANES : (r + 1) * LANES]
        out_ref[:, groups + r, :] = asked_ent[:, r * LANES : (r + 1) * LANES]
    out_ref[:, 2 * groups, :] = hits.astype(jnp.int32)


def gather_rows(low_ref, high_ref, rows, table_refs, firsts, hot_ref):
    at = 0
    low, high = low_ref[rows, :], high_ref[rows, :]
    for table, first in zip(table_refs, firsts):
        for k in range(table.shape[0] // LANES):
            hot_ref[:, at : at + LANES] = pick_block(low, high, (first + k).astype(F32).astype(BF))
            at += LANES
    total, at = None, 0
    for table in table_refs:
        part = dot(hot_ref[:, at : at + table.shape[0]], table[...])
        total = part if total is None else total + part
        at += table.shape[0]
    return total


def ring_at(place, n):
    place = lax.rem(place + 2 * n, n)
    return jnp.where(place < n // 2, 2 * place, 2 * (n - 1 - place) + 1)


def ring_place(index, n):
    half = lax.div(index, 2)
    return jnp.where(lax.rem(index, 2) == 0, half, n - 1 - half)


def look_kernel(n, pieces, low_ref, high_ref, *refs):
    count = len(pieces)
    tables, base_ref, out_ref, hot_ref = refs[:count], refs[count], refs[-2], refs[-1]
    facts = low_ref.shape[0]
    step = hot_ref.shape[0]
    place = ring_place(lax.axis_index("fact"), n)
    firsts = [lax.div(ring_at(place + hops, n) * dims + row, LANES) for hops, row, dims in pieces]
    for c in range(facts // step):
        rows = slice(c * step, (c + 1) * step)
        out_ref[rows, :] = base_ref[rows, :] + gather_rows(low_ref, high_ref, rows, tables, firsts, hot_ref)


def message_kernel(n, pieces, low_ref, high_ref, *refs):
    count = len(pieces)
    sources, refs = refs[:count], refs[count:]
    base_ref, xw_ref, ent_ref, slope_out, part_ref, slope_ref, hot_ref, msg_ref, erlow_ref, erhigh_ref = refs[:10]
    tables, (sem, table_sem) = refs[10 : 10 + count], refs[10 + count :]
    arrivals = [pltpu.make_async_copy(src, dst, table_sem) for src, dst in zip(sources, tables)]
    for copy in arrivals:
        copy.start()
    facts = low_ref.shape[0]
    step = hot_ref.shape[0]
    place = ring_place(lax.axis_index("fact"), n)
    firsts = [lax.div(ring_at(place + hops, n) * dims + row, LANES) for hops, row, dims in pieces]
    for k in range(ent_ref.shape[0]):
        here = slice(k * LANES, (k + 1) * LANES)
        erlow_ref[:, here], erhigh_ref[:, here] = row_codes(ent_ref[k : k + 1, :])
    for copy in arrivals:
        copy.wait()
    for c in range(facts // step):
        rows = slice(c * step, (c + 1) * step)
        pre = xw_ref[rows, :] + base_ref[rows, :]
        if count:
            pre = pre + gather_rows(low_ref, high_ref, rows, tables, firsts, hot_ref)
        gate = jax.nn.sigmoid(pre)
        msg_ref[rows, :] = (pre * gate).astype(BF)
        slope_ref[rows, :] = gate * (1.0 + pre * (1.0 - gate))
    keep = pltpu.make_async_copy(slope_ref, slope_out, sem)
    keep.start()

    def add(pair, carry):
        hot = jnp.concatenate(
            [pick_rows(erlow_ref[...], erhigh_ref[...], (pair * 2 + i).astype(F32).astype(BF)) for i in range(2)], axis=0
        )
        rows = pl.ds(pl.multiple_of(pair * 256, 256), 256)
        part_ref[rows, :] = dot(hot, msg_ref[...]).astype(BF)
        return carry

    lax.fori_loop(0, part_ref.shape[0] // 256, add, 0)
    keep.wait()


def project_kernel(m, w_ref, *refs):
    blocks, out_ref = refs[:m], refs[m]
    me = lax.axis_index("feat")
    total = None
    for j, ref in enumerate(blocks):
        rows = pl.ds(pl.multiple_of((me ^ j) * LANES, LANES), LANES)
        part = dot(ref[...], w_ref[rows, :])
        total = part if total is None else total + part
    out_ref[...] = total


def ready_kernel(m, width, ents, *refs):
    x_refs, all_refs, (hidden_ref, xt_ref) = refs[:m], refs[m : 2 * m], refs[2 * m :]
    me = lax.axis_index("feat")
    for j in range(m):
        hidden_ref[me ^ j] = all_refs[j][2 * width : 2 * width + ents, :]
        xt_ref[pl.ds(pl.multiple_of((me ^ j) * LANES, LANES), LANES), :] = x_refs[j][...].T


def entity_kernel(n, m, width, ents, sums_ref, idx_ref, *refs):
    all_refs, (back_ref, out_ref, pre_ref, agg_ref, own_ref, hold_ref, words_ref, sem) = refs[:m], refs[m:]
    fetch = pltpu.make_async_copy(idx_ref, words_ref, sem)
    fetch.start()
    rows_each = ents // m
    me = lax.axis_index("feat")
    totals = []
    for b in range(m):
        total = sums_ref[b].astype(F32)
        for f in range(1, n):
            total += sums_ref[f * m + b].astype(F32)
        totals.append(total)
    fetch.wait()
    hits = jnp.sum(words_ref[:, words_ref.shape[1] - 1, :], axis=0, keepdims=True).astype(F32)
    hold_ref[...] = jnp.maximum(jnp.broadcast_to(hits, (LANES, ents)).T, 1.0)
    divisor = hold_ref[pl.ds(pl.multiple_of(me * rows_each, rows_each), rows_each), :]
    for b in range(m):
        agg_ref[b * rows_each : (b + 1) * rows_each, :] = (totals[b] / divisor).astype(BF)
    at = pl.multiple_of(2 * width + me * rows_each, rows_each)
    for j in range(m):
        own_ref[me ^ j] = all_refs[j][pl.ds(at, rows_each), :]
    aggregate = jnp.concatenate([agg_ref[b * rows_each : (b + 1) * rows_each, :] for b in range(m)], axis=1)
    hidden = jnp.concatenate([own_ref[b] for b in range(m)], axis=1)
    d_agg = None
    for j in range(m):
        pre = dot(hidden, all_refs[j][0:width, :]) + dot(aggregate, all_refs[j][width : 2 * width, :])
        gate = jax.nn.sigmoid(pre)
        cot = all_refs[j][pl.ds(at + ents, rows_each), :].astype(F32)
        d_pre = (cot * (gate * (1.0 + pre * (1.0 - gate)))).astype(BF)
        out_ref[me ^ j] = (pre * gate).astype(BF)
        pre_ref[me ^ j] = d_pre
        term = nt(d_pre, all_refs[j][width : 2 * width, :])
        d_agg = term if d_agg is None else d_agg + term
    for b in range(m):
        scaled = (d_agg[:, b * LANES : (b + 1) * LANES] / divisor).astype(BF)
        for f in range(n):
            back_ref[f * m + b] = scaled


def share_kernel(m, out_ref, pre_ref, agg_ref, *share_refs):
    rows_each = out_ref.shape[1]
    me = lax.axis_index("feat")
    for j, ref in enumerate(share_refs):
        ref[0:rows_each, :] = out_ref[me ^ j]
        ref[rows_each : 2 * rows_each, :] = pre_ref[me ^ j]
        ref[2 * rows_each :, :] = agg_ref[...]


def weight_kernel(n, m, width, stride, hidden_ref, *refs):
    got, (out_ref, back_ref, total_ref, pre_ref, agg_ref) = refs[:m], refs[m:]
    rows_each = got[0].shape[0] // (2 + m)
    own = width // n
    me = lax.axis_index("feat")
    for j, ref in enumerate(got):
        here = pl.ds(pl.multiple_of((me ^ j) * rows_each, rows_each), rows_each)
        out_ref[here, :] = ref[0:rows_each, :]
        pre_ref[here, :] = ref[rows_each : 2 * rows_each, :]
        for b in range(m):
            agg_ref[b, here, :] = ref[(2 + b) * rows_each : (3 + b) * rows_each, :]
    d_pre = pre_ref[...]
    for which, blocks in enumerate((hidden_ref, agg_ref)):
        for b in range(m):
            total_ref[b * LANES : (b + 1) * LANES, :] = tn(blocks[b], d_pre)
        for d in range(n):
            back_ref[d % 2, d // 2, which * stride : (which + 1) * stride, :] = padded(
                total_ref[d * own : (d + 1) * own, :], stride
            )


def halves_kernel(back_ref, keep_ref, give_ref):
    odd = lax.rem(lax.axis_index("fact"), 2)
    keep_ref[...] = back_ref[odd]
    give_ref[...] = back_ref[1 - odd].astype(BF)


def padded(piece, rows):
    if piece.shape[0] == rows:
        return piece
    return jnp.concatenate([piece, jnp.zeros((rows - piece.shape[0], LANES), F32)], axis=0)


def codes_kernel(pos_ref, ent_ref, plow_ref, phigh_ref, elow_ref, ehigh_ref):
    for k in range(pos_ref.shape[0]):
        here = slice(k * LANES, (k + 1) * LANES)
        plow_ref[:, here], phigh_ref[:, here] = row_codes(pos_ref[k : k + 1, :])
        elow_ref[here, :], ehigh_ref[here, :] = column_codes(ent_ref[k : k + 1, :])


def request_kernel(n, cap, req_ref, low_ref, high_ref):
    for s in range(n):
        for r in range(cap // LANES):
            at = s * cap + r * LANES
            low_ref[:, at : at + LANES], high_ref[:, at : at + LANES] = row_codes(req_ref[s, r : r + 1, :])


def backward_kernel(n, stride, slope_in, scaled_ref, low_ref, high_ref, xt_ref, dmsg_ref, share_ref, hot_ref, slope_ref, sem):
    fetch = pltpu.make_async_copy(slope_in, slope_ref, sem)
    fetch.start()
    facts = slope_ref.shape[0]
    own = xt_ref.shape[0] // n
    step = hot_ref.shape[0]
    for c in range(facts // step):
        rows = slice(c * step, (c + 1) * step)
        found = gather_rows(low_ref, high_ref, rows, [scaled_ref], [jnp.int32(0)], hot_ref)
        if c == 0:
            fetch.wait()
        dmsg_ref[rows, :] = (found * slope_ref[rows, :]).astype(BF)
    total = dot(xt_ref[...], dmsg_ref[...])
    for d in range(n):
        share_ref[d] = padded(total[d * own : (d + 1) * own, :], stride).astype(BF)


def slots_of(d, cap, plow_ref, phigh_ref):
    return jnp.concatenate(
        [
            pick_rows(plow_ref[...], phigh_ref[...], (d * (cap // LANES) + i).astype(F32).astype(BF))
            for i in range(cap // LANES)
        ],
        axis=0,
    )


def early_kernel(n, cap, offset, plow_ref, phigh_ref, slope_ref, out_ref):
    d = lax.rem(lax.axis_index("fact") + offset, n)
    out_ref[...] = dot(slots_of(d, cap, plow_ref, phigh_ref), slope_ref[...].astype(BF)).astype(BF)


def form_kernel(n, cap, offset, scaled_ref, slopes_ref, idx_ref, rest_ref, out_ref, hot_ref, low_ref, high_ref):
    groups = cap // LANES
    source = lax.rem(lax.axis_index("fact") + (n - offset), n)
    for r in range(groups):
        here = slice(r * LANES, (r + 1) * LANES)
        low_ref[here, :], high_ref[here, :] = column_codes(idx_ref[source, groups + r : groups + r + 1, :])
    found = gather_rows(low_ref, high_ref, slice(0, cap), [scaled_ref], [jnp.int32(0)], hot_ref)
    out_ref[0:cap, :] = (found * slopes_ref[...].astype(F32)).astype(BF)
    out_ref[cap:, :] = rest_ref[...]


def spread_kernel(n, cap, stride, offsets, plow_ref, phigh_ref, dmsg_ref, share_ref, *refs):
    pair_refs, out_refs = refs[:-len(offsets)], refs[-len(offsets) :]
    me = lax.axis_index("fact")
    for offset, out_ref in zip(offsets, out_refs):
        d = lax.rem(me + offset, n)
        at = 0
        if out_ref.shape[0] >= cap:
            out_ref[0:cap, :] = dot(slots_of(d, cap, plow_ref, phigh_ref), dmsg_ref[...]).astype(BF)
            at = cap
        out_ref[at : at + stride, :] = share_ref[d]
        if out_ref.shape[0] > at + stride:
            pair = pair_refs[0][lax.div(d, 2)]
            for ref in pair_refs[1:]:
                pair = pair + ref[lax.div(d, 2)].astype(F32)
            out_ref[at + stride :, :] = pair.astype(BF)


def table_kernel(n, cap, stride, offsets, first, final, low_ref, high_ref, *refs):
    count = len(offsets)
    got, refs = refs[:count], refs[count:]
    if not first:
        (base_ref, weight_base_ref), refs = refs[:2], refs[2:]
    out_ref, refs = refs[0], refs[1:]
    final_refs, refs = (refs[:3], refs[3:]) if final else ((), refs[1:] + refs[:1])
    rows_ref, klow_ref, khigh_ref, weight_ref = refs[:4]
    me = lax.axis_index("fact")
    if first:
        weight_ref[...] = jnp.zeros(weight_ref.shape, F32)
    else:
        weight_ref[...] = weight_base_ref[...]
    for j, (offset, ref) in enumerate(zip(offsets, got)):
        source = lax.rem(me + (n - offset), n)
        here = slice(j * cap, (j + 1) * cap)
        there = pl.ds(pl.multiple_of(source * cap, LANES), cap)
        rows_ref[here, :] = ref[0:cap, :]
        klow_ref[:, here] = low_ref[:, there]
        khigh_ref[:, here] = high_ref[:, there]
        rows = ref.shape[0] - cap
        weight_ref[0:rows, :] += ref[cap:, :].astype(F32)
    copies = []
    for which, ref in enumerate(final_refs):
        copies.append(
            pltpu.make_async_copy(
                weight_ref.at[which * stride : which * stride + ref.shape[0], :], ref, refs[6].at[which]
            )
        )
        copies[-1].start()
    blocks = out_ref.shape[0] // LANES
    join = 2 if blocks % 2 == 0 else 1

    target_ref = refs[4] if final else out_ref
    for group in range(blocks // join):
        hot = jnp.concatenate(
            [pick_rows(klow_ref[...], khigh_ref[...], jnp.array(group * join + i, BF)) for i in range(join)], axis=0
        )
        rows = slice(group * join * LANES, (group + 1) * join * LANES)
        sums = dot(hot, rows_ref[...])
        target_ref[rows, :] = sums if first else base_ref[rows, :] + sums
        if final:
            copies.append(pltpu.make_async_copy(target_ref.at[rows, :], out_ref.at[rows, :], refs[5].at[group]))
            copies[-1].start()
    for copy in copies:
        copy.wait()


def shards(fact_x, dim_owner, dim_slot, fact_owner, fact_slot, dim_table, entity_h, w_msg, w_self, w_neigh, cotangent):
    n, m = lax.axis_size("fact"), lax.axis_size("feat")
    assert m == 4 and n % 2 == 0
    facts = fact_x.shape[0]
    chunks = facts // LANES
    ents = entity_h.shape[0]
    rows_each = ents // m
    width = w_msg.shape[0]
    dims = dim_table.shape[0]
    cap = -(-(3 * facts // n) // LANES) * LANES
    slots = n * cap
    groups = 2 * (cap // LANES) + 1
    own = width // n
    stride = max(16, own)
    step = 512
    tie = lax.optimization_barrier
    ringed = n <= 8
    limit = VMEM_LIMIT if ringed else VMEM_LIMIT_LARGE

    ring = [2 * p if p < n // 2 else 2 * (n - 1 - p) + 1 for p in range(n)]
    to_right = [(ring[p], ring[(p + 1) % n]) for p in range(n)]
    to_left = [(ring[(p + 1) % n], ring[p]) for p in range(n)]

    def pass_on(right, left):
        return lax.ppermute(right, "fact", to_right), lax.ppermute(left, "fact", to_left)

    def swap(block, bit):
        return lax.ppermute(block, "feat", [(i, i ^ bit) for i in range(m)])

    if ringed:
        right, left = pass_on(dim_table, dim_table)
    x_near = swap(fact_x, 1)
    by_lane = (chunks, LANES)
    columns = shape((facts, LANES), BF)
    asks, pos, entity, dlow, dhigh = call(
        functools.partial(route_kernel, n, cap, ents, dims),
        (
            shape((n, groups, LANES), jnp.int32),
            shape(by_lane, jnp.int32),
            shape(by_lane, jnp.int32),
            columns,
            columns,
        ),
        [pltpu.VMEM(by_lane, jnp.int32)] * 4 + [pltpu.SemaphoreType.DMA((4,))],
        1 << 28,
        "route",
        in_specs=[IN_HBM] * 4,
    )(dim_owner.reshape(by_lane), dim_slot.reshape(by_lane), fact_owner.reshape(by_lane), fact_slot.reshape(by_lane))
    if ringed:
        right, left, x_near, asks, pos, entity, dlow, dhigh = tie(
            (right, left, x_near, asks, pos, entity, dlow, dhigh)
        )

    def look(pieces, tables, base):
        rows = sum(t.shape[0] for t in tables)
        return call(
            functools.partial(look_kernel, n, pieces),
            shape((facts, LANES), F32),
            [pltpu.VMEM((step, rows), BF)],
            2 * facts * rows * LANES,
            "look",
            limit,
        )(dlow, dhigh, *tables, base)

    def project(blocks):
        return call(
            functools.partial(project_kernel, m), shape((facts, LANES), F32), [], 2 * facts * width * LANES, "project"
        )(w_msg, *blocks)

    found = jnp.zeros((facts, LANES), F32)
    weights = jnp.concatenate([w_self, w_neigh, entity_h, cotangent], axis=0)
    if ringed:
        near = (right, left)
        after = pass_on(*near)
        x_far = swap(fact_x, 2)
        found = look([(0, 0, dims), (-1, 0, dims), (1, 0, dims)], [dim_table, *near], found)
        right, left, x_far, found, weights = tie((*after, x_far, found, weights))
        for k in range(2, n // 2 - 1):
            after = pass_on(right, left)
            x_last = swap(x_far, 1)
            found = look([(-k, 0, dims), (k, 0, dims)], [right, left], found)
            right, left, found, x_last = tie((*after, found, x_last))
        all_far = swap(weights, 2)
        k = n // 2 - 1
        after = lax.ppermute(right, "fact", to_right)
        xw = project([fact_x, x_near, x_far, x_last])
        found = look([(k, 0, dims)], [left], found)
        found, asks = tie((found, asks))
        asked = lax.all_to_all(asks, "fact", 0, 0)
        found = look([(-k, 0, dims)], [right], found)
        all_near = swap(weights, 1)
        found, all_far, all_near = tie((found, all_far, all_near))
        last, last_pieces = [after], [(n // 2, 0, dims)]
    else:
        asked = lax.all_to_all(asks, "fact", 0, 0)
        x_far = swap(fact_x, 2)
        x_last = swap(x_far, 1)
        xw = project([fact_x, x_near, x_far, x_last])
        all_far, all_near = swap(weights, 2), swap(weights, 1)
        whole = lax.all_gather(dim_table, "fact")
        order = jnp.take(whole, ring_at(ring_place(lax.axis_index("fact"), n) + jnp.arange(n), n), axis=0)
        for k in range(0, n, 8):
            found = look([(k + i, 0, dims) for i in range(8)], [order[k + i] for i in range(8)], found)
        last, last_pieces = [], []
    all_last = swap(all_far, 1)
    x_blocks, all_blocks = [fact_x, x_near, x_far, x_last], [weights, all_near, all_far, all_last]
    last_rows = max(LANES, sum(t.shape[0] for t in last))
    slope, part = call(
        functools.partial(message_kernel, n, last_pieces),
        (pltpu.HBM((facts, LANES), F32), shape((n * ents, LANES), BF)),
        [
            pltpu.VMEM((facts, LANES), F32),
            pltpu.VMEM((step, last_rows), BF),
            pltpu.VMEM((facts, LANES), BF),
            pltpu.VMEM((LANES, facts), BF),
            pltpu.VMEM((16, facts), BF),
            *[pltpu.VMEM(t.shape, BF) for t in last],
            pltpu.SemaphoreType.DMA,
            pltpu.SemaphoreType.DMA,
        ],
        2 * facts * (last_rows + n * ents) * LANES,
        "message",
        limit,
        in_specs=[IN_VMEM] * 2 + [pl.BlockSpec(memory_space=pl.ANY)] * len(last) + [IN_VMEM] * 3,
        out_specs=(IN_HBM, IN_VMEM),
    )(dlow, dhigh, *last, found, xw, entity)
    sums = lax.all_to_all(part.reshape(n * m, rows_each, LANES), ("fact", "feat"), 0, 0)
    pos, entity, x_blocks, _ = tie((pos, entity, x_blocks, part))
    hidden, x_turned = call(
        functools.partial(ready_kernel, m, width, ents),
        (shape((m, ents, LANES), BF), shape((width, facts), BF)),
        [],
        1 << 28,
        "ready",
    )(*x_blocks, *all_blocks)
    by_feat = shape((m, rows_each, LANES), BF)
    back, out_parts, pre_parts, agg_parts = call(
        functools.partial(entity_kernel, n, m, width, ents),
        (shape((n * m, rows_each, LANES), BF), by_feat, by_feat, shape((m * rows_each, LANES), BF)),
        [
            pltpu.VMEM((m, rows_each, LANES), BF),
            pltpu.VMEM((ents, LANES), F32),
            pltpu.VMEM(asked.shape, jnp.int32),
            pltpu.SemaphoreType.DMA,
        ],
        6 * rows_each * width * width,
        "entity",
        in_specs=[IN_VMEM, pl.BlockSpec(memory_space=pl.ANY)] + [IN_VMEM] * m,
    )(sums, asked, *all_blocks)
    scaled = lax.all_to_all(back, ("fact", "feat"), 0, 0).reshape(n * ents, LANES)
    shares = call(
        functools.partial(share_kernel, m),
        tuple(shape(((2 + m) * rows_each, LANES), BF) for _ in range(m)),
        [],
        1 << 20,
        "share",
    )(out_parts, pre_parts, agg_parts)
    got = [shares[0]] + [swap(shares[j], j) for j in range(1, m)]
    pos, entity, asked, _ = tie((pos, entity, asked, back))
    plow, phigh, elow, ehigh = call(
        codes_kernel,
        (shape((LANES, facts), BF), shape((16, facts), BF), columns, columns),
        [],
        1 << 26,
        "codes",
    )(pos, entity)
    if ringed:
        slope_early, _ = tie((slope, back))
        slopes = call(
            functools.partial(early_kernel, n, cap, n // 2),
            shape((cap, LANES), BF),
            [],
            2 * facts * cap * LANES,
            "early",
        )(plow, phigh, slope_early)
        slopes = lax.ppermute(slopes, "fact", [(i, (i + n // 2) % n) for i in range(n)])
        elow, slopes = tie((elow, slopes))
    rlow, rhigh = call(
        functools.partial(request_kernel, n, cap),
        (shape((LANES, slots), BF), shape((16, slots), BF)),
        [],
        1 << 26,
        "requests",
        limit,
    )(asked)
    pair_shape = (n // 2, 2 * stride, LANES)
    output_h, pair = call(
        functools.partial(weight_kernel, n, m, width, stride),
        (shape((ents, LANES), BF), shape((2, *pair_shape), F32)),
        [pltpu.VMEM((width, LANES), F32), pltpu.VMEM((ents, LANES), BF), pltpu.VMEM((m, ents, LANES), BF)],
        4 * ents * width * LANES,
        "weight",
    )(hidden, *got)
    if ringed:
        keep, give = call(halves_kernel, (shape(pair_shape, F32), shape(pair_shape, BF)), [], 1 << 20, "halves")(pair)
        pairs = [keep, lax.ppermute(give, "fact", [(i, i ^ 1) for i in range(n)])]
    else:
        pairs = [jnp.stack([pair[0], pair[1]], axis=1).reshape(n, 2 * stride, LANES)]
    d_msg, msg_share = call(
        functools.partial(backward_kernel, n, stride),
        (columns, shape((n, stride, LANES), BF)),
        [pltpu.VMEM((step, n * ents), BF), pltpu.VMEM((facts, LANES), F32), pltpu.SemaphoreType.DMA],
        2 * facts * (n * ents + width) * LANES,
        "backward",
        limit,
        in_specs=[IN_HBM] + [IN_VMEM] * 4,
    )(slope, scaled, elow, ehigh, x_turned)

    def spread(offsets):
        lengths = [cap + (3 if ringed and k % 2 == 0 else 1) * stride for k in offsets]
        if ringed and offsets == [n // 2]:
            lengths = [3 * stride]
        return call(
            functools.partial(spread_kernel, n, cap, stride, offsets),
            tuple(shape((rows, LANES), BF) for rows in lengths),
            [],
            2 * facts * cap * LANES * len(offsets),
            "spread",
            limit,
        )(plow, phigh, d_msg, msg_share, *(pairs if ringed and any(k % 2 == 0 for k in offsets) else ()))

    def add_up(offsets, got, base, final):
        weight = shape((3 * stride, LANES), F32)
        scratch = [
            pltpu.VMEM((cap * len(got), LANES), BF),
            pltpu.VMEM((LANES, cap * len(got)), BF),
            pltpu.VMEM((16, cap * len(got)), BF),
        ]
        return call(
            functools.partial(table_kernel, n, cap, stride, offsets, base is None, final),
            (shape((dims, LANES), F32),) + ((shape((own, LANES), F32),) * 3 if final else (weight,)),
            scratch
            + (
                [
                    pltpu.VMEM(weight.shape, F32),
                    pltpu.VMEM((dims, LANES), F32),
                    pltpu.SemaphoreType.DMA((dims // LANES,)),
                    pltpu.SemaphoreType.DMA((3,)),
                ]
                if final
                else []
            ),
            2 * cap * dims * LANES * len(got),
            "table",
            limit,
            **(dict(out_specs=(IN_HBM,) * 4) if final else {}),
        )(rlow, rhigh, *got, *(base or ()))

    totals = None
    if ringed:
        messages = {}
        rest = [[k, n - k] for k in range(n // 2 - 1, 1, -1)]
        for offsets in [rest[0], [n // 2], [1, n - 1], *rest[1:]]:
            for offset, message in zip(offsets, spread(offsets)):
                messages[offset] = lax.ppermute(message, "fact", [(i, (i + offset) % n) for i in range(n)])
        messages[0] = spread([0])[0]
        messages[n // 2] = call(
            functools.partial(form_kernel, n, cap, n // 2),
            shape((cap + 3 * stride, LANES), BF),
            [pltpu.VMEM((cap, n * ents), BF), pltpu.VMEM((cap, LANES), BF), pltpu.VMEM((cap, LANES), BF)],
            2 * cap * n * ents * LANES,
            "form",
        )(scaled, slopes, asked, messages[n // 2])
        for offsets in [[0, 1, n - 1], [n // 2], *rest[::-1]]:
            totals = add_up(offsets, [messages[k] for k in offsets], totals, offsets == rest[0])
        grad_dim, grad_msg, grad_self, grad_neigh = totals
    else:
        fact_me = lax.axis_index("fact")
        sent = [message for k in range(0, n, 8) for message in spread(list(range(k, k + 8)))]
        by_owner = jnp.take(jnp.stack(sent), lax.rem(jnp.arange(n) - fact_me + n, n), axis=0)
        owned = lax.all_to_all(by_owner, "fact", 0, 0)
        by_offset = jnp.take(owned, lax.rem(fact_me - jnp.arange(n) + n, n), axis=0)
        for k in range(0, n, 8):
            totals = add_up(list(range(k, k + 8)), [by_offset[k + i] for i in range(8)], totals, k + 8 >= n)
        grad_dim, grad_msg, _, _ = totals
        pair_sum = lax.psum_scatter(pairs[0], "fact", scatter_dimension=0, tiled=True)[0]
        grad_self, grad_neigh = pair_sum[0:own], pair_sum[stride : stride + own]
    return output_h, grad_msg, grad_self, grad_neigh, grad_dim


def solution(mesh):
    placed = (
        P("fact", "feat"),
        P("fact", None),
        P("fact"),
        P("fact", None),
        P("fact"),
        P("fact", "feat"),
        P("fact", "feat"),
        P(None, "feat"),
        P(None, "feat"),
        P(None, "feat"),
        P("fact", "feat"),
    )
    return jax.shard_map(
        shards,
        mesh=mesh,
        in_specs=placed,
        out_specs=(P("fact", "feat"),) * 5,
        check_vma=False,
    )
```

```python
import functools

import jax
import jax.numpy as jnp
from jax import lax
from jax.experimental import pallas as pl
from jax.experimental.pallas import tpu as pltpu
from jax.sharding import PartitionSpec as P

LANES = 128
BF = jnp.bfloat16
IN_HBM = pl.BlockSpec(memory_space=pltpu.HBM)
IN_VMEM = pl.BlockSpec(memory_space=pltpu.VMEM)
F32 = jnp.float32
VMEM_LIMIT = 16 * 1024 * 1024
VMEM_LIMIT_LARGE = 40 * 1024 * 1024


def call(kernel, out_shape, scratch, flops, name, limit=VMEM_LIMIT, **specs):
    return pl.pallas_call(
        kernel,
        out_shape=out_shape,
        scratch_shapes=scratch,
        compiler_params=pltpu.CompilerParams(vmem_limit_bytes=limit),
        cost_estimate=pl.CostEstimate(flops=flops, bytes_accessed=1 << 20, transcendentals=0),
        name=name,
        **specs,
    )


def shape(dims, dtype):
    return jax.ShapeDtypeStruct(dims, dtype)


def nt(a, b):
    return lax.dot_general(a, b, (((1,), (1,)), ((), ())), preferred_element_type=F32)


def tn(a, b):
    return lax.dot_general(a, b, (((0,), (0,)), ((), ())), preferred_element_type=F32)


def dot(a, b):
    return jnp.dot(a, b, preferred_element_type=F32)


def flag(condition):
    return jnp.where(condition, 1.0, 0.0).astype(BF)


def column_codes(row):
    keys = jnp.broadcast_to(row, (LANES, LANES)).astype(F32).T.astype(jnp.int32)
    lane = lax.broadcasted_iota(jnp.int32, (LANES, LANES), 1)
    return flag((keys & (LANES - 1)) == lane), (keys >> 7).astype(F32).astype(BF)


def row_codes(row):
    keys = jnp.broadcast_to(row, (LANES, LANES))
    sub = lax.broadcasted_iota(jnp.int32, (LANES, LANES), 0)
    high = jnp.broadcast_to((row >> 7).astype(F32), (16, LANES)).astype(BF)
    return flag((keys & (LANES - 1)) == sub), high


def pick_block(low, high, block):
    zero = jnp.zeros((), BF)
    return jnp.where(high == block, low, zero)


def pick_rows(low, high, block):
    wide = low.reshape(LANES // 16, 16, low.shape[1])
    picked = pick_block(wide, high[None], block)
    return picked.reshape(low.shape)


def route_kernel(n, cap, ents, dims, *refs):
    given, (out_ref, pos_ref, ent_ref, dlow_ref, dhigh_ref), held_refs, sems = refs[:4], refs[4:9], refs[9:13], refs[13]
    copies = [pltpu.make_async_copy(src, dst, sems.at[i]) for i, (src, dst) in enumerate(zip(given, held_refs))]
    for copy in copies:
        copy.start()
    for copy in copies:
        copy.wait()
    do_ref, ds_ref, fo_ref, fs_ref = held_refs
    chunks = do_ref.shape[0]
    owner = do_ref[...]
    kind = lax.broadcasted_iota(jnp.int32, (n, chunks, LANES), 0)
    held = jnp.where(kind == owner[None], 1.0, 0.0).reshape(n * chunks, LANES)
    held_bf = held.astype(BF)
    i0 = lax.broadcasted_iota(jnp.int32, (LANES, LANES), 0)
    i1 = lax.broadcasted_iota(jnp.int32, (LANES, LANES), 1)
    inside = dot(held_bf, flag(i0 < i1))
    r0 = lax.broadcasted_iota(jnp.int32, (n * chunks, n * chunks), 0)
    r1 = lax.broadcasted_iota(jnp.int32, (n * chunks, n * chunks), 1)
    earlier = flag((r0 // chunks == r1 // chunks) & (r1 < r0))
    before = dot(dot(earlier, held_bf).astype(BF), jnp.ones((LANES, LANES), BF))
    rank = jnp.sum((held * (inside + before)).reshape(n, chunks, LANES), axis=0)
    rank = rank.astype(jnp.int32)
    entity_owner = fo_ref[...]
    entity_slot = fs_ref[...]
    value = ds_ref[...]
    pos_ref[...] = owner * cap + rank
    ent_ref[...] = entity_owner * ents + entity_slot
    fact_dim = owner * dims + value
    high = (value >> 5).astype(F32)
    low = (value & 31).astype(F32)
    names = lax.broadcasted_iota(jnp.int32, (n, LANES), 0)
    places = lax.broadcasted_iota(jnp.int32, (cap, LANES), 0)
    slots = lax.broadcasted_iota(jnp.int32, (ents, LANES), 0)
    asked_high = jnp.zeros((n, cap), F32)
    asked_low = jnp.zeros((n, cap), F32)
    hits = jnp.zeros((n, ents), F32)
    for k in range(chunks):
        here = slice(k * LANES, (k + 1) * LANES)
        mine = jnp.where(names == owner[k : k + 1], 1.0, 0.0)
        at = flag(places == rank[k : k + 1])
        asked_high += nt((mine * high[k : k + 1]).astype(BF), at)
        asked_low += nt((mine * low[k : k + 1]).astype(BF), at)
        hits += nt(flag(names == entity_owner[k : k + 1]), flag(slots == entity_slot[k : k + 1]))
        dlow_ref[here, :], dhigh_ref[here, :] = column_codes(fact_dim[k : k + 1])
    asked = (asked_high * 32.0 + asked_low).astype(jnp.int32)
    for r in range(cap // LANES):
        out_ref[:, r, :] = asked[:, r * LANES : (r + 1) * LANES]
    out_ref[:, cap // LANES, :] = hits.astype(jnp.int32)


def fill_rows(low_ref, high_ref, rows, blocks, firsts, hot_ref):
    at = 0
    low, high = low_ref[rows, :], high_ref[rows, :]
    for count, first in zip(blocks, firsts):
        for k in range(count):
            hot_ref[:, at : at + LANES] = pick_block(low, high, (first + k).astype(F32).astype(BF))
            at += LANES


def multiply_rows(table_refs, hot_ref):
    total, at = None, 0
    for table in table_refs:
        part = dot(hot_ref[:, at : at + table.shape[0]], table[...])
        total = part if total is None else total + part
        at += table.shape[0]
    return total


def gather_rows(low_ref, high_ref, rows, table_refs, firsts, hot_ref):
    fill_rows(low_ref, high_ref, rows, [table.shape[0] // LANES for table in table_refs], firsts, hot_ref)
    return multiply_rows(table_refs, hot_ref)


def ring_at(place, n):
    place = lax.rem(place + 2 * n, n)
    return jnp.where(place < n // 2, 2 * place, 2 * (n - 1 - place) + 1)


def ring_place(index, n):
    half = lax.div(index, 2)
    return jnp.where(lax.rem(index, 2) == 0, half, n - 1 - half)


def look_kernel(n, pieces, low_ref, high_ref, *refs):
    count = len(pieces)
    tables, base_ref, out_ref, hot_ref = refs[:count], refs[count], refs[-2], refs[-1]
    facts = low_ref.shape[0]
    step = hot_ref.shape[0]
    place = ring_place(lax.axis_index("fact"), n)
    firsts = [lax.div(ring_at(place + hops, n) * dims + row, LANES) for hops, row, dims in pieces]
    for c in range(facts // step):
        rows = slice(c * step, (c + 1) * step)
        out_ref[rows, :] = base_ref[rows, :] + gather_rows(low_ref, high_ref, rows, tables, firsts, hot_ref)


def message_kernel(n, pieces, low_ref, high_ref, *refs):
    count = len(pieces)
    sources, refs = refs[:count], refs[count:]
    base_ref, xw_ref, ent_ref, slope_out, part_out, slope_ref, hot_ref, msg_ref, erlow_ref, erhigh_ref = refs[:10]
    part_ref, tables, (sem, table_sem, part_sem) = refs[10], refs[11 : 11 + count], refs[11 + count :]
    arrivals = [pltpu.make_async_copy(src, dst, table_sem) for src, dst in zip(sources, tables)]
    for copy in arrivals:
        copy.start()
    facts = low_ref.shape[0]
    step = hot_ref.shape[1]
    place = ring_place(lax.axis_index("fact"), n)
    firsts = [lax.div(ring_at(place + hops, n) * dims + row, LANES) for hops, row, dims in pieces]
    if count:
        for c in range(facts // step):
            rows = slice(c * step, (c + 1) * step)
            fill_rows(low_ref, high_ref, rows, [table.shape[0] // LANES for table in tables], firsts, hot_ref.at[c])
    for k in range(ent_ref.shape[0]):
        here = slice(k * LANES, (k + 1) * LANES)
        erlow_ref[:, here], erhigh_ref[:, here] = row_codes(ent_ref[k : k + 1, :])
    for copy in arrivals:
        copy.wait()
    for c in range(facts // step):
        rows = slice(c * step, (c + 1) * step)
        pre = xw_ref[rows, :] + base_ref[rows, :]
        if count:
            pre = pre + multiply_rows(tables, hot_ref.at[c])
        gate = jax.nn.sigmoid(pre)
        msg_ref[rows, :] = (pre * gate).astype(BF)
        slope_ref[rows, :] = gate * (1.0 + pre * (1.0 - gate))
    keep = pltpu.make_async_copy(slope_ref, slope_out, sem)
    keep.start()

    def add(pair, carry):
        hot = jnp.concatenate(
            [pick_rows(erlow_ref[...], erhigh_ref[...], (pair * 2 + i).astype(F32).astype(BF)) for i in range(2)], axis=0
        )
        rows = pl.ds(pl.multiple_of(pair * 256, 256), 256)
        part_ref[rows, :] = dot(hot, msg_ref[...]).astype(BF)
        return carry

    groups = part_ref.shape[0] // 256
    copies = [keep]
    if groups <= 8:
        for pair in range(groups):
            add(jnp.int32(pair), 0)
            rows = slice(pair * 256, (pair + 1) * 256)
            copies.append(pltpu.make_async_copy(part_ref.at[rows, :], part_out.at[rows, :], part_sem.at[pair]))
            copies[-1].start()
    else:
        lax.fori_loop(0, groups, add, 0)
        copies.append(pltpu.make_async_copy(part_ref, part_out, part_sem.at[0]))
        copies[-1].start()
    for copy in copies:
        copy.wait()


def project_kernel(m, w_ref, *refs):
    blocks, out_ref = refs[:m], refs[m]
    me = lax.axis_index("feat")
    total = None
    for j, ref in enumerate(blocks):
        rows = pl.ds(pl.multiple_of((me ^ j) * LANES, LANES), LANES)
        part = dot(ref[...], w_ref[rows, :])
        total = part if total is None else total + part
    out_ref[...] = total


def ready_kernel(m, width, ents, *refs):
    x_refs, all_refs, (hidden_ref, xt_ref) = refs[:m], refs[m : 2 * m], refs[2 * m :]
    me = lax.axis_index("feat")
    for j in range(m):
        hidden_ref[me ^ j] = all_refs[j][2 * width : 2 * width + ents, :]
        xt_ref[pl.ds(pl.multiple_of((me ^ j) * LANES, LANES), LANES), :] = x_refs[j][...].T


def entity_kernel(n, m, width, ents, sums_ref, idx_ref, *refs):
    all_refs, refs = refs[:m], refs[m:]
    back_ref, out_ref, pre_ref, agg_ref, own_ref, hold_ref, words_ref, scaled_ref, sem, back_sem = refs
    fetch = pltpu.make_async_copy(idx_ref, words_ref, sem)
    fetch.start()
    rows_each = ents // m
    me = lax.axis_index("feat")
    totals = []
    for b in range(m):
        total = sums_ref[b].astype(F32)
        for f in range(1, n):
            total += sums_ref[f * m + b].astype(F32)
        totals.append(total)
    fetch.wait()
    hits = jnp.sum(words_ref[:, words_ref.shape[1] - 1, :], axis=0, keepdims=True).astype(F32)
    hold_ref[...] = jnp.maximum(jnp.broadcast_to(hits, (LANES, ents)).T, 1.0)
    divisor = hold_ref[pl.ds(pl.multiple_of(me * rows_each, rows_each), rows_each), :]
    for b in range(m):
        agg_ref[b * rows_each : (b + 1) * rows_each, :] = (totals[b] / divisor).astype(BF)
    at = pl.multiple_of(2 * width + me * rows_each, rows_each)
    for j in range(m):
        own_ref[me ^ j] = all_refs[j][pl.ds(at, rows_each), :]
    aggregate = jnp.concatenate([agg_ref[b * rows_each : (b + 1) * rows_each, :] for b in range(m)], axis=1)
    hidden = jnp.concatenate([own_ref[b] for b in range(m)], axis=1)
    d_agg = None
    for j in range(m):
        pre = dot(hidden, all_refs[j][0:width, :]) + dot(aggregate, all_refs[j][width : 2 * width, :])
        gate = jax.nn.sigmoid(pre)
        cot = all_refs[j][pl.ds(at + ents, rows_each), :].astype(F32)
        d_pre = (cot * (gate * (1.0 + pre * (1.0 - gate)))).astype(BF)
        out_ref[me ^ j] = (pre * gate).astype(BF)
        pre_ref[me ^ j] = d_pre
        term = nt(d_pre, all_refs[j][width : 2 * width, :])
        d_agg = term if d_agg is None else d_agg + term
    for b in range(m):
        scaled_ref[b] = (d_agg[:, b * LANES : (b + 1) * LANES] / divisor).astype(BF)
    copies = [
        pltpu.make_async_copy(scaled_ref, back_ref.at[f * m : (f + 1) * m], back_sem.at[f]) for f in range(n)
    ]
    for copy in copies:
        copy.start()
    for copy in copies:
        copy.wait()


def share_kernel(m, out_ref, pre_ref, agg_ref, *share_refs):
    rows_each = out_ref.shape[1]
    me = lax.axis_index("feat")
    for j, ref in enumerate(share_refs):
        ref[0:rows_each, :] = out_ref[me ^ j]
        ref[rows_each : 2 * rows_each, :] = pre_ref[me ^ j]
        ref[2 * rows_each :, :] = agg_ref[...]


def weight_kernel(n, m, width, stride, hidden_ref, *refs):
    got, (out_ref, back_ref, total_ref, pre_ref, agg_ref) = refs[:m], refs[m:]
    rows_each = got[0].shape[0] // (2 + m)
    own = width // n
    me = lax.axis_index("feat")
    for j, ref in enumerate(got):
        here = pl.ds(pl.multiple_of((me ^ j) * rows_each, rows_each), rows_each)
        out_ref[here, :] = ref[0:rows_each, :]
        pre_ref[here, :] = ref[rows_each : 2 * rows_each, :]
        for b in range(m):
            agg_ref[b, here, :] = ref[(2 + b) * rows_each : (3 + b) * rows_each, :]
    d_pre = pre_ref[...]
    for which, blocks in enumerate((hidden_ref, agg_ref)):
        for b in range(m):
            total_ref[b * LANES : (b + 1) * LANES, :] = tn(blocks[b], d_pre)
        for d in range(n):
            back_ref[d % 2, d // 2, which * stride : (which + 1) * stride, :] = padded(
                total_ref[d * own : (d + 1) * own, :], stride
            )


def halves_kernel(back_ref, keep_ref, give_ref):
    odd = lax.rem(lax.axis_index("fact"), 2)
    keep_ref[...] = back_ref[odd]
    give_ref[...] = back_ref[1 - odd].astype(BF)


def padded(piece, rows):
    if piece.shape[0] == rows:
        return piece
    return jnp.concatenate([piece, jnp.zeros((rows - piece.shape[0], LANES), F32)], axis=0)


def codes_kernel(pos_ref, ent_ref, plow_ref, phigh_ref, elow_ref, ehigh_ref):
    for k in range(pos_ref.shape[0]):
        here = slice(k * LANES, (k + 1) * LANES)
        plow_ref[:, here], phigh_ref[:, here] = row_codes(pos_ref[k : k + 1, :])
        elow_ref[here, :], ehigh_ref[here, :] = column_codes(ent_ref[k : k + 1, :])


def request_kernel(n, cap, req_ref, low_ref, high_ref):
    for s in range(n):
        for r in range(cap // LANES):
            at = s * cap + r * LANES
            low_ref[:, at : at + LANES], high_ref[:, at : at + LANES] = row_codes(req_ref[s, r : r + 1, :])


def backward_kernel(n, stride, slope_in, scaled_ref, low_ref, high_ref, xt_ref, dmsg_ref, share_ref, hot_ref, slope_ref, sem):
    fetch = pltpu.make_async_copy(slope_in, slope_ref, sem)
    fetch.start()
    facts = slope_ref.shape[0]
    own = xt_ref.shape[0] // n
    step = hot_ref.shape[0]
    for c in range(facts // step):
        rows = slice(c * step, (c + 1) * step)
        found = gather_rows(low_ref, high_ref, rows, [scaled_ref], [jnp.int32(0)], hot_ref)
        if c == 0:
            fetch.wait()
        dmsg_ref[rows, :] = (found * slope_ref[rows, :]).astype(BF)
    total = dot(xt_ref[...], dmsg_ref[...])
    for d in range(n):
        share_ref[d] = padded(total[d * own : (d + 1) * own, :], stride).astype(BF)


def spread_kernel(n, cap, stride, offsets, plow_ref, phigh_ref, dmsg_ref, share_ref, *refs):
    pair_refs, out_refs = refs[:-len(offsets)], refs[-len(offsets) :]
    me = lax.axis_index("fact")
    for offset, out_ref in zip(offsets, out_refs):
        d = lax.rem(me + offset, n)
        hot = jnp.concatenate(
            [
                pick_rows(plow_ref[...], phigh_ref[...], (d * (cap // LANES) + i).astype(F32).astype(BF))
                for i in range(cap // LANES)
            ],
            axis=0,
        )
        out_ref[0:cap, :] = dot(hot, dmsg_ref[...]).astype(BF)
        out_ref[cap : cap + stride, :] = share_ref[d]
        if out_ref.shape[0] > cap + stride:
            pair = pair_refs[0][lax.div(d, 2)]
            for ref in pair_refs[1:]:
                pair = pair + ref[lax.div(d, 2)].astype(F32)
            out_ref[cap + stride :, :] = pair.astype(BF)


def table_kernel(n, cap, stride, offsets, first, final, low_ref, high_ref, *refs):
    count = len(offsets)
    got, refs = refs[:count], refs[count:]
    if not first:
        (base_ref, weight_base_ref), refs = refs[:2], refs[2:]
    out_ref, refs = refs[0], refs[1:]
    final_refs, refs = (refs[:3], refs[3:]) if final else ((), refs[1:] + refs[:1])
    rows_ref, klow_ref, khigh_ref, weight_ref = refs[:4]
    me = lax.axis_index("fact")
    if first:
        weight_ref[...] = jnp.zeros(weight_ref.shape, F32)
    else:
        weight_ref[...] = weight_base_ref[...]
    for j, (offset, ref) in enumerate(zip(offsets, got)):
        source = lax.rem(me + (n - offset), n)
        here = slice(j * cap, (j + 1) * cap)
        there = pl.ds(pl.multiple_of(source * cap, LANES), cap)
        rows_ref[here, :] = ref[0:cap, :]
        klow_ref[:, here] = low_ref[:, there]
        khigh_ref[:, here] = high_ref[:, there]
        rows = ref.shape[0] - cap
        weight_ref[0:rows, :] += ref[cap:, :].astype(F32)
    copies = []
    for which, ref in enumerate(final_refs):
        copies.append(
            pltpu.make_async_copy(
                weight_ref.at[which * stride : which * stride + ref.shape[0], :], ref, refs[6].at[which]
            )
        )
        copies[-1].start()
    blocks = out_ref.shape[0] // LANES
    join = 2 if blocks % 2 == 0 else 1

    target_ref = refs[4] if final else out_ref
    for group in range(blocks // join):
        hot = jnp.concatenate(
            [pick_rows(klow_ref[...], khigh_ref[...], jnp.array(group * join + i, BF)) for i in range(join)], axis=0
        )
        rows = slice(group * join * LANES, (group + 1) * join * LANES)
        sums = dot(hot, rows_ref[...])
        target_ref[rows, :] = sums if first else base_ref[rows, :] + sums
        if final:
            copies.append(pltpu.make_async_copy(target_ref.at[rows, :], out_ref.at[rows, :], refs[5].at[group]))
            copies[-1].start()
    for copy in copies:
        copy.wait()


def shards(fact_x, dim_owner, dim_slot, fact_owner, fact_slot, dim_table, entity_h, w_msg, w_self, w_neigh, cotangent):
    n, m = lax.axis_size("fact"), lax.axis_size("feat")
    assert m == 4 and n % 2 == 0
    facts = fact_x.shape[0]
    chunks = facts // LANES
    ents = entity_h.shape[0]
    rows_each = ents // m
    width = w_msg.shape[0]
    dims = dim_table.shape[0]
    cap = -(-(3 * facts // n) // LANES) * LANES
    slots = n * cap
    groups = cap // LANES + 1
    own = width // n
    stride = max(16, own)
    step = 512
    tie = lax.optimization_barrier
    ringed = n <= 8
    limit = VMEM_LIMIT if ringed else VMEM_LIMIT_LARGE

    ring = [2 * p if p < n // 2 else 2 * (n - 1 - p) + 1 for p in range(n)]
    to_right = [(ring[p], ring[(p + 1) % n]) for p in range(n)]
    to_left = [(ring[(p + 1) % n], ring[p]) for p in range(n)]

    def pass_on(right, left):
        return lax.ppermute(right, "fact", to_right), lax.ppermute(left, "fact", to_left)

    def swap(block, bit):
        return lax.ppermute(block, "feat", [(i, i ^ bit) for i in range(m)])

    if ringed:
        right, left = pass_on(dim_table, dim_table)
    x_near = swap(fact_x, 1)
    by_lane = (chunks, LANES)
    columns = shape((facts, LANES), BF)
    asks, pos, entity, dlow, dhigh = call(
        functools.partial(route_kernel, n, cap, ents, dims),
        (
            shape((n, groups, LANES), jnp.int32),
            shape(by_lane, jnp.int32),
            shape(by_lane, jnp.int32),
            columns,
            columns,
        ),
        [pltpu.VMEM(by_lane, jnp.int32)] * 4 + [pltpu.SemaphoreType.DMA((4,))],
        1 << 28,
        "route",
        in_specs=[IN_HBM] * 4,
    )(dim_owner.reshape(by_lane), dim_slot.reshape(by_lane), fact_owner.reshape(by_lane), fact_slot.reshape(by_lane))
    if ringed:
        right, left, x_near, asks, pos, entity, dlow, dhigh = tie(
            (right, left, x_near, asks, pos, entity, dlow, dhigh)
        )

    def look(pieces, tables, base):
        rows = sum(t.shape[0] for t in tables)
        return call(
            functools.partial(look_kernel, n, pieces),
            shape((facts, LANES), F32),
            [pltpu.VMEM((step, rows), BF)],
            2 * facts * rows * LANES,
            "look",
            limit,
        )(dlow, dhigh, *tables, base)

    def project(blocks):
        return call(
            functools.partial(project_kernel, m), shape((facts, LANES), F32), [], 2 * facts * width * LANES, "project"
        )(w_msg, *blocks)

    found = jnp.zeros((facts, LANES), F32)
    weights = jnp.concatenate([w_self, w_neigh, entity_h, cotangent], axis=0)
    if ringed:
        near = (right, left)
        after = pass_on(*near)
        x_far = swap(fact_x, 2)
        found = look([(0, 0, dims), (-1, 0, dims), (1, 0, dims)], [dim_table, *near], found)
        right, left, x_far, found, weights = tie((*after, x_far, found, weights))
        for k in range(2, n // 2 - 1):
            after = pass_on(right, left)
            x_last = swap(x_far, 1)
            found = look([(-k, 0, dims), (k, 0, dims)], [right, left], found)
            right, left, found, x_last = tie((*after, found, x_last))
        all_far = swap(weights, 2)
        k = n // 2 - 1
        after = lax.ppermute(right, "fact", to_right)
        xw = project([fact_x, x_near, x_far, x_last])
        found = look([(k, 0, dims)], [left], found)
        found, asks = tie((found, asks))
        asked = lax.all_to_all(asks, "fact", 0, 0)
        found = look([(-k, 0, dims)], [right], found)
        all_near = swap(weights, 1)
        found, all_far, all_near = tie((found, all_far, all_near))
        last, last_pieces = [after], [(n // 2, 0, dims)]
    else:
        asked = lax.all_to_all(asks, "fact", 0, 0)
        x_far = swap(fact_x, 2)
        x_last = swap(x_far, 1)
        xw = project([fact_x, x_near, x_far, x_last])
        all_far, all_near = swap(weights, 2), swap(weights, 1)
        whole = lax.all_gather(dim_table, "fact")
        order = jnp.take(whole, ring_at(ring_place(lax.axis_index("fact"), n) + jnp.arange(n), n), axis=0)
        for k in range(0, n, 8):
            found = look([(k + i, 0, dims) for i in range(8)], [order[k + i] for i in range(8)], found)
        last, last_pieces = [], []
    all_last = swap(all_far, 1)
    x_blocks, all_blocks = [fact_x, x_near, x_far, x_last], [weights, all_near, all_far, all_last]
    last_rows = max(LANES, sum(t.shape[0] for t in last))
    slope, part = call(
        functools.partial(message_kernel, n, last_pieces),
        (pltpu.HBM((facts, LANES), F32), shape((n * ents, LANES), BF)),
        [
            pltpu.VMEM((facts, LANES), F32),
            pltpu.VMEM((facts // step, step, last_rows), BF),
            pltpu.VMEM((facts, LANES), BF),
            pltpu.VMEM((LANES, facts), BF),
            pltpu.VMEM((16, facts), BF),
            pltpu.VMEM((n * ents, LANES), BF),
            *[pltpu.VMEM(t.shape, BF) for t in last],
            pltpu.SemaphoreType.DMA,
            pltpu.SemaphoreType.DMA,
            pltpu.SemaphoreType.DMA((8,)),
        ],
        2 * facts * (last_rows + n * ents) * LANES,
        "message",
        limit,
        in_specs=[IN_VMEM] * 2 + [pl.BlockSpec(memory_space=pl.ANY)] * len(last) + [IN_VMEM] * 3,
        out_specs=(IN_HBM, IN_HBM),
    )(dlow, dhigh, *last, found, xw, entity)
    sums = lax.all_to_all(part.reshape(n * m, rows_each, LANES), ("fact", "feat"), 0, 0)
    pos, entity, x_blocks, _ = tie((pos, entity, x_blocks, part))
    hidden, x_turned = call(
        functools.partial(ready_kernel, m, width, ents),
        (shape((m, ents, LANES), BF), shape((width, facts), BF)),
        [],
        1 << 28,
        "ready",
    )(*x_blocks, *all_blocks)
    by_feat = shape((m, rows_each, LANES), BF)
    back, out_parts, pre_parts, agg_parts = call(
        functools.partial(entity_kernel, n, m, width, ents),
        (shape((n * m, rows_each, LANES), BF), by_feat, by_feat, shape((m * rows_each, LANES), BF)),
        [
            pltpu.VMEM((m, rows_each, LANES), BF),
            pltpu.VMEM((ents, LANES), F32),
            pltpu.VMEM(asked.shape, jnp.int32),
            pltpu.VMEM((m, rows_each, LANES), BF),
            pltpu.SemaphoreType.DMA,
            pltpu.SemaphoreType.DMA((n,)),
        ],
        6 * rows_each * width * width,
        "entity",
        in_specs=[IN_VMEM, pl.BlockSpec(memory_space=pl.ANY)] + [IN_VMEM] * m,
        out_specs=(IN_HBM, IN_VMEM, IN_VMEM, IN_VMEM),
    )(sums, asked, *all_blocks)
    scaled = lax.all_to_all(back, ("fact", "feat"), 0, 0).reshape(n * ents, LANES)
    shares = call(
        functools.partial(share_kernel, m),
        tuple(shape(((2 + m) * rows_each, LANES), BF) for _ in range(m)),
        [],
        1 << 20,
        "share",
    )(out_parts, pre_parts, agg_parts)
    got = [shares[0]] + [swap(shares[j], j) for j in range(1, m)]
    pos, entity, asked, _ = tie((pos, entity, asked, back))
    plow, phigh, elow, ehigh = call(
        codes_kernel,
        (shape((LANES, facts), BF), shape((16, facts), BF), columns, columns),
        [],
        1 << 26,
        "codes",
    )(pos, entity)
    rlow, rhigh = call(
        functools.partial(request_kernel, n, cap),
        (shape((LANES, slots), BF), shape((16, slots), BF)),
        [],
        1 << 26,
        "requests",
        limit,
    )(asked)
    pair_shape = (n // 2, 2 * stride, LANES)
    output_h, pair = call(
        functools.partial(weight_kernel, n, m, width, stride),
        (shape((ents, LANES), BF), shape((2, *pair_shape), F32)),
        [pltpu.VMEM((width, LANES), F32), pltpu.VMEM((ents, LANES), BF), pltpu.VMEM((m, ents, LANES), BF)],
        4 * ents * width * LANES,
        "weight",
    )(hidden, *got)
    if ringed:
        keep, give = call(halves_kernel, (shape(pair_shape, F32), shape(pair_shape, BF)), [], 1 << 20, "halves")(pair)
        pairs = [keep, lax.ppermute(give, "fact", [(i, i ^ 1) for i in range(n)])]
    else:
        pairs = [jnp.stack([pair[0], pair[1]], axis=1).reshape(n, 2 * stride, LANES)]
    d_msg, msg_share = call(
        functools.partial(backward_kernel, n, stride),
        (columns, shape((n, stride, LANES), BF)),
        [pltpu.VMEM((step, n * ents), BF), pltpu.VMEM((facts, LANES), F32), pltpu.SemaphoreType.DMA],
        2 * facts * (n * ents + width) * LANES,
        "backward",
        limit,
        in_specs=[IN_HBM] + [IN_VMEM] * 4,
    )(slope, scaled, elow, ehigh, x_turned)

    def spread(offsets):
        lengths = [cap + (3 if ringed and k % 2 == 0 else 1) * stride for k in offsets]
        return call(
            functools.partial(spread_kernel, n, cap, stride, offsets),
            tuple(shape((rows, LANES), BF) for rows in lengths),
            [],
            2 * facts * cap * LANES * len(offsets),
            "spread",
            limit,
        )(plow, phigh, d_msg, msg_share, *(pairs if max(lengths) > cap + stride else ()))

    def add_up(offsets, got, base, final):
        weight = shape((3 * stride, LANES), F32)
        scratch = [
            pltpu.VMEM((cap * len(got), LANES), BF),
            pltpu.VMEM((LANES, cap * len(got)), BF),
            pltpu.VMEM((16, cap * len(got)), BF),
        ]
        return call(
            functools.partial(table_kernel, n, cap, stride, offsets, base is None, final),
            (shape((dims, LANES), F32),) + ((shape((own, LANES), F32),) * 3 if final else (weight,)),
            scratch
            + (
                [
                    pltpu.VMEM(weight.shape, F32),
                    pltpu.VMEM((dims, LANES), F32),
                    pltpu.SemaphoreType.DMA((dims // LANES,)),
                    pltpu.SemaphoreType.DMA((3,)),
                ]
                if final
                else []
            ),
            2 * cap * dims * LANES * len(got),
            "table",
            limit,
            **(dict(out_specs=(IN_HBM,) * 4) if final else {}),
        )(rlow, rhigh, *got, *(base or ()))

    totals = None
    if ringed:
        messages = {}
        rest = [[k, n - k] for k in range(n // 2 - 1, 1, -1)]
        for offsets in [rest[0], [n // 2], [1, n - 1], *rest[1:]]:
            for offset, message in zip(offsets, spread(offsets)):
                messages[offset] = lax.ppermute(message, "fact", [(i, (i + offset) % n) for i in range(n)])
        messages[0] = spread([0])[0]
        for offsets in [[0, 1, n - 1], [n // 2], *rest[::-1]]:
            totals = add_up(offsets, [messages[k] for k in offsets], totals, offsets == rest[0])
        grad_dim, grad_msg, grad_self, grad_neigh = totals
    else:
        fact_me = lax.axis_index("fact")
        sent = [message for k in range(0, n, 8) for message in spread(list(range(k, k + 8)))]
        by_owner = jnp.take(jnp.stack(sent), lax.rem(jnp.arange(n) - fact_me + n, n), axis=0)
        owned = lax.all_to_all(by_owner, "fact", 0, 0)
        by_offset = jnp.take(owned, lax.rem(fact_me - jnp.arange(n) + n, n), axis=0)
        for k in range(0, n, 8):
            totals = add_up(list(range(k, k + 8)), [by_offset[k + i] for i in range(8)], totals, k + 8 >= n)
        grad_dim, grad_msg, _, _ = totals
        pair_sum = lax.psum_scatter(pairs[0], "fact", scatter_dimension=0, tiled=True)[0]
        grad_self, grad_neigh = pair_sum[0:own], pair_sum[stride : stride + own]
    return output_h, grad_msg, grad_self, grad_neigh, grad_dim


def solution(mesh):
    placed = (
        P("fact", "feat"),
        P("fact", None),
        P("fact"),
        P("fact", None),
        P("fact"),
        P("fact", "feat"),
        P("fact", "feat"),
        P(None, "feat"),
        P(None, "feat"),
        P(None, "feat"),
        P("fact", "feat"),
    )
    return jax.shard_map(
        shards,
        mesh=mesh,
        in_specs=placed,
        out_specs=(P("fact", "feat"),) * 5,
        check_vma=False,
    )
```

```python
import functools

import jax
import jax.numpy as jnp
from jax import lax
from jax.experimental import pallas as pl
from jax.experimental.pallas import tpu as pltpu
from jax.sharding import PartitionSpec as P

LANES = 128
BF = jnp.bfloat16
IN_HBM = pl.BlockSpec(memory_space=pltpu.HBM)
IN_VMEM = pl.BlockSpec(memory_space=pltpu.VMEM)
F32 = jnp.float32
VMEM_LIMIT = 10 * 1024 * 1024
VMEM_LIMIT_LARGE = 40 * 1024 * 1024


def call(kernel, out_shape, scratch, flops, name, limit=VMEM_LIMIT, **specs):
    return pl.pallas_call(
        kernel,
        out_shape=out_shape,
        scratch_shapes=scratch,
        compiler_params=pltpu.CompilerParams(vmem_limit_bytes=limit),
        cost_estimate=pl.CostEstimate(flops=flops, bytes_accessed=1 << 20, transcendentals=0),
        name=name,
        **specs,
    )


def shape(dims, dtype):
    return jax.ShapeDtypeStruct(dims, dtype)


def nt(a, b):
    return lax.dot_general(a, b, (((1,), (1,)), ((), ())), preferred_element_type=F32)


def tn(a, b):
    return lax.dot_general(a, b, (((0,), (0,)), ((), ())), preferred_element_type=F32)


def dot(a, b):
    return jnp.dot(a, b, preferred_element_type=F32)


def flag(condition):
    return jnp.where(condition, 1.0, 0.0).astype(BF)


def column_codes(row):
    keys = jnp.broadcast_to(row, (LANES, LANES)).astype(F32).T.astype(jnp.int32)
    lane = lax.broadcasted_iota(jnp.int32, (LANES, LANES), 1)
    return flag((keys & (LANES - 1)) == lane), (keys >> 7).astype(F32).astype(BF)


def row_codes(row):
    keys = jnp.broadcast_to(row, (LANES, LANES))
    sub = lax.broadcasted_iota(jnp.int32, (LANES, LANES), 0)
    high = jnp.broadcast_to((row >> 7).astype(F32), (16, LANES)).astype(BF)
    return flag((keys & (LANES - 1)) == sub), high


def pick_block(low, high, block):
    zero = jnp.zeros((), BF)
    return jnp.where(high == block, low, zero)


def pick_rows(low, high, block):
    wide = low.reshape(LANES // 16, 16, low.shape[1])
    picked = pick_block(wide, high[None], block)
    return picked.reshape(low.shape)


def route_kernel(n, cap, ents, dims, *refs):
    given, (out_ref, pos_ref, ent_ref, dlow_ref, dhigh_ref), held_refs, sems = refs[:4], refs[4:9], refs[9:13], refs[13]
    copies = [pltpu.make_async_copy(src, dst, sems.at[i]) for i, (src, dst) in enumerate(zip(given, held_refs))]
    for copy in copies:
        copy.start()
    for copy in copies:
        copy.wait()
    do_ref, ds_ref, fo_ref, fs_ref = held_refs
    chunks = do_ref.shape[0]
    owner = do_ref[...]
    kind = lax.broadcasted_iota(jnp.int32, (n, chunks, LANES), 0)
    held = jnp.where(kind == owner[None], 1.0, 0.0).reshape(n * chunks, LANES)
    held_bf = held.astype(BF)
    i0 = lax.broadcasted_iota(jnp.int32, (LANES, LANES), 0)
    i1 = lax.broadcasted_iota(jnp.int32, (LANES, LANES), 1)
    inside = dot(held_bf, flag(i0 < i1))
    r0 = lax.broadcasted_iota(jnp.int32, (n * chunks, n * chunks), 0)
    r1 = lax.broadcasted_iota(jnp.int32, (n * chunks, n * chunks), 1)
    earlier = flag((r0 // chunks == r1 // chunks) & (r1 < r0))
    before = dot(dot(earlier, held_bf).astype(BF), jnp.ones((LANES, LANES), BF))
    rank = jnp.sum((held * (inside + before)).reshape(n, chunks, LANES), axis=0)
    rank = rank.astype(jnp.int32)
    entity_owner = fo_ref[...]
    entity_slot = fs_ref[...]
    value = ds_ref[...]
    pos_ref[...] = owner * cap + rank
    ent_ref[...] = entity_owner * ents + entity_slot
    fact_dim = owner * dims + value
    high = (value >> 5).astype(F32)
    low = (value & 31).astype(F32)
    names = lax.broadcasted_iota(jnp.int32, (n, LANES), 0)
    places = lax.broadcasted_iota(jnp.int32, (cap, LANES), 0)
    slots = lax.broadcasted_iota(jnp.int32, (ents, LANES), 0)
    asked_high = jnp.zeros((n, cap), F32)
    asked_low = jnp.zeros((n, cap), F32)
    hits = jnp.zeros((n, ents), F32)
    for k in range(chunks):
        here = slice(k * LANES, (k + 1) * LANES)
        mine = jnp.where(names == owner[k : k + 1], 1.0, 0.0)
        at = flag(places == rank[k : k + 1])
        asked_high += nt((mine * high[k : k + 1]).astype(BF), at)
        asked_low += nt((mine * low[k : k + 1]).astype(BF), at)
        hits += nt(flag(names == entity_owner[k : k + 1]), flag(slots == entity_slot[k : k + 1]))
        dlow_ref[here, :], dhigh_ref[here, :] = column_codes(fact_dim[k : k + 1])
    asked = (asked_high * 32.0 + asked_low).astype(jnp.int32)
    for r in range(cap // LANES):
        out_ref[:, r, :] = asked[:, r * LANES : (r + 1) * LANES]
    out_ref[:, cap // LANES, :] = hits.astype(jnp.int32)


def fill_rows(low_ref, high_ref, rows, blocks, firsts, hot_ref):
    at = 0
    low, high = low_ref[rows, :], high_ref[rows, :]
    for count, first in zip(blocks, firsts):
        for k in range(count):
            hot_ref[:, at : at + LANES] = pick_block(low, high, (first + k).astype(F32).astype(BF))
            at += LANES


def multiply_rows(table_refs, hot_ref):
    total, at = None, 0
    for table in table_refs:
        part = dot(hot_ref[:, at : at + table.shape[0]], table[...])
        total = part if total is None else total + part
        at += table.shape[0]
    return total


def gather_rows(low_ref, high_ref, rows, table_refs, firsts, hot_ref):
    fill_rows(low_ref, high_ref, rows, [table.shape[0] // LANES for table in table_refs], firsts, hot_ref)
    return multiply_rows(table_refs, hot_ref)


def ring_at(place, n):
    place = lax.rem(place + 2 * n, n)
    return jnp.where(place < n // 2, 2 * place, 2 * (n - 1 - place) + 1)


def ring_place(index, n):
    half = lax.div(index, 2)
    return jnp.where(lax.rem(index, 2) == 0, half, n - 1 - half)


def look_kernel(n, pieces, low_ref, high_ref, *refs):
    count = len(pieces)
    tables, base_ref, out_ref, hot_ref = refs[:count], refs[count], refs[-2], refs[-1]
    facts = low_ref.shape[0]
    step = hot_ref.shape[0]
    place = ring_place(lax.axis_index("fact"), n)
    firsts = [lax.div(ring_at(place + hops, n) * dims + row, LANES) for hops, row, dims in pieces]
    for c in range(facts // step):
        rows = slice(c * step, (c + 1) * step)
        out_ref[rows, :] = base_ref[rows, :] + gather_rows(low_ref, high_ref, rows, tables, firsts, hot_ref)


def message_kernel(n, pieces, low_ref, high_ref, *refs):
    count = len(pieces)
    sources, refs = refs[:count], refs[count:]
    base_ref, xw_ref, ent_ref, slope_out, part_out, slope_ref, hot_ref, msg_ref, erlow_ref, erhigh_ref = refs[:10]
    part_ref, tables, (sem, table_sem, part_sem) = refs[10], refs[11 : 11 + count], refs[11 + count :]
    arrivals = [pltpu.make_async_copy(src, dst, table_sem) for src, dst in zip(sources, tables)]
    for copy in arrivals:
        copy.start()
    facts = low_ref.shape[0]
    step = hot_ref.shape[1]
    place = ring_place(lax.axis_index("fact"), n)
    firsts = [lax.div(ring_at(place + hops, n) * dims + row, LANES) for hops, row, dims in pieces]
    if count:
        for c in range(facts // step):
            rows = slice(c * step, (c + 1) * step)
            fill_rows(low_ref, high_ref, rows, [table.shape[0] // LANES for table in tables], firsts, hot_ref.at[c])
    for k in range(ent_ref.shape[0]):
        here = slice(k * LANES, (k + 1) * LANES)
        erlow_ref[:, here], erhigh_ref[:, here] = row_codes(ent_ref[k : k + 1, :])
    for copy in arrivals:
        copy.wait()
    for c in range(facts // step):
        rows = slice(c * step, (c + 1) * step)
        pre = xw_ref[rows, :] + base_ref[rows, :]
        if count:
            pre = pre + multiply_rows(tables, hot_ref.at[c])
        gate = jax.nn.sigmoid(pre)
        msg_ref[rows, :] = (pre * gate).astype(BF)
        slope_ref[rows, :] = gate * (1.0 + pre * (1.0 - gate))
    keep = pltpu.make_async_copy(slope_ref, slope_out, sem)
    keep.start()

    def add(pair, carry):
        hot = jnp.concatenate(
            [pick_rows(erlow_ref[...], erhigh_ref[...], (pair * 2 + i).astype(F32).astype(BF)) for i in range(2)], axis=0
        )
        rows = pl.ds(pl.multiple_of(pair * 256, 256), 256)
        part_ref[rows, :] = dot(hot, msg_ref[...]).astype(BF)
        return carry

    groups = part_ref.shape[0] // 256
    copies = [keep]
    if groups <= 8:
        for pair in range(groups):
            add(jnp.int32(pair), 0)
            rows = slice(pair * 256, (pair + 1) * 256)
            copies.append(pltpu.make_async_copy(part_ref.at[rows, :], part_out.at[rows, :], part_sem.at[pair]))
            copies[-1].start()
    else:
        lax.fori_loop(0, groups, add, 0)
        copies.append(pltpu.make_async_copy(part_ref, part_out, part_sem.at[0]))
        copies[-1].start()
    for copy in copies:
        copy.wait()


def project_kernel(m, w_ref, *refs):
    blocks, out_ref = refs[:m], refs[m]
    me = lax.axis_index("feat")
    total = None
    for j, ref in enumerate(blocks):
        rows = pl.ds(pl.multiple_of((me ^ j) * LANES, LANES), LANES)
        part = dot(ref[...], w_ref[rows, :])
        total = part if total is None else total + part
    out_ref[...] = total


def ready_kernel(m, width, ents, *refs):
    x_refs, all_refs, (hidden_ref, xt_ref) = refs[:m], refs[m : 2 * m], refs[2 * m :]
    me = lax.axis_index("feat")
    for j in range(m):
        hidden_ref[me ^ j] = all_refs[j][2 * width : 2 * width + ents, :]
        xt_ref[pl.ds(pl.multiple_of((me ^ j) * LANES, LANES), LANES), :] = x_refs[j][...].T


def entity_kernel(n, m, width, ents, sums_ref, idx_ref, *refs):
    all_refs, refs = refs[:m], refs[m:]
    back_ref, out_ref, pre_ref, agg_ref, own_ref, hold_ref, words_ref, scaled_ref, sem, back_sem = refs
    fetch = pltpu.make_async_copy(idx_ref, words_ref, sem)
    fetch.start()
    rows_each = ents // m
    me = lax.axis_index("feat")
    totals = []
    for b in range(m):
        total = sums_ref[b].astype(F32)
        for f in range(1, n):
            total += sums_ref[f * m + b].astype(F32)
        totals.append(total)
    fetch.wait()
    hits = jnp.sum(words_ref[:, words_ref.shape[1] - 1, :], axis=0, keepdims=True).astype(F32)
    hold_ref[...] = jnp.maximum(jnp.broadcast_to(hits, (LANES, ents)).T, 1.0)
    divisor = hold_ref[pl.ds(pl.multiple_of(me * rows_each, rows_each), rows_each), :]
    for b in range(m):
        agg_ref[b * rows_each : (b + 1) * rows_each, :] = (totals[b] / divisor).astype(BF)
    at = pl.multiple_of(2 * width + me * rows_each, rows_each)
    for j in range(m):
        own_ref[me ^ j] = all_refs[j][pl.ds(at, rows_each), :]
    aggregate = jnp.concatenate([agg_ref[b * rows_each : (b + 1) * rows_each, :] for b in range(m)], axis=1)
    hidden = jnp.concatenate([own_ref[b] for b in range(m)], axis=1)
    d_agg = None
    for j in range(m):
        pre = dot(hidden, all_refs[j][0:width, :]) + dot(aggregate, all_refs[j][width : 2 * width, :])
        gate = jax.nn.sigmoid(pre)
        cot = all_refs[j][pl.ds(at + ents, rows_each), :].astype(F32)
        d_pre = (cot * (gate * (1.0 + pre * (1.0 - gate)))).astype(BF)
        out_ref[me ^ j] = (pre * gate).astype(BF)
        pre_ref[me ^ j] = d_pre
        term = nt(d_pre, all_refs[j][width : 2 * width, :])
        d_agg = term if d_agg is None else d_agg + term
    for b in range(m):
        scaled_ref[b] = (d_agg[:, b * LANES : (b + 1) * LANES] / divisor).astype(BF)
    copies = [
        pltpu.make_async_copy(scaled_ref, back_ref.at[f * m : (f + 1) * m], back_sem.at[f]) for f in range(n)
    ]
    for copy in copies:
        copy.start()
    for copy in copies:
        copy.wait()


def share_kernel(m, out_ref, pre_ref, agg_ref, *share_refs):
    rows_each = out_ref.shape[1]
    me = lax.axis_index("feat")
    for j, ref in enumerate(share_refs):
        ref[0:rows_each, :] = out_ref[me ^ j]
        ref[rows_each : 2 * rows_each, :] = pre_ref[me ^ j]
        ref[2 * rows_each :, :] = agg_ref[...]


def weight_kernel(n, m, width, stride, hidden_ref, *refs):
    got, (out_ref, back_ref, total_ref, pre_ref, agg_ref) = refs[:m], refs[m:]
    rows_each = got[0].shape[0] // (2 + m)
    own = width // n
    me = lax.axis_index("feat")
    for j, ref in enumerate(got):
        here = pl.ds(pl.multiple_of((me ^ j) * rows_each, rows_each), rows_each)
        out_ref[here, :] = ref[0:rows_each, :]
        pre_ref[here, :] = ref[rows_each : 2 * rows_each, :]
        for b in range(m):
            agg_ref[b, here, :] = ref[(2 + b) * rows_each : (3 + b) * rows_each, :]
    d_pre = pre_ref[...]
    for which, blocks in enumerate((hidden_ref, agg_ref)):
        for b in range(m):
            total_ref[b * LANES : (b + 1) * LANES, :] = tn(blocks[b], d_pre)
        for d in range(n):
            back_ref[d % 2, d // 2, which * stride : (which + 1) * stride, :] = padded(
                total_ref[d * own : (d + 1) * own, :], stride
            )


def halves_kernel(back_ref, keep_ref, give_ref):
    odd = lax.rem(lax.axis_index("fact"), 2)
    keep_ref[...] = back_ref[odd]
    give_ref[...] = back_ref[1 - odd].astype(BF)


def padded(piece, rows):
    if piece.shape[0] == rows:
        return piece
    return jnp.concatenate([piece, jnp.zeros((rows - piece.shape[0], LANES), F32)], axis=0)


def codes_kernel(pos_ref, ent_ref, plow_ref, phigh_ref, elow_ref, ehigh_ref):
    for k in range(pos_ref.shape[0]):
        here = slice(k * LANES, (k + 1) * LANES)
        plow_ref[:, here], phigh_ref[:, here] = row_codes(pos_ref[k : k + 1, :])
        elow_ref[here, :], ehigh_ref[here, :] = column_codes(ent_ref[k : k + 1, :])


def request_kernel(n, cap, req_ref, low_ref, high_ref):
    for s in range(n):
        for r in range(cap // LANES):
            at = s * cap + r * LANES
            low_ref[:, at : at + LANES], high_ref[:, at : at + LANES] = row_codes(req_ref[s, r : r + 1, :])


def backward_kernel(n, stride, slope_in, scaled_ref, low_ref, high_ref, xt_ref, dmsg_ref, share_ref, hot_ref, slope_ref, sem):
    fetch = pltpu.make_async_copy(slope_in, slope_ref, sem)
    fetch.start()
    facts = slope_ref.shape[0]
    own = xt_ref.shape[0] // n
    step = hot_ref.shape[0]
    for c in range(facts // step):
        rows = slice(c * step, (c + 1) * step)
        found = gather_rows(low_ref, high_ref, rows, [scaled_ref], [jnp.int32(0)], hot_ref)
        if c == 0:
            fetch.wait()
        dmsg_ref[rows, :] = (found * slope_ref[rows, :]).astype(BF)
    total = dot(xt_ref[...], dmsg_ref[...])
    for d in range(n):
        share_ref[d] = padded(total[d * own : (d + 1) * own, :], stride).astype(BF)


def spread_kernel(n, cap, stride, offsets, plow_ref, phigh_ref, dmsg_ref, share_ref, *refs):
    pair_refs, out_refs = refs[:-len(offsets)], refs[-len(offsets) :]
    me = lax.axis_index("fact")
    for offset, out_ref in zip(offsets, out_refs):
        d = lax.rem(me + offset, n)
        hot = jnp.concatenate(
            [
                pick_rows(plow_ref[...], phigh_ref[...], (d * (cap // LANES) + i).astype(F32).astype(BF))
                for i in range(cap // LANES)
            ],
            axis=0,
        )
        out_ref[0:cap, :] = dot(hot, dmsg_ref[...]).astype(BF)
        out_ref[cap : cap + stride, :] = share_ref[d]
        if out_ref.shape[0] > cap + stride:
            pair = pair_refs[0][lax.div(d, 2)]
            for ref in pair_refs[1:]:
                pair = pair + ref[lax.div(d, 2)].astype(F32)
            out_ref[cap + stride :, :] = pair.astype(BF)


def table_kernel(n, cap, stride, offsets, first, final, low_ref, high_ref, *refs):
    count = len(offsets)
    got, refs = refs[:count], refs[count:]
    if not first:
        (base_ref, weight_base_ref), refs = refs[:2], refs[2:]
    out_ref, refs = refs[0], refs[1:]
    final_refs, refs = (refs[:3], refs[3:]) if final else ((), refs[1:] + refs[:1])
    rows_ref, klow_ref, khigh_ref, weight_ref = refs[:4]
    me = lax.axis_index("fact")
    if first:
        weight_ref[...] = jnp.zeros(weight_ref.shape, F32)
    else:
        weight_ref[...] = weight_base_ref[...]
    for j, (offset, ref) in enumerate(zip(offsets, got)):
        source = lax.rem(me + (n - offset), n)
        here = slice(j * cap, (j + 1) * cap)
        there = pl.ds(pl.multiple_of(source * cap, LANES), cap)
        rows_ref[here, :] = ref[0:cap, :]
        klow_ref[:, here] = low_ref[:, there]
        khigh_ref[:, here] = high_ref[:, there]
        rows = ref.shape[0] - cap
        weight_ref[0:rows, :] += ref[cap:, :].astype(F32)
    copies = []
    for which, ref in enumerate(final_refs):
        copies.append(
            pltpu.make_async_copy(
                weight_ref.at[which * stride : which * stride + ref.shape[0], :], ref, refs[6].at[which]
            )
        )
        copies[-1].start()
    blocks = out_ref.shape[0] // LANES
    join = 2 if blocks % 2 == 0 else 1

    target_ref = refs[4] if final else out_ref
    for group in range(blocks // join):
        hot = jnp.concatenate(
            [pick_rows(klow_ref[...], khigh_ref[...], jnp.array(group * join + i, BF)) for i in range(join)], axis=0
        )
        rows = slice(group * join * LANES, (group + 1) * join * LANES)
        sums = dot(hot, rows_ref[...])
        target_ref[rows, :] = sums if first else base_ref[rows, :] + sums
        if final:
            copies.append(pltpu.make_async_copy(target_ref.at[rows, :], out_ref.at[rows, :], refs[5].at[group]))
            copies[-1].start()
    for copy in copies:
        copy.wait()


def shards(fact_x, dim_owner, dim_slot, fact_owner, fact_slot, dim_table, entity_h, w_msg, w_self, w_neigh, cotangent):
    n, m = lax.axis_size("fact"), lax.axis_size("feat")
    assert m == 4 and n % 2 == 0
    facts = fact_x.shape[0]
    chunks = facts // LANES
    ents = entity_h.shape[0]
    rows_each = ents // m
    width = w_msg.shape[0]
    dims = dim_table.shape[0]
    cap = -(-(3 * facts // n) // LANES) * LANES
    slots = n * cap
    groups = cap // LANES + 1
    own = width // n
    stride = max(16, own)
    step = 512
    tie = lax.optimization_barrier
    ringed = n <= 8
    limit = VMEM_LIMIT if ringed else VMEM_LIMIT_LARGE

    ring = [2 * p if p < n // 2 else 2 * (n - 1 - p) + 1 for p in range(n)]
    to_right = [(ring[p], ring[(p + 1) % n]) for p in range(n)]
    to_left = [(ring[(p + 1) % n], ring[p]) for p in range(n)]

    def pass_on(right, left):
        return lax.ppermute(right, "fact", to_right), lax.ppermute(left, "fact", to_left)

    def swap(block, bit):
        return lax.ppermute(block, "feat", [(i, i ^ bit) for i in range(m)])

    if ringed:
        right, left = pass_on(dim_table, dim_table)
    x_near = swap(fact_x, 1)
    by_lane = (chunks, LANES)
    columns = shape((facts, LANES), BF)
    asks, pos, entity, dlow, dhigh = call(
        functools.partial(route_kernel, n, cap, ents, dims),
        (
            shape((n, groups, LANES), jnp.int32),
            shape(by_lane, jnp.int32),
            shape(by_lane, jnp.int32),
            columns,
            columns,
        ),
        [pltpu.VMEM(by_lane, jnp.int32)] * 4 + [pltpu.SemaphoreType.DMA((4,))],
        1 << 28,
        "route",
        in_specs=[IN_HBM] * 4,
    )(dim_owner.reshape(by_lane), dim_slot.reshape(by_lane), fact_owner.reshape(by_lane), fact_slot.reshape(by_lane))
    if ringed:
        right, left, x_near, asks, pos, entity, dlow, dhigh = tie(
            (right, left, x_near, asks, pos, entity, dlow, dhigh)
        )

    def look(pieces, tables, base):
        rows = sum(t.shape[0] for t in tables)
        return call(
            functools.partial(look_kernel, n, pieces),
            shape((facts, LANES), F32),
            [pltpu.VMEM((step, rows), BF)],
            2 * facts * rows * LANES,
            "look",
            limit,
        )(dlow, dhigh, *tables, base)

    def project(blocks):
        return call(
            functools.partial(project_kernel, m), shape((facts, LANES), F32), [], 2 * facts * width * LANES, "project"
        )(w_msg, *blocks)

    found = jnp.zeros((facts, LANES), F32)
    weights = jnp.concatenate([w_self, w_neigh, entity_h, cotangent], axis=0)
    if ringed:
        near = (right, left)
        after = pass_on(*near)
        x_far = swap(fact_x, 2)
        found = look([(0, 0, dims), (-1, 0, dims), (1, 0, dims)], [dim_table, *near], found)
        right, left, x_far, found, weights = tie((*after, x_far, found, weights))
        for k in range(2, n // 2 - 1):
            after = pass_on(right, left)
            x_last = swap(x_far, 1)
            found = look([(-k, 0, dims), (k, 0, dims)], [right, left], found)
            right, left, found, x_last = tie((*after, found, x_last))
        all_far = swap(weights, 2)
        k = n // 2 - 1
        after = lax.ppermute(right, "fact", to_right)
        xw = project([fact_x, x_near, x_far, x_last])
        found = look([(k, 0, dims)], [left], found)
        found, asks = tie((found, asks))
        asked = lax.all_to_all(asks, "fact", 0, 0)
        found = look([(-k, 0, dims)], [right], found)
        all_near = swap(weights, 1)
        found, all_far, all_near = tie((found, all_far, all_near))
        last, last_pieces = [after], [(n // 2, 0, dims)]
    else:
        asked = lax.all_to_all(asks, "fact", 0, 0)
        x_far = swap(fact_x, 2)
        x_last = swap(x_far, 1)
        xw = project([fact_x, x_near, x_far, x_last])
        all_far, all_near = swap(weights, 2), swap(weights, 1)
        whole = lax.all_gather(dim_table, "fact")
        order = jnp.take(whole, ring_at(ring_place(lax.axis_index("fact"), n) + jnp.arange(n), n), axis=0)
        for k in range(0, n, 8):
            found = look([(k + i, 0, dims) for i in range(8)], [order[k + i] for i in range(8)], found)
        last, last_pieces = [], []
    all_last = swap(all_far, 1)
    x_blocks, all_blocks = [fact_x, x_near, x_far, x_last], [weights, all_near, all_far, all_last]
    last_rows = max(LANES, sum(t.shape[0] for t in last))
    slope, part = call(
        functools.partial(message_kernel, n, last_pieces),
        (pltpu.HBM((facts, LANES), F32), shape((n * ents, LANES), BF)),
        [
            pltpu.VMEM((facts, LANES), F32),
            pltpu.VMEM((facts // step, step, last_rows), BF),
            pltpu.VMEM((facts, LANES), BF),
            pltpu.VMEM((LANES, facts), BF),
            pltpu.VMEM((16, facts), BF),
            pltpu.VMEM((n * ents, LANES), BF),
            *[pltpu.VMEM(t.shape, BF) for t in last],
            pltpu.SemaphoreType.DMA,
            pltpu.SemaphoreType.DMA,
            pltpu.SemaphoreType.DMA((8,)),
        ],
        2 * facts * (last_rows + n * ents) * LANES,
        "message",
        limit,
        in_specs=[IN_VMEM] * 2 + [pl.BlockSpec(memory_space=pl.ANY)] * len(last) + [IN_VMEM] * 3,
        out_specs=(IN_HBM, IN_HBM),
    )(dlow, dhigh, *last, found, xw, entity)
    sums = lax.all_to_all(part.reshape(n * m, rows_each, LANES), ("fact", "feat"), 0, 0)
    pos, entity, x_blocks, _ = tie((pos, entity, x_blocks, part))
    hidden, x_turned = call(
        functools.partial(ready_kernel, m, width, ents),
        (shape((m, ents, LANES), BF), shape((width, facts), BF)),
        [],
        1 << 28,
        "ready",
    )(*x_blocks, *all_blocks)
    by_feat = shape((m, rows_each, LANES), BF)
    back, out_parts, pre_parts, agg_parts = call(
        functools.partial(entity_kernel, n, m, width, ents),
        (shape((n * m, rows_each, LANES), BF), by_feat, by_feat, shape((m * rows_each, LANES), BF)),
        [
            pltpu.VMEM((m, rows_each, LANES), BF),
            pltpu.VMEM((ents, LANES), F32),
            pltpu.VMEM(asked.shape, jnp.int32),
            pltpu.VMEM((m, rows_each, LANES), BF),
            pltpu.SemaphoreType.DMA,
            pltpu.SemaphoreType.DMA((n,)),
        ],
        6 * rows_each * width * width,
        "entity",
        in_specs=[IN_VMEM, pl.BlockSpec(memory_space=pl.ANY)] + [IN_VMEM] * m,
        out_specs=(IN_HBM, IN_VMEM, IN_VMEM, IN_VMEM),
    )(sums, asked, *all_blocks)
    scaled = lax.all_to_all(back, ("fact", "feat"), 0, 0).reshape(n * ents, LANES)
    shares = call(
        functools.partial(share_kernel, m),
        tuple(shape(((2 + m) * rows_each, LANES), BF) for _ in range(m)),
        [],
        1 << 20,
        "share",
    )(out_parts, pre_parts, agg_parts)
    got = [shares[0]] + [swap(shares[j], j) for j in range(1, m)]
    pos, entity, asked, _ = tie((pos, entity, asked, back))
    plow, phigh, elow, ehigh = call(
        codes_kernel,
        (shape((LANES, facts), BF), shape((16, facts), BF), columns, columns),
        [],
        1 << 26,
        "codes",
    )(pos, entity)
    rlow, rhigh = call(
        functools.partial(request_kernel, n, cap),
        (shape((LANES, slots), BF), shape((16, slots), BF)),
        [],
        1 << 26,
        "requests",
        limit,
    )(asked)
    pair_shape = (n // 2, 2 * stride, LANES)
    output_h, pair = call(
        functools.partial(weight_kernel, n, m, width, stride),
        (shape((ents, LANES), BF), shape((2, *pair_shape), F32)),
        [pltpu.VMEM((width, LANES), F32), pltpu.VMEM((ents, LANES), BF), pltpu.VMEM((m, ents, LANES), BF)],
        4 * ents * width * LANES,
        "weight",
    )(hidden, *got)
    if ringed:
        keep, give = call(halves_kernel, (shape(pair_shape, F32), shape(pair_shape, BF)), [], 1 << 20, "halves")(pair)
        pairs = [keep, lax.ppermute(give, "fact", [(i, i ^ 1) for i in range(n)])]
    else:
        pairs = [jnp.stack([pair[0], pair[1]], axis=1).reshape(n, 2 * stride, LANES)]
    d_msg, msg_share = call(
        functools.partial(backward_kernel, n, stride),
        (columns, shape((n, stride, LANES), BF)),
        [pltpu.VMEM((step, n * ents), BF), pltpu.VMEM((facts, LANES), F32), pltpu.SemaphoreType.DMA],
        2 * facts * (n * ents + width) * LANES,
        "backward",
        limit,
        in_specs=[IN_HBM] + [IN_VMEM] * 4,
    )(slope, scaled, elow, ehigh, x_turned)

    def spread(offsets):
        lengths = [cap + (3 if ringed and k % 2 == 0 else 1) * stride for k in offsets]
        return call(
            functools.partial(spread_kernel, n, cap, stride, offsets),
            tuple(shape((rows, LANES), BF) for rows in lengths),
            [],
            2 * facts * cap * LANES * len(offsets),
            "spread",
            limit,
        )(plow, phigh, d_msg, msg_share, *(pairs if max(lengths) > cap + stride else ()))

    def add_up(offsets, got, base, final):
        weight = shape((3 * stride, LANES), F32)
        scratch = [
            pltpu.VMEM((cap * len(got), LANES), BF),
            pltpu.VMEM((LANES, cap * len(got)), BF),
            pltpu.VMEM((16, cap * len(got)), BF),
        ]
        return call(
            functools.partial(table_kernel, n, cap, stride, offsets, base is None, final),
            (shape((dims, LANES), F32),) + ((shape((own, LANES), F32),) * 3 if final else (weight,)),
            scratch
            + (
                [
                    pltpu.VMEM(weight.shape, F32),
                    pltpu.VMEM((dims, LANES), F32),
                    pltpu.SemaphoreType.DMA((dims // LANES,)),
                    pltpu.SemaphoreType.DMA((3,)),
                ]
                if final
                else []
            ),
            2 * cap * dims * LANES * len(got),
            "table",
            limit,
            **(dict(out_specs=(IN_HBM,) * 4) if final else {}),
        )(rlow, rhigh, *got, *(base or ()))

    totals = None
    if ringed:
        messages = {}
        rest = [[k, n - k] for k in range(n // 2 - 1, 1, -1)]
        for offsets in [rest[0], [n // 2], [1, n - 1], *rest[1:]]:
            for offset, message in zip(offsets, spread(offsets)):
                messages[offset] = lax.ppermute(message, "fact", [(i, (i + offset) % n) for i in range(n)])
        messages[0] = spread([0])[0]
        for offsets in [[0, 1, n - 1], [n // 2], *rest[::-1]]:
            totals = add_up(offsets, [messages[k] for k in offsets], totals, offsets == rest[0])
        grad_dim, grad_msg, grad_self, grad_neigh = totals
    else:
        fact_me = lax.axis_index("fact")
        sent = [message for k in range(0, n, 8) for message in spread(list(range(k, k + 8)))]
        by_owner = jnp.take(jnp.stack(sent), lax.rem(jnp.arange(n) - fact_me + n, n), axis=0)
        owned = lax.all_to_all(by_owner, "fact", 0, 0)
        by_offset = jnp.take(owned, lax.rem(fact_me - jnp.arange(n) + n, n), axis=0)
        for k in range(0, n, 8):
            totals = add_up(list(range(k, k + 8)), [by_offset[k + i] for i in range(8)], totals, k + 8 >= n)
        grad_dim, grad_msg, _, _ = totals
        pair_sum = lax.psum_scatter(pairs[0], "fact", scatter_dimension=0, tiled=True)[0]
        grad_self, grad_neigh = pair_sum[0:own], pair_sum[stride : stride + own]
    return output_h, grad_msg, grad_self, grad_neigh, grad_dim


def solution(mesh):
    placed = (
        P("fact", "feat"),
        P("fact", None),
        P("fact"),
        P("fact", None),
        P("fact"),
        P("fact", "feat"),
        P("fact", "feat"),
        P(None, "feat"),
        P(None, "feat"),
        P(None, "feat"),
        P("fact", "feat"),
    )
    return jax.shard_map(
        shards,
        mesh=mesh,
        in_specs=placed,
        out_specs=(P("fact", "feat"),) * 5,
        check_vma=False,
    )
```

```python
import functools

import jax
import jax.numpy as jnp
from jax import lax
from jax.experimental import pallas as pl
from jax.experimental.pallas import tpu as pltpu
from jax.sharding import PartitionSpec as P

LANES = 128
BF = jnp.bfloat16
IN_HBM = pl.BlockSpec(memory_space=pltpu.HBM)
IN_VMEM = pl.BlockSpec(memory_space=pltpu.VMEM)
F32 = jnp.float32
VMEM_LIMIT = 10 * 1024 * 1024
VMEM_LIMIT_LARGE = 40 * 1024 * 1024


def call(kernel, out_shape, scratch, flops, name, limit=VMEM_LIMIT, **specs):
    return pl.pallas_call(
        kernel,
        out_shape=out_shape,
        scratch_shapes=scratch,
        compiler_params=pltpu.CompilerParams(vmem_limit_bytes=limit),
        cost_estimate=pl.CostEstimate(flops=flops, bytes_accessed=1 << 20, transcendentals=0),
        name=name,
        **specs,
    )


def shape(dims, dtype):
    return jax.ShapeDtypeStruct(dims, dtype)


def nt(a, b):
    return lax.dot_general(a, b, (((1,), (1,)), ((), ())), preferred_element_type=F32)


def tn(a, b):
    return lax.dot_general(a, b, (((0,), (0,)), ((), ())), preferred_element_type=F32)


def dot(a, b):
    return jnp.dot(a, b, preferred_element_type=F32)


def flag(condition):
    return jnp.where(condition, 1.0, 0.0).astype(BF)


def column_codes(row):
    keys = jnp.broadcast_to(row, (LANES, LANES)).astype(F32).T.astype(jnp.int32)
    lane = lax.broadcasted_iota(jnp.int32, (LANES, LANES), 1)
    return flag((keys & (LANES - 1)) == lane), (keys >> 7).astype(F32).astype(BF)


def row_codes(row):
    keys = jnp.broadcast_to(row, (LANES, LANES))
    sub = lax.broadcasted_iota(jnp.int32, (LANES, LANES), 0)
    high = jnp.broadcast_to((row >> 7).astype(F32), (16, LANES)).astype(BF)
    return flag((keys & (LANES - 1)) == sub), high


def pick_block(low, high, block):
    zero = jnp.zeros((), BF)
    return jnp.where(high == block, low, zero)


def pick_rows(low, high, block):
    wide = low.reshape(LANES // 16, 16, low.shape[1])
    picked = pick_block(wide, high[None], block)
    return picked.reshape(low.shape)


def route_kernel(n, cap, ents, dims, *refs):
    given, (out_ref, pos_ref, ent_ref, dlow_ref, dhigh_ref), held_refs, sems = refs[:4], refs[4:9], refs[9:13], refs[13]
    copies = [pltpu.make_async_copy(src, dst, sems.at[i]) for i, (src, dst) in enumerate(zip(given, held_refs))]
    for copy in copies:
        copy.start()
    for copy in copies:
        copy.wait()
    do_ref, ds_ref, fo_ref, fs_ref = held_refs
    chunks = do_ref.shape[0]
    owner = do_ref[...]
    kind = lax.broadcasted_iota(jnp.int32, (n, chunks, LANES), 0)
    held = jnp.where(kind == owner[None], 1.0, 0.0).reshape(n * chunks, LANES)
    held_bf = held.astype(BF)
    i0 = lax.broadcasted_iota(jnp.int32, (LANES, LANES), 0)
    i1 = lax.broadcasted_iota(jnp.int32, (LANES, LANES), 1)
    inside = dot(held_bf, flag(i0 < i1))
    r0 = lax.broadcasted_iota(jnp.int32, (n * chunks, n * chunks), 0)
    r1 = lax.broadcasted_iota(jnp.int32, (n * chunks, n * chunks), 1)
    earlier = flag((r0 // chunks == r1 // chunks) & (r1 < r0))
    before = dot(dot(earlier, held_bf).astype(BF), jnp.ones((LANES, LANES), BF))
    rank = jnp.sum((held * (inside + before)).reshape(n, chunks, LANES), axis=0)
    rank = rank.astype(jnp.int32)
    entity_owner = fo_ref[...]
    entity_slot = fs_ref[...]
    value = ds_ref[...]
    pos_ref[...] = owner * cap + rank
    ent_ref[...] = entity_owner * ents + entity_slot
    fact_dim = owner * dims + value
    high = (value >> 5).astype(F32)
    low = (value & 31).astype(F32)
    names = lax.broadcasted_iota(jnp.int32, (n, LANES), 0)
    places = lax.broadcasted_iota(jnp.int32, (cap, LANES), 0)
    slots = lax.broadcasted_iota(jnp.int32, (ents, LANES), 0)
    asked_high = jnp.zeros((n, cap), F32)
    asked_low = jnp.zeros((n, cap), F32)
    hits = jnp.zeros((n, ents), F32)
    for k in range(chunks):
        here = slice(k * LANES, (k + 1) * LANES)
        mine = jnp.where(names == owner[k : k + 1], 1.0, 0.0)
        at = flag(places == rank[k : k + 1])
        asked_high += nt((mine * high[k : k + 1]).astype(BF), at)
        asked_low += nt((mine * low[k : k + 1]).astype(BF), at)
        hits += nt(flag(names == entity_owner[k : k + 1]), flag(slots == entity_slot[k : k + 1]))
        dlow_ref[here, :], dhigh_ref[here, :] = column_codes(fact_dim[k : k + 1])
    asked = (asked_high * 32.0 + asked_low).astype(jnp.int32)
    for r in range(cap // LANES):
        out_ref[:, r, :] = asked[:, r * LANES : (r + 1) * LANES]
    out_ref[:, cap // LANES, :] = hits.astype(jnp.int32)


def fill_rows(low_ref, high_ref, rows, blocks, firsts, hot_ref):
    at = 0
    low, high = low_ref[rows, :], high_ref[rows, :]
    for count, first in zip(blocks, firsts):
        for k in range(count):
            hot_ref[:, at : at + LANES] = pick_block(low, high, (first + k).astype(F32).astype(BF))
            at += LANES


def multiply_rows(table_refs, hot_ref):
    total, at = None, 0
    for table in table_refs:
        part = dot(hot_ref[:, at : at + table.shape[0]], table[...])
        total = part if total is None else total + part
        at += table.shape[0]
    return total


def gather_rows(low_ref, high_ref, rows, table_refs, firsts, hot_ref):
    fill_rows(low_ref, high_ref, rows, [table.shape[0] // LANES for table in table_refs], firsts, hot_ref)
    return multiply_rows(table_refs, hot_ref)


def ring_at(place, n):
    place = lax.rem(place + 2 * n, n)
    return jnp.where(place < n // 2, 2 * place, 2 * (n - 1 - place) + 1)


def ring_place(index, n):
    half = lax.div(index, 2)
    return jnp.where(lax.rem(index, 2) == 0, half, n - 1 - half)


def look_kernel(n, pieces, low_ref, high_ref, *refs):
    count = len(pieces)
    tables, base_ref, out_ref, hot_ref = refs[:count], refs[count], refs[-2], refs[-1]
    facts = low_ref.shape[0]
    step = hot_ref.shape[0]
    place = ring_place(lax.axis_index("fact"), n)
    firsts = [lax.div(ring_at(place + hops, n) * dims + row, LANES) for hops, row, dims in pieces]
    for c in range(facts // step):
        rows = slice(c * step, (c + 1) * step)
        out_ref[rows, :] = base_ref[rows, :] + gather_rows(low_ref, high_ref, rows, tables, firsts, hot_ref)


def message_kernel(n, pieces, low_ref, high_ref, *refs):
    count = len(pieces)
    sources, refs = refs[:count], refs[count:]
    base_ref, xw_ref, ent_ref, slope_out, part_out, slope_ref, hot_ref, msg_ref, erlow_ref, erhigh_ref = refs[:10]
    part_ref, tables, (sem, table_sem, part_sem) = refs[10], refs[11 : 11 + count], refs[11 + count :]
    arrivals = [pltpu.make_async_copy(src, dst, table_sem) for src, dst in zip(sources, tables)]
    for copy in arrivals:
        copy.start()
    facts = low_ref.shape[0]
    step = hot_ref.shape[1]
    place = ring_place(lax.axis_index("fact"), n)
    firsts = [lax.div(ring_at(place + hops, n) * dims + row, LANES) for hops, row, dims in pieces]
    if count:
        for c in range(facts // step):
            rows = slice(c * step, (c + 1) * step)
            fill_rows(low_ref, high_ref, rows, [table.shape[0] // LANES for table in tables], firsts, hot_ref.at[c])
    for k in range(ent_ref.shape[0]):
        here = slice(k * LANES, (k + 1) * LANES)
        erlow_ref[:, here], erhigh_ref[:, here] = row_codes(ent_ref[k : k + 1, :])
    for copy in arrivals:
        copy.wait()
    for c in range(facts // step):
        rows = slice(c * step, (c + 1) * step)
        pre = xw_ref[rows, :] + base_ref[rows, :]
        if count:
            pre = pre + multiply_rows(tables, hot_ref.at[c])
        gate = jax.nn.sigmoid(pre)
        msg_ref[rows, :] = (pre * gate).astype(BF)
        slope_ref[rows, :] = gate * (1.0 + pre * (1.0 - gate))
    keep = pltpu.make_async_copy(slope_ref, slope_out, sem)
    keep.start()

    def add(pair, carry):
        hot = jnp.concatenate(
            [pick_rows(erlow_ref[...], erhigh_ref[...], (pair * 2 + i).astype(F32).astype(BF)) for i in range(2)], axis=0
        )
        rows = pl.ds(pl.multiple_of(pair * 256, 256), 256)
        part_ref[rows, :] = dot(hot, msg_ref[...]).astype(BF)
        return carry

    groups = part_ref.shape[0] // 256
    copies = [keep]
    if groups <= 8:
        for pair in range(groups):
            add(jnp.int32(pair), 0)
            rows = slice(pair * 256, (pair + 1) * 256)
            copies.append(pltpu.make_async_copy(part_ref.at[rows, :], part_out.at[rows, :], part_sem.at[pair]))
            copies[-1].start()
    else:
        lax.fori_loop(0, groups, add, 0)
        copies.append(pltpu.make_async_copy(part_ref, part_out, part_sem.at[0]))
        copies[-1].start()
    for copy in copies:
        copy.wait()


def project_kernel(m, w_ref, *refs):
    blocks, out_ref = refs[:m], refs[m]
    me = lax.axis_index("feat")
    total = None
    for j, ref in enumerate(blocks):
        rows = pl.ds(pl.multiple_of((me ^ j) * LANES, LANES), LANES)
        part = dot(ref[...], w_ref[rows, :])
        total = part if total is None else total + part
    out_ref[...] = total


def ready_kernel(m, width, ents, *refs):
    x_refs, all_refs, (hidden_ref, xt_ref) = refs[:m], refs[m : 2 * m], refs[2 * m :]
    me = lax.axis_index("feat")
    for j in range(m):
        hidden_ref[me ^ j] = all_refs[j][2 * width : 2 * width + ents, :]
        xt_ref[pl.ds(pl.multiple_of((me ^ j) * LANES, LANES), LANES), :] = x_refs[j][...].T


def entity_kernel(n, m, width, ents, sums_ref, idx_ref, *refs):
    all_refs, refs = refs[:m], refs[m:]
    back_ref, out_ref, pre_ref, agg_ref, own_ref, hold_ref, words_ref, scaled_ref, sem, back_sem = refs
    fetch = pltpu.make_async_copy(idx_ref, words_ref, sem)
    fetch.start()
    rows_each = ents // m
    me = lax.axis_index("feat")
    totals = []
    for b in range(m):
        total = sums_ref[b].astype(F32)
        for f in range(1, n):
            total += sums_ref[f * m + b].astype(F32)
        totals.append(total)
    fetch.wait()
    hits = jnp.sum(words_ref[:, words_ref.shape[1] - 1, :], axis=0, keepdims=True).astype(F32)
    hold_ref[...] = jnp.maximum(jnp.broadcast_to(hits, (LANES, ents)).T, 1.0)
    divisor = hold_ref[pl.ds(pl.multiple_of(me * rows_each, rows_each), rows_each), :]
    for b in range(m):
        agg_ref[b * rows_each : (b + 1) * rows_each, :] = (totals[b] / divisor).astype(BF)
    at = pl.multiple_of(2 * width + me * rows_each, rows_each)
    for j in range(m):
        own_ref[me ^ j] = all_refs[j][pl.ds(at, rows_each), :]
    aggregate = jnp.concatenate([agg_ref[b * rows_each : (b + 1) * rows_each, :] for b in range(m)], axis=1)
    both = jnp.concatenate([own_ref[b] for b in range(m)] + [aggregate], axis=1)
    d_agg = None
    for j in range(m):
        pre = dot(both, all_refs[j][0 : 2 * width, :])
        gate = jax.nn.sigmoid(pre)
        cot = all_refs[j][pl.ds(at + ents, rows_each), :].astype(F32)
        d_pre = (cot * (gate * (1.0 + pre * (1.0 - gate)))).astype(BF)
        out_ref[me ^ j] = (pre * gate).astype(BF)
        pre_ref[me ^ j] = d_pre
        term = nt(d_pre, all_refs[j][width : 2 * width, :])
        d_agg = term if d_agg is None else d_agg + term
    for b in range(m):
        scaled_ref[b] = (d_agg[:, b * LANES : (b + 1) * LANES] / divisor).astype(BF)
    copies = [
        pltpu.make_async_copy(scaled_ref, back_ref.at[f * m : (f + 1) * m], back_sem.at[f]) for f in range(n)
    ]
    for copy in copies:
        copy.start()
    for copy in copies:
        copy.wait()


def share_kernel(m, out_ref, pre_ref, agg_ref, *share_refs):
    rows_each = out_ref.shape[1]
    me = lax.axis_index("feat")
    for j, ref in enumerate(share_refs):
        ref[0:rows_each, :] = out_ref[me ^ j]
        ref[rows_each : 2 * rows_each, :] = pre_ref[me ^ j]
        ref[2 * rows_each :, :] = agg_ref[...]


def weight_kernel(n, m, width, stride, hidden_ref, *refs):
    got, (out_ref, back_ref, total_ref, pre_ref, agg_ref) = refs[:m], refs[m:]
    rows_each = got[0].shape[0] // (2 + m)
    own = width // n
    me = lax.axis_index("feat")
    for j, ref in enumerate(got):
        here = pl.ds(pl.multiple_of((me ^ j) * rows_each, rows_each), rows_each)
        out_ref[here, :] = ref[0:rows_each, :]
        pre_ref[here, :] = ref[rows_each : 2 * rows_each, :]
        for b in range(m):
            agg_ref[b, here, :] = ref[(2 + b) * rows_each : (3 + b) * rows_each, :]
    d_pre = pre_ref[...]
    for which, blocks in enumerate((hidden_ref, agg_ref)):
        for b in range(m):
            total_ref[b * LANES : (b + 1) * LANES, :] = tn(blocks[b], d_pre)
        for d in range(n):
            back_ref[d % 2, d // 2, which * stride : (which + 1) * stride, :] = padded(
                total_ref[d * own : (d + 1) * own, :], stride
            )


def halves_kernel(back_ref, keep_ref, give_ref):
    odd = lax.rem(lax.axis_index("fact"), 2)
    keep_ref[...] = back_ref[odd]
    give_ref[...] = back_ref[1 - odd].astype(BF)


def padded(piece, rows):
    if piece.shape[0] == rows:
        return piece
    return jnp.concatenate([piece, jnp.zeros((rows - piece.shape[0], LANES), F32)], axis=0)


def codes_kernel(pos_ref, ent_ref, plow_ref, phigh_ref, elow_ref, ehigh_ref):
    for k in range(pos_ref.shape[0]):
        here = slice(k * LANES, (k + 1) * LANES)
        plow_ref[:, here], phigh_ref[:, here] = row_codes(pos_ref[k : k + 1, :])
        elow_ref[here, :], ehigh_ref[here, :] = column_codes(ent_ref[k : k + 1, :])


def request_kernel(n, cap, req_ref, low_ref, high_ref):
    for s in range(n):
        for r in range(cap // LANES):
            at = s * cap + r * LANES
            low_ref[:, at : at + LANES], high_ref[:, at : at + LANES] = row_codes(req_ref[s, r : r + 1, :])


def backward_kernel(n, stride, slope_in, scaled_ref, low_ref, high_ref, xt_ref, dmsg_ref, share_ref, hot_ref, slope_ref, sem):
    fetch = pltpu.make_async_copy(slope_in, slope_ref, sem)
    fetch.start()
    facts = slope_ref.shape[0]
    own = xt_ref.shape[0] // n
    step = hot_ref.shape[0]
    for c in range(facts // step):
        rows = slice(c * step, (c + 1) * step)
        found = gather_rows(low_ref, high_ref, rows, [scaled_ref], [jnp.int32(0)], hot_ref)
        if c == 0:
            fetch.wait()
        dmsg_ref[rows, :] = (found * slope_ref[rows, :]).astype(BF)
    total = dot(xt_ref[...], dmsg_ref[...])
    for d in range(n):
        share_ref[d] = padded(total[d * own : (d + 1) * own, :], stride).astype(BF)


def spread_kernel(n, cap, stride, offsets, plow_ref, phigh_ref, dmsg_ref, share_ref, *refs):
    pair_refs, out_refs = refs[:-len(offsets)], refs[-len(offsets) :]
    me = lax.axis_index("fact")
    for offset, out_ref in zip(offsets, out_refs):
        d = lax.rem(me + offset, n)
        hot = jnp.concatenate(
            [
                pick_rows(plow_ref[...], phigh_ref[...], (d * (cap // LANES) + i).astype(F32).astype(BF))
                for i in range(cap // LANES)
            ],
            axis=0,
        )
        out_ref[0:cap, :] = dot(hot, dmsg_ref[...]).astype(BF)
        out_ref[cap : cap + stride, :] = share_ref[d]
        if out_ref.shape[0] > cap + stride:
            pair = pair_refs[0][lax.div(d, 2)]
            for ref in pair_refs[1:]:
                pair = pair + ref[lax.div(d, 2)].astype(F32)
            out_ref[cap + stride :, :] = pair.astype(BF)


def table_kernel(n, cap, stride, offsets, first, final, low_ref, high_ref, *refs):
    count = len(offsets)
    got, refs = refs[:count], refs[count:]
    if not first:
        (base_ref, weight_base_ref), refs = refs[:2], refs[2:]
    out_ref, refs = refs[0], refs[1:]
    final_refs, refs = (refs[:3], refs[3:]) if final else ((), refs[1:] + refs[:1])
    rows_ref, klow_ref, khigh_ref, weight_ref = refs[:4]
    me = lax.axis_index("fact")
    if first:
        weight_ref[...] = jnp.zeros(weight_ref.shape, F32)
    else:
        weight_ref[...] = weight_base_ref[...]
    for j, (offset, ref) in enumerate(zip(offsets, got)):
        source = lax.rem(me + (n - offset), n)
        here = slice(j * cap, (j + 1) * cap)
        there = pl.ds(pl.multiple_of(source * cap, LANES), cap)
        rows_ref[here, :] = ref[0:cap, :]
        klow_ref[:, here] = low_ref[:, there]
        khigh_ref[:, here] = high_ref[:, there]
        rows = ref.shape[0] - cap
        weight_ref[0:rows, :] += ref[cap:, :].astype(F32)
    copies = []
    for which, ref in enumerate(final_refs):
        copies.append(
            pltpu.make_async_copy(
                weight_ref.at[which * stride : which * stride + ref.shape[0], :], ref, refs[6].at[which]
            )
        )
        copies[-1].start()
    blocks = out_ref.shape[0] // LANES
    join = 2 if blocks % 2 == 0 else 1

    target_ref = refs[4] if final else out_ref
    for group in range(blocks // join):
        hot = jnp.concatenate(
            [pick_rows(klow_ref[...], khigh_ref[...], jnp.array(group * join + i, BF)) for i in range(join)], axis=0
        )
        rows = slice(group * join * LANES, (group + 1) * join * LANES)
        sums = dot(hot, rows_ref[...])
        target_ref[rows, :] = sums if first else base_ref[rows, :] + sums
        if final:
            copies.append(pltpu.make_async_copy(target_ref.at[rows, :], out_ref.at[rows, :], refs[5].at[group]))
            copies[-1].start()
    for copy in copies:
        copy.wait()


def shards(fact_x, dim_owner, dim_slot, fact_owner, fact_slot, dim_table, entity_h, w_msg, w_self, w_neigh, cotangent):
    n, m = lax.axis_size("fact"), lax.axis_size("feat")
    assert m == 4 and n % 2 == 0
    facts = fact_x.shape[0]
    chunks = facts // LANES
    ents = entity_h.shape[0]
    rows_each = ents // m
    width = w_msg.shape[0]
    dims = dim_table.shape[0]
    cap = -(-(3 * facts // n) // LANES) * LANES
    slots = n * cap
    groups = cap // LANES + 1
    own = width // n
    stride = max(16, own)
    step = 512
    tie = lax.optimization_barrier
    ringed = n <= 8
    limit = VMEM_LIMIT if ringed else VMEM_LIMIT_LARGE

    ring = [2 * p if p < n // 2 else 2 * (n - 1 - p) + 1 for p in range(n)]
    to_right = [(ring[p], ring[(p + 1) % n]) for p in range(n)]
    to_left = [(ring[(p + 1) % n], ring[p]) for p in range(n)]

    def pass_on(right, left):
        return lax.ppermute(right, "fact", to_right), lax.ppermute(left, "fact", to_left)

    def swap(block, bit):
        return lax.ppermute(block, "feat", [(i, i ^ bit) for i in range(m)])

    if ringed:
        right, left = pass_on(dim_table, dim_table)
    x_near = swap(fact_x, 1)
    by_lane = (chunks, LANES)
    columns = shape((facts, LANES), BF)
    asks, pos, entity, dlow, dhigh = call(
        functools.partial(route_kernel, n, cap, ents, dims),
        (
            shape((n, groups, LANES), jnp.int32),
            shape(by_lane, jnp.int32),
            shape(by_lane, jnp.int32),
            columns,
            columns,
        ),
        [pltpu.VMEM(by_lane, jnp.int32)] * 4 + [pltpu.SemaphoreType.DMA((4,))],
        1 << 28,
        "route",
        in_specs=[IN_HBM] * 4,
    )(dim_owner.reshape(by_lane), dim_slot.reshape(by_lane), fact_owner.reshape(by_lane), fact_slot.reshape(by_lane))
    if ringed:
        right, left, x_near, asks, pos, entity, dlow, dhigh = tie(
            (right, left, x_near, asks, pos, entity, dlow, dhigh)
        )

    def look(pieces, tables, base):
        rows = sum(t.shape[0] for t in tables)
        return call(
            functools.partial(look_kernel, n, pieces),
            shape((facts, LANES), F32),
            [pltpu.VMEM((step, rows), BF)],
            2 * facts * rows * LANES,
            "look",
            limit,
        )(dlow, dhigh, *tables, base)

    def project(blocks):
        return call(
            functools.partial(project_kernel, m), shape((facts, LANES), F32), [], 2 * facts * width * LANES, "project"
        )(w_msg, *blocks)

    found = jnp.zeros((facts, LANES), F32)
    weights = jnp.concatenate([w_self, w_neigh, entity_h, cotangent], axis=0)
    if ringed:
        near = (right, left)
        after = pass_on(*near)
        x_far = swap(fact_x, 2)
        found = look([(0, 0, dims), (-1, 0, dims), (1, 0, dims)], [dim_table, *near], found)
        right, left, x_far, found, weights = tie((*after, x_far, found, weights))
        for k in range(2, n // 2 - 1):
            after = pass_on(right, left)
            x_last = swap(x_far, 1)
            found = look([(-k, 0, dims), (k, 0, dims)], [right, left], found)
            right, left, found, x_last = tie((*after, found, x_last))
        all_far = swap(weights, 2)
        k = n // 2 - 1
        after = lax.ppermute(right, "fact", to_right)
        xw = project([fact_x, x_near, x_far, x_last])
        found = look([(k, 0, dims)], [left], found)
        found, asks = tie((found, asks))
        asked = lax.all_to_all(asks, "fact", 0, 0)
        found = look([(-k, 0, dims)], [right], found)
        all_near = swap(weights, 1)
        found, all_far, all_near = tie((found, all_far, all_near))
        last, last_pieces = [after], [(n // 2, 0, dims)]
    else:
        asked = lax.all_to_all(asks, "fact", 0, 0)
        x_far = swap(fact_x, 2)
        x_last = swap(x_far, 1)
        xw = project([fact_x, x_near, x_far, x_last])
        all_far, all_near = swap(weights, 2), swap(weights, 1)
        whole = lax.all_gather(dim_table, "fact")
        order = jnp.take(whole, ring_at(ring_place(lax.axis_index("fact"), n) + jnp.arange(n), n), axis=0)
        for k in range(0, n, 8):
            found = look([(k + i, 0, dims) for i in range(8)], [order[k + i] for i in range(8)], found)
        last, last_pieces = [], []
    all_last = swap(all_far, 1)
    x_blocks, all_blocks = [fact_x, x_near, x_far, x_last], [weights, all_near, all_far, all_last]
    last_rows = max(LANES, sum(t.shape[0] for t in last))
    slope, part = call(
        functools.partial(message_kernel, n, last_pieces),
        (pltpu.HBM((facts, LANES), F32), shape((n * ents, LANES), BF)),
        [
            pltpu.VMEM((facts, LANES), F32),
            pltpu.VMEM((facts // step, step, last_rows), BF),
            pltpu.VMEM((facts, LANES), BF),
            pltpu.VMEM((LANES, facts), BF),
            pltpu.VMEM((16, facts), BF),
            pltpu.VMEM((n * ents, LANES), BF),
            *[pltpu.VMEM(t.shape, BF) for t in last],
            pltpu.SemaphoreType.DMA,
            pltpu.SemaphoreType.DMA,
            pltpu.SemaphoreType.DMA((8,)),
        ],
        2 * facts * (last_rows + n * ents) * LANES,
        "message",
        limit,
        in_specs=[IN_VMEM] * 2 + [pl.BlockSpec(memory_space=pl.ANY)] * len(last) + [IN_VMEM] * 3,
        out_specs=(IN_HBM, IN_HBM),
    )(dlow, dhigh, *last, found, xw, entity)
    sums = lax.all_to_all(part.reshape(n * m, rows_each, LANES), ("fact", "feat"), 0, 0)
    pos, entity, x_blocks, _ = tie((pos, entity, x_blocks, part))
    hidden, x_turned = call(
        functools.partial(ready_kernel, m, width, ents),
        (shape((m, ents, LANES), BF), shape((width, facts), BF)),
        [],
        1 << 28,
        "ready",
    )(*x_blocks, *all_blocks)
    by_feat = shape((m, rows_each, LANES), BF)
    back, out_parts, pre_parts, agg_parts = call(
        functools.partial(entity_kernel, n, m, width, ents),
        (shape((n * m, rows_each, LANES), BF), by_feat, by_feat, shape((m * rows_each, LANES), BF)),
        [
            pltpu.VMEM((m, rows_each, LANES), BF),
            pltpu.VMEM((ents, LANES), F32),
            pltpu.VMEM(asked.shape, jnp.int32),
            pltpu.VMEM((m, rows_each, LANES), BF),
            pltpu.SemaphoreType.DMA,
            pltpu.SemaphoreType.DMA((n,)),
        ],
        6 * rows_each * width * width,
        "entity",
        in_specs=[IN_VMEM, pl.BlockSpec(memory_space=pl.ANY)] + [IN_VMEM] * m,
        out_specs=(IN_HBM, IN_VMEM, IN_VMEM, IN_VMEM),
    )(sums, asked, *all_blocks)
    scaled = lax.all_to_all(back, ("fact", "feat"), 0, 0).reshape(n * ents, LANES)
    shares = call(
        functools.partial(share_kernel, m),
        tuple(shape(((2 + m) * rows_each, LANES), BF) for _ in range(m)),
        [],
        1 << 20,
        "share",
    )(out_parts, pre_parts, agg_parts)
    got = [shares[0]] + [swap(shares[j], j) for j in range(1, m)]
    pos, entity, asked, _ = tie((pos, entity, asked, back))
    plow, phigh, elow, ehigh = call(
        codes_kernel,
        (shape((LANES, facts), BF), shape((16, facts), BF), columns, columns),
        [],
        1 << 26,
        "codes",
    )(pos, entity)
    rlow, rhigh = call(
        functools.partial(request_kernel, n, cap),
        (shape((LANES, slots), BF), shape((16, slots), BF)),
        [],
        1 << 26,
        "requests",
        limit,
    )(asked)
    pair_shape = (n // 2, 2 * stride, LANES)
    output_h, pair = call(
        functools.partial(weight_kernel, n, m, width, stride),
        (shape((ents, LANES), BF), shape((2, *pair_shape), F32)),
        [pltpu.VMEM((width, LANES), F32), pltpu.VMEM((ents, LANES), BF), pltpu.VMEM((m, ents, LANES), BF)],
        4 * ents * width * LANES,
        "weight",
    )(hidden, *got)
    if ringed:
        keep, give = call(halves_kernel, (shape(pair_shape, F32), shape(pair_shape, BF)), [], 1 << 20, "halves")(pair)
        pairs = [keep, lax.ppermute(give, "fact", [(i, i ^ 1) for i in range(n)])]
    else:
        pairs = [jnp.stack([pair[0], pair[1]], axis=1).reshape(n, 2 * stride, LANES)]
    d_msg, msg_share = call(
        functools.partial(backward_kernel, n, stride),
        (columns, shape((n, stride, LANES), BF)),
        [pltpu.VMEM((step, n * ents), BF), pltpu.VMEM((facts, LANES), F32), pltpu.SemaphoreType.DMA],
        2 * facts * (n * ents + width) * LANES,
        "backward",
        limit,
        in_specs=[IN_HBM] + [IN_VMEM] * 4,
    )(slope, scaled, elow, ehigh, x_turned)

    def spread(offsets):
        lengths = [cap + (3 if ringed and k % 2 == 0 else 1) * stride for k in offsets]
        return call(
            functools.partial(spread_kernel, n, cap, stride, offsets),
            tuple(shape((rows, LANES), BF) for rows in lengths),
            [],
            2 * facts * cap * LANES * len(offsets),
            "spread",
            limit,
        )(plow, phigh, d_msg, msg_share, *(pairs if max(lengths) > cap + stride else ()))

    def add_up(offsets, got, base, final):
        weight = shape((3 * stride, LANES), F32)
        scratch = [
            pltpu.VMEM((cap * len(got), LANES), BF),
            pltpu.VMEM((LANES, cap * len(got)), BF),
            pltpu.VMEM((16, cap * len(got)), BF),
        ]
        return call(
            functools.partial(table_kernel, n, cap, stride, offsets, base is None, final),
            (shape((dims, LANES), F32),) + ((shape((own, LANES), F32),) * 3 if final else (weight,)),
            scratch
            + (
                [
                    pltpu.VMEM(weight.shape, F32),
                    pltpu.VMEM((dims, LANES), F32),
                    pltpu.SemaphoreType.DMA((dims // LANES,)),
                    pltpu.SemaphoreType.DMA((3,)),
                ]
                if final
                else []
            ),
            2 * cap * dims * LANES * len(got),
            "table",
            limit,
            **(dict(out_specs=(IN_HBM,) * 4) if final else {}),
        )(rlow, rhigh, *got, *(base or ()))

    totals = None
    if ringed:
        messages = {}
        rest = [[k, n - k] for k in range(n // 2 - 1, 1, -1)]
        for offsets in [rest[0][:1], rest[0][1:], [n // 2], [1, n - 1], *rest[1:]]:
            for offset, message in zip(offsets, spread(offsets)):
                messages[offset] = lax.ppermute(message, "fact", [(i, (i + offset) % n) for i in range(n)])
        messages[0] = spread([0])[0]
        for offsets in [[0, 1, n - 1], [n // 2], *rest[::-1]]:
            totals = add_up(offsets, [messages[k] for k in offsets], totals, offsets == rest[0])
        grad_dim, grad_msg, grad_self, grad_neigh = totals
    else:
        fact_me = lax.axis_index("fact")
        sent = [message for k in range(0, n, 8) for message in spread(list(range(k, k + 8)))]
        by_owner = jnp.take(jnp.stack(sent), lax.rem(jnp.arange(n) - fact_me + n, n), axis=0)
        owned = lax.all_to_all(by_owner, "fact", 0, 0)
        by_offset = jnp.take(owned, lax.rem(fact_me - jnp.arange(n) + n, n), axis=0)
        for k in range(0, n, 8):
            totals = add_up(list(range(k, k + 8)), [by_offset[k + i] for i in range(8)], totals, k + 8 >= n)
        grad_dim, grad_msg, _, _ = totals
        pair_sum = lax.psum_scatter(pairs[0], "fact", scatter_dimension=0, tiled=True)[0]
        grad_self, grad_neigh = pair_sum[0:own], pair_sum[stride : stride + own]
    return output_h, grad_msg, grad_self, grad_neigh, grad_dim


def solution(mesh):
    placed = (
        P("fact", "feat"),
        P("fact", None),
        P("fact"),
        P("fact", None),
        P("fact"),
        P("fact", "feat"),
        P("fact", "feat"),
        P(None, "feat"),
        P(None, "feat"),
        P(None, "feat"),
        P("fact", "feat"),
    )
    return jax.shard_map(
        shards,
        mesh=mesh,
        in_specs=placed,
        out_specs=(P("fact", "feat"),) * 5,
        check_vma=False,
    )
```
